32 devices in a mesh: ctx: 8 (over y, x, core), wa: 4 (over z).
Axes of the slice: x: 2, y: 2, z: 4, core: 2. Of those that a mesh axis runs over, the one named last changes fastest.
Arguments:
- tokens: bfloat16 [4, 1024, 1152], P('wa', 'ctx'), may hold values from -6 to 6
- out_grad: bfloat16 [4, 1024, 1152], P('wa', 'ctx'), may hold values from -6 to 6
- doc_starts: int32 [4, 4], P('wa'), may hold values from 0 to 1023, as said below
- routes: int32 [4, 1024, 1], P('wa', 'ctx'), may hold values from 0 to 3; in each aligned block of 128 rows (0 to 127, 128 to 255, ..., all dimensions but the last counted through in order) at most 64 rows name the same one
- keep_mask: int32 [4, 1024], P('wa', 'ctx'), may hold values 0 or 1
- norm_mix: bfloat16 [1152], P('wa'), may hold values from 0.5 to 1.5
- w_in: bfloat16 [1152, 4608], P(None, 'wa'), may hold values from -0.1875 to 0.1875
- conv_w: bfloat16 [4, 2304], P(None, 'wa'), may hold values from -3 to 3
- conv_b: bfloat16 [2304], P('wa'), may hold values from -3 to 3
- w_x: bfloat16 [2304, 104], P('wa'), may hold values from -0.125 to 0.125
- w_dt: bfloat16 [72, 2304], P(None, 'wa'), may hold values from -0.75 to 0.75
- dt_bias: bfloat16 [2304], P('wa'), may hold values from -4 to 0
- a_log: bfloat16 [16, 2304], P(None, 'wa'), may hold values from -9 to 0
- d_skip: bfloat16 [2304], P('wa'), may hold values from 0.5 to 1.5
- w_out: bfloat16 [2304, 1152], P('wa'), may hold values from -0.125 to 0.125
- norm_moe: bfloat16 [1152], P('wa'), may hold values from 0.5 to 1.5
- w_router: bfloat16 [1152, 4], P('wa'), may hold values from -0.1875 to 0.1875
- w_up: bfloat16 [4, 1152, 3072], P('wa', None, 'ctx'), may hold values from -0.1875 to 0.1875
- w_down: bfloat16 [4, 3072, 1152], P('wa', 'ctx'), may hold values from -0.3125 to 0.3125
Outputs:
- layer_out: float32 [4, 1024, 1152], P('wa', 'ctx')
- input_grad: float32 [4, 1024, 1152], P('wa', 'ctx')
- grad_norm_mix: float32 [1152], P('wa')
- grad_w_in: float32 [1152, 4608], P(None, 'wa')
- grad_conv_w: float32 [4, 2304], P(None, 'wa')
- grad_conv_b: float32 [2304], P('wa')
- grad_w_x: float32 [2304, 104], P('wa')
- grad_w_dt: float32 [72, 2304], P(None, 'wa')
- grad_dt_bias: float32 [2304], P('wa')
- grad_a_log: float32 [16, 2304], P(None, 'wa')
- grad_d_skip: float32 [2304], P('wa')
- grad_w_out: float32 [2304, 1152], P('wa')
- grad_norm_moe: float32 [1152], P('wa')
- grad_w_router: float32 [1152, 4], P('wa')
- grad_w_up: float32 [4, 1152, 3072], P('wa', None, 'ctx')
- grad_w_down: float32 [4, 3072, 1152], P('wa', 'ctx')
- rms_stats: float32 [4, 3], P('wa')
The draws below stay inside these ranges and needn't reach their ends.
Inputs may be any that keep to these rules, and one draw needn't show every extreme that they name: `doc_starts`: each row holds 4 strictly ascending document starts, the first 0. `routes`: in each aligned block of 128 positions of a stream (the tokens of one device), no expert is named by more than 64 tokens.
All inputs are finite; a program needn't handle non-finite values. No bound on the sum of `keep_mask` on one device may be relied on, other than what follows from the above.
Results may differ from the reference program's by a relative error of at most 0.018.
Values may be sent and summed in bfloat16 or wider, within the bound.
A program may use at most 256 MiB of HBM per device.

```python
import math
import jax
import jax.numpy as jnp
import numpy as np
from jax import lax

D = 1152
DI = 2304
NS = 16
DTR = 72
KC = 4
FF = 3072
TOK_DEV = 128
EXPERTS = 4
CAP = 64
SEQ = 1024
STREAMS = 4
XW = 104


def draw_doc_starts(key, part):
    keys = jax.random.split(key, 3)
    early = jax.random.randint(keys[0], (STREAMS, 1), 1, TOK_DEV // 2)
    second = jax.random.randint(keys[1], (STREAMS, 1), TOK_DEV // 2, TOK_DEV)
    closing = jax.random.randint(keys[2], (STREAMS, 1), SEQ - TOK_DEV // 2, SEQ)
    opening = jnp.zeros((STREAMS, 1), jnp.int32)
    return jnp.concatenate([opening, early, second, closing], axis=1).astype(jnp.int32)


def with_ends(values, own_key, low, largest):
    dims = values.shape
    spot = [jax.random.randint(jax.random.fold_in(own_key, axis), (), 0, dims[axis]) for axis in range(len(dims))]
    values = values.at[tuple(spot)].set(low)
    longest = dims.index(max(dims))
    spot[longest] = (spot[longest] + 1) % dims[longest]
    return values.at[tuple(spot)].set(largest)


def steps_of(key, extent, cuts, least, top_value):
    factor_of = 1.0
    for position, blocks in cuts:
        draws = jax.random.uniform(jax.random.fold_in(jax.random.fold_in(key, 6), position), (blocks,), jnp.float32, least / len(cuts), top_value / len(cuts))
        factor_of = factor_of * jnp.repeat(jnp.exp(draws), extent[position] // blocks).reshape((-1,) + (1,) * (len(extent) - 1 - position))
    return factor_of


def deal_out(key, own, number, rows, number_of, top, reach, slope):
    ranking = jax.random.permutation(key, number_of)
    packed, common = load_shares(number_of, rows * top, reach, slope, True), load_shares(number_of, rows * top, reach, slope, False)
    places = jnp.arange(number_of)

    def named(tallies, offset_by):
        used = int((tallies > 0).sum())
        fixed = max(1, used // 4)
        moved = fixed + (places - fixed + offset_by * (used - fixed)) % max(1, number_of - fixed)
        return jnp.zeros((number_of,), jnp.int32).at[ranking[jnp.where(places < fixed, places, moved)]].set(jnp.asarray(tallies, jnp.int32))

    tallies = jnp.where(number % 4 == 0, named(packed, number // 4), named(common, number - number // 4 - 1))
    mixed = jax.random.permutation(jax.random.fold_in(own, 3), number_of)
    donor, sink = mixed[0:number_of // 2 * 2:2], mixed[1:number_of // 2 * 2:2]
    slack = jnp.minimum(tallies[donor] - 1, reach - tallies[sink]) // 2
    slack = jnp.where((donor == ranking[0]) | (sink == ranking[0]) | (tallies[sink] == 0), 0, jnp.maximum(slack, 0))
    moved = jax.random.randint(jax.random.fold_in(own, 4), (number_of // 2,), 0, 1 << 20) % (slack + 1)
    tallies = tallies.at[donor].add(-moved).at[sink].add(moved)
    items = jnp.searchsorted(jnp.cumsum(tallies), jnp.arange(rows * top), side="right").astype(jnp.int32)
    grid = items.reshape(top, rows).T
    grid = grid[jax.random.permutation(jax.random.fold_in(own, 1), rows)]
    offset_by = jax.random.randint(jax.random.fold_in(own, 2), (rows, 1), 0, top)
    return jnp.take_along_axis(grid, (jnp.arange(top)[None, :] + offset_by) % top, axis=1)


def load_shares(count, total, reach, slope, full):
    portions = [(1 << 20) // math.isqrt(grade ** slope) + 1 for grade in range(1, count + 1)]
    largest = reach if full else min(reach, max(-(-total // count), total * portions[0] // sum(portions)))
    least = 1 if total - largest >= count - 1 else 0
    holding, surplus = [largest] + [least] * (count - 1), total - largest - least * (count - 1)
    while surplus > 0:
        candidates = [i for i in range(1, count) if holding[i] < largest] or [i for i in range(1, count) if holding[i] < reach]
        pool, budget = sum([portions[i] for i in candidates]), surplus
        for i in candidates:
            more = min(reach - holding[i], max(1, budget * portions[i] // pool), surplus)
            holding[i] = holding[i] + more
            surplus = surplus - more
    return np.array(holding)


def scatter_about(key, extent, scale, bound, cuts=(), kind=jnp.bfloat16):
    factor_of = steps_of(key, extent, cuts, -0.22, 0.18) if cuts else 1.0
    entries = jax.random.normal(key, extent, jnp.float32) * scale * factor_of
    return jnp.minimum(jnp.maximum(entries, -bound), bound).astype(kind)


def setup_inputs(seed: int = 0) -> dict:
    streams_of = jax.random.split(jax.random.key(seed), 20)
    tokens = scatter_about(streams_of[0], (STREAMS, SEQ, D), 1.0, 6.0, ((0, 4), (1, 8)))
    out_grad = scatter_about(streams_of[1], (STREAMS, SEQ, D), 1.0, 6.0, ((0, 4), (1, 8)))
    doc_starts = draw_doc_starts(jax.random.fold_in(streams_of[19], 71), 0)
    routes_keys = jax.random.split(jax.random.fold_in(streams_of[3], 1), STREAMS * SEQ // TOK_DEV)
    routes_turns = jax.random.permutation(jax.random.fold_in(streams_of[3], 3), STREAMS * SEQ // TOK_DEV)
    routes = jax.vmap(lambda own, number: deal_out(jax.random.fold_in(streams_of[3], 2), own, number, TOK_DEV, EXPERTS, 1, CAP, 1))(routes_keys, routes_turns).reshape((STREAMS, SEQ, 1))
    keep_mask = with_ends((jax.random.randint(streams_of[4], (STREAMS, SEQ), 0, 8) < 7).astype(jnp.int32), jax.random.fold_in(streams_of[4], 1), 0, 1)
    norm_mix = jnp.clip(1.0 + 0.1 * jax.random.normal(streams_of[5], (D,), jnp.float32), 0.5, 1.5).astype(jnp.bfloat16)
    w_in = scatter_about(streams_of[6], (D, 2 * DI), D ** -0.5, 0.1875, ((1, 4),))
    conv_w = scatter_about(streams_of[7], (KC, DI), KC ** -0.5, 3.0, ((1, 4),))
    conv_b = scatter_about(streams_of[8], (DI,), 0.5, 3.0, ((0, 4),))
    w_x = scatter_about(streams_of[9], (DI, XW), DI ** -0.5, 0.125, ((0, 4),))
    w_dt = scatter_about(streams_of[10], (DTR, DI), DTR ** -0.5, 0.75, ((1, 4),))
    dt_bias = jnp.clip(-4.0 + 4.0 * jax.random.uniform(streams_of[11], (DI,), jnp.float32) ** steps_of(streams_of[11], (DI,), ((0, 4),), -0.2, 0.2), -4.0, 0.0).astype(jnp.bfloat16)
    a_log = jnp.clip(-9.0 + 9.0 * jax.random.uniform(streams_of[12], (NS, DI), jnp.float32) ** steps_of(streams_of[12], (NS, DI), ((1, 4),), -0.2, 0.2), -9.0, 0.0).astype(jnp.bfloat16)
    d_skip = jnp.clip(0.5 + 1.0 * jax.random.uniform(streams_of[13], (DI,), jnp.float32) ** steps_of(streams_of[13], (DI,), ((0, 4),), -0.2, 0.2), 0.5, 1.5).astype(jnp.bfloat16)
    w_out = scatter_about(streams_of[14], (DI, D), DI ** -0.5, 0.125, ((0, 4),))
    norm_moe = jnp.clip(1.0 + 0.1 * jax.random.normal(streams_of[15], (D,), jnp.float32), 0.5, 1.5).astype(jnp.bfloat16)
    w_router = scatter_about(streams_of[16], (D, EXPERTS), D ** -0.5, 0.1875, ((0, 4),))
    w_up = scatter_about(streams_of[17], (EXPERTS, D, FF), D ** -0.5, 0.1875, ((0, 4), (2, 8)))
    w_down = scatter_about(streams_of[18], (EXPERTS, FF, D), (FF // 8) ** -0.5, 0.3125, ((0, 4), (1, 8)))
    return {"tokens": tokens, "out_grad": out_grad, "doc_starts": doc_starts, "routes": routes, "keep_mask": keep_mask, "norm_mix": norm_mix, "w_in": w_in, "conv_w": conv_w, "conv_b": conv_b, "w_x": w_x, "w_dt": w_dt, "dt_bias": dt_bias, "a_log": a_log, "d_skip": d_skip, "w_out": w_out, "norm_moe": norm_moe, "w_router": w_router, "w_up": w_up, "w_down": w_down}


EPS = 1e-05
HIGH = lax.Precision.HIGHEST

@jax.custom_vjp
def low(v):
    return lax.optimization_barrier(v.astype(jnp.bfloat16)).astype(jnp.float32)

@jax.custom_vjp
def low_back(v):
    return v

def low_keep(v):
    return (low(v), None)

def low_pass(kept, grad):
    return (grad,)

def back_keep(v):
    return (v, None)

def back_low(kept, grad):
    return (low(grad),)
low.defvjp(low_keep, low_pass)
low_back.defvjp(back_keep, back_low)

def matmul(left, right):
    return jnp.dot(left, right, precision=HIGH, preferred_element_type=jnp.float32)

def normed(values, gain):
    scale = lax.rsqrt(lax.optimization_barrier(jnp.mean(values * values, axis=-1, keepdims=True)) + EPS)
    return values * scale * gain

def mixer_scan(step_size, inputs, b_sel, c_sel, keeps, a_mat):
    length = step_size.shape[0]
    block = math.gcd(128, length)
    count = length // block

    def token_step(state, pieces):
        step_t, input_t, b_t, c_t, keep_t = pieces
        state = jnp.exp(step_t[None, :] * a_mat) * keep_t * state + b_t[:, None] * (step_t * input_t)[None, :]
        return (state, lax.optimization_barrier(jnp.sum(c_t[:, None] * state, axis=0)))

    def block_step(state, pieces):
        return lax.scan(token_step, state, pieces)
    pieces = tuple((array.reshape((count, block) + array.shape[1:]) for array in (step_size, inputs, b_sel, c_sel, keeps)))
    _, outputs = lax.scan(jax.checkpoint(block_step), jnp.zeros(a_mat.shape, jnp.float32), pieces)
    return outputs.reshape(length, -1)

def expert_block(normed_rows, route_rows, w_up, w_down):
    length = route_rows.shape[0]
    experts = w_up.shape[0]
    capacity = CAP
    onehot = (route_rows[:, None] == jnp.arange(experts, dtype=jnp.int32)[None, :]).astype(jnp.int32)
    before = jnp.cumsum(onehot, axis=0) - onehot
    within = lax.optimization_barrier(jnp.sum(before * onehot, axis=1))
    slot = route_rows * capacity + within
    match = slot[None, :] == jnp.arange(experts * capacity, dtype=jnp.int32)[:, None]
    filled = jnp.any(match, axis=1).astype(jnp.float32)
    source = lax.optimization_barrier(jnp.sum(match.astype(jnp.int32) * jnp.arange(length, dtype=jnp.int32)[None, :], axis=1)).astype(jnp.int32)
    sent = low_back(normed_rows[source] * filled[:, None]).reshape(experts, capacity, -1)
    hidden_pre = low_back(jnp.einsum('ecd,edf->ecf', sent, w_up, precision=HIGH))
    activated = low(jax.nn.gelu(hidden_pre))
    produced = low(low_back(jnp.einsum('ecf,efd->ecd', activated, w_down, precision=HIGH)))
    return produced.reshape(experts * capacity, -1)[slot]

def stream_forward(x_rows, starts, route_row, mask_row, params):
    norm_mix, w_in, conv_w, conv_b, w_x, w_dt, dt_bias, a_log, d_skip, w_out, norm_moe, w_router, w_up, w_down = params
    length = x_rows.shape[0]
    inner = w_in.shape[1] // 2
    taps = conv_w.shape[0]
    ranked = w_dt.shape[0]
    states = a_log.shape[0]
    place = jnp.arange(length, dtype=jnp.int32)
    resets = jnp.any(place[:, None] == starts[None, :], axis=1)
    keeps = 1.0 - resets.astype(jnp.float32)
    normed_mix = low(normed(x_rows, norm_mix))
    joined = low_back(low(matmul(normed_mix, w_in)))
    x_inner = joined[:, :inner]
    gate_z = joined[:, inner:]
    padded = jnp.pad(x_inner, ((taps - 1, 0), (0, 0)))
    pre_conv = conv_b + conv_w[0] * x_inner
    for offset in range(1, taps):
        cut = jnp.any((starts[None, :] > place[:, None] - offset) & (starts[None, :] <= place[:, None]), axis=1)
        lag_keep = 1.0 - cut.astype(jnp.float32)
        pre_conv = pre_conv + conv_w[offset] * padded[taps - 1 - offset:taps - 1 - offset + length] * lag_keep[:, None]
    mixed = low(jax.nn.silu(pre_conv))
    projected = low_back(low(matmul(mixed, w_x)))
    dt_low = projected[:, :ranked]
    b_sel = projected[:, ranked:ranked + states]
    c_sel = projected[:, ranked + states:]
    step_pre = low_back(matmul(dt_low, w_dt)) + dt_bias
    step_size = jax.nn.softplus(step_pre)
    a_mat = -jnp.exp(a_log)
    scanned = mixer_scan(step_size, mixed, b_sel, c_sel, keeps, a_mat)
    y_full = scanned + d_skip * mixed
    gated = low(y_full * jax.nn.silu(gate_z))
    mix = low_back(matmul(gated, w_out))
    after_mix = x_rows + mix
    normed_moe = low(normed(after_mix, norm_moe))
    logits = low_back(matmul(normed_moe, w_router))
    experts = logits.shape[1]
    onehot = (route_row[:, None] == jnp.arange(experts, dtype=jnp.int32)[None, :]).astype(jnp.float32)
    gates = mask_row * jax.nn.sigmoid(lax.optimization_barrier(jnp.sum(logits * onehot, axis=1)))
    blocks = length // TOK_DEV

    def one_block(pieces):
        return expert_block(pieces[0], pieces[1], w_up, w_down)
    expert_rows = lax.map(jax.checkpoint(one_block), (normed_moe.reshape(blocks, TOK_DEV, -1), route_row.reshape(blocks, TOK_DEV)))
    moe = gates[:, None] * expert_rows.reshape(length, -1)
    return (after_mix + moe, mix, moe)

def reference(tokens, out_grad, doc_starts, routes, keep_mask, norm_mix, w_in, conv_w, conv_b, w_x, w_dt, dt_bias, a_log, d_skip, w_out, norm_moe, w_router, w_up, w_down):
    weights = tuple((array.astype(jnp.float32) for array in (norm_mix, w_in, conv_w, conv_b, w_x, w_dt, dt_bias, a_log, d_skip, w_out, norm_moe, w_router, w_up, w_down)))
    route_rows = routes[:, :, 0]
    mask_rows = keep_mask.astype(jnp.float32)

    def forward(inputs, params):

        def one_stream(pieces):
            return stream_forward(pieces[0], pieces[1], pieces[2], pieces[3], params)
        return lax.map(jax.checkpoint(one_stream), (inputs, doc_starts, route_rows, mask_rows))
    (layer_out, mix, moe), pullback = jax.vjp(forward, tokens.astype(jnp.float32), weights)
    d_tokens, grads = pullback((out_grad.astype(jnp.float32), jnp.zeros_like(mix), jnp.zeros_like(moe)))
    stats = jnp.stack([jnp.sqrt(lax.optimization_barrier(jnp.mean(layer_out * layer_out, axis=(1, 2)))), jnp.sqrt(lax.optimization_barrier(jnp.mean(mix * mix, axis=(1, 2)))), jnp.sqrt(lax.optimization_barrier(jnp.mean(moe * moe, axis=(1, 2))))], axis=1)
    return (layer_out, d_tokens, grads[0], grads[1], grads[2], grads[3], grads[4], grads[5], grads[6], grads[7], grads[8], grads[9], grads[10], grads[11], grads[12], grads[13], stats)
```

```python
import functools

import jax
import jax.numpy as jnp
from jax import lax
from jax.experimental import pallas as pl
from jax.experimental.pallas import tpu as pltpu
from jax.sharding import PartitionSpec as P

EPS = 1e-05
F32 = jnp.float32
BF16 = jnp.bfloat16
SEG = 8
LANE = 128
CUT = 1e30
MESH = pl.DeviceIdType.MESH
VMEM_LIMIT = 48 * 2**20


def greet(axis, count):
    me = lax.axis_index(axis)
    barrier = pltpu.get_barrier_semaphore()
    for k in range(1, count):
        pl.semaphore_signal(
            barrier, inc=1, device_id={axis: lax.rem(me + k, count)}, device_id_type=MESH
        )
    pl.semaphore_wait(barrier, count - 1)
    return me


def gather_kernel(axis, count, x_ref, o_ref, send, recv, own):
    me = greet(axis, count)
    copies = []
    for k in range(1, count):
        copy = pltpu.make_async_remote_copy(
            src_ref=x_ref,
            dst_ref=o_ref.at[me],
            send_sem=send.at[k],
            recv_sem=recv.at[k],
            device_id={axis: lax.rem(me + k, count)},
            device_id_type=MESH,
        )
        copy.start()
        copies.append(copy)
    local = pltpu.make_async_copy(x_ref, o_ref.at[me], own)
    local.start()
    local.wait()
    for copy in copies:
        copy.wait()


def trade_kernel(axis, count, x_ref, o_ref, send, recv, own):
    me = greet(axis, count)
    copies = []
    for k in range(1, count):
        other = lax.rem(me + k, count)
        copy = pltpu.make_async_remote_copy(
            src_ref=x_ref.at[other],
            dst_ref=o_ref.at[me],
            send_sem=send.at[k],
            recv_sem=recv.at[k],
            device_id={axis: other},
            device_id_type=MESH,
        )
        copy.start()
        copies.append(copy)
    local = pltpu.make_async_copy(x_ref.at[me], o_ref.at[me], own)
    local.start()
    local.wait()
    for copy in copies:
        copy.wait()


def exchange(kernel, x, out_shape, axis, cid):
    count = lax.axis_size(axis)
    return pl.pallas_call(
        functools.partial(kernel, axis, count),
        out_shape=jax.ShapeDtypeStruct(out_shape, x.dtype),
        in_specs=[pl.BlockSpec(memory_space=pl.ANY)],
        out_specs=pl.BlockSpec(memory_space=pl.ANY),
        scratch_shapes=[
            pltpu.SemaphoreType.DMA((count,)),
            pltpu.SemaphoreType.DMA((count,)),
            pltpu.SemaphoreType.DMA,
        ],
        compiler_params=pltpu.CompilerParams(collective_id=cid, has_side_effects=True),
    )(x)


def gather_all(x, axis, cid):
    return exchange(gather_kernel, x, (lax.axis_size(axis),) + x.shape, axis, cid)


def trade(x, axis, cid):
    return exchange(trade_kernel, x, x.shape, axis, cid)


def spread(rows, states):
    shape = (states, states * LANE)
    line = lax.broadcasted_iota(jnp.int32, shape, 0)
    place = lax.broadcasted_iota(jnp.int32, shape, 1)
    lower = line * LANE
    pick = jnp.where((place >= lower) & (place < lower + LANE), 1.0, 0.0).astype(BF16)
    return jnp.dot(rows, pick, preferred_element_type=F32)


def rolled(value, by):
    return pltpu.roll(value, by % SEG, 0)


def lanes_of(g):
    return pl.ds(pl.multiple_of(g * LANE, LANE), LANE)


def rows_of(j):
    return pl.ds(pl.multiple_of(j * SEG, SEG), SEG)


def wide(ref, n, lanes):
    return jnp.broadcast_to(ref[pl.ds(n, 1), lanes], (SEG, LANE))


def state_cols(n):
    return slice(n * LANE, (n + 1) * LANE)


def summary_kernel(states, steps, groups, st_ref, dr_ref, b_ref, a_ref, hx_ref, sx_ref, hd_ref, sd_ref, bb):
    bb[...] = spread(b_ref[0], states)
    zero = jnp.zeros((SEG, LANE), F32)
    seg = lax.broadcasted_iota(jnp.int32, (SEG, LANE), 0)

    def group(g, _):
        lanes = lanes_of(g)
        a = [wide(a_ref, n, lanes) for n in range(states)]

        def step(j, carry):
            rows = rows_of(j)
            st = st_ref[0, rows, lanes]
            dr = dr_ref[0, rows, lanes]
            new = [carry[0] + st]
            for n in range(states):
                new.append(jnp.exp(st * a[n]) * carry[n + 1] + bb[rows, state_cols(n)] * dr)
            return tuple(new)

        out = lax.fori_loop(0, steps, step, (zero,) * (states + 1), unroll=2)
        total, h = out[0], list(out[1:])
        for k in (1, 2, 4):
            ok = seg >= k
            for n in range(states):
                h[n] = h[n] + jnp.where(ok, jnp.exp(total * a[n]) * rolled(h[n], k), 0.0)
            total = total + jnp.where(ok, rolled(total, k), 0.0)
        ok = seg >= 1
        sx_ref[0, :, lanes] = jnp.where(ok, rolled(total, 1), 0.0)
        sd_ref[0, :, lanes] = total[SEG - 1 : SEG]
        for n in range(states):
            hx_ref[0, n, :, lanes] = jnp.where(ok, rolled(h[n], 1), 0.0)
            hd_ref[0, pl.ds(n, 1), lanes] = h[n][SEG - 1 : SEG]
        return 0

    lax.fori_loop(0, groups, group, 0)


def output_kernel(states, steps, groups, st_ref, dr_ref, b_ref, c_ref, a_ref, hx_ref, sx_ref, e_ref, y_ref, bb, cb):
    bb[...] = spread(b_ref[0], states)
    cb[...] = spread(c_ref[0], states)

    def group(g, _):
        lanes = lanes_of(g)
        a = [wide(a_ref, n, lanes) for n in range(states)]
        sx = sx_ref[0, :, lanes]
        start = tuple(
            jnp.exp(sx * a[n]) * wide(e_ref.at[0], n, lanes) + hx_ref[0, n, :, lanes]
            for n in range(states)
        )

        def step(j, h):
            rows = rows_of(j)
            st = st_ref[0, rows, lanes]
            dr = dr_ref[0, rows, lanes]
            new = []
            y = None
            for n in range(states):
                state = jnp.exp(st * a[n]) * h[n] + bb[rows, state_cols(n)] * dr
                new.append(state)
                part = cb[rows, state_cols(n)] * state
                y = part if y is None else y + part
            y_ref[0, rows, lanes] = y
            return tuple(new)

        lax.fori_loop(0, steps, step, start, unroll=2)
        return 0

    lax.fori_loop(0, groups, group, 0)


def back_summary_kernel(states, steps, groups, st_ref, c_ref, dy_ref, a_ref, fx_ref, sx_ref, fd_ref, cb):
    cb[...] = spread(c_ref[0], states)
    zero = jnp.zeros((SEG, LANE), F32)
    seg = lax.broadcasted_iota(jnp.int32, (SEG, LANE), 0)

    def group(g, _):
        lanes = lanes_of(g)
        a = [wide(a_ref, n, lanes) for n in range(states)]

        def step(lap, carry):
            rows = rows_of(steps - 1 - lap)
            st = st_ref[0, rows, lanes]
            dy = dy_ref[0, rows, lanes]
            new = [carry[0] + st]
            for n in range(states):
                new.append(jnp.exp(st * a[n]) * (carry[n + 1] + cb[rows, state_cols(n)] * dy))
            return tuple(new)

        out = lax.fori_loop(0, steps, step, (zero,) * (states + 1), unroll=2)
        total, f = out[0], list(out[1:])
        for k in (1, 2, 4):
            ok = seg < SEG - k
            for n in range(states):
                f[n] = f[n] + jnp.where(ok, jnp.exp(total * a[n]) * rolled(f[n], -k), 0.0)
            total = total + jnp.where(ok, rolled(total, -k), 0.0)
        ok = seg < SEG - 1
        sx_ref[0, :, lanes] = jnp.where(ok, rolled(total, -1), 0.0)
        for n in range(states):
            fx_ref[0, n, :, lanes] = jnp.where(ok, rolled(f[n], -1), 0.0)
            fd_ref[0, pl.ds(n, 1), lanes] = f[n][0:1]
        return 0

    lax.fori_loop(0, groups, group, 0)


def back_kernel(
    states, steps, groups,
    st_ref, dr_ref, u_ref, b_ref, c_ref, dy_ref, a_ref, hx_ref, sx_ref, e_ref, fx_ref, tx_ref, o_ref,
    ds_ref, dd_ref, gb_ref, gc_ref, ga_ref,
    bb, cb, dec, pri, accb, accc,
):
    bb[...] = spread(b_ref[0], states)
    cb[...] = spread(c_ref[0], states)
    accb[...] = jnp.zeros_like(accb)
    accc[...] = jnp.zeros_like(accc)

    @pl.when(pl.program_id(0) == 0)
    def _():
        ga_ref[...] = jnp.zeros_like(ga_ref)

    def group(g, _):
        lanes = lanes_of(g)
        a = [wide(a_ref, n, lanes) for n in range(states)]
        sx = sx_ref[0, :, lanes]
        start = tuple(
            jnp.exp(sx * a[n]) * wide(e_ref.at[0], n, lanes) + hx_ref[0, n, :, lanes]
            for n in range(states)
        )

        def ahead(j, h):
            rows = rows_of(j)
            st = st_ref[0, rows, lanes]
            dr = dr_ref[0, rows, lanes]
            new = []
            for n in range(states):
                decay = jnp.exp(st * a[n])
                dec[rows, state_cols(n)] = decay
                pri[rows, state_cols(n)] = h[n]
                new.append(decay * h[n] + bb[rows, state_cols(n)] * dr)
            return tuple(new)

        last = lax.fori_loop(0, steps, ahead, start, unroll=2)
        end = rows_of(steps)
        for n in range(states):
            pri[end, state_cols(n)] = last[n]
        tx = tx_ref[0, :, lanes]
        flow = tuple(
            jnp.exp(tx * a[n]) * wide(o_ref.at[0], n, lanes) + fx_ref[0, n, :, lanes]
            for n in range(states)
        )

        def back(lap, f):
            j = steps - 1 - lap
            rows = rows_of(j)
            after = rows_of(j + 1)
            st = st_ref[0, rows, lanes]
            dr = dr_ref[0, rows, lanes]
            dy = dy_ref[0, rows, lanes]
            u = u_ref[0, rows, lanes]
            true_step = jnp.where(st >= 0.5 * CUT, 0.0, st)
            new = []
            d_step = None
            d_drive = None
            for n in range(states):
                cols = state_cols(n)
                d = f[n] + cb[rows, cols] * dy
                accc[rows, cols] += pri[after, cols] * dy
                accb[rows, cols] += d * dr
                flowing = dec[rows, cols] * d
                new.append(flowing)
                d_log = flowing * pri[rows, cols]
                ga_ref[n, :, lanes] += d_log * true_step
                part = d_log * a[n]
                d_step = part if d_step is None else d_step + part
                part = d * bb[rows, cols]
                d_drive = part if d_drive is None else d_drive + part
            ds_ref[0, rows, lanes] = d_step + d_drive * u
            dd_ref[0, rows, lanes] = d_drive
            return tuple(new)

        lax.fori_loop(0, steps, back, flow, unroll=2)
        return 0

    lax.fori_loop(0, groups, group, 0)
    shape = (states * LANE, states)
    line = lax.broadcasted_iota(jnp.int32, shape, 0)
    lower = lax.broadcasted_iota(jnp.int32, shape, 1) * LANE
    pick = jnp.where((line >= lower) & (line < lower + LANE), 1.0, 0.0)
    gb_ref[0] = jnp.dot(accb[...], pick, precision=lax.Precision.HIGHEST, preferred_element_type=F32)
    gc_ref[0] = jnp.dot(accc[...], pick, precision=lax.Precision.HIGHEST, preferred_element_type=F32)


def per_stream(shape):
    rest = len(shape) - 1
    return pl.BlockSpec((1,) + shape[1:], lambda s: (s,) + (0,) * rest)


def whole(shape):
    return pl.BlockSpec(shape, lambda s: (0,) * len(shape))


def scan_call(kernel, name, args, shared, outs, shared_outs, scratch, flops):
    ordered = []
    specs = []
    for arg in args:
        if isinstance(arg, int):
            ordered.append(shared[arg])
            specs.append(whole(shared[arg].shape))
        else:
            ordered.append(arg)
            specs.append(per_stream(arg.shape))
    streams = args[0].shape[0]
    moved = sum(a.size * a.dtype.itemsize for a in ordered)
    return pl.pallas_call(
        kernel,
        grid=(streams,),
        out_shape=[jax.ShapeDtypeStruct(s, F32) for s in outs + shared_outs],
        in_specs=specs,
        out_specs=[per_stream(s) for s in outs] + [whole(s) for s in shared_outs],
        scratch_shapes=scratch,
        compiler_params=pltpu.CompilerParams(vmem_limit_bytes=VMEM_LIMIT),
        cost_estimate=pl.CostEstimate(flops=flops, bytes_accessed=moved, transcendentals=flops // 10),
        name=name,
    )(*ordered)


def rms_scale(values):
    return lax.rsqrt(jnp.mean(values * values, axis=-1, keepdims=True) + EPS)


def norm_grads(values, scale, gain, d_out):
    unit = values * scale
    d_unit = d_out * gain
    d_values = scale * (d_unit - unit * jnp.mean(d_unit * unit, axis=-1, keepdims=True))
    return d_values, d_out * unit


def interleaved(rows):
    length = rows.shape[0]
    folded = rows.reshape((SEG, length // SEG) + rows.shape[1:])
    return jnp.swapaxes(folded, 0, 1).reshape(rows.shape)


def in_order(rows):
    length = rows.shape[0]
    folded = rows.reshape((length // SEG, SEG) + rows.shape[1:])
    return jnp.swapaxes(folded, 0, 1).reshape(rows.shape)


def silu_slope(v):
    s = jax.nn.sigmoid(v)
    return s * (1.0 + v * (1.0 - s))


def padded_lanes(array, width, axis):
    pads = [(0, 0)] * array.ndim
    pads[axis] = (0, width - array.shape[axis])
    return jnp.pad(array, pads)


def shift_pairs(group):
    half = group // 2
    first = [(v, 2 * v) if v < half else (v, 2 * (v - half) + 1) for v in range(group)]
    second = [(v, 2 * v + 1) if v < half else (v, 2 * (v - half)) for v in range(group)]
    return first, second


def body(
    tokens, out_grad, doc_starts, routes, keep_mask, norm_mix, w_in, conv_w, conv_b, w_x, w_dt,
    dt_bias, a_log, d_skip, w_out, norm_moe, w_router, w_up, w_down,
):
    group = lax.axis_size("wa")
    ring = lax.axis_size("ctx")
    mine = lax.axis_index("wa")
    place = lax.axis_index("ctx")
    length, width = tokens.shape[1:]
    taps, local = conv_w.shape
    states = a_log.shape[0]
    ranked = w_dt.shape[0]
    experts = w_router.shape[1]
    padded = -(-local // LANE) * LANE
    lane_groups = padded // LANE
    steps = length // SEG
    total_rows = group * length
    edge = taps - 1

    first, second = shift_pairs(group)
    rows_in = width // ring
    part_in = lax.dynamic_slice_in_dim(w_in, place * rows_in, rows_in, 0)
    low_half, high_half = part_in[:, :local], part_in[:, local:]
    upper = mine >= group // 2
    came_a = lax.ppermute(jnp.where(upper, high_half, low_half), "wa", first)
    came_b = lax.ppermute(jnp.where(upper, low_half, high_half), "wa", second)
    odd = mine % 2 == 1
    both = jnp.concatenate(
        [
            padded_lanes(jnp.where(odd, came_b, came_a), padded, 1),
            padded_lanes(jnp.where(odd, came_a, came_b), padded, 1),
        ],
        axis=1,
    )
    proj_in = lax.all_gather(both, "ctx", axis=0, tiled=True)

    up_rows, down_rows, proj_in = lax.optimization_barrier((w_up[0].T, w_down[0], proj_in))
    expert_up = lax.all_gather(up_rows, "ctx", axis=0, tiled=True)
    expert_down = lax.all_gather(down_rows, "ctx", axis=0, tiled=True)

    at = place * length + lax.iota(jnp.int32, length)
    starts = doc_starts[0]
    resets = jnp.any(at[:, None] == starts[None, :], axis=1)
    marks = [resets]
    for lag in range(1, taps):
        cut = jnp.any(
            (starts[None, :] > at[:, None] - lag) & (starts[None, :] <= at[:, None]), axis=1
        )
        marks.append(~cut)
    marks = interleaved(jnp.stack(marks, axis=1).astype(BF16))
    small = jnp.concatenate(
        [norm_mix, norm_moe, w_router.reshape(-1), marks.reshape(-1)], axis=0
    )
    smalls = lax.all_gather(small, "wa")
    share = norm_mix.shape[0]
    gain_mix = smalls[:, :share].reshape(-1).astype(F32)
    gain_moe = smalls[:, share : 2 * share].reshape(-1).astype(F32)
    router = smalls[:, 2 * share : (2 + experts) * share].reshape(width, experts)
    masks = smalls[:, (2 + experts) * share :].reshape(total_rows, taps).astype(F32)
    cuts = masks[:, 0:1] * CUT
    lag_keep = [None] + [masks[:, lag : lag + 1] for lag in range(1, taps)]

    own_tokens = interleaved(tokens[0])
    pairs = [(i, i + 1) for i in range(ring - 1)]
    before_edge = lax.ppermute(tokens[0, length - edge :], "ctx", pairs)
    before_edge = jnp.pad(before_edge, ((SEG - edge, 0), (0, 0)))
    with_edge = jnp.concatenate([own_tokens, before_edge], axis=0)
    with_edge = jnp.pad(with_edge, ((0, 8), (0, 0)))
    all_tokens = gather_all(with_edge, "wa", 1)[:, : length + SEG].astype(F32)
    scale_in = rms_scale(all_tokens)
    n1 = (all_tokens * scale_in * gain_mix).astype(BF16)
    flat_n1 = n1.reshape(group * (length + SEG), width)
    joined = jnp.dot(flat_n1, proj_in, preferred_element_type=F32).astype(BF16)
    joined = joined.reshape(group, length + SEG, 2 * padded)
    gate_z = joined[:, :length, padded:].astype(F32)

    conv_taps = padded_lanes(conv_w, padded, 1).astype(F32)
    conv_bias = padded_lanes(conv_b, padded, 0).astype(F32)
    proj_x = padded_lanes(w_x, padded, 0)
    proj_dt = padded_lanes(w_dt, padded, 1)
    step_bias = padded_lanes(dt_bias, padded, 0).astype(F32)
    a_mat = -jnp.exp(padded_lanes(a_log, padded, 1).astype(F32))
    skip_gain = padded_lanes(d_skip, padded, 0).astype(F32)
    proj_out = padded_lanes(w_out, padded, 0)

    x_inner = joined[:, :length, :padded].astype(F32).reshape(group, steps, SEG, padded)
    x_edge = joined[:, length + SEG - edge :, :padded].astype(F32)
    head = jnp.concatenate(
        [x_edge[:, :, None, :], x_inner[:, steps - edge :, : SEG - 1, :]], axis=2
    )
    extended = jnp.concatenate([head, x_inner], axis=1)

    def window(lag):
        return extended[:, edge - lag : edge - lag + steps]

    def folded(column):
        return column.reshape(group, steps, SEG, 1)

    pre_conv = conv_bias + conv_taps[0] * window(0)
    for lag in range(1, taps):
        pre_conv = pre_conv + conv_taps[lag] * window(lag) * folded(lag_keep[lag])
    pre_conv = pre_conv.reshape(total_rows, padded)
    u = jax.nn.silu(pre_conv).astype(BF16)
    u_f = u.astype(F32)
    part = jnp.dot(u, proj_x, preferred_element_type=F32).astype(BF16)
    projected = jnp.sum(gather_all(part, "wa", 2).astype(F32), axis=0).astype(BF16)
    dt_low = projected[:, :ranked]
    b_sel = projected[:, ranked : ranked + states].reshape(group, length, states)
    c_sel = projected[:, ranked + states :].reshape(group, length, states)
    step_pre = jnp.dot(dt_low, proj_dt, preferred_element_type=F32) + step_bias
    step_size = jax.nn.softplus(step_pre)
    drive = step_size * u_f
    step_cut = jnp.where(cuts > 0, CUT, step_size)

    def streams(array):
        return array.reshape(group, length, padded)

    st, dr, us = streams(step_cut), streams(drive), streams(u_f)
    vreg = (group, length, padded)
    seg_states = (group, states, SEG, padded)
    seg_sums = (group, SEG, padded)
    dev_states = (group, states, padded)
    dev_sums = (group, 1, padded)
    updates = group * length * states * padded
    broad = pltpu.VMEM((length, states * LANE), F32)
    sizes = (states, steps, lane_groups)
    h_in, s_in, h_dev, s_dev = scan_call(
        functools.partial(summary_kernel, *sizes), "scan_summary",
        [st, dr, b_sel, 0], [a_mat],
        [seg_states, seg_sums, dev_states, dev_sums], [], [broad], 6 * updates,
    )
    sent = jnp.concatenate([h_dev, s_dev], axis=1).reshape(group * (states + 1), padded)
    all_dev = gather_all(sent, "ctx", 3).reshape(ring, group, states + 1, padded)
    all_sums = all_dev[:, :, states:, :]
    order = lax.iota(jnp.int32, ring)

    def reached(finals, ahead):
        between = (
            ((order[None, :] > order[:, None]) & (order[None, :] < place))
            if ahead
            else ((order[None, :] < order[:, None]) & (order[None, :] > place))
        )
        gap = jnp.sum(
            jnp.where(between[:, :, None, None, None], all_sums[None], 0.0), axis=1
        )
        use = (order < place) if ahead else (order > place)
        terms = jnp.exp(gap * a_mat) * finals
        return jnp.sum(jnp.where(use[:, None, None, None], terms, 0.0), axis=0)

    entering = reached(all_dev[:, :, :states], True)
    (y_scan,) = scan_call(
        functools.partial(output_kernel, *sizes), "scan_output",
        [st, dr, b_sel, c_sel, 0, h_in, s_in, entering], [a_mat],
        [vreg], [], [broad, broad], 8 * updates,
    )
    gate_z = gate_z.reshape(total_rows, padded)
    y_full = y_scan.reshape(total_rows, padded) + skip_gain * u_f
    silu_z = jax.nn.silu(gate_z)
    gated = (y_full * silu_z).astype(BF16)
    mix_part = jnp.dot(gated, proj_out, preferred_element_type=F32).astype(BF16)
    mix_terms = trade(mix_part.reshape(group, length, width), "wa", 4)
    mix = jnp.sum(mix_terms.astype(F32), axis=0)

    stream = own_tokens.astype(F32)
    h1 = stream + mix
    scale_moe = rms_scale(h1)
    n2 = (h1 * scale_moe * gain_moe).astype(BF16)
    logits = jnp.dot(n2, router, preferred_element_type=F32)
    route_in_order = routes[0, :, 0]
    onehot_in_order = route_in_order[:, None] == lax.iota(jnp.int32, experts)[None, :]
    counted = onehot_in_order.astype(jnp.int32)
    within = jnp.sum((jnp.cumsum(counted, axis=0) - counted) * counted, axis=1)
    capacity = length // 2
    slot = interleaved(route_in_order * capacity + within)
    onehot = interleaved(onehot_in_order.astype(F32))
    kept = interleaved(keep_mask[0].astype(F32))
    sig = jax.nn.sigmoid(jnp.sum(logits * onehot, axis=1))
    gates = kept * sig
    slots = experts * capacity
    match = (slot[None, :] == lax.iota(jnp.int32, slots)[:, None]).astype(BF16)
    upstream = interleaved(out_grad[0]).astype(F32)
    d_rows = (gates[:, None] * upstream).astype(BF16)
    outgoing = jnp.dot(
        match, jnp.concatenate([n2, d_rows], axis=1), preferred_element_type=F32
    ).astype(BF16)
    arrived = trade(outgoing.reshape(group, slots // group, 2 * width), "wa", 5)
    arrived = arrived.reshape(slots, 2 * width)
    expert_in, d_out = arrived[:, :width], arrived[:, width:]
    hidden_pre = lax.dot_general(
        expert_in, expert_up, (((1,), (1,)), ((), ())), preferred_element_type=F32
    )
    act, gelu_back = jax.vjp(jax.nn.gelu, hidden_pre)
    act = act.astype(BF16)
    produced = jnp.dot(act, expert_down, preferred_element_type=F32).astype(BF16)
    d_act = lax.dot_general(
        d_out, expert_down, (((1,), (1,)), ((), ())), preferred_element_type=F32
    )
    d_pre = gelu_back(d_act)[0].astype(BF16)
    d_in = jnp.dot(d_pre, expert_up, preferred_element_type=F32).astype(BF16)
    returning = jnp.concatenate([produced, d_in], axis=1)
    returned = trade(returning.reshape(group, slots // group, 2 * width), "wa", 6)
    back_rows = lax.dot_general(
        match, returned.reshape(slots, 2 * width), (((0,), (0,)), ((), ())),
        preferred_element_type=F32,
    )
    grad_up = lax.dot_general(
        d_pre, expert_in, (((0,), (0,)), ((), ())), preferred_element_type=F32
    ).astype(BF16)
    grad_down = lax.dot_general(
        act, d_out, (((0,), (0,)), ((), ())), preferred_element_type=F32
    ).astype(BF16)
    share_up = lax.psum_scatter(grad_up, "ctx", scatter_dimension=0, tiled=True)
    share_down = lax.psum_scatter(grad_down, "ctx", scatter_dimension=0, tiled=True)
    expert_rows, d_slot = back_rows[:, :width], back_rows[:, width:]
    moe = gates[:, None] * expert_rows
    result = h1 + moe
    sums = jnp.stack([jnp.sum(result * result), jnp.sum(mix * mix), jnp.sum(moe * moe)])

    d_gate = jnp.sum(expert_rows * upstream, axis=1)
    d_pick = d_gate * kept * sig * (1.0 - sig)
    d_logits = (onehot * d_pick[:, None]).astype(BF16)
    grad_router = lax.dot_general(
        n2, d_logits, (((0,), (0,)), ((), ())), preferred_element_type=F32
    )
    d_n2 = d_slot + lax.dot_general(
        d_logits, router, (((1,), (1,)), ((), ())), preferred_element_type=F32
    )
    d_norm, gain_terms = norm_grads(h1, scale_moe, gain_moe, d_n2)
    grad_gain_moe = jnp.sum(gain_terms, axis=0)
    d_h1 = upstream + d_norm
    d_mix = gather_all(d_h1.astype(BF16), "wa", 7).reshape(total_rows, width)

    grad_out = lax.dot_general(
        gated, d_mix, (((0,), (0,)), ((), ())), preferred_element_type=F32
    )
    d_gated = lax.dot_general(
        d_mix, proj_out, (((1,), (1,)), ((), ())), preferred_element_type=F32
    )
    d_y = d_gated * silu_z
    d_z = d_gated * y_full * silu_slope(gate_z)
    grad_skip = jnp.sum(d_y * u_f, axis=0)
    dys = streams(d_y)
    f_in, t_in, f_dev = scan_call(
        functools.partial(back_summary_kernel, *sizes), "scan_back_summary",
        [st, c_sel, dys, 0], [a_mat],
        [seg_states, seg_sums, dev_states], [], [broad], 6 * updates,
    )
    all_back = gather_all(f_dev.reshape(group * states, padded), "ctx", 8)
    leaving = reached(all_back.reshape(ring, group, states, padded), False)
    small_rows = (group, length, states)
    longer = pltpu.VMEM((length + SEG, states * LANE), F32)
    d_step, d_drive, grad_b, grad_c, grad_a = scan_call(
        functools.partial(back_kernel, *sizes), "scan_back",
        [st, dr, us, b_sel, c_sel, dys, 0, h_in, s_in, entering, f_in, t_in, leaving], [a_mat],
        [vreg, vreg, small_rows, small_rows], [(states, SEG, padded)],
        [broad, broad, broad, longer, broad, broad], 20 * updates,
    )
    grad_a_log = jnp.sum(grad_a, axis=1) * a_mat
    d_step_pre = d_step.reshape(total_rows, padded) * jax.nn.sigmoid(step_pre)
    grad_step_bias = jnp.sum(d_step_pre, axis=0)
    d_proj_dt = d_step_pre.astype(BF16)
    grad_dt = lax.dot_general(
        dt_low, d_proj_dt, (((0,), (0,)), ((), ())), preferred_element_type=F32
    )
    d_low = lax.dot_general(
        d_proj_dt, proj_dt, (((1,), (1,)), ((), ())), preferred_element_type=F32
    )
    d_part = jnp.concatenate(
        [d_low, grad_b.reshape(total_rows, states), grad_c.reshape(total_rows, states)], axis=1
    ).astype(BF16)
    d_projected = jnp.sum(gather_all(d_part, "wa", 9).astype(F32), axis=0).astype(BF16)
    grad_x = lax.dot_general(
        u, d_projected, (((0,), (0,)), ((), ())), preferred_element_type=F32
    )
    d_u = (
        lax.dot_general(d_projected, proj_x, (((1,), (1,)), ((), ())), preferred_element_type=F32)
        + d_drive.reshape(total_rows, padded) * step_size
        + d_y * skip_gain
    )
    d_pre_conv = d_u * silu_slope(pre_conv)
    grad_conv_bias = jnp.sum(d_pre_conv, axis=0)
    d_conv = d_pre_conv.reshape(group, steps, SEG, padded)
    tap_grads = []
    d_extended = None
    for lag in range(taps):
        weighted = d_conv if lag == 0 else d_conv * folded(lag_keep[lag])
        tap_grads.append(jnp.sum(weighted * window(lag), axis=(0, 1, 2)))
        moved = jnp.pad(
            weighted * conv_taps[lag], ((0, 0), (edge - lag, lag), (0, 0), (0, 0))
        )
        d_extended = moved if d_extended is None else d_extended + moved
    head = d_extended[:, :edge]
    inside = jnp.pad(head[:, :, 1:], ((0, 0), (steps - edge, 0), (0, 1), (0, 0)))
    d_inner = (d_extended[:, edge:] + inside).reshape(group, length, padded)
    d_edge = jnp.pad(head[:, :, 0], ((0, 0), (SEG - edge, 0), (0, 0)))
    d_x = jnp.concatenate([d_inner, d_edge], axis=1)
    d_zs = jnp.pad(d_z.reshape(group, length, padded), ((0, 0), (0, SEG), (0, 0)))
    d_joined = jnp.concatenate([d_x, d_zs], axis=2).astype(BF16)
    d_joined = d_joined.reshape(group * (length + SEG), 2 * padded)
    grad_in = lax.dot_general(
        flat_n1, d_joined, (((0,), (0,)), ((), ())), preferred_element_type=F32
    )
    d_n1_part = lax.dot_general(
        d_joined, proj_in, (((1,), (1,)), ((), ())), preferred_element_type=F32
    ).astype(BF16)
    d_n1_part = jnp.pad(
        d_n1_part.reshape(group, length + SEG, width), ((0, 0), (0, 8), (0, 0))
    )
    d_n1_terms = trade(d_n1_part, "wa", 10)
    d_n1_sum = jnp.sum(d_n1_terms[:, : length + SEG].astype(F32), axis=0)
    back_pairs = [(i + 1, i) for i in range(ring - 1)]
    came = lax.ppermute(d_n1_sum[length + SEG - edge :], "ctx", back_pairs)
    last_rows = jnp.pad(came[:, None, :], ((steps - edge, 0), (SEG - 1, 0), (0, 0)))
    d_n1 = d_n1_sum[:length] + last_rows.reshape(length, width)
    scale_mix = rms_scale(stream)
    d_stream, gain_terms = norm_grads(stream, scale_mix, gain_mix, d_n1)
    grad_gain_mix = jnp.sum(gain_terms, axis=0)
    input_grad = d_h1 + d_stream

    grad_in = jnp.concatenate(
        [grad_in[:, :local], grad_in[:, padded : padded + local]], axis=1
    ).astype(BF16)
    slice_in = lax.psum_scatter(grad_in, "ctx", scatter_dimension=0, tiled=True)
    of_x, of_z = slice_in[:, :local], slice_in[:, local:]
    went_a = lax.ppermute(jnp.where(odd, of_z, of_x), "wa", [(b, a) for a, b in first])
    went_b = lax.ppermute(jnp.where(odd, of_x, of_z), "wa", [(b, a) for a, b in second])
    slice_in = jnp.concatenate(
        [jnp.where(upper, went_b, went_a), jnp.where(upper, went_a, went_b)], axis=1
    )
    share_in = lax.all_gather(slice_in, "ctx", axis=0, tiled=True).astype(F32)
    share_out = lax.all_gather(
        lax.psum_scatter(grad_out[:local].astype(BF16), "ctx", scatter_dimension=0, tiled=True),
        "ctx", axis=0, tiled=True,
    ).astype(F32)
    totals = lax.psum(
        (
            jnp.stack(tap_grads, axis=0)[:, :local],
            grad_conv_bias[:local],
            grad_x[:local],
            grad_dt[:, :local],
            grad_step_bias[:local],
            grad_a_log[:, :local],
            grad_skip[:local],
            sums,
        ),
        "ctx",
    )
    wide_totals = lax.psum((grad_gain_mix, grad_gain_moe, grad_router), ("ctx", "wa"))
    share_mix, share_moe, share_router = [
        lax.dynamic_slice_in_dim(t, mine * share, share, 0) for t in wide_totals
    ]
    denom = length * ring * width
    rms_stats = jnp.sqrt(totals[7] / denom)[None]
    return (
        in_order(result)[None],
        in_order(input_grad)[None],
        share_mix,
        share_in,
        totals[0],
        totals[1],
        totals[2],
        totals[3],
        totals[4],
        totals[5],
        totals[6],
        share_out,
        share_moe,
        share_router,
        share_up.T.astype(F32)[None],
        share_down.astype(F32)[None],
        rms_stats,
    )


def solution(mesh):
    placed = (
        P("wa", "ctx", None),
        P("wa", "ctx", None),
        P("wa", None),
        P("wa", "ctx", None),
        P("wa", "ctx"),
        P("wa"),
        P(None, "wa"),
        P(None, "wa"),
        P("wa"),
        P("wa", None),
        P(None, "wa"),
        P("wa"),
        P(None, "wa"),
        P("wa"),
        P("wa", None),
        P("wa"),
        P("wa", None),
        P("wa", None, "ctx"),
        P("wa", "ctx", None),
    )
    return jax.shard_map(
        body,
        mesh=mesh,
        in_specs=placed,
        out_specs=(
            P("wa", "ctx", None),
            P("wa", "ctx", None),
            P("wa"),
            P(None, "wa"),
            P(None, "wa"),
            P("wa"),
            P("wa", None),
            P(None, "wa"),
            P("wa"),
            P(None, "wa"),
            P("wa"),
            P("wa", None),
            P("wa"),
            P("wa", None),
            P("wa", None, "ctx"),
            P("wa", "ctx", None),
            P("wa", None),
        ),
        check_vma=False,
    )
```

```python
import functools

import jax
import jax.numpy as jnp
from jax import lax
from jax.experimental import pallas as pl
from jax.experimental.pallas import tpu as pltpu
from jax.sharding import PartitionSpec as P

EPS = 1e-05
F32 = jnp.float32
BF16 = jnp.bfloat16
SEG = 8
LANE = 128
CUT = 1e30
MESH = pl.DeviceIdType.MESH
VMEM_LIMIT = 48 * 2**20


def lasting(us):
    return pl.CostEstimate(
        flops=int(us * 1.1e9), bytes_accessed=int(us * 3.5e6), transcendentals=0
    )


def greet(axis, count):
    me = lax.axis_index(axis)
    barrier = pltpu.get_barrier_semaphore()
    for k in range(1, count):
        pl.semaphore_signal(
            barrier, inc=1, device_id={axis: lax.rem(me + k, count)}, device_id_type=MESH
        )
    pl.semaphore_wait(barrier, count - 1)
    return me


def gather_kernel(axis, count, x_ref, o_ref, send, recv, own):
    me = greet(axis, count)
    copies = []
    for k in range(1, count):
        copy = pltpu.make_async_remote_copy(
            src_ref=x_ref,
            dst_ref=o_ref.at[me],
            send_sem=send.at[k],
            recv_sem=recv.at[k],
            device_id={axis: lax.rem(me + k, count)},
            device_id_type=MESH,
        )
        copy.start()
        copies.append(copy)
    local = pltpu.make_async_copy(x_ref, o_ref.at[me], own)
    local.start()
    local.wait()
    for copy in copies:
        copy.wait()


def trade_kernel(axis, count, x_ref, o_ref, send, recv, own):
    me = greet(axis, count)
    copies = []
    for k in range(1, count):
        other = lax.rem(me + k, count)
        copy = pltpu.make_async_remote_copy(
            src_ref=x_ref.at[other],
            dst_ref=o_ref.at[me],
            send_sem=send.at[k],
            recv_sem=recv.at[k],
            device_id={axis: other},
            device_id_type=MESH,
        )
        copy.start()
        copies.append(copy)
    local = pltpu.make_async_copy(x_ref.at[me], o_ref.at[me], own)
    local.start()
    local.wait()
    for copy in copies:
        copy.wait()


def exchange(kernel, x, out_shape, axis, cid, us):
    count = lax.axis_size(axis)
    return pl.pallas_call(
        functools.partial(kernel, axis, count),
        out_shape=jax.ShapeDtypeStruct(out_shape, x.dtype),
        in_specs=[pl.BlockSpec(memory_space=pl.ANY)],
        out_specs=pl.BlockSpec(memory_space=pl.ANY),
        scratch_shapes=[
            pltpu.SemaphoreType.DMA((count,)),
            pltpu.SemaphoreType.DMA((count,)),
            pltpu.SemaphoreType.DMA,
        ],
        compiler_params=pltpu.CompilerParams(collective_id=cid, has_side_effects=True),
        cost_estimate=lasting(us),
    )(x)


def gather_all(x, axis, cid, us):
    return exchange(gather_kernel, x, (lax.axis_size(axis),) + x.shape, axis, cid, us)


def trade(x, axis, cid, us):
    return exchange(trade_kernel, x, x.shape, axis, cid, us)


def remote(src, dst, send, recv, where):
    return pltpu.make_async_remote_copy(
        src_ref=src, dst_ref=dst, send_sem=send, recv_sem=recv,
        device_id=where, device_id_type=MESH,
    )


def add_rows(out, parts, rows):
    def one(i, _):
        at = pl.ds(pl.multiple_of(i * 16, 16), 16)
        total = parts[0][at, :].astype(F32)
        for part in parts[1:]:
            total = total + part[at, :].astype(F32)
        out[at, :] = total.astype(out.dtype)
        return 0

    lax.fori_loop(0, rows // 16, one, 0)


def finish_kernel(
    ring, group, in_rows, small_rows,
    g_ref, z_ref, f_ref, d_ref, o_ref, dt_ref,
    from_pair, paired, came, own, zin, tiles,
    pair_s, pair_r, ctx_s, ctx_r, z_s, z_r, tile_s, tile_r, d_s, d_r, d_own, last_s, last_r, fwd_s, fwd_r,
):
    me = lax.axis_index("ctx")
    mine = lax.axis_index("wa")
    half = ring // 2
    lane = lax.rem(me, 2)
    chip = me // 2
    pair = me + 1 - 2 * lane
    rows = in_rows + small_rows + 16
    barrier = pltpu.get_barrier_semaphore()
    peers = [lax.rem(chip + k, half) * 2 + lane for k in range(1, half)]
    mates = [lax.rem(mine + k, group) for k in range(1, group)]
    for who in [pair] + peers:
        pl.semaphore_signal(barrier, inc=1, device_id={"ctx": who}, device_id_type=MESH)
    for who in mates:
        pl.semaphore_signal(barrier, inc=1, device_id={"wa": who}, device_id_type=MESH)
    pl.semaphore_wait(barrier, half + group - 1)

    to_pair = remote(g_ref.at[1 - lane], from_pair, pair_s, pair_r, {"ctx": pair})
    to_pair.start()
    trades = []
    for k, who in enumerate(mates):
        copy = remote(d_ref.at[who], dt_ref.at[mine], d_s.at[k], d_r.at[k], {"wa": who})
        copy.start()
        trades.append(copy)
    kept = pltpu.make_async_copy(d_ref.at[mine], dt_ref.at[mine], d_own)
    kept.start()
    to_pair.wait_recv()
    scattered = []
    for k, who in enumerate(peers):
        to = lax.rem(chip + k + 1, half)
        add_rows(paired.at[to], [g_ref.at[lane, to], from_pair.at[to]], rows)
        copy = remote(paired.at[to], came.at[k], ctx_s.at[k], ctx_r.at[k], {"ctx": who})
        copy.start()
        scattered.append(copy)
    add_rows(paired.at[chip], [g_ref.at[lane, chip], from_pair.at[chip]], rows)
    for copy in scattered:
        copy.wait_recv()
    add_rows(own, [paired.at[chip]] + [came.at[k] for k in range(half - 1)], rows)

    x_to = mine // 2
    z_to = group // 2 + mine // 2
    slot = lax.rem(mine, 2)
    send_x = remote(own.at[pl.ds(0, in_rows)], zin.at[slot], z_s.at[0], z_r.at[slot], {"wa": x_to})
    send_z = remote(z_ref, zin.at[slot], z_s.at[1], z_r.at[slot], {"wa": z_to})
    keep_x = pltpu.make_async_copy(own.at[pl.ds(0, in_rows)], zin.at[slot], z_r.at[slot])
    keep_z = pltpu.make_async_copy(z_ref, zin.at[slot], z_r.at[slot])

    @pl.when(x_to != mine)
    def _():
        send_x.start()

    @pl.when(x_to == mine)
    def _():
        keep_x.start()

    @pl.when(z_to != mine)
    def _():
        send_z.start()

    @pl.when(z_to == mine)
    def _():
        keep_z.start()

    tile = pl.ds(in_rows + small_rows, 16)
    spread_tiles = []
    for k, who in enumerate(mates):
        copy = remote(own.at[tile], tiles.at[k], tile_s.at[k], tile_r.at[k], {"wa": who})
        copy.start()
        spread_tiles.append(copy)
    fin = o_ref.at[me]
    fin[pl.ds(2 * in_rows, in_rows)] = f_ref[...]
    fin[pl.ds(3 * in_rows, small_rows)] = own[pl.ds(in_rows, small_rows)]
    for copy in spread_tiles:
        copy.wait_recv()
    add_rows(
        fin.at[pl.ds(3 * in_rows + small_rows, 16)],
        [own.at[tile]] + [tiles.at[k] for k in range(group - 1)],
        16,
    )
    for s in range(2):
        pltpu.make_async_copy(zin.at[s], zin.at[s], z_r.at[s]).wait()
        fin[pl.ds(s * in_rows, in_rows)] = zin[s]

    lasts = []
    for k, who in enumerate(peers):
        copy = remote(fin, o_ref.at[me], last_s.at[k], last_r.at[k], {"ctx": who})
        copy.start()
        lasts.append(copy)
    forwards = [remote(fin, o_ref.at[me], fwd_s.at[0], fwd_r.at[0], {"ctx": pair})]
    forwards[0].start()
    for k in range(1, half):
        lasts[k - 1].wait_recv()
        source = lax.rem(chip + half - k, half) * 2 + lane
        copy = remote(o_ref.at[source], o_ref.at[source], fwd_s.at[k], fwd_r.at[k], {"ctx": pair})
        copy.start()
        forwards.append(copy)
    for copy in forwards:
        copy.wait_recv()

    to_pair.wait_send()
    for copy in scattered + spread_tiles + lasts + forwards:
        copy.wait_send()

    @pl.when(x_to != mine)
    def _():
        send_x.wait_send()

    @pl.when(z_to != mine)
    def _():
        send_z.wait_send()

    kept.wait()
    for copy in trades:
        copy.wait()


def finish(g, z, f, d, in_rows, small_rows, cid):
    ring, group = lax.axis_size("ctx"), lax.axis_size("wa")
    half = ring // 2
    rows, lanes = g.shape[2:]
    out_rows = 3 * in_rows + small_rows + 16
    vmem = pl.BlockSpec(memory_space=pltpu.VMEM)
    hbm = pl.BlockSpec(memory_space=pl.ANY)
    dma = pltpu.SemaphoreType.DMA
    return pl.pallas_call(
        functools.partial(finish_kernel, ring, group, in_rows, small_rows),
        out_shape=[
            jax.ShapeDtypeStruct((ring, out_rows, lanes), BF16),
            jax.ShapeDtypeStruct(d.shape, d.dtype),
        ],
        in_specs=[vmem, vmem, vmem, hbm],
        out_specs=[vmem, hbm],
        scratch_shapes=[
            pltpu.VMEM((half, rows, lanes), BF16),
            pltpu.VMEM((half, rows, lanes), BF16),
            pltpu.VMEM((half - 1, rows, lanes), BF16),
            pltpu.VMEM((rows, lanes), BF16),
            pltpu.VMEM((2, in_rows, lanes), BF16),
            pltpu.VMEM((group - 1, 16, lanes), BF16),
            dma, dma,
            dma((half - 1,)), dma((half - 1,)),
            dma((2,)), dma((2,)),
            dma((group - 1,)), dma((group - 1,)),
            dma((group - 1,)), dma((group - 1,)), dma,
            dma((half - 1,)), dma((half - 1,)),
            dma((half,)), dma((half,)),
        ],
        compiler_params=pltpu.CompilerParams(
            collective_id=cid, has_side_effects=True, vmem_limit_bytes=VMEM_LIMIT
        ),
        cost_estimate=lasting(60),
        name="finish",
    )(g, z, f, d)


def start_kernel(
    ring, group, tok, edge, par, doc, w_ref, tok_o, edge_o, par_o, doc_o, w_o,
    mate_s, mate_r, own_s, edge_s, edge_r, relay_s, relay_r, shift_s, shift_r, out_s, out_r, fwd_s, fwd_r,
):
    me = lax.axis_index("ctx")
    mine = lax.axis_index("wa")
    half = ring // 2
    lane = lax.rem(me, 2)
    chip = me // 2
    pair = me + 1 - 2 * lane
    peers = [lax.rem(chip + k, half) * 2 + lane for k in range(1, half)]
    mates = [lax.rem(mine + k, group) for k in range(1, group)]
    barrier = pltpu.get_barrier_semaphore()
    for who in [pair] + peers:
        pl.semaphore_signal(barrier, inc=1, device_id={"ctx": who}, device_id_type=MESH)
    for who in mates:
        pl.semaphore_signal(barrier, inc=1, device_id={"wa": who}, device_id_type=MESH)
    has_next = me < ring - 1
    has_last = me > 0

    @pl.when(has_next)
    def _():
        pl.semaphore_signal(barrier, inc=1, device_id={"ctx": me + 1}, device_id_type=MESH)

    @pl.when(has_last)
    def _():
        pl.semaphore_signal(barrier, inc=1, device_id={"ctx": me - 1}, device_id_type=MESH)

    around = jnp.where(has_next, 1, 0) + jnp.where(has_last, 1, 0)
    pl.semaphore_wait(barrier, half + group - 1 + around)

    to_next = remote(edge, edge_o.at[mine], edge_s, edge_r, {"ctx": me + 1})

    @pl.when(has_next)
    def _():
        to_next.start()

    kind = mine // (group // 2)
    base = 2 * lax.rem(mine, group // 2)
    for h in range(2):
        where = base + h
        send = remote(
            w_ref.at[h], w_o.at[kind, me], shift_s.at[h], shift_r.at[kind], {"wa": where}
        )
        keep = pltpu.make_async_copy(w_ref.at[h], w_o.at[kind, me], shift_r.at[kind])

        @pl.when(where != mine)
        def _():
            send.start()

        @pl.when(where == mine)
        def _():
            keep.start()

    trades = []
    for i, (src, dst) in enumerate(((par, par_o), (doc, doc_o), (tok, tok_o))):
        for k, who in enumerate(mates):
            copy = remote(src, dst.at[mine], mate_s.at[i, k], mate_r.at[i, k], {"wa": who})
            copy.start()
            trades.append(copy)
        keep = pltpu.make_async_copy(src, dst.at[mine], own_s.at[i])
        keep.start()

    @pl.when(has_last)
    def _():
        to_next.wait_recv()
        for k, who in enumerate(mates):
            remote(
                edge_o.at[mine], edge_o.at[mine], relay_s.at[k], relay_r.at[k], {"wa": who}
            ).start()

    sends = []
    for t in range(2):
        block = w_o.at[t, me]
        pltpu.make_async_copy(block, block, shift_r.at[t]).wait()
        for k, who in enumerate(peers):
            copy = remote(block, block, out_s.at[t, k], out_r.at[t, k], {"ctx": who})
            copy.start()
            sends.append(copy)
        copy = remote(block, block, fwd_s.at[t, 0], fwd_r.at[t, 0], {"ctx": pair})
        copy.start()
        sends.append(copy)
    forwards = []
    for t in range(2):
        for k in range(1, half):
            source = lax.rem(chip + half - k, half) * 2 + lane
            block = w_o.at[t, source]
            pltpu.make_async_copy(block, block, out_r.at[t, k - 1]).wait()
            copy = remote(block, block, fwd_s.at[t, k], fwd_r.at[t, k], {"ctx": pair})
            copy.start()
            forwards.append(copy)
    for t in range(2):
        for k in range(half):
            pltpu.make_async_copy(w_o.at[t, me], w_o.at[t, me], fwd_r.at[t, k]).wait()
    for copy in sends + forwards:
        copy.wait_send()
    for h in range(2):

        @pl.when(base + h != mine)
        def _():
            remote(
                w_ref.at[h], w_o.at[kind, me], shift_s.at[h], shift_r.at[kind], {"wa": mine}
            ).wait_send()

    for copy in trades:
        copy.wait()
    for i, (src, dst) in enumerate(((par, par_o), (doc, doc_o), (tok, tok_o))):
        pltpu.make_async_copy(src, dst.at[mine], own_s.at[i]).wait()

    @pl.when(has_next)
    def _():
        to_next.wait_send()

    @pl.when(has_last)
    def _():
        for k, who in enumerate(mates):
            remote(
                edge_o.at[mine], edge_o.at[mine], relay_s.at[k], relay_r.at[k], {"wa": who}
            ).wait()


def start(tok, edge, par, doc, halves, cid):
    ring, group = lax.axis_size("ctx"), lax.axis_size("wa")
    half = ring // 2
    hbm = pl.BlockSpec(memory_space=pl.ANY)
    dma = pltpu.SemaphoreType.DMA
    outs = [(group,) + a.shape for a in (tok, edge, par, doc)] + [(2, ring) + halves.shape[1:]]
    types = [a.dtype for a in (tok, edge, par, doc, halves)]
    return pl.pallas_call(
        functools.partial(start_kernel, ring, group),
        out_shape=[jax.ShapeDtypeStruct(s, t) for s, t in zip(outs, types)],
        in_specs=[hbm] * 5,
        out_specs=[hbm] * 5,
        scratch_shapes=[
            dma((3, group - 1)), dma((3, group - 1)), dma((3,)),
            dma, dma,
            dma((group - 1,)), dma((group - 1,)),
            dma((2,)), dma((2,)),
            dma((2, half - 1)), dma((2, half - 1)),
            dma((2, half)), dma((2, half)),
        ],
        compiler_params=pltpu.CompilerParams(collective_id=cid, has_side_effects=True),
        cost_estimate=lasting(35),
        name="start",
    )(tok, edge, par, doc, halves)


def spread(rows, states):
    shape = (states, states * LANE)
    line = lax.broadcasted_iota(jnp.int32, shape, 0)
    place = lax.broadcasted_iota(jnp.int32, shape, 1)
    lower = line * LANE
    pick = jnp.where((place >= lower) & (place < lower + LANE), 1.0, 0.0).astype(BF16)
    return jnp.dot(rows, pick, preferred_element_type=F32)


def rolled(value, by):
    return pltpu.roll(value, by % SEG, 0)


def lanes_of(g):
    return pl.ds(pl.multiple_of(g * LANE, LANE), LANE)


def rows_of(j):
    return pl.ds(pl.multiple_of(j * SEG, SEG), SEG)


def wide(ref, n, lanes):
    return jnp.broadcast_to(ref[pl.ds(n, 1), lanes], (SEG, LANE))


def state_cols(n):
    return slice(n * LANE, (n + 1) * LANE)


def summary_kernel(states, steps, groups, st_ref, dr_ref, b_ref, a_ref, hx_ref, sx_ref, hd_ref, sd_ref, bb):
    bb[...] = spread(b_ref[0], states)
    zero = jnp.zeros((SEG, LANE), F32)
    seg = lax.broadcasted_iota(jnp.int32, (SEG, LANE), 0)

    def group(g, _):
        lanes = lanes_of(g)
        a = [wide(a_ref, n, lanes) for n in range(states)]

        def step(j, carry):
            rows = rows_of(j)
            st = st_ref[0, rows, lanes]
            dr = dr_ref[0, rows, lanes]
            new = [carry[0] + st]
            for n in range(states):
                new.append(jnp.exp(st * a[n]) * carry[n + 1] + bb[rows, state_cols(n)] * dr)
            return tuple(new)

        out = lax.fori_loop(0, steps, step, (zero,) * (states + 1), unroll=2)
        total, h = out[0], list(out[1:])
        for k in (1, 2, 4):
            ok = seg >= k
            for n in range(states):
                h[n] = h[n] + jnp.where(ok, jnp.exp(total * a[n]) * rolled(h[n], k), 0.0)
            total = total + jnp.where(ok, rolled(total, k), 0.0)
        ok = seg >= 1
        sx_ref[0, :, lanes] = jnp.where(ok, rolled(total, 1), 0.0)
        sd_ref[0, :, lanes] = total[SEG - 1 : SEG]
        for n in range(states):
            hx_ref[0, n, :, lanes] = jnp.where(ok, rolled(h[n], 1), 0.0)
            hd_ref[0, pl.ds(n, 1), lanes] = h[n][SEG - 1 : SEG]
        return 0

    lax.fori_loop(0, groups, group, 0)


def output_kernel(states, steps, groups, st_ref, dr_ref, b_ref, c_ref, a_ref, hx_ref, sx_ref, e_ref, y_ref, bb, cb):
    bb[...] = spread(b_ref[0], states)
    cb[...] = spread(c_ref[0], states)

    def group(g, _):
        lanes = lanes_of(g)
        a = [wide(a_ref, n, lanes) for n in range(states)]
        sx = sx_ref[0, :, lanes]
        start = tuple(
            jnp.exp(sx * a[n]) * wide(e_ref.at[0], n, lanes) + hx_ref[0, n, :, lanes]
            for n in range(states)
        )

        def step(j, h):
            rows = rows_of(j)
            st = st_ref[0, rows, lanes]
            dr = dr_ref[0, rows, lanes]
            new = []
            y = None
            for n in range(states):
                state = jnp.exp(st * a[n]) * h[n] + bb[rows, state_cols(n)] * dr
                new.append(state)
                part = cb[rows, state_cols(n)] * state
                y = part if y is None else y + part
            y_ref[0, rows, lanes] = y
            return tuple(new)

        lax.fori_loop(0, steps, step, start, unroll=2)
        return 0

    lax.fori_loop(0, groups, group, 0)


def back_summary_kernel(states, steps, groups, st_ref, c_ref, dy_ref, a_ref, fx_ref, sx_ref, fd_ref, cb):
    cb[...] = spread(c_ref[0], states)
    zero = jnp.zeros((SEG, LANE), F32)
    seg = lax.broadcasted_iota(jnp.int32, (SEG, LANE), 0)

    def group(g, _):
        lanes = lanes_of(g)
        a = [wide(a_ref, n, lanes) for n in range(states)]

        def step(lap, carry):
            rows = rows_of(steps - 1 - lap)
            st = st_ref[0, rows, lanes]
            dy = dy_ref[0, rows, lanes]
            new = [carry[0] + st]
            for n in range(states):
                new.append(jnp.exp(st * a[n]) * (carry[n + 1] + cb[rows, state_cols(n)] * dy))
            return tuple(new)

        out = lax.fori_loop(0, steps, step, (zero,) * (states + 1), unroll=2)
        total, f = out[0], list(out[1:])
        for k in (1, 2, 4):
            ok = seg < SEG - k
            for n in range(states):
                f[n] = f[n] + jnp.where(ok, jnp.exp(total * a[n]) * rolled(f[n], -k), 0.0)
            total = total + jnp.where(ok, rolled(total, -k), 0.0)
        ok = seg < SEG - 1
        sx_ref[0, :, lanes] = jnp.where(ok, rolled(total, -1), 0.0)
        for n in range(states):
            fx_ref[0, n, :, lanes] = jnp.where(ok, rolled(f[n], -1), 0.0)
            fd_ref[0, pl.ds(n, 1), lanes] = f[n][0:1]
        return 0

    lax.fori_loop(0, groups, group, 0)


def back_kernel(
    states, steps, groups,
    st_ref, dr_ref, u_ref, b_ref, c_ref, dy_ref, a_ref, hx_ref, sx_ref, e_ref, fx_ref, tx_ref, o_ref,
    ds_ref, dd_ref, gb_ref, gc_ref, ga_ref,
    bb, cb, dec, pri, accb, accc,
):
    bb[...] = spread(b_ref[0], states)
    cb[...] = spread(c_ref[0], states)
    accb[...] = jnp.zeros_like(accb)
    accc[...] = jnp.zeros_like(accc)

    @pl.when(pl.program_id(0) == 0)
    def _():
        ga_ref[...] = jnp.zeros_like(ga_ref)

    def group(g, _):
        lanes = lanes_of(g)
        a = [wide(a_ref, n, lanes) for n in range(states)]
        sx = sx_ref[0, :, lanes]
        start = tuple(
            jnp.exp(sx * a[n]) * wide(e_ref.at[0], n, lanes) + hx_ref[0, n, :, lanes]
            for n in range(states)
        )

        def ahead(j, h):
            rows = rows_of(j)
            st = st_ref[0, rows, lanes]
            dr = dr_ref[0, rows, lanes]
            new = []
            for n in range(states):
                decay = jnp.exp(st * a[n])
                dec[rows, state_cols(n)] = decay
                pri[rows, state_cols(n)] = h[n]
                new.append(decay * h[n] + bb[rows, state_cols(n)] * dr)
            return tuple(new)

        last = lax.fori_loop(0, steps, ahead, start, unroll=2)
        end = rows_of(steps)
        for n in range(states):
            pri[end, state_cols(n)] = last[n]
        tx = tx_ref[0, :, lanes]
        flow = tuple(
            jnp.exp(tx * a[n]) * wide(o_ref.at[0], n, lanes) + fx_ref[0, n, :, lanes]
            for n in range(states)
        )

        def back(lap, f):
            j = steps - 1 - lap
            rows = rows_of(j)
            after = rows_of(j + 1)
            st = st_ref[0, rows, lanes]
            dr = dr_ref[0, rows, lanes]
            dy = dy_ref[0, rows, lanes]
            u = u_ref[0, rows, lanes]
            true_step = jnp.where(st >= 0.5 * CUT, 0.0, st)
            new = []
            d_step = None
            d_drive = None
            for n in range(states):
                cols = state_cols(n)
                d = f[n] + cb[rows, cols] * dy
                accc[rows, cols] += pri[after, cols] * dy
                accb[rows, cols] += d * dr
                flowing = dec[rows, cols] * d
                new.append(flowing)
                d_log = flowing * pri[rows, cols]
                ga_ref[n, :, lanes] += d_log * true_step
                part = d_log * a[n]
                d_step = part if d_step is None else d_step + part
                part = d * bb[rows, cols]
                d_drive = part if d_drive is None else d_drive + part
            ds_ref[0, rows, lanes] = d_step + d_drive * u
            dd_ref[0, rows, lanes] = d_drive
            return tuple(new)

        lax.fori_loop(0, steps, back, flow, unroll=2)
        return 0

    lax.fori_loop(0, groups, group, 0)
    shape = (states * LANE, states)
    line = lax.broadcasted_iota(jnp.int32, shape, 0)
    lower = lax.broadcasted_iota(jnp.int32, shape, 1) * LANE
    pick = jnp.where((line >= lower) & (line < lower + LANE), 1.0, 0.0)
    gb_ref[0] = jnp.dot(accb[...], pick, precision=lax.Precision.HIGHEST, preferred_element_type=F32)
    gc_ref[0] = jnp.dot(accc[...], pick, precision=lax.Precision.HIGHEST, preferred_element_type=F32)


def per_stream(shape):
    rest = len(shape) - 1
    return pl.BlockSpec((1,) + shape[1:], lambda s: (s,) + (0,) * rest)


def whole(shape):
    return pl.BlockSpec(shape, lambda s: (0,) * len(shape))


def scan_call(kernel, name, args, shared, outs, shared_outs, scratch, us):
    ordered = []
    specs = []
    for arg in args:
        if isinstance(arg, int):
            ordered.append(shared[arg])
            specs.append(whole(shared[arg].shape))
        else:
            ordered.append(arg)
            specs.append(per_stream(arg.shape))
    streams = args[0].shape[0]
    return pl.pallas_call(
        kernel,
        grid=(streams,),
        out_shape=[jax.ShapeDtypeStruct(s, F32) for s in outs + shared_outs],
        in_specs=specs,
        out_specs=[per_stream(s) for s in outs] + [whole(s) for s in shared_outs],
        scratch_shapes=scratch,
        compiler_params=pltpu.CompilerParams(vmem_limit_bytes=VMEM_LIMIT),
        cost_estimate=lasting(us),
        name=name,
    )(*ordered)


def rms_scale(values):
    return lax.rsqrt(jnp.mean(values * values, axis=-1, keepdims=True) + EPS)


def norm_grads(values, scale, gain, d_out):
    unit = values * scale
    d_unit = d_out * gain
    d_values = scale * (d_unit - unit * jnp.mean(d_unit * unit, axis=-1, keepdims=True))
    return d_values, d_out * unit


def interleaved(rows):
    length = rows.shape[0]
    folded = rows.reshape((SEG, length // SEG) + rows.shape[1:])
    return jnp.swapaxes(folded, 0, 1).reshape(rows.shape)


def in_order(rows):
    length = rows.shape[0]
    folded = rows.reshape((length // SEG, SEG) + rows.shape[1:])
    return jnp.swapaxes(folded, 0, 1).reshape(rows.shape)


def silu_slope(v):
    s = jax.nn.sigmoid(v)
    return s * (1.0 + v * (1.0 - s))


def padded_lanes(array, width, axis):
    pads = [(0, 0)] * array.ndim
    pads[axis] = (0, width - array.shape[axis])
    return jnp.pad(array, pads)


def body(
    tokens, out_grad, doc_starts, routes, keep_mask, norm_mix, w_in, conv_w, conv_b, w_x, w_dt,
    dt_bias, a_log, d_skip, w_out, norm_moe, w_router, w_up, w_down,
):
    group = lax.axis_size("wa")
    ring = lax.axis_size("ctx")
    mine = lax.axis_index("wa")
    place = lax.axis_index("ctx")
    length, width = tokens.shape[1:]
    taps, local = conv_w.shape
    states = a_log.shape[0]
    ranked = w_dt.shape[0]
    experts = w_router.shape[1]
    padded = -(-local // LANE) * LANE
    lane_groups = padded // LANE
    steps = length // SEG
    total_rows = group * length
    edge = taps - 1

    def up16(n):
        return -(-n // 16) * 16

    expert_up = lax.all_gather(w_up[0].T, "ctx", axis=0, tiled=True)
    expert_down = lax.all_gather(w_down[0], "ctx", axis=0, tiled=True)

    in_each = -(-width // ring)
    in_rows = up16(in_each)
    part_in = lax.dynamic_slice_in_dim(w_in, place * in_each, in_each, 0)
    halves = jnp.stack([part_in[:, :local], part_in[:, local:]], axis=0)
    halves = jnp.pad(halves, ((0, 0), (0, in_rows - in_each), (0, padded - local)))
    share = norm_mix.shape[0]
    small = jnp.concatenate([norm_mix, norm_moe, w_router.T.reshape(-1)], axis=0)
    small_count = up16(-(-small.shape[0] // LANE))
    small = jnp.pad(small, (0, small_count * LANE - small.shape[0])).reshape(small_count, LANE)
    first_rows = doc_starts.shape[1]
    doc_tile = jnp.pad(doc_starts, ((0, 7), (0, LANE - first_rows)))
    own_tokens = interleaved(tokens[0])
    all_rows, all_edges, smalls, docs, w_blocks = start(
        own_tokens, tokens[0, length - 16 :], small, doc_tile, halves, 1
    )
    proj_in_x, proj_in_z = [w_blocks[t, :, :in_each].reshape(width, padded) for t in range(2)]
    smalls = smalls.reshape(group, -1)[:, : (2 + experts) * share]
    smalls = smalls.reshape(group, 2 + experts, share).swapaxes(0, 1).reshape(2 + experts, width)
    gain_mix, gain_moe = smalls[0].astype(F32), smalls[1].astype(F32)
    router = smalls[2:]

    at = interleaved(place * length + lax.iota(jnp.int32, length))[None, :, None]
    begins = docs[:, :1, :first_rows]
    cuts = jnp.any(at == begins, axis=2).reshape(total_rows, 1)
    lag_keep = [None]
    for lag in range(1, taps):
        cut = jnp.any((begins > at - lag) & (begins <= at), axis=2)
        lag_keep.append(1.0 - cut.astype(F32).reshape(total_rows, 1))

    edge_rows = jnp.where(place > 0, all_edges[:, 16 - SEG :], jnp.zeros((), BF16))
    all_tokens = jnp.concatenate([all_rows, edge_rows], axis=1).astype(F32)
    scale_in = rms_scale(all_tokens)
    n1 = (all_tokens * scale_in * gain_mix).astype(BF16)
    flat_n1 = n1.reshape(group * (length + SEG), width)
    n1_rows = n1[:, :length].reshape(total_rows, width)
    joined_x = jnp.dot(flat_n1, proj_in_x, preferred_element_type=F32).astype(BF16)
    joined_x = joined_x.reshape(group, length + SEG, padded)
    gate_z = jnp.dot(n1_rows, proj_in_z, preferred_element_type=F32).astype(BF16).astype(F32)

    conv_taps = padded_lanes(conv_w, padded, 1).astype(F32)
    conv_bias = padded_lanes(conv_b, padded, 0).astype(F32)
    proj_x = padded_lanes(w_x, padded, 0)
    proj_dt = padded_lanes(w_dt, padded, 1)
    step_bias = padded_lanes(dt_bias, padded, 0).astype(F32)
    a_mat = -jnp.exp(padded_lanes(a_log, padded, 1).astype(F32))
    skip_gain = padded_lanes(d_skip, padded, 0).astype(F32)
    proj_out = padded_lanes(w_out, padded, 0)

    x_inner = joined_x[:, :length].astype(F32).reshape(group, steps, SEG, padded)
    x_edge = joined_x[:, length + SEG - edge :].astype(F32)
    head = jnp.concatenate(
        [x_edge[:, :, None, :], x_inner[:, steps - edge :, : SEG - 1, :]], axis=2
    )
    extended = jnp.concatenate([head, x_inner], axis=1)

    def window(lag):
        return extended[:, edge - lag : edge - lag + steps]

    def folded(column):
        return column.reshape(group, steps, SEG, 1)

    pre_conv = conv_bias + conv_taps[0] * window(0)
    for lag in range(1, taps):
        pre_conv = pre_conv + conv_taps[lag] * window(lag) * folded(lag_keep[lag])
    pre_conv = pre_conv.reshape(total_rows, padded)
    u = jax.nn.silu(pre_conv).astype(BF16)
    u_f = u.astype(F32)
    part = jnp.dot(u, proj_x, preferred_element_type=F32).astype(BF16)
    projected = jnp.sum(gather_all(part, "wa", 2, 15).astype(F32), axis=0).astype(BF16)
    dt_low = projected[:, :ranked]
    b_sel = projected[:, ranked : ranked + states].reshape(group, length, states)
    c_sel = projected[:, ranked + states :].reshape(group, length, states)
    step_pre = jnp.dot(dt_low, proj_dt, preferred_element_type=F32) + step_bias
    step_size = jax.nn.softplus(step_pre)
    drive = step_size * u_f
    step_cut = jnp.where(cuts, CUT, step_size)

    def streams(array):
        return array.reshape(group, length, padded)

    st, dr, us = streams(step_cut), streams(drive), streams(u_f)
    vreg = (group, length, padded)
    seg_states = (group, states, SEG, padded)
    seg_sums = (group, SEG, padded)
    dev_states = (group, states, padded)
    dev_sums = (group, 1, padded)
    broad = pltpu.VMEM((length, states * LANE), F32)
    sizes = (states, steps, lane_groups)
    h_in, s_in, h_dev, s_dev = scan_call(
        functools.partial(summary_kernel, *sizes), "scan_summary",
        [st, dr, b_sel, 0], [a_mat],
        [seg_states, seg_sums, dev_states, dev_sums], [], [broad], 8,
    )
    sent = jnp.concatenate([h_dev, s_dev], axis=1).reshape(group * (states + 1), padded)
    all_dev = gather_all(sent, "ctx", 3, 18).reshape(ring, group, states + 1, padded)
    all_sums = all_dev[:, :, states:, :]
    order = lax.iota(jnp.int32, ring)

    def reached(finals, ahead):
        between = (
            ((order[None, :] > order[:, None]) & (order[None, :] < place))
            if ahead
            else ((order[None, :] < order[:, None]) & (order[None, :] > place))
        )
        gap = jnp.sum(
            jnp.where(between[:, :, None, None, None], all_sums[None], 0.0), axis=1
        )
        use = (order < place) if ahead else (order > place)
        terms = jnp.exp(gap * a_mat) * finals
        return jnp.sum(jnp.where(use[:, None, None, None], terms, 0.0), axis=0)

    entering = reached(all_dev[:, :, :states], True)
    (y_scan,) = scan_call(
        functools.partial(output_kernel, *sizes), "scan_output",
        [st, dr, b_sel, c_sel, 0, h_in, s_in, entering], [a_mat],
        [vreg], [], [broad, broad], 10,
    )
    y_full = y_scan.reshape(total_rows, padded) + skip_gain * u_f
    silu_z = jax.nn.silu(gate_z)
    gated = (y_full * silu_z).astype(BF16)
    mix_part = jnp.dot(gated, proj_out, preferred_element_type=F32).astype(BF16)
    mix_terms = trade(mix_part.reshape(group, length, width), "wa", 4, 25)
    mix = jnp.sum(mix_terms.astype(F32), axis=0)

    stream = own_tokens.astype(F32)
    h1 = stream + mix
    scale_moe = rms_scale(h1)
    n2 = (h1 * scale_moe * gain_moe).astype(BF16)
    logits = lax.dot_general(
        n2, router, (((1,), (1,)), ((), ())), preferred_element_type=F32
    )
    route_in_order = routes[0, :, 0]
    onehot_in_order = route_in_order[:, None] == lax.iota(jnp.int32, experts)[None, :]
    counted = onehot_in_order.astype(jnp.int32)
    within = jnp.sum((jnp.cumsum(counted, axis=0) - counted) * counted, axis=1)
    capacity = length // 2
    slot = interleaved(route_in_order * capacity + within)
    onehot = interleaved(onehot_in_order.astype(F32))
    kept = interleaved(keep_mask[0].astype(F32))
    sig = jax.nn.sigmoid(jnp.sum(logits * onehot, axis=1))
    gates = kept * sig
    slots = experts * capacity
    match = (slot[None, :] == lax.iota(jnp.int32, slots)[:, None]).astype(BF16)
    upstream = interleaved(out_grad[0]).astype(F32)
    d_rows = (gates[:, None] * upstream).astype(BF16)
    outgoing = jnp.dot(
        match, jnp.concatenate([n2, d_rows], axis=1), preferred_element_type=F32
    ).astype(BF16)
    arrived = trade(outgoing.reshape(group, slots // group, 2 * width), "wa", 5, 29)
    arrived = arrived.reshape(slots, 2 * width)
    expert_in, d_out = arrived[:, :width], arrived[:, width:]
    hidden_pre = lax.dot_general(
        expert_in, expert_up, (((1,), (1,)), ((), ())), preferred_element_type=F32
    )
    act, gelu_back = jax.vjp(jax.nn.gelu, hidden_pre)
    act = act.astype(BF16)
    produced = jnp.dot(act, expert_down, preferred_element_type=F32).astype(BF16)
    d_act = lax.dot_general(
        d_out, expert_down, (((1,), (1,)), ((), ())), preferred_element_type=F32
    )
    d_pre = gelu_back(d_act)[0].astype(BF16)
    d_in = jnp.dot(d_pre, expert_up, preferred_element_type=F32).astype(BF16)
    returning = jnp.concatenate([produced, d_in], axis=1)
    grad_up = lax.dot_general(
        d_pre, expert_in, (((0,), (0,)), ((), ())), preferred_element_type=F32
    ).astype(BF16)
    grad_down = lax.dot_general(
        act, d_out, (((0,), (0,)), ((), ())), preferred_element_type=F32
    ).astype(BF16)
    returning, grad_up, grad_down = lax.optimization_barrier((returning, grad_up, grad_down))
    share_up, share_down = lax.psum_scatter(
        (grad_up, grad_down), "ctx", scatter_dimension=0, tiled=True
    )
    returned = trade(returning.reshape(group, slots // group, 2 * width), "wa", 6, 29)
    back_rows = lax.dot_general(
        match, returned.reshape(slots, 2 * width), (((0,), (0,)), ((), ())),
        preferred_element_type=F32,
    )
    expert_rows, d_slot = back_rows[:, :width], back_rows[:, width:]
    moe = gates[:, None] * expert_rows
    result = h1 + moe
    sums = jnp.stack([jnp.sum(result * result), jnp.sum(mix * mix), jnp.sum(moe * moe)])

    d_gate = jnp.sum(expert_rows * upstream, axis=1)
    d_pick = d_gate * kept * sig * (1.0 - sig)
    d_logits = (onehot * d_pick[:, None]).astype(BF16)
    grad_router = lax.dot_general(
        n2, d_logits, (((0,), (0,)), ((), ())), preferred_element_type=F32
    )
    d_n2 = d_slot + jnp.dot(d_logits, router, preferred_element_type=F32)
    d_norm, gain_terms = norm_grads(h1, scale_moe, gain_moe, d_n2)
    grad_gain_moe = jnp.sum(gain_terms, axis=0)
    d_h1 = upstream + d_norm
    d_mix = gather_all(d_h1.astype(BF16), "wa", 7, 28).reshape(total_rows, width)

    d_gated = lax.dot_general(
        d_mix, proj_out, (((1,), (1,)), ((), ())), preferred_element_type=F32
    )
    d_y = d_gated * silu_z
    d_z = d_gated * y_full * silu_slope(gate_z)
    grad_skip = jnp.sum(d_y * u_f, axis=0)
    d_zs = d_z.astype(BF16)
    grad_in_z = lax.dot_general(
        n1_rows, d_zs, (((0,), (0,)), ((), ())), preferred_element_type=F32
    )
    grad_out = lax.dot_general(
        d_mix, gated, (((0,), (0,)), ((), ())), preferred_element_type=F32
    )
    grad_zo = jnp.concatenate([grad_in_z[:, :local], grad_out[:, :local]], axis=1).astype(BF16)
    dys = streams(d_y)
    f_in, t_in, f_dev = scan_call(
        functools.partial(back_summary_kernel, *sizes), "scan_back_summary",
        [st, c_sel, dys, 0], [a_mat],
        [seg_states, seg_sums, dev_states], [], [broad], 8,
    )
    all_back = gather_all(f_dev.reshape(group * states, padded), "ctx", 8, 18)
    all_back, share_up, share_down, grad_zo = lax.optimization_barrier(
        (all_back, share_up, share_down, grad_zo)
    )
    chunk_zo = lax.psum_scatter(grad_zo, "ctx", scatter_dimension=0, tiled=True)
    leaving = reached(all_back.reshape(ring, group, states, padded), False)
    small_rows = (group, length, states)
    longer = pltpu.VMEM((length + SEG, states * LANE), F32)
    d_step, d_drive, grad_b, grad_c, grad_a = scan_call(
        functools.partial(back_kernel, *sizes), "scan_back",
        [st, dr, us, b_sel, c_sel, dys, 0, h_in, s_in, entering, f_in, t_in, leaving], [a_mat],
        [vreg, vreg, small_rows, small_rows], [(states, SEG, padded)],
        [broad, broad, broad, longer, broad, broad], 30,
    )
    grad_a_log = jnp.sum(grad_a, axis=1) * a_mat
    d_step_pre = d_step.reshape(total_rows, padded) * jax.nn.sigmoid(step_pre)
    grad_step_bias = jnp.sum(d_step_pre, axis=0)
    d_proj_dt = d_step_pre.astype(BF16)
    grad_dt = lax.dot_general(
        dt_low, d_proj_dt, (((0,), (0,)), ((), ())), preferred_element_type=F32
    )
    d_low = lax.dot_general(
        d_proj_dt, proj_dt, (((1,), (1,)), ((), ())), preferred_element_type=F32
    )
    d_part = jnp.concatenate(
        [d_low, grad_b.reshape(total_rows, states), grad_c.reshape(total_rows, states)], axis=1
    ).astype(BF16)
    d_projected = jnp.sum(gather_all(d_part, "wa", 9, 14).astype(F32), axis=0).astype(BF16)
    grad_x = lax.dot_general(
        u, d_projected, (((0,), (0,)), ((), ())), preferred_element_type=F32
    )
    d_u = (
        lax.dot_general(d_projected, proj_x, (((1,), (1,)), ((), ())), preferred_element_type=F32)
        + d_drive.reshape(total_rows, padded) * step_size
        + d_y * skip_gain
    )
    d_pre_conv = d_u * silu_slope(pre_conv)
    grad_conv_bias = jnp.sum(d_pre_conv, axis=0)
    d_conv = d_pre_conv.reshape(group, steps, SEG, padded)
    tap_grads = []
    d_extended = None
    for lag in range(taps):
        weighted = d_conv if lag == 0 else d_conv * folded(lag_keep[lag])
        tap_grads.append(jnp.sum(weighted * window(lag), axis=(0, 1, 2)))
        moved = jnp.pad(
            weighted * conv_taps[lag], ((0, 0), (edge - lag, lag), (0, 0), (0, 0))
        )
        d_extended = moved if d_extended is None else d_extended + moved
    head = d_extended[:, :edge]
    inside = jnp.pad(head[:, :, 1:], ((0, 0), (steps - edge, 0), (0, 1), (0, 0)))
    d_inner = (d_extended[:, edge:] + inside).reshape(group, length, padded)
    d_edge = jnp.pad(head[:, :, 0], ((0, 0), (SEG - edge, 0), (0, 0)))
    d_x = jnp.concatenate([d_inner, d_edge], axis=1)
    d_x = d_x.astype(BF16).reshape(group * (length + SEG), padded)
    grad_in_x = lax.dot_general(
        flat_n1, d_x, (((0,), (0,)), ((), ())), preferred_element_type=F32
    )[:, :local]
    d_n1_z = lax.dot_general(
        d_zs, proj_in_z, (((1,), (1,)), ((), ())), preferred_element_type=F32
    ).reshape(group, length, width)
    d_n1_part = lax.dot_general(
        d_x, proj_in_x, (((1,), (1,)), ((), ())), preferred_element_type=F32
    )
    d_n1_part = d_n1_part.reshape(group, length + SEG, width)
    d_n1_part = d_n1_part + jnp.pad(d_n1_z, ((0, 0), (0, SEG), (0, 0)))
    unit = all_tokens * scale_in
    grad_gain_mix = jnp.sum(d_n1_part * unit, axis=(0, 1))
    d_n1_part = jnp.pad(d_n1_part.astype(BF16), ((0, 0), (0, 8), (0, 0)))

    def dealt(rows, count):
        each = -(-rows.shape[0] // ring)
        rows = jnp.pad(rows, ((0, each * ring - rows.shape[0]), (0, 0)))
        return jnp.pad(rows.reshape(ring, each, -1), ((0, 0), (0, count - each), (0, 0)))

    small = jnp.concatenate(
        [
            jnp.stack(tap_grads, axis=0),
            grad_conv_bias[None],
            grad_step_bias[None],
            grad_skip[None],
            grad_a_log,
            grad_dt,
            grad_x.T,
        ],
        axis=0,
    )[:, :local].astype(BF16)
    small_each = -(-small.shape[0] // ring)
    small_rows = up16(small_each)
    fulls = jnp.stack([grad_gain_mix, grad_gain_moe] + [grad_router[:, e] for e in range(experts)])
    fulls = fulls.reshape(2 + experts, group, share).swapaxes(0, 1).reshape(group, -1)
    full_each = -(-fulls.shape[1] // ring)
    fulls = jnp.pad(fulls, ((0, 0), (0, full_each * ring - fulls.shape[1])))
    fulls = fulls.reshape(group, ring, full_each).swapaxes(0, 1)
    coarse = sums.astype(BF16).astype(F32)
    stat_row = jnp.concatenate([coarse, (sums - coarse)])
    is_mine = (lax.iota(jnp.int32, group) == mine).astype(F32)
    stat_rows = jnp.broadcast_to(
        is_mine[None, :, None] * stat_row[None, None, :], (ring, group, stat_row.shape[0])
    )
    fulls = jnp.pad(fulls, ((0, 0), (0, 0), (0, local - full_each)))
    stat_rows = jnp.pad(stat_rows, ((0, 0), (0, 0), (0, local - stat_row.shape[0])))
    tile = jnp.concatenate([fulls, stat_rows], axis=1)
    tile = jnp.pad(tile, ((0, 0), (0, 16 - tile.shape[1]), (0, 0))).astype(BF16)
    packed = jnp.concatenate(
        [dealt(grad_in_x.astype(BF16), in_rows), dealt(small, small_rows), tile], axis=1
    )
    packed = packed.reshape((ring // 2, 2) + packed.shape[1:]).swapaxes(0, 1)
    chunk_zo = jnp.pad(chunk_zo, ((0, in_rows - in_each), (0, 0)))
    chunk_z, chunk_o = chunk_zo[:, :local], chunk_zo[:, local:]
    done, d_n1_terms = finish(packed, chunk_z, chunk_o, d_n1_part, in_rows, small_rows, 11)
    share_in = jnp.concatenate(
        [done[:, :in_each], done[:, in_rows : in_rows + in_each]], axis=2
    ).reshape(width, 2 * local).astype(F32)
    base = 2 * in_rows
    share_out = done[:, base : base + in_each].reshape(width, local).T.astype(F32)
    base = base + in_rows
    smalls_sum = done[:, base : base + small_each].reshape(ring * small_each, local).astype(F32)
    base = base + small_rows
    full_sum = lax.dynamic_index_in_dim(done, base + mine, 1, False)[:, :full_each]
    full_sum = full_sum.reshape(-1)[: (2 + experts) * share].reshape(2 + experts, share).astype(F32)
    stat_sum = lax.dynamic_index_in_dim(done, base + group + mine, 1, False)[0, :6].astype(F32)

    d_n1_sum = jnp.sum(d_n1_terms[:, : length + SEG].astype(F32), axis=0)
    back_pairs = [(i + 1, i) for i in range(ring - 1)]
    came = lax.ppermute(d_n1_sum[length + SEG - edge :], "ctx", back_pairs)
    last_rows = jnp.pad(came[:, None, :], ((steps - edge, 0), (SEG - 1, 0), (0, 0)))
    d_n1 = d_n1_sum[:length] + last_rows.reshape(length, width)
    scale_mix = rms_scale(stream)
    d_stream, _ = norm_grads(stream, scale_mix, gain_mix, d_n1)
    input_grad = d_h1 + d_stream
    marks_at = [0, taps, taps + 1, taps + 2, taps + 3, taps + 3 + states]
    marks_at += [marks_at[-1] + ranked, marks_at[-1] + ranked + w_x.shape[1]]
    cut_at = [smalls_sum[a:b] for a, b in zip(marks_at[:-1], marks_at[1:])]
    stat_sums = stat_sum[:3] + stat_sum[3:]
    denom = length * ring * width
    rms_stats = jnp.sqrt(stat_sums / denom)[None]
    return (
        in_order(result)[None],
        in_order(input_grad)[None],
        full_sum[0],
        share_in,
        cut_at[0],
        cut_at[1][0],
        cut_at[6].T,
        cut_at[5],
        cut_at[2][0],
        cut_at[4],
        cut_at[3][0],
        share_out,
        full_sum[1],
        full_sum[2:].T,
        share_up.T.astype(F32)[None],
        share_down.astype(F32)[None],
        rms_stats,
    )


def solution(mesh):
    placed = (
        P("wa", "ctx", None),
        P("wa", "ctx", None),
        P("wa", None),
        P("wa", "ctx", None),
        P("wa", "ctx"),
        P("wa"),
        P(None, "wa"),
        P(None, "wa"),
        P("wa"),
        P("wa", None),
        P(None, "wa"),
        P("wa"),
        P(None, "wa"),
        P("wa"),
        P("wa", None),
        P("wa"),
        P("wa", None),
        P("wa", None, "ctx"),
        P("wa", "ctx", None),
    )
    return jax.shard_map(
        body,
        mesh=mesh,
        in_specs=placed,
        out_specs=(
            P("wa", "ctx", None),
            P("wa", "ctx", None),
            P("wa"),
            P(None, "wa"),
            P(None, "wa"),
            P("wa"),
            P("wa", None),
            P(None, "wa"),
            P("wa"),
            P(None, "wa"),
            P("wa"),
            P("wa", None),
            P("wa"),
            P("wa", None),
            P("wa", None, "ctx"),
            P("wa", "ctx", None),
            P("wa", None),
        ),
        check_vma=False,
    )
```

```python
import functools

import jax
import jax.numpy as jnp
from jax import lax
from jax.experimental import pallas as pl
from jax.experimental.pallas import tpu as pltpu
from jax.sharding import PartitionSpec as P

EPS = 1e-05
F32 = jnp.float32
BF16 = jnp.bfloat16
SEG = 8
LANE = 128
EDGE = 16
CUT = 1e30
MESH = pl.DeviceIdType.MESH
VMEM_LIMIT = 60 * 2**20


def lasting(us):
    return pl.CostEstimate(
        flops=int(us * 1.1e9), bytes_accessed=int(us * 3.5e6), transcendentals=0
    )


def greet(axis, count):
    me = lax.axis_index(axis)
    barrier = pltpu.get_barrier_semaphore()
    for k in range(1, count):
        pl.semaphore_signal(
            barrier, inc=1, device_id={axis: lax.rem(me + k, count)}, device_id_type=MESH
        )
    pl.semaphore_wait(barrier, count - 1)
    return me


def gather_kernel(axis, count, arrays, *refs):
    srcs, dsts = refs[:arrays], refs[arrays : 2 * arrays]
    send, recv, own = refs[-3:]
    me = greet(axis, count)
    copies = []
    for i in range(arrays):
        for k in range(1, count):
            copy = pltpu.make_async_remote_copy(
                src_ref=srcs[i],
                dst_ref=dsts[i].at[me],
                send_sem=send.at[i, k],
                recv_sem=recv.at[i, k],
                device_id={axis: lax.rem(me + k, count)},
                device_id_type=MESH,
            )
            copy.start()
            copies.append(copy)
    for i in range(arrays):
        local = pltpu.make_async_copy(srcs[i], dsts[i].at[me], own.at[i])
        local.start()
        copies.append(local)
    for copy in copies:
        copy.wait()


def trade_kernel(axis, count, x_ref, o_ref, send, recv, own):
    me = greet(axis, count)
    copies = []
    for k in range(1, count):
        other = lax.rem(me + k, count)
        copy = pltpu.make_async_remote_copy(
            src_ref=x_ref.at[other],
            dst_ref=o_ref.at[me],
            send_sem=send.at[k],
            recv_sem=recv.at[k],
            device_id={axis: other},
            device_id_type=MESH,
        )
        copy.start()
        copies.append(copy)
    local = pltpu.make_async_copy(x_ref.at[me], o_ref.at[me], own)
    local.start()
    local.wait()
    for copy in copies:
        copy.wait()


def trade(x, axis, cid, us):
    count = lax.axis_size(axis)
    return pl.pallas_call(
        functools.partial(trade_kernel, axis, count),
        out_shape=jax.ShapeDtypeStruct(x.shape, x.dtype),
        in_specs=[pl.BlockSpec(memory_space=pl.ANY)],
        out_specs=pl.BlockSpec(memory_space=pl.ANY),
        scratch_shapes=[
            pltpu.SemaphoreType.DMA((count,)),
            pltpu.SemaphoreType.DMA((count,)),
            pltpu.SemaphoreType.DMA,
        ],
        compiler_params=pltpu.CompilerParams(
            collective_id=cid, has_side_effects=True, vmem_limit_bytes=VMEM_LIMIT
        ),
        cost_estimate=lasting(us),
        name=f"trade_{cid}",
    )(x)


def gather_all(xs, axis, cid, us):
    count, arrays = lax.axis_size(axis), len(xs)
    return pl.pallas_call(
        functools.partial(gather_kernel, axis, count, arrays),
        out_shape=[jax.ShapeDtypeStruct((count,) + x.shape, x.dtype) for x in xs],
        in_specs=[pl.BlockSpec(memory_space=pl.ANY)] * arrays,
        out_specs=[pl.BlockSpec(memory_space=pl.ANY)] * arrays,
        scratch_shapes=[
            pltpu.SemaphoreType.DMA((arrays, count)),
            pltpu.SemaphoreType.DMA((arrays, count)),
            pltpu.SemaphoreType.DMA((arrays,)),
        ],
        compiler_params=pltpu.CompilerParams(
            collective_id=cid, has_side_effects=True, vmem_limit_bytes=VMEM_LIMIT
        ),
        cost_estimate=lasting(us),
        name=f"gather_{cid}",
    )(*xs)


def remote(src, dst, send, recv, where):
    return pltpu.make_async_remote_copy(
        src_ref=src, dst_ref=dst, send_sem=send, recv_sem=recv,
        device_id=where, device_id_type=MESH,
    )


def add_rows(out, parts, rows):
    def one(i, _):
        at = pl.ds(pl.multiple_of(i * 16, 16), 16)
        total = parts[0][at, :].astype(F32)
        for part in parts[1:]:
            total = total + part[at, :].astype(F32)
        out[at, :] = total.astype(out.dtype)
        return 0

    lax.fori_loop(0, rows // 16, one, 0)


def neighbours(ring):
    me = lax.axis_index("ctx")
    half = ring // 2
    lane = lax.rem(me, 2)
    chip = me // 2
    peers = [lax.rem(chip + k, half) * 2 + lane for k in range(1, half)]
    return me, chip, lane, me + 1 - 2 * lane, peers


def mates_of(group):
    mine = lax.axis_index("wa")
    return mine, [lax.rem(mine + k, group) for k in range(1, group)]


def hello(barrier, axis, who):
    pl.semaphore_signal(barrier, inc=1, device_id={axis: who}, device_id_type=MESH)


def carry_back_kernel(ring, f_ref, g_ref, f_o, p_o, send, recv, own, pair_s, pair_r):
    me, _, lane, pair, _ = neighbours(ring)
    greet("ctx", ring)
    to_pair = remote(g_ref.at[:, 1 - lane], p_o, pair_s, pair_r, {"ctx": pair})
    copies = []
    for k in range(1, ring):
        copy = remote(f_ref, f_o.at[me], send.at[k], recv.at[k], {"ctx": lax.rem(me + k, ring)})
        copy.start()
        copies.append(copy)
    to_pair.start()
    local = pltpu.make_async_copy(f_ref, f_o.at[me], own)
    local.start()
    for copy in copies + [to_pair, local]:
        copy.wait()


def carry_back(f, g, cid, us):
    ring = lax.axis_size("ctx")
    hbm = pl.BlockSpec(memory_space=pl.ANY)
    dma = pltpu.SemaphoreType.DMA
    return pl.pallas_call(
        functools.partial(carry_back_kernel, ring),
        out_shape=[
            jax.ShapeDtypeStruct((ring,) + f.shape, f.dtype),
            jax.ShapeDtypeStruct(g.shape[:1] + g.shape[2:], g.dtype),
        ],
        in_specs=[hbm] * 2,
        out_specs=[hbm] * 2,
        scratch_shapes=[dma((ring,)), dma((ring,)), dma, dma, dma],
        compiler_params=pltpu.CompilerParams(
            collective_id=cid, has_side_effects=True, vmem_limit_bytes=VMEM_LIMIT
        ),
        cost_estimate=lasting(us),
        name="carry_back",
    )(f, g)


def proj_back_kernel(
    ring, group, x_ref, g_ref, p_ref, x_o, g_o,
    kept, paired, came, mate_s, mate_r, own_s, load, ctx_s, ctx_r,
):
    _, chip, lane, _, peers = neighbours(ring)
    mine, mates = mates_of(group)
    half = ring // 2
    rows = g_o.shape[0]
    loads = [
        pltpu.make_async_copy(g_ref.at[:, lane], kept, load.at[0]),
        pltpu.make_async_copy(p_ref, paired, load.at[1]),
    ]
    for copy in loads:
        copy.start()
    barrier = pltpu.get_barrier_semaphore()
    for who in peers:
        hello(barrier, "ctx", who)
    for who in mates:
        hello(barrier, "wa", who)
    pl.semaphore_wait(barrier, half + group - 2)
    copies = []
    for k, who in enumerate(mates):
        copy = remote(x_ref, x_o.at[mine], mate_s.at[k], mate_r.at[k], {"wa": who})
        copy.start()
        copies.append(copy)
    local = pltpu.make_async_copy(x_ref, x_o.at[mine], own_s)
    local.start()
    for copy in loads:
        copy.wait()
    scattered = []
    for k, who in enumerate(peers):
        to = lax.rem(chip + k + 1, half)
        add_rows(kept.at[to], [kept.at[to], paired.at[to]], rows)
        copy = remote(kept.at[to], came.at[k], ctx_s.at[k], ctx_r.at[k], {"ctx": who})
        copy.start()
        scattered.append(copy)
    add_rows(kept.at[chip], [kept.at[chip], paired.at[chip]], rows)
    for copy in scattered:
        copy.wait_recv()
    add_rows(g_o, [kept.at[chip]] + [came.at[k] for k in range(half - 1)], rows)
    for copy in scattered:
        copy.wait_send()
    for copy in copies + [local]:
        copy.wait()


def proj_back(x, g, p, cid, us):
    ring, group = lax.axis_size("ctx"), lax.axis_size("wa")
    half = ring // 2
    hbm = pl.BlockSpec(memory_space=pl.ANY)
    dma = pltpu.SemaphoreType.DMA
    block = pltpu.VMEM((half,) + g.shape[2:], g.dtype)
    return pl.pallas_call(
        functools.partial(proj_back_kernel, ring, group),
        out_shape=[
            jax.ShapeDtypeStruct((group,) + x.shape, x.dtype),
            jax.ShapeDtypeStruct(g.shape[2:], g.dtype),
        ],
        in_specs=[hbm] * 3,
        out_specs=[hbm, pl.BlockSpec(memory_space=pltpu.VMEM)],
        scratch_shapes=[
            block, block, pltpu.VMEM((half - 1,) + g.shape[2:], g.dtype),
            dma((group - 1,)), dma((group - 1,)), dma, dma((2,)),
            dma((half - 1,)), dma((half - 1,)),
        ],
        compiler_params=pltpu.CompilerParams(
            collective_id=cid, has_side_effects=True, vmem_limit_bytes=VMEM_LIMIT
        ),
        cost_estimate=lasting(us),
        name="proj_back",
    )(x, g, p)


def finish_kernel(
    ring, group, in_rows, small_rows,
    g_ref, zf_ref, d_ref, o_ref, dt_ref, de_ref,
    from_pair, paired, came, own, zin, tiles,
    pair_s, pair_r, ctx_s, ctx_r, z_s, z_r, tile_s, tile_r, d_s, d_r, d_own, last_s, last_r, fwd_s, fwd_r,
    edge_s, edge_r,
):
    me, chip, lane, pair, peers = neighbours(ring)
    mine, mates = mates_of(group)
    half = ring // 2
    rows = in_rows + small_rows + 16
    lanes = g_ref.shape[3]
    barrier = pltpu.get_barrier_semaphore()
    for who in [pair] + peers:
        hello(barrier, "ctx", who)
    for who in mates:
        hello(barrier, "wa", who)
    has_next = me < ring - 1
    has_last = me > 0

    @pl.when(has_next)
    def _():
        hello(barrier, "ctx", me + 1)

    @pl.when(has_last)
    def _():
        hello(barrier, "ctx", me - 1)

    around = jnp.where(has_next, 1, 0) + jnp.where(has_last, 1, 0)
    pl.semaphore_wait(barrier, half + group - 1 + around)

    to_pair = remote(g_ref.at[:, 1 - lane], from_pair, pair_s, pair_r, {"ctx": pair})
    to_pair.start()
    ready = 2 * in_rows + small_rows + 16
    parts = [pl.ds(ready, in_rows), pl.ds(0, ready)]
    o_ref[me, parts[0]] = zf_ref[:, lanes:]

    def to_all(i):
        src = o_ref.at[me, parts[i]]
        copies = []
        for k, who in enumerate(peers):
            copies.append(remote(src, src, last_s.at[i, k], last_r.at[i, k], {"ctx": who}))
        copies.append(remote(src, src, fwd_s.at[i, 0], fwd_r.at[i, 0], {"ctx": pair}))
        for copy in copies:
            copy.start()
        return copies

    def forward(i, copies):
        for k in range(1, half):
            copies[k - 1].wait_recv()
            source = lax.rem(chip + half - k, half) * 2 + lane
            block = o_ref.at[source, parts[i]]
            copy = remote(block, block, fwd_s.at[i, k], fwd_r.at[i, k], {"ctx": pair})
            copy.start()
            copies.append(copy)

    early = to_all(0)

    x_to = mine // 2
    z_to = group // 2 + mine // 2
    slot = lax.rem(mine, 2)
    z_ref = zf_ref.at[:, pl.ds(0, lanes)]
    x_ref = own.at[pl.ds(0, in_rows)]
    send_x = remote(x_ref, zin.at[slot], z_s.at[0], z_r.at[slot], {"wa": x_to})
    send_z = remote(z_ref, zin.at[slot], z_s.at[1], z_r.at[slot], {"wa": z_to})
    keep_x = pltpu.make_async_copy(x_ref, zin.at[slot], z_r.at[slot])
    keep_z = pltpu.make_async_copy(z_ref, zin.at[slot], z_r.at[slot])

    @pl.when(z_to != mine)
    def _():
        send_z.start()

    @pl.when(z_to == mine)
    def _():
        keep_z.start()

    cut = d_ref.shape[1] // 32 * 16
    pieces = [pl.ds(0, cut), pl.ds(cut, d_ref.shape[1] - cut)]
    trades = []

    def trade_rows(i):
        for k, who in enumerate(mates):
            copy = remote(
                d_ref.at[who, pieces[i]], dt_ref.at[mine, pieces[i]], d_s.at[i, k], d_r.at[i, k],
                {"wa": who},
            )
            copy.start()
            trades.append(copy)

    trade_rows(0)
    kept = pltpu.make_async_copy(d_ref.at[mine], dt_ref.at[mine], d_own)
    kept.start()

    to_pair.wait_recv()
    scattered = []
    for k, who in enumerate(peers):
        to = lax.rem(chip + k + 1, half)
        add_rows(paired.at[to], [g_ref.at[to, lane], from_pair.at[to]], rows)
        copy = remote(paired.at[to], came.at[k], ctx_s.at[k], ctx_r.at[k], {"ctx": who})
        copy.start()
        scattered.append(copy)
    add_rows(paired.at[chip], [g_ref.at[chip, lane], from_pair.at[chip]], rows)
    for copy in scattered:
        copy.wait_recv()
    add_rows(own, [paired.at[chip]] + [came.at[k] for k in range(half - 1)], rows)

    @pl.when(x_to != mine)
    def _():
        send_x.start()

    @pl.when(x_to == mine)
    def _():
        keep_x.start()

    tile = pl.ds(in_rows + small_rows, 16)
    spread_tiles = []
    for k, who in enumerate(mates):
        copy = remote(own.at[tile], tiles.at[k], tile_s.at[k], tile_r.at[k], {"wa": who})
        copy.start()
        spread_tiles.append(copy)
    forward(0, early)
    o_ref[me, pl.ds(2 * in_rows, small_rows)] = own[pl.ds(in_rows, small_rows)]
    for copy in spread_tiles:
        copy.wait_recv()
    add_rows(
        o_ref.at[me, pl.ds(2 * in_rows + small_rows, 16)],
        [own.at[tile]] + [tiles.at[k] for k in range(group - 1)],
        16,
    )
    for s in range(2):
        pltpu.make_async_copy(zin.at[s], zin.at[s], z_r.at[s]).wait()
        o_ref[me, pl.ds(s * in_rows, in_rows)] = zin[s]
    late = to_all(1)
    trade_rows(1)
    kept.wait()
    forward(1, late)

    for copy in trades:
        copy.wait_recv()
    edges = dt_ref.at[:, pl.ds(d_ref.shape[1] - EDGE, EDGE)]
    to_last = remote(edges, de_ref, edge_s, edge_r, {"ctx": me - 1})

    @pl.when(has_last)
    def _():
        to_last.start()

    for copies in (early, late):
        for copy in copies[half - 1 :]:
            copy.wait_recv()

    to_pair.wait_send()
    for copy in scattered + spread_tiles + early + late + trades:
        copy.wait_send()

    @pl.when(x_to != mine)
    def _():
        send_x.wait_send()

    @pl.when(z_to != mine)
    def _():
        send_z.wait_send()

    @pl.when(has_last)
    def _():
        to_last.wait_send()

    @pl.when(has_next)
    def _():
        to_last.wait_recv()


def finish(g, zf, d, in_rows, small_rows, cid):
    ring, group = lax.axis_size("ctx"), lax.axis_size("wa")
    half = ring // 2
    rows, lanes = g.shape[2:]
    out_rows = 3 * in_rows + small_rows + 16
    vmem = pl.BlockSpec(memory_space=pltpu.VMEM)
    hbm = pl.BlockSpec(memory_space=pl.ANY)
    dma = pltpu.SemaphoreType.DMA
    return pl.pallas_call(
        functools.partial(finish_kernel, ring, group, in_rows, small_rows),
        out_shape=[
            jax.ShapeDtypeStruct((ring, out_rows, lanes), BF16),
            jax.ShapeDtypeStruct(d.shape, d.dtype),
            jax.ShapeDtypeStruct((group, EDGE, d.shape[2]), d.dtype),
        ],
        in_specs=[vmem, vmem, hbm],
        out_specs=[vmem, hbm, hbm],
        scratch_shapes=[
            pltpu.VMEM((half, rows, lanes), BF16),
            pltpu.VMEM((half, rows, lanes), BF16),
            pltpu.VMEM((half - 1, rows, lanes), BF16),
            pltpu.VMEM((rows, lanes), BF16),
            pltpu.VMEM((2, in_rows, lanes), BF16),
            pltpu.VMEM((group - 1, 16, lanes), BF16),
            dma, dma,
            dma((half - 1,)), dma((half - 1,)),
            dma((2,)), dma((2,)),
            dma((group - 1,)), dma((group - 1,)),
            dma((2, group - 1)), dma((2, group - 1)), dma,
            dma((2, half - 1)), dma((2, half - 1)),
            dma((2, half)), dma((2, half)),
            dma, dma,
        ],
        compiler_params=pltpu.CompilerParams(
            collective_id=cid, has_side_effects=True, vmem_limit_bytes=VMEM_LIMIT
        ),
        cost_estimate=lasting(60),
        name="finish",
    )(g, zf, d)


def start_kernel(
    ring, group, tok, par, doc, w_ref, tok_o, edge_o, par_o, doc_o, w_o,
    mate_s, mate_r, own_s, edge_s, edge_r, relay_s, relay_r, shift_s, shift_r, out_s, out_r, fwd_s, fwd_r,
):
    me = lax.axis_index("ctx")
    mine = lax.axis_index("wa")
    half = ring // 2
    lane = lax.rem(me, 2)
    chip = me // 2
    pair = me + 1 - 2 * lane
    peers = [lax.rem(chip + k, half) * 2 + lane for k in range(1, half)]
    mates = [lax.rem(mine + k, group) for k in range(1, group)]
    barrier = pltpu.get_barrier_semaphore()
    for who in [pair] + peers:
        pl.semaphore_signal(barrier, inc=1, device_id={"ctx": who}, device_id_type=MESH)
    for who in mates:
        pl.semaphore_signal(barrier, inc=1, device_id={"wa": who}, device_id_type=MESH)
    has_next = me < ring - 1
    has_last = me > 0

    @pl.when(has_next)
    def _():
        pl.semaphore_signal(barrier, inc=1, device_id={"ctx": me + 1}, device_id_type=MESH)

    @pl.when(has_last)
    def _():
        pl.semaphore_signal(barrier, inc=1, device_id={"ctx": me - 1}, device_id_type=MESH)

    around = jnp.where(has_next, 1, 0) + jnp.where(has_last, 1, 0)
    pl.semaphore_wait(barrier, half + group - 1 + around)

    edge = tok.at[pl.ds(tok.shape[0] - EDGE, EDGE)]
    to_next = remote(edge, edge_o.at[mine], edge_s, edge_r, {"ctx": me + 1})

    @pl.when(has_next)
    def _():
        to_next.start()

    kind = mine // (group // 2)
    base = 2 * lax.rem(mine, group // 2)
    for h in range(2):
        where = base + h
        send = remote(
            w_ref.at[h], w_o.at[kind, me], shift_s.at[h], shift_r.at[kind], {"wa": where}
        )
        keep = pltpu.make_async_copy(w_ref.at[h], w_o.at[kind, me], shift_r.at[kind])

        @pl.when(where != mine)
        def _():
            send.start()

        @pl.when(where == mine)
        def _():
            keep.start()

    trades = []
    for i, (src, dst) in enumerate(((par, par_o), (doc, doc_o), (tok, tok_o))):
        for k, who in enumerate(mates):
            copy = remote(src, dst.at[mine], mate_s.at[i, k], mate_r.at[i, k], {"wa": who})
            copy.start()
            trades.append(copy)
        keep = pltpu.make_async_copy(src, dst.at[mine], own_s.at[i])
        keep.start()

    @pl.when(has_last)
    def _():
        to_next.wait_recv()
        for k, who in enumerate(mates):
            remote(
                edge_o.at[mine], edge_o.at[mine], relay_s.at[k], relay_r.at[k], {"wa": who}
            ).start()

    sends = []
    for t in range(2):
        block = w_o.at[t, me]
        pltpu.make_async_copy(block, block, shift_r.at[t]).wait()
        for k, who in enumerate(peers):
            copy = remote(block, block, out_s.at[t, k], out_r.at[t, k], {"ctx": who})
            copy.start()
            sends.append(copy)
        copy = remote(block, block, fwd_s.at[t, 0], fwd_r.at[t, 0], {"ctx": pair})
        copy.start()
        sends.append(copy)
    forwards = []
    for t in range(2):
        for k in range(1, half):
            source = lax.rem(chip + half - k, half) * 2 + lane
            block = w_o.at[t, source]
            pltpu.make_async_copy(block, block, out_r.at[t, k - 1]).wait()
            copy = remote(block, block, fwd_s.at[t, k], fwd_r.at[t, k], {"ctx": pair})
            copy.start()
            forwards.append(copy)
    for t in range(2):
        for k in range(half):
            pltpu.make_async_copy(w_o.at[t, me], w_o.at[t, me], fwd_r.at[t, k]).wait()
    for copy in sends + forwards:
        copy.wait_send()
    for h in range(2):

        @pl.when(base + h != mine)
        def _():
            remote(
                w_ref.at[h], w_o.at[kind, me], shift_s.at[h], shift_r.at[kind], {"wa": mine}
            ).wait_send()

    for copy in trades:
        copy.wait()
    for i, (src, dst) in enumerate(((par, par_o), (doc, doc_o), (tok, tok_o))):
        pltpu.make_async_copy(src, dst.at[mine], own_s.at[i]).wait()

    @pl.when(has_next)
    def _():
        to_next.wait_send()

    @pl.when(has_last)
    def _():
        for k, who in enumerate(mates):
            remote(
                edge_o.at[mine], edge_o.at[mine], relay_s.at[k], relay_r.at[k], {"wa": who}
            ).wait()


def start(tok, par, doc, halves, cid):
    ring, group = lax.axis_size("ctx"), lax.axis_size("wa")
    half = ring // 2
    hbm = pl.BlockSpec(memory_space=pl.ANY)
    dma = pltpu.SemaphoreType.DMA
    outs = [(group,) + a.shape for a in (tok, tok[:EDGE], par, doc)] + [(2, ring) + halves.shape[1:]]
    types = [a.dtype for a in (tok, tok, par, doc, halves)]
    return pl.pallas_call(
        functools.partial(start_kernel, ring, group),
        out_shape=[jax.ShapeDtypeStruct(s, t) for s, t in zip(outs, types)],
        in_specs=[hbm] * 4,
        out_specs=[hbm] * 5,
        scratch_shapes=[
            dma((3, group - 1)), dma((3, group - 1)), dma((3,)),
            dma, dma,
            dma((group - 1,)), dma((group - 1,)),
            dma((2,)), dma((2,)),
            dma((2, half - 1)), dma((2, half - 1)),
            dma((2, half)), dma((2, half)),
        ],
        compiler_params=pltpu.CompilerParams(
            collective_id=cid, has_side_effects=True, vmem_limit_bytes=VMEM_LIMIT
        ),
        cost_estimate=lasting(35),
        name="start",
    )(tok, par, doc, halves)


def pick(rows, states, at):
    shape = (rows, states * LANE)
    lower = (lax.broadcasted_iota(jnp.int32, shape, 0) - at) * LANE
    place = lax.broadcasted_iota(jnp.int32, shape, 1)
    return jnp.where((place >= lower) & (place < lower + LANE), 1.0, 0.0)


def spread(rows, states, at):
    return jnp.dot(rows, pick(rows.shape[1], states, at).astype(BF16), preferred_element_type=F32)


def collected(wide_rows, states, columns, at):
    shape = (states * LANE, columns)
    lower = (lax.broadcasted_iota(jnp.int32, shape, 1) - at) * LANE
    place = lax.broadcasted_iota(jnp.int32, shape, 0)
    ones = jnp.where((place >= lower) & (place < lower + LANE), 1.0, 0.0)
    return jnp.dot(wide_rows, ones, precision=lax.Precision.HIGHEST, preferred_element_type=F32)


def position_of(shape, axis, steps):
    row = lax.broadcasted_iota(jnp.int32, shape, axis)
    return (row & (SEG - 1)) * steps + (row >> 3)


def permutation(length):
    shape = (length, length)
    at = position_of(shape, 0, length // SEG)
    return jnp.where(at == lax.broadcasted_iota(jnp.int32, shape, 1), 1.0, 0.0).astype(BF16)


def rolled(value, by):
    return pltpu.roll(value, by % SEG, 0)


def lanes_of(g):
    return pl.ds(pl.multiple_of(g * LANE, LANE), LANE)


def rows_of(j):
    return pl.ds(pl.multiple_of(j * SEG, SEG), SEG)


def wide(ref, n, lanes):
    return jnp.broadcast_to(ref[pl.ds(n, 1), lanes], (SEG, LANE))


def state_cols(n):
    return slice(n * LANE, (n + 1) * LANE)


def dot_nt(a, b):
    return lax.dot_general(a, b, (((1,), (1,)), ((), ())), preferred_element_type=F32)


def dot_tn(a, b):
    return lax.dot_general(a, b, (((0,), (0,)), ((), ())), preferred_element_type=F32)


def dot_nn(a, b):
    return jnp.dot(a, b, preferred_element_type=F32)


def rms_scale(values):
    return lax.rsqrt(jnp.mean(values * values, axis=-1, keepdims=True) + EPS)


def norm_grads(values, scale, gain, d_out):
    unit = values * scale
    d_unit = d_out * gain
    d_values = scale * (d_unit - unit * jnp.mean(d_unit * unit, axis=-1, keepdims=True))
    return d_values, d_out * unit


def silu_slope(v):
    s = jax.nn.sigmoid(v)
    return s * (1.0 + v * (1.0 - s))


def seg_of():
    return lax.broadcasted_iota(jnp.int32, (SEG, LANE), 0)


def lag_masks(place, doc_ref, stream, length, taps):
    at = place * length + position_of((length, LANE), 0, length // SEG)
    masks = [None]
    for lag in range(1, taps):
        cut = None
        for d in range(doc_ref.shape[1]):
            begin = doc_ref[stream, d]
            here = (begin > at - lag) & (begin <= at)
            cut = here if cut is None else cut | here
        masks.append(jnp.where(cut, 0.0, 1.0))
    hit = None
    for d in range(doc_ref.shape[1]):
        here = doc_ref[stream, d] == at
        hit = here if hit is None else hit | here
    return masks, jnp.where(hit, CUT, 0.0)


def enter_kernel(
    taps, place_ref, doc_ref, tok, edge, gain, wx, wz, conv, wproj,
    n1_o, ext_o, pre_o, uf_o, u_o, z_o, part_o, cut_o,
):
    length = tok.shape[1]
    steps = length // SEG
    place = place_ref[0]
    gains = gain[...]

    def normal(rows):
        return (rows * rms_scale(rows) * gains).astype(BF16)

    n1_o[0, :length] = normal(dot_nn(permutation(length), tok[0]))
    n1_o[0, length:] = normal(jnp.where(place > 0, edge[0].astype(F32), 0.0))
    inner = dot_nn(n1_o[0], wx[0]).astype(BF16).astype(F32)
    z_o[0] = dot_nn(n1_o[0, :length], wz[0]).astype(BF16)
    masks, cut = lag_masks(place, doc_ref, pl.program_id(0), length, taps)
    cut_o[0] = cut
    seg = seg_of()
    behind = taps - 1
    for g in range(inner.shape[1] // LANE):
        cols = slice(g * LANE, (g + 1) * LANE)
        rows, before = inner[:length, cols], inner[length:, cols]
        parts = []
        for i in range(behind):
            j = steps - behind + i
            last = jnp.broadcast_to(before[EDGE - behind + i : EDGE - behind + i + 1], (SEG, LANE))
            parts.append(jnp.where(seg == 0, last, rolled(rows[j * SEG : (j + 1) * SEG], 1)))
        ext = jnp.concatenate(parts + [rows], axis=0)
        ext_o[0, :, cols] = ext
        pre = conv[taps : taps + 1, cols] + conv[0:1, cols] * rows
        for lag in range(1, taps):
            window = ext[(behind - lag) * SEG : (behind - lag) * SEG + length]
            pre = pre + conv[lag : lag + 1, cols] * window * masks[lag]
        pre_o[0, :, cols] = pre
        u = (pre * jax.nn.sigmoid(pre)).astype(BF16)
        u_o[0, :, cols] = u
        uf_o[0, :, cols] = u.astype(F32)
    part_o[0] = dot_nn(u_o[0], wproj[...]).astype(BF16)


def summary_kernel(
    states, b_at, terms, wdt, bias, uf, cut, a_ref,
    proj_o, step_o, sig_o, hx_ref, sx_ref, hd_o, sd_ref, bb, st_s, dr_s, hd_s,
):
    length, width = step_o.shape[1:]
    groups, steps = width // LANE, length // SEG
    total = terms[0, 0].astype(F32)
    for w in range(1, terms.shape[0]):
        total = total + terms[w, 0].astype(F32)
    proj = total.astype(BF16)
    proj_o[0] = proj
    bb[...] = spread(proj, states, b_at)
    pre = dot_nn(proj, wdt[...]) + bias[...]
    step_size = jnp.maximum(pre, 0.0) + jnp.log1p(jnp.exp(-jnp.abs(pre)))
    step_o[0] = step_size
    sig_o[0] = jax.nn.sigmoid(pre)
    dr_s[...] = step_size * uf[0]
    for g in range(groups):
        cols = slice(g * LANE, (g + 1) * LANE)
        st_s[:, cols] = step_size[:, cols] + cut[0]
    zero = jnp.zeros((SEG, LANE), F32)
    seg = seg_of()

    def group(g, _):
        lanes = lanes_of(g)
        a = [wide(a_ref, n, lanes) for n in range(states)]

        def step(j, carry):
            rows = rows_of(j)
            st = st_s[rows, lanes]
            dr = dr_s[rows, lanes]
            new = [carry[0] + st]
            for n in range(states):
                new.append(jnp.exp(st * a[n]) * carry[n + 1] + bb[rows, state_cols(n)] * dr)
            return tuple(new)

        out = lax.fori_loop(0, steps, step, (zero,) * (states + 1), unroll=2)
        total, h = out[0], list(out[1:])
        for k in (1, 2, 4):
            ok = seg >= k
            for n in range(states):
                h[n] = h[n] + jnp.where(ok, jnp.exp(total * a[n]) * rolled(h[n], k), 0.0)
            total = total + jnp.where(ok, rolled(total, k), 0.0)
        ok = seg >= 1
        sx_ref[0, :, lanes] = jnp.where(ok, rolled(total, 1), 0.0)
        sd_ref[0, :, lanes] = total[SEG - 1 : SEG]
        for n in range(states):
            hx_ref[0, n, :, lanes] = jnp.where(ok, rolled(h[n], 1), 0.0)
            hd_s[pl.ds(n, 1), lanes] = h[n][SEG - 1 : SEG]
        return 0

    lax.fori_loop(0, groups, group, 0)
    hd_o[0] = hd_s[...].astype(BF16)


def entering(e_ref, finals, sums, a_ref, place, ahead):
    ring = finals.shape[0]
    e_ref[...] = jnp.zeros_like(e_ref)

    def one(lap, _):
        c = lap if ahead else ring - 1 - lap
        use = (c < place) if ahead else (c > place)

        @pl.when(use)
        def _():
            e_ref[...] = jnp.exp(sums[c, 0] * a_ref[...]) * e_ref[...] + finals[c, 0].astype(F32)

        return 0

    lax.fori_loop(0, ring, one, 0)


def output_kernel(
    states, b_at, place_ref, proj, step_i, uf, cut, a_ref, hx_ref, sx_ref, finals, sums, z, skip, wout,
    y_o, gated_o, mix_o, e_o, bb, cb, st_s, dr_s,
):
    length, width = step_i.shape[1:]
    groups, steps = width // LANE, length // SEG
    bb[...] = spread(proj[0], states, b_at)
    cb[...] = spread(proj[0], states, b_at + states)
    e_ref = e_o.at[0]
    entering(e_ref, finals, sums, a_ref, place_ref[0], True)
    dr_s[...] = step_i[0] * uf[0]
    for g in range(groups):
        cols = slice(g * LANE, (g + 1) * LANE)
        st_s[:, cols] = step_i[0, :, cols] + cut[0]

    def group(g, _):
        lanes = lanes_of(g)
        a = [wide(a_ref, n, lanes) for n in range(states)]
        sx = sx_ref[0, :, lanes]
        first = tuple(
            jnp.exp(sx * a[n]) * wide(e_ref, n, lanes) + hx_ref[0, n, :, lanes]
            for n in range(states)
        )
        gain = wide(skip, 0, lanes)

        def step(j, h):
            rows = rows_of(j)
            st = st_s[rows, lanes]
            dr = dr_s[rows, lanes]
            new = []
            y = gain * uf[0, rows, lanes]
            for n in range(states):
                state = jnp.exp(st * a[n]) * h[n] + bb[rows, state_cols(n)] * dr
                new.append(state)
                y = y + cb[rows, state_cols(n)] * state
            y_o[0, rows, lanes] = y
            return tuple(new)

        lax.fori_loop(0, steps, step, first, unroll=2)
        return 0

    lax.fori_loop(0, groups, group, 0)
    zf = z[0].astype(F32)
    gated = (y_o[0] * (zf * jax.nn.sigmoid(zf))).astype(BF16)
    gated_o[0] = gated
    mix_o[0] = dot_nn(gated, wout[...]).astype(BF16)


def route_kernel(
    experts, terms, tok, gain, router, route, keep, grad,
    h1_o, n2_o, up_o, cols_o, match_o, out_o, sums_o,
):
    length, width = tok.shape
    shift = permutation(length)
    mix = terms[0].astype(F32)
    for w in range(1, terms.shape[0]):
        mix = mix + terms[w].astype(F32)
    h1 = dot_nn(shift, tok[...]) + mix
    h1_o[...] = h1
    n2 = (h1 * rms_scale(h1) * gain[...]).astype(BF16)
    n2_o[...] = n2
    logits = dot_nt(n2, router[...])
    lane = lax.broadcasted_iota(jnp.int32, (length, LANE), 1)
    named = route[...]
    onehot = jnp.where(named == lane, 1.0, 0.0)
    one = lax.broadcasted_iota(jnp.int32, (length, length), 0)
    two = lax.broadcasted_iota(jnp.int32, (length, length), 1)
    earlier = jnp.where(two < one, 1.0, 0.0).astype(BF16)
    before = dot_nn(earlier, onehot.astype(BF16))
    within = jnp.sum(before * onehot, axis=1, keepdims=True)
    slot = named.astype(F32) * (length // 2) + within
    facts = jnp.where(lane == experts, slot, jnp.where(lane == experts + 1, keep[...].astype(F32), onehot))
    facts = dot_nn(shift, facts.astype(BF16))
    onehot = jnp.where(lane < experts, facts, 0.0)
    slot = jnp.sum(jnp.where(lane == experts, facts, 0.0), axis=1, keepdims=True)
    kept = jnp.sum(jnp.where(lane == experts + 1, facts, 0.0), axis=1, keepdims=True)
    sig = jax.nn.sigmoid(jnp.sum(logits * onehot, axis=1, keepdims=True))
    gates = kept * sig
    cols_o[...] = jnp.where(
        lane == experts, gates, jnp.where(lane == experts + 1, gates * (1.0 - sig), onehot)
    )
    up = dot_nn(shift, grad[...])
    up_o[...] = up
    slots = match_o.shape[1]
    spot = lax.broadcasted_iota(jnp.int32, (length, slots), 1).astype(F32)
    match = jnp.where(slot == spot, 1.0, 0.0).astype(BF16)
    match_o[...] = match
    out_o[:, :width] = dot_tn(match, n2).astype(BF16)
    out_o[:, width:] = dot_tn(match, (gates * up).astype(BF16)).astype(BF16)
    sums_o[...] = jnp.broadcast_to(jnp.sum(mix * mix, keepdims=True), (SEG, LANE))


def pack_kernel(up, down, _, out):
    width = up.shape[0]
    units = up.shape[1]
    line = lax.broadcasted_iota(jnp.int32, (units, units), 0)
    same = jnp.where(line == lax.broadcasted_iota(jnp.int32, (units, units), 1), 1.0, 0.0)
    out[:, :width] = dot_nt(same.astype(BF16), up[...]).astype(BF16)
    out[:, width:] = down[...]


def experts_kernel(x_ref, w_ref, g_ref, o_ref, acc):
    width = x_ref.shape[1] // 2
    at = pl.program_id(0)

    @pl.when(at == 0)
    def _():
        acc[...] = jnp.zeros_like(acc)

    up, down = w_ref[:, :width], w_ref[:, width:]
    rows, d_out = x_ref[:, :width], x_ref[:, width:]
    hidden = dot_nt(up, rows)
    d_act = dot_nt(down, d_out)
    c = 0.7978845608
    t = jnp.tanh(c * (hidden + 0.044715 * hidden * hidden * hidden))
    act = (0.5 * hidden * (1.0 + t)).astype(BF16)
    slope = 0.5 * (1.0 + t) + 0.5 * hidden * (1.0 - t * t) * c * (
        1.0 + 3.0 * 0.044715 * hidden * hidden
    )
    d_pre = (d_act * slope).astype(BF16)
    acc[:, :width] += dot_tn(act, down)
    acc[:, width:] += dot_tn(d_pre, up)
    g_ref[:, :width] = dot_nn(d_pre, rows).astype(BF16)
    g_ref[:, width:] = dot_nn(act, d_out).astype(BF16)

    @pl.when(at == pl.num_programs(0) - 1)
    def _():
        o_ref[...] = acc[...].astype(BF16)


def store_in_order(out, rows, order_s):
    steps = rows.shape[0] // SEG
    for g in range(rows.shape[1] // LANE):
        cols = slice(g * LANE, (g + 1) * LANE)
        for j in range(steps):
            order_s[g, pl.ds(j, SEG, stride=steps), :] = rows[j * SEG : (j + 1) * SEG, cols]
        out[:, cols] = order_s[g]


def combine_kernel(
    experts, back, match, h1_i, n2, up_i, cols, gain, router,
    out_o, dh_o, dmix_o, router_o, gain_o, sums_o, order_s,
):
    length, width = h1_i.shape
    h1, up = h1_i[...], up_i[...]
    lane = lax.broadcasted_iota(jnp.int32, (length, LANE), 1)
    facts = cols[...]

    def column(at):
        return jnp.sum(jnp.where(lane == at, facts, 0.0), axis=1, keepdims=True)

    gates, slope = column(experts), column(experts + 1)
    onehot = jnp.where(lane < experts, facts, 0.0)
    rows = dot_nn(match[...], back[:, :width])
    moe = gates * rows
    result = h1 + moe
    store_in_order(out_o, result, order_s)
    d_gate = jnp.sum(rows * up, axis=1, keepdims=True)
    d_logits = (onehot * (d_gate * slope)).astype(BF16)
    router_o[...] = dot_tn(d_logits, n2[...])
    d_n2 = dot_nn(match[...], back[:, width:]) + dot_nn(d_logits, router[...])
    d_norm, terms = norm_grads(h1, rms_scale(h1), gain[...], d_n2)
    gain_o[...] = jnp.sum(terms, axis=0, keepdims=True)
    d_h1 = up + d_norm
    dh_o[...] = d_h1
    dmix_o[...] = d_h1.astype(BF16)
    sums_o[0:1] = jnp.broadcast_to(jnp.sum(result * result, keepdims=True), (1, LANE))
    sums_o[1:2] = jnp.broadcast_to(jnp.sum(moe * moe, keepdims=True), (1, LANE))


def gate_back_kernel(
    states, c_at, d_mix, wout, y, z, uf, proj, step_i, cut, a_ref,
    dy_o, dz_o, skip_o, fx_ref, tx_ref, fd_o, cb, st_s, fd_s,
):
    length, width = step_i.shape[1:]
    groups, steps = width // LANE, length // SEG
    d_gated = dot_nt(d_mix[0], wout[...])
    zf = z[0].astype(F32)
    dy = d_gated * (zf * jax.nn.sigmoid(zf))
    dy_o[0] = dy
    dz_o[0, :length] = (d_gated * y[0] * silu_slope(zf)).astype(BF16)
    dz_o[0, length:] = jnp.zeros((EDGE, width), BF16)

    @pl.when(pl.program_id(0) == 0)
    def _():
        skip_o[...] = jnp.zeros_like(skip_o)

    skip_o[...] += jnp.sum(dy * uf[0], axis=0, keepdims=True)
    cb[...] = spread(proj[0], states, c_at)
    for g in range(groups):
        cols = slice(g * LANE, (g + 1) * LANE)
        st_s[:, cols] = step_i[0, :, cols] + cut[0]
    zero = jnp.zeros((SEG, LANE), F32)
    seg = seg_of()

    def group(g, _):
        lanes = lanes_of(g)
        a = [wide(a_ref, n, lanes) for n in range(states)]

        def step(lap, carry):
            rows = rows_of(steps - 1 - lap)
            st = st_s[rows, lanes]
            d = dy_o[0, rows, lanes]
            new = [carry[0] + st]
            for n in range(states):
                new.append(jnp.exp(st * a[n]) * (carry[n + 1] + cb[rows, state_cols(n)] * d))
            return tuple(new)

        out = lax.fori_loop(0, steps, step, (zero,) * (states + 1), unroll=2)
        total, f = out[0], list(out[1:])
        for k in (1, 2, 4):
            ok = seg < SEG - k
            for n in range(states):
                f[n] = f[n] + jnp.where(ok, jnp.exp(total * a[n]) * rolled(f[n], -k), 0.0)
            total = total + jnp.where(ok, rolled(total, -k), 0.0)
        ok = seg < SEG - 1
        tx_ref[0, :, lanes] = jnp.where(ok, rolled(total, -1), 0.0)
        for n in range(states):
            fx_ref[0, n, :, lanes] = jnp.where(ok, rolled(f[n], -1), 0.0)
            fd_s[pl.ds(n, 1), lanes] = f[n][0:1]
        return 0

    lax.fori_loop(0, groups, group, 0)
    fd_o[0] = fd_s[...].astype(BF16)


def scan_back_kernel(
    states, b_at, place_ref, proj, step_i, sig, uf, cut, dy_i, a_ref, skip, wdt, hx_ref, sx_ref, e_i,
    fx_ref, tx_ref, finals, sums,
    part_o, du_o, dt_o, bias_o, ga_ref,
    bb, cb, dec, pri, accb, accc, st_s, dr_s, ds_s, out_s,
):
    length, width = step_i.shape[1:]
    groups, steps = width // LANE, length // SEG
    bb[...] = spread(proj[0], states, b_at)
    cb[...] = spread(proj[0], states, b_at + states)
    accb[...] = jnp.zeros_like(accb)
    accc[...] = jnp.zeros_like(accc)
    entering(out_s, finals, sums, a_ref, place_ref[0], False)
    e_ref = e_i.at[0]
    dr_s[...] = step_i[0] * uf[0]
    for g in range(groups):
        cols = slice(g * LANE, (g + 1) * LANE)
        st_s[:, cols] = step_i[0, :, cols] + cut[0]

    @pl.when(pl.program_id(0) == 0)
    def _():
        ga_ref[...] = jnp.zeros_like(ga_ref)
        dt_o[...] = jnp.zeros_like(dt_o)
        bias_o[...] = jnp.zeros_like(bias_o)

    def group(g, _):
        lanes = lanes_of(g)
        a = [wide(a_ref, n, lanes) for n in range(states)]
        sx = sx_ref[0, :, lanes]
        first = tuple(
            jnp.exp(sx * a[n]) * wide(e_ref, n, lanes) + hx_ref[0, n, :, lanes]
            for n in range(states)
        )

        def ahead(j, h):
            rows = rows_of(j)
            st = st_s[rows, lanes]
            dr = dr_s[rows, lanes]
            new = []
            for n in range(states):
                decay = jnp.exp(st * a[n])
                dec[rows, state_cols(n)] = decay
                pri[rows, state_cols(n)] = h[n]
                new.append(decay * h[n] + bb[rows, state_cols(n)] * dr)
            return tuple(new)

        last = lax.fori_loop(0, steps, ahead, first, unroll=2)
        end = rows_of(steps)
        for n in range(states):
            pri[end, state_cols(n)] = last[n]
        tx = tx_ref[0, :, lanes]
        flow = tuple(
            jnp.exp(tx * a[n]) * wide(out_s, n, lanes) + fx_ref[0, n, :, lanes]
            for n in range(states)
        )
        gain = wide(skip, 0, lanes)

        def back(lap, f):
            j = steps - 1 - lap
            rows = rows_of(j)
            after = rows_of(j + 1)
            st = step_i[0, rows, lanes]
            dr = dr_s[rows, lanes]
            dy = dy_i[0, rows, lanes]
            new = []
            d_step = None
            d_drive = None
            for n in range(states):
                cols = state_cols(n)
                d = f[n] + cb[rows, cols] * dy
                accc[rows, cols] += pri[after, cols] * dy
                accb[rows, cols] += d * dr
                flowing = dec[rows, cols] * d
                new.append(flowing)
                d_log = flowing * pri[rows, cols]
                ga_ref[n, :, lanes] += d_log * st
                part = d_log * a[n]
                d_step = part if d_step is None else d_step + part
                part = d * bb[rows, cols]
                d_drive = part if d_drive is None else d_drive + part
            ds_s[rows, lanes] = (d_step + d_drive * uf[0, rows, lanes]) * sig[0, rows, lanes]
            du_o[0, rows, lanes] = d_drive * st + dy * gain
            return tuple(new)

        lax.fori_loop(0, steps, back, flow, unroll=2)
        return 0

    lax.fori_loop(0, groups, group, 0)
    d_pre = ds_s[...]
    bias_o[...] += jnp.sum(d_pre, axis=0, keepdims=True)
    d_pre = d_pre.astype(BF16)
    dt_o[...] += dot_tn(proj[0], d_pre)
    columns = part_o.shape[2]
    part = dot_nt(d_pre, wdt[...])
    part = part + collected(accb[...], states, columns, b_at)
    part = part + collected(accc[...], states, columns, b_at + states)
    part_o[0] = part.astype(BF16)


def conv_back_kernel(
    taps, place_ref, doc_ref, terms, wproj, du, pre, ext, u, conv, dz, wx, wz, n1,
    dx_o, dn_o, gconv_o, gx_o, gain_o, dext,
):
    length, width = du.shape[1:]
    steps = length // SEG
    behind = taps - 1

    @pl.when(pl.program_id(0) == 0)
    def _():
        gconv_o[...] = jnp.zeros_like(gconv_o)
        gx_o[...] = jnp.zeros_like(gx_o)
        gain_o[...] = jnp.zeros_like(gain_o)

    total = terms[0, 0].astype(F32)
    for w in range(1, terms.shape[0]):
        total = total + terms[w, 0].astype(F32)
    proj = total.astype(BF16)
    gx_o[...] += dot_tn(proj, u[0])
    d_u = dot_nt(proj, wproj[...]) + du[0]
    masks, _ = lag_masks(place_ref[0], doc_ref, pl.program_id(0), length, taps)
    seg = seg_of()
    row = lax.broadcasted_iota(jnp.int32, (EDGE, LANE), 0)
    for g in range(width // LANE):
        cols = slice(g * LANE, (g + 1) * LANE)
        d = d_u[:, cols] * silu_slope(pre[0, :, cols])
        gconv_o[taps : taps + 1, cols] += jnp.sum(d, axis=0, keepdims=True)
        dext[...] = jnp.zeros_like(dext)
        for lag in range(taps):
            weighted = d if lag == 0 else d * masks[lag]
            at = pl.ds((behind - lag) * SEG, length)
            gconv_o[lag : lag + 1, cols] += jnp.sum(weighted * ext[0, at, cols], axis=0, keepdims=True)
            dext[at, :] += weighted * conv[lag : lag + 1, cols]
        before = jnp.zeros((EDGE, LANE), F32)
        for i in range(behind):
            head = dext[i * SEG : (i + 1) * SEG]
            j = pl.ds((steps + i) * SEG, SEG)
            dext[j, :] += jnp.where(seg < SEG - 1, rolled(head, -1), 0.0)
            first = jnp.broadcast_to(head[0:1], (EDGE, LANE))
            before = before + jnp.where(row == EDGE - behind + i, first, 0.0)
        dx_o[0, :length, cols] = dext[behind * SEG :].astype(BF16)
        dx_o[0, length:, cols] = before.astype(BF16)
    d_n1 = dot_nt(dx_o[0], wx[0]) + dot_nt(dz[0], wz[0])
    gain_o[...] += jnp.sum(d_n1 * n1[0].astype(F32), axis=0, keepdims=True)
    dn_o[0] = d_n1.astype(BF16)


def leave_kernel(taps, last_ref, terms, edges, tok, gain, dh, out_o, dn_s, order_s):
    length = tok.shape[0]
    steps = length // SEG
    behind = taps - 1
    total = terms[0, :length].astype(F32)
    edge = edges[0].astype(F32)
    for w in range(1, terms.shape[0]):
        total = total + terms[w, :length].astype(F32)
        edge = edge + edges[w].astype(F32)
    edge = jnp.where(last_ref[0] > 0, 0.0, edge)
    dn_s[...] = total
    seg = lax.broadcasted_iota(jnp.int32, (SEG, tok.shape[1]), 0)
    for i in range(behind):
        j = pl.ds((steps - behind + i) * SEG, SEG)
        row = EDGE - behind + i
        came = jnp.broadcast_to(edge[row : row + 1], seg.shape)
        dn_s[j, :] += jnp.where(seg == SEG - 1, came, 0.0)
    x = dot_nn(permutation(length), tok[...])
    d_x, _ = norm_grads(x, rms_scale(x), gain[...], dn_s[...])
    result = dh[...] + d_x
    store_in_order(out_o, result, order_s)


SMEM = "smem"
ANY = "any"


def by_stream(shape, at=0):
    block = tuple(1 if i == at else n for i, n in enumerate(shape))
    rank = len(shape)

    def index(s):
        return tuple(s if i == at else 0 for i in range(rank))

    return pl.BlockSpec(block, index)


def whole(shape):
    return pl.BlockSpec(shape, lambda s: (0,) * len(shape))


def call(kernel, name, grid, args, outs, scratch, us):
    arrays, specs = [], []
    for array, at in args:
        arrays.append(array)
        if at == SMEM:
            specs.append(pl.BlockSpec(memory_space=pltpu.SMEM))
        elif at == ANY:
            specs.append(pl.BlockSpec(memory_space=pl.ANY))
        elif callable(at):
            specs.append(at(array.shape))
        else:
            specs.append(whole(array.shape) if at is None else by_stream(array.shape, at))
    out_specs = []
    for shape, _, at in outs:
        if callable(at):
            out_specs.append(at(shape))
        else:
            out_specs.append(whole(shape) if at is None else by_stream(shape, at))
    return pl.pallas_call(
        kernel,
        grid=(grid,),
        out_shape=[jax.ShapeDtypeStruct(shape, dtype) for shape, dtype, _ in outs],
        in_specs=specs,
        out_specs=out_specs,
        scratch_shapes=scratch,
        compiler_params=pltpu.CompilerParams(vmem_limit_bytes=VMEM_LIMIT),
        cost_estimate=lasting(us),
        name=name,
    )(*arrays)


def padded_to(array, width, axis):
    pads = [(0, 0)] * array.ndim
    pads[axis] = (0, width - array.shape[axis])
    return jnp.pad(array, pads)


def up_to(n, multiple):
    return -(-n // multiple) * multiple


def body(
    tokens, out_grad, doc_starts, routes, keep_mask, norm_mix, w_in, conv_w, conv_b, w_x, w_dt,
    dt_bias, a_log, d_skip, w_out, norm_moe, w_router, w_up, w_down,
):
    group = lax.axis_size("wa")
    ring = lax.axis_size("ctx")
    mine = lax.axis_index("wa")
    place = lax.axis_index("ctx")
    length, width = tokens.shape[1:]
    taps, local = conv_w.shape
    states = a_log.shape[0]
    ranked = w_dt.shape[0]
    experts = w_router.shape[1]
    padded = up_to(local, LANE)
    columns = up_to(w_x.shape[1], LANE)
    steps = length // SEG
    rows = length + EDGE
    slots = experts * (length // 2)
    share = norm_mix.shape[0]
    order_vmem = pltpu.VMEM((width // LANE, length, LANE), F32)
    place_s = place.astype(jnp.int32).reshape(1)
    last_s = (place == ring - 1).astype(jnp.int32).reshape(1)
    f32_vmem = lambda *shape: pltpu.VMEM(shape, F32)

    in_each = -(-width // ring)
    in_rows = up_to(in_each, 16)
    part_in = lax.dynamic_slice_in_dim(w_in, place * in_each, in_each, 0)
    halves = jnp.stack([part_in[:, :local], part_in[:, local:]], axis=0)
    halves = jnp.pad(halves, ((0, 0), (0, in_rows - in_each), (0, padded - local)))
    small = jnp.concatenate([norm_mix, norm_moe, w_router.T.reshape(-1)], axis=0)
    small_count = up_to(-(-small.shape[0] // LANE), 16)
    small = jnp.pad(small, (0, small_count * LANE - small.shape[0])).reshape(small_count, LANE)
    documents = doc_starts.shape[1]
    doc_tile = jnp.pad(doc_starts, ((0, SEG - 1), (0, LANE - documents)))
    all_rows, all_edges, smalls, docs, w_blocks = start(tokens[0], small, doc_tile, halves, 1)
    proj_in = w_blocks[:, :, :in_each].reshape(2, width, padded)
    of_x = lambda shape: pl.BlockSpec((1,) + shape[1:], lambda i: (0, 0, 0))
    of_z = lambda shape: pl.BlockSpec((1,) + shape[1:], lambda i: (1, 0, 0))
    (own_experts,) = call(
        pack_kernel, "pack", 1, [(w_up[0], None), (w_down[0], None), (docs, ANY)],
        [((w_down.shape[1], 2 * width), BF16, None)], [], 3,
    )
    expert_w = lax.all_gather(own_experts, "ctx", axis=0, tiled=True)
    smalls = smalls.reshape(group, -1)[:, : (2 + experts) * share]
    smalls = smalls.reshape(group, 2 + experts, share).swapaxes(0, 1).reshape(2 + experts, width)
    gain_mix, gain_moe = smalls[0:1].astype(F32), smalls[1:2].astype(F32)
    router = padded_to(smalls[2:], LANE, 0)
    docs = docs[:, 0, :documents]

    conv = jnp.concatenate([conv_w, conv_b[None]], axis=0).astype(F32)
    conv = jnp.pad(conv, ((0, SEG - taps - 1), (0, padded - local)))
    wproj = jnp.pad(w_x, ((0, padded - local), (0, columns - w_x.shape[1])))
    wdt = jnp.pad(w_dt, ((0, columns - ranked), (0, padded - local)))
    step_bias = padded_to(dt_bias[None], padded, 1).astype(F32)
    a_mat = -jnp.exp(padded_to(a_log, padded, 1).astype(F32))
    skip = padded_to(d_skip[None], padded, 1).astype(F32)
    wout = padded_to(w_out, padded, 0)

    vec = (group, length, padded)
    n1, ext, pre_conv, u_f, u, z, part, cut = call(
        functools.partial(enter_kernel, taps), "enter", group,
        [(place_s, SMEM), (docs, SMEM), (all_rows, 0), (all_edges, 0), (gain_mix, None),
         (proj_in, of_x), (proj_in, of_z), (conv, None), (wproj, None)],
        [((group, rows, width), BF16, 0), ((group, (taps - 1) * SEG + length, padded), F32, 0),
         (vec, F32, 0), (vec, F32, 0), (vec, BF16, 0), (vec, BF16, 0),
         ((group, length, columns), BF16, 0), ((group, length, LANE), F32, 0)],
        [], 8,
    )
    (parts,) = gather_all([part], "wa", 2, 15)
    seg_states = (group, states, SEG, padded)
    seg_sums = (group, SEG, padded)
    dev_states = (group, states, padded)
    dev_sums = (group, 1, padded)
    spread_vmem = f32_vmem(length, states * LANE)
    lane_vmem = f32_vmem(length, padded)
    state_vmem = f32_vmem(states, padded)
    proj, step_size, sig, h_in, s_in, h_dev, s_dev = call(
        functools.partial(summary_kernel, states, ranked), "scan_summary", group,
        [(parts, 1), (wdt, None), (step_bias, None), (u_f, 0), (cut, 0), (a_mat, None)],
        [((group, length, columns), BF16, 0), (vec, F32, 0), (vec, F32, 0), (seg_states, F32, 0),
         (seg_sums, F32, 0), (dev_states, BF16, 0), (dev_sums, F32, 0)],
        [spread_vmem, lane_vmem, lane_vmem, state_vmem], 10,
    )
    all_h, all_s = gather_all([h_dev, s_dev], "ctx", 3, 15)
    y_full, gated, mix_part, e_in = call(
        functools.partial(output_kernel, states, ranked), "scan_output", group,
        [(place_s, SMEM), (proj, 0), (step_size, 0), (u_f, 0), (cut, 0), (a_mat, None), (h_in, 0),
         (s_in, 0), (all_h, 1), (all_s, 1), (z, 0), (skip, None), (wout, None)],
        [(vec, F32, 0), (vec, BF16, 0), ((group, length, width), BF16, 0), (dev_states, F32, 0)],
        [spread_vmem, spread_vmem, lane_vmem, lane_vmem], 13,
    )
    mix_terms = trade(mix_part, "wa", 4, 25)

    row_f = (length, width)
    h1, n2, upstream, facts, match, outgoing, mix_sum = call(
        functools.partial(route_kernel, experts), "route", 1,
        [(mix_terms, None), (tokens[0], None), (gain_moe, None), (router, None),
         (routes[0], None), (keep_mask[0][:, None], None), (out_grad[0], None)],
        [(row_f, F32, None), (row_f, BF16, None), (row_f, F32, None), ((length, LANE), F32, None),
         ((length, slots), BF16, None), ((slots, 2 * width), BF16, None), ((SEG, LANE), F32, None)],
        [], 5,
    )
    arrived = trade(outgoing.reshape(group, slots // group, 2 * width), "wa", 5, 29)
    hidden_units = expert_w.shape[0]
    block = hidden_units // 8
    of_block = lambda shape: pl.BlockSpec((block, shape[1]), lambda i: (i, 0))
    grad_experts, returning = call(
        experts_kernel, "experts", 8,
        [(arrived.reshape(slots, 2 * width), None), (expert_w, of_block)],
        [((hidden_units, 2 * width), BF16, of_block), ((slots, 2 * width), BF16, None)],
        [f32_vmem(slots, 2 * width)], 18,
    )
    share_experts = lax.psum_scatter(grad_experts, "ctx", scatter_dimension=0, tiled=True)
    returned = trade(returning.reshape(group, slots // group, 2 * width), "wa", 6, 29)
    result, d_h1, d_mix_own, grad_router, grad_gain_moe, out_sums = call(
        functools.partial(combine_kernel, experts), "combine", 1,
        [(returned.reshape(slots, 2 * width), None), (match, None), (h1, None), (n2, None),
         (upstream, None), (facts, None), (gain_moe, None), (router, None)],
        [(row_f, F32, None), (row_f, F32, None), (row_f, BF16, None), ((LANE, width), F32, None),
         ((1, width), F32, None), ((SEG, LANE), F32, None)],
        [order_vmem], 6,
    )
    (d_mix,) = gather_all([d_mix_own], "wa", 7, 28)

    d_y, d_z, grad_skip, f_in, t_in, f_dev = call(
        functools.partial(gate_back_kernel, states, ranked + states), "gate_back", group,
        [(d_mix, 0), (wout, None), (y_full, 0), (z, 0), (u_f, 0), (proj, 0), (step_size, 0),
         (cut, 0), (a_mat, None)],
        [(vec, F32, 0), ((group, rows, padded), BF16, 0), ((1, padded), F32, None),
         (seg_states, F32, 0), (seg_sums, F32, 0), (dev_states, BF16, 0)],
        [spread_vmem, lane_vmem, state_vmem], 11,
    )
    grad_in_z = dot_tn(n1.reshape(group * rows, width), d_z.reshape(group * rows, padded))
    grad_out = dot_tn(
        d_mix.reshape(group * length, width), gated.reshape(group * length, padded)
    )
    grad_zo = jnp.concatenate([grad_in_z, grad_out], axis=1).astype(BF16)
    grad_zo = jnp.pad(
        grad_zo.reshape(ring // 2, 2, in_each, 2 * padded),
        ((0, 0), (0, 0), (0, in_rows - in_each), (0, 0)),
    )
    all_f, pair_zo = carry_back(f_dev, grad_zo, 8, 14)
    d_part, d_u, grad_dt, grad_step_bias, grad_a = call(
        functools.partial(scan_back_kernel, states, ranked), "scan_back", group,
        [(place_s, SMEM), (proj, 0), (step_size, 0), (sig, 0), (u_f, 0), (cut, 0), (d_y, 0),
         (a_mat, None), (skip, None), (wdt, None), (h_in, 0), (s_in, 0), (e_in, 0), (f_in, 0),
         (t_in, 0), (all_f, 1), (all_s, 1)],
        [((group, length, columns), BF16, 0), (vec, F32, 0), ((columns, padded), F32, None),
         ((1, padded), F32, None), ((states, SEG, padded), F32, None)],
        [spread_vmem, spread_vmem, spread_vmem, f32_vmem(length + SEG, states * LANE), spread_vmem,
         spread_vmem, lane_vmem, lane_vmem, lane_vmem, state_vmem], 34,
    )
    d_parts, chunk_zo = proj_back(d_part, grad_zo, pair_zo, 9, 20)
    d_x, d_n1_part, grad_conv, grad_x, gain_terms = call(
        functools.partial(conv_back_kernel, taps), "conv_back", group,
        [(place_s, SMEM), (docs, SMEM), (d_parts, 1), (wproj, None), (d_u, 0), (pre_conv, 0),
         (ext, 0), (u, 0), (conv, None), (d_z, 0), (proj_in, of_x), (proj_in, of_z), (n1, 0)],
        [((group, rows, padded), BF16, 0), ((group, rows, width), BF16, 0),
         ((SEG, padded), F32, None), ((columns, padded), F32, None), ((1, width), F32, None)],
        [f32_vmem((taps - 1) * SEG + length, LANE)], 10,
    )
    grad_gain_mix = gain_terms / gain_mix
    grad_in_x = dot_tn(n1.reshape(group * rows, width), d_x.reshape(group * rows, padded))
    grad_a_log = jnp.sum(grad_a, axis=1) * a_mat

    def dealt(rows, count):
        each = -(-rows.shape[0] // ring)
        rows = jnp.pad(rows, ((0, each * ring - rows.shape[0]), (0, 0)))
        return jnp.pad(rows.reshape(ring, each, -1), ((0, 0), (0, count - each), (0, 0)))

    small = jnp.concatenate(
        [grad_conv[: taps + 1], grad_step_bias, grad_skip, grad_a_log, grad_dt[:ranked],
         grad_x[: w_x.shape[1]]],
        axis=0,
    ).astype(BF16)
    small_each = -(-small.shape[0] // ring)
    small_rows = up_to(small_each, 16)
    fulls = jnp.concatenate([grad_gain_mix, grad_gain_moe, grad_router[:experts]], axis=0)
    fulls = fulls.reshape(2 + experts, group, share).swapaxes(0, 1).reshape(group, -1)
    full_each = -(-fulls.shape[1] // ring)
    fulls = jnp.pad(fulls, ((0, 0), (0, full_each * ring - fulls.shape[1])))
    fulls = fulls.reshape(group, ring, full_each).swapaxes(0, 1)
    fulls = jnp.pad(fulls, ((0, 0), (0, 0), (0, padded - full_each)))
    stat_row = jnp.stack([out_sums[0, 0], mix_sum[0, 0], out_sums[1, 0]])
    is_mine = (lax.iota(jnp.int32, group) == mine).astype(F32)
    stat_rows = padded_to(is_mine[:, None] * stat_row[None, :], padded, 1)
    stat_rows = jnp.broadcast_to(stat_rows[None], (ring, group, padded))
    tile = jnp.concatenate([fulls, stat_rows], axis=1)
    tile = jnp.pad(tile, ((0, 0), (0, 16 - tile.shape[1]), (0, 0))).astype(BF16)
    packed = jnp.concatenate(
        [dealt(grad_in_x.astype(BF16), in_rows), dealt(small, small_rows), tile], axis=1
    )
    packed = packed.reshape((ring // 2, 2) + packed.shape[1:])
    done, d_n1_terms, d_edges = finish(packed, chunk_zo, d_n1_part, in_rows, small_rows, 11)
    share_in = jnp.concatenate(
        [done[:, :in_each, :local], done[:, in_rows : in_rows + in_each, :local]], axis=2
    ).reshape(width, 2 * local).astype(F32)
    base = 2 * in_rows + small_rows + 16
    share_out = done[:, base : base + in_each, :local].reshape(width, local).T.astype(F32)
    base = 2 * in_rows
    smalls_sum = done[:, base : base + small_each, :local].reshape(ring * small_each, local)
    smalls_sum = smalls_sum.astype(F32)
    base = base + small_rows
    full_sum = lax.dynamic_index_in_dim(done, base + mine, 1, False)[:, :full_each]
    full_sum = full_sum.reshape(-1)[: (2 + experts) * share].reshape(2 + experts, share).astype(F32)
    stat_sums = lax.dynamic_index_in_dim(done, base + group + mine, 1, False)[0, :3].astype(F32)
    (input_grad,) = call(
        functools.partial(leave_kernel, taps), "leave", 1,
        [(last_s, SMEM), (d_n1_terms, None), (d_edges, None), (tokens[0], None), (gain_mix, None),
         (d_h1, None)],
        [(row_f, F32, None)], [f32_vmem(length, width), order_vmem], 4,
    )
    marks_at = [0, taps, taps + 1, taps + 2, taps + 3, taps + 3 + states]
    marks_at += [marks_at[-1] + ranked, marks_at[-1] + ranked + w_x.shape[1]]
    cut_at = [smalls_sum[a:b] for a, b in zip(marks_at[:-1], marks_at[1:])]
    denom = length * ring * width
    rms_stats = jnp.sqrt(stat_sums / denom)[None]
    return (
        result[None],
        input_grad[None],
        full_sum[0],
        share_in,
        cut_at[0],
        cut_at[1][0],
        cut_at[6].T,
        cut_at[5],
        cut_at[2][0],
        cut_at[4],
        cut_at[3][0],
        share_out,
        full_sum[1],
        full_sum[2:].T,
        share_experts[:, :width].T.astype(F32)[None],
        share_experts[:, width:].astype(F32)[None],
        rms_stats,
    )


def solution(mesh):
    placed = (
        P("wa", "ctx", None),
        P("wa", "ctx", None),
        P("wa", None),
        P("wa", "ctx", None),
        P("wa", "ctx"),
        P("wa"),
        P(None, "wa"),
        P(None, "wa"),
        P("wa"),
        P("wa", None),
        P(None, "wa"),
        P("wa"),
        P(None, "wa"),
        P("wa"),
        P("wa", None),
        P("wa"),
        P("wa", None),
        P("wa", None, "ctx"),
        P("wa", "ctx", None),
    )
    return jax.shard_map(
        body,
        mesh=mesh,
        in_specs=placed,
        out_specs=(
            P("wa", "ctx", None),
            P("wa", "ctx", None),
            P("wa"),
            P(None, "wa"),
            P(None, "wa"),
            P("wa"),
            P("wa", None),
            P(None, "wa"),
            P("wa"),
            P(None, "wa"),
            P("wa"),
            P("wa", None),
            P("wa"),
            P("wa", None),
            P("wa", None, "ctx"),
            P("wa", "ctx", None),
            P("wa", None),
        ),
        check_vma=False,
    )
```

```python
import functools

import jax
import jax.numpy as jnp
from jax import lax
from jax.experimental import pallas as pl
from jax.experimental.pallas import tpu as pltpu
from jax.sharding import PartitionSpec as P

EPS = 1e-05
F32 = jnp.float32
BF16 = jnp.bfloat16
SEG = 8
LANE = 128
EDGE = 16
CUT = 1e30
MESH = pl.DeviceIdType.MESH
VMEM_LIMIT = 24 * 2**20


def lasting(us):
    return pl.CostEstimate(
        flops=int(us * 1.1e9), bytes_accessed=int(us * 3.5e6), transcendentals=0
    )


def greet(axis, count):
    me = lax.axis_index(axis)
    barrier = pltpu.get_barrier_semaphore()
    for k in range(1, count):
        pl.semaphore_signal(
            barrier, inc=1, device_id={axis: lax.rem(me + k, count)}, device_id_type=MESH
        )
    pl.semaphore_wait(barrier, count - 1)
    return me


def gather_kernel(axis, count, arrays, *refs):
    srcs, dsts = refs[:arrays], refs[arrays : 2 * arrays]
    send, recv, own = refs[-3:]
    me = greet(axis, count)
    copies = []
    for i in range(arrays):
        for k in range(1, count):
            copy = pltpu.make_async_remote_copy(
                src_ref=srcs[i],
                dst_ref=dsts[i].at[me],
                send_sem=send.at[i, k],
                recv_sem=recv.at[i, k],
                device_id={axis: lax.rem(me + k, count)},
                device_id_type=MESH,
            )
            copy.start()
            copies.append(copy)
    for i in range(arrays):
        local = pltpu.make_async_copy(srcs[i], dsts[i].at[me], own.at[i])
        local.start()
        copies.append(local)
    for copy in copies:
        copy.wait()


def trade_kernel(axis, count, x_ref, o_ref, send, recv, own):
    me = greet(axis, count)
    copies = []
    for k in range(1, count):
        other = lax.rem(me + k, count)
        copy = pltpu.make_async_remote_copy(
            src_ref=x_ref.at[other],
            dst_ref=o_ref.at[me],
            send_sem=send.at[k],
            recv_sem=recv.at[k],
            device_id={axis: other},
            device_id_type=MESH,
        )
        copy.start()
        copies.append(copy)
    local = pltpu.make_async_copy(x_ref.at[me], o_ref.at[me], own)
    local.start()
    local.wait()
    for copy in copies:
        copy.wait()


def trade(x, axis, cid, us):
    count = lax.axis_size(axis)
    return pl.pallas_call(
        functools.partial(trade_kernel, axis, count),
        out_shape=jax.ShapeDtypeStruct(x.shape, x.dtype),
        in_specs=[pl.BlockSpec(memory_space=pl.ANY)],
        out_specs=pl.BlockSpec(memory_space=pl.ANY),
        scratch_shapes=[
            pltpu.SemaphoreType.DMA((count,)),
            pltpu.SemaphoreType.DMA((count,)),
            pltpu.SemaphoreType.DMA,
        ],
        compiler_params=pltpu.CompilerParams(
            collective_id=cid, has_side_effects=True, vmem_limit_bytes=VMEM_LIMIT
        ),
        cost_estimate=lasting(us),
        name=f"trade_{cid}",
    )(x)


def sum_start(mates, x_ref, got, send, recv):
    copies = []
    for k, who in enumerate(mates):
        copy = remote(x_ref.at[who], got.at[k], send.at[k], recv.at[k], {"wa": who})
        copy.start()
        copies.append(copy)
    return copies


def sum_spread(mine, mates, x_ref, got, o_ref, copies, send, recv):
    for copy in copies:
        copy.wait_recv()
    parts = [x_ref.at[mine]] + [got.at[k] for k in range(len(mates))]
    add_rows(o_ref.at[mine], parts, x_ref.shape[1])
    spreads = []
    for k, who in enumerate(mates):
        copy = remote(o_ref.at[mine], o_ref.at[mine], send.at[k], recv.at[k], {"wa": who})
        copy.start()
        spreads.append(copy)
    return spreads


def sum_all_kernel(group, x_ref, o_ref, got, s1, r1, s2, r2):
    greet("wa", group)
    mine, mates = mates_of(group)
    copies = sum_start(mates, x_ref, got, s1, r1)
    spreads = sum_spread(mine, mates, x_ref, got, o_ref, copies, s2, r2)
    for copy in spreads:
        copy.wait()
    for copy in copies:
        copy.wait_send()


def sum_all(x, cid, us):
    group = lax.axis_size("wa")
    vmem = pl.BlockSpec(memory_space=pltpu.VMEM)
    dma = pltpu.SemaphoreType.DMA
    return pl.pallas_call(
        functools.partial(sum_all_kernel, group),
        out_shape=jax.ShapeDtypeStruct(x.shape, x.dtype),
        in_specs=[vmem],
        out_specs=vmem,
        scratch_shapes=[pltpu.VMEM((group - 1,) + x.shape[1:], x.dtype)] + [dma((group - 1,))] * 4,
        compiler_params=pltpu.CompilerParams(
            collective_id=cid, has_side_effects=True, vmem_limit_bytes=VMEM_LIMIT
        ),
        cost_estimate=lasting(us),
        name="sum_all",
    )(x)


def gather_all(xs, axis, cid, us):
    count, arrays = lax.axis_size(axis), len(xs)
    return pl.pallas_call(
        functools.partial(gather_kernel, axis, count, arrays),
        out_shape=[jax.ShapeDtypeStruct((count,) + x.shape, x.dtype) for x in xs],
        in_specs=[pl.BlockSpec(memory_space=pl.ANY)] * arrays,
        out_specs=[pl.BlockSpec(memory_space=pl.ANY)] * arrays,
        scratch_shapes=[
            pltpu.SemaphoreType.DMA((arrays, count)),
            pltpu.SemaphoreType.DMA((arrays, count)),
            pltpu.SemaphoreType.DMA((arrays,)),
        ],
        compiler_params=pltpu.CompilerParams(
            collective_id=cid, has_side_effects=True, vmem_limit_bytes=VMEM_LIMIT
        ),
        cost_estimate=lasting(us),
        name=f"gather_{cid}",
    )(*xs)


def remote(src, dst, send, recv, where):
    return pltpu.make_async_remote_copy(
        src_ref=src, dst_ref=dst, send_sem=send, recv_sem=recv,
        device_id=where, device_id_type=MESH,
    )


def add_rows(out, parts, rows):
    def one(i, _):
        at = pl.ds(pl.multiple_of(i * 16, 16), 16)
        total = parts[0][at, :].astype(F32)
        for part in parts[1:]:
            total = total + part[at, :].astype(F32)
        out[at, :] = total.astype(out.dtype)
        return 0

    lax.fori_loop(0, rows // 16, one, 0)


def neighbours(ring):
    me = lax.axis_index("ctx")
    half = ring // 2
    lane = lax.rem(me, 2)
    chip = me // 2
    peers = [lax.rem(chip + k, half) * 2 + lane for k in range(1, half)]
    return me, chip, lane, me + 1 - 2 * lane, peers


def mates_of(group):
    mine = lax.axis_index("wa")
    return mine, [lax.rem(mine + k, group) for k in range(1, group)]


def hello(barrier, axis, who):
    pl.semaphore_signal(barrier, inc=1, device_id={axis: who}, device_id_type=MESH)


def carry_back_kernel(ring, f_ref, g_ref, f_o, p_o, send, recv, own, pair_s, pair_r):
    me, _, lane, pair, _ = neighbours(ring)
    greet("ctx", ring)
    to_pair = remote(g_ref.at[:, 1 - lane], p_o, pair_s, pair_r, {"ctx": pair})
    copies = []
    for k in range(1, ring):
        copy = remote(f_ref, f_o.at[me], send.at[k], recv.at[k], {"ctx": lax.rem(me + k, ring)})
        copy.start()
        copies.append(copy)
    to_pair.start()
    local = pltpu.make_async_copy(f_ref, f_o.at[me], own)
    local.start()
    for copy in copies + [to_pair, local]:
        copy.wait()


def carry_back(f, g, cid, us):
    ring = lax.axis_size("ctx")
    hbm = pl.BlockSpec(memory_space=pl.ANY)
    dma = pltpu.SemaphoreType.DMA
    return pl.pallas_call(
        functools.partial(carry_back_kernel, ring),
        out_shape=[
            jax.ShapeDtypeStruct((ring,) + f.shape, f.dtype),
            jax.ShapeDtypeStruct(g.shape[:1] + g.shape[2:], g.dtype),
        ],
        in_specs=[hbm] * 2,
        out_specs=[hbm] * 2,
        scratch_shapes=[dma((ring,)), dma((ring,)), dma, dma, dma],
        compiler_params=pltpu.CompilerParams(
            collective_id=cid, has_side_effects=True, vmem_limit_bytes=VMEM_LIMIT
        ),
        cost_estimate=lasting(us),
        name="carry_back",
    )(f, g)


def proj_back_kernel(
    ring, group, x_ref, g_ref, p_ref, x_o, g_o,
    kept, paired, came, got, s1, r1, s2, r2, load, ctx_s, ctx_r,
):
    _, chip, lane, _, peers = neighbours(ring)
    mine, mates = mates_of(group)
    half = ring // 2
    rows = g_o.shape[0]
    loads = [
        pltpu.make_async_copy(g_ref.at[:, lane], kept, load.at[0]),
        pltpu.make_async_copy(p_ref, paired, load.at[1]),
    ]
    for copy in loads:
        copy.start()
    barrier = pltpu.get_barrier_semaphore()
    for who in peers:
        hello(barrier, "ctx", who)
    for who in mates:
        hello(barrier, "wa", who)
    pl.semaphore_wait(barrier, half + group - 2)
    copies = sum_start(mates, x_ref, got, s1, r1)
    for copy in loads:
        copy.wait()
    scattered = []
    for k, who in enumerate(peers):
        to = lax.rem(chip + k + 1, half)
        add_rows(kept.at[to], [kept.at[to], paired.at[to]], rows)
        copy = remote(kept.at[to], came.at[k], ctx_s.at[k], ctx_r.at[k], {"ctx": who})
        copy.start()
        scattered.append(copy)
    spreads = sum_spread(mine, mates, x_ref, got, x_o, copies, s2, r2)
    add_rows(kept.at[chip], [kept.at[chip], paired.at[chip]], rows)
    for copy in scattered:
        copy.wait_recv()
    add_rows(g_o, [kept.at[chip]] + [came.at[k] for k in range(half - 1)], rows)
    for copy in scattered + copies:
        copy.wait_send()
    for copy in spreads:
        copy.wait()


def proj_back(x, g, p, cid, us):
    ring, group = lax.axis_size("ctx"), lax.axis_size("wa")
    half = ring // 2
    hbm = pl.BlockSpec(memory_space=pl.ANY)
    vmem = pl.BlockSpec(memory_space=pltpu.VMEM)
    dma = pltpu.SemaphoreType.DMA
    block = pltpu.VMEM((half,) + g.shape[2:], g.dtype)
    return pl.pallas_call(
        functools.partial(proj_back_kernel, ring, group),
        out_shape=[
            jax.ShapeDtypeStruct(x.shape, x.dtype),
            jax.ShapeDtypeStruct(g.shape[2:], g.dtype),
        ],
        in_specs=[vmem, hbm, hbm],
        out_specs=[vmem, vmem],
        scratch_shapes=[
            block, block, pltpu.VMEM((half - 1,) + g.shape[2:], g.dtype),
            pltpu.VMEM((group - 1,) + x.shape[1:], x.dtype),
            dma((group - 1,)), dma((group - 1,)), dma((group - 1,)), dma((group - 1,)), dma((2,)),
            dma((half - 1,)), dma((half - 1,)),
        ],
        compiler_params=pltpu.CompilerParams(
            collective_id=cid, has_side_effects=True, vmem_limit_bytes=VMEM_LIMIT
        ),
        cost_estimate=lasting(us),
        name="proj_back",
    )(x, g, p)


def finish_kernel(
    ring, group, in_rows, small_rows,
    g_ref, zf_ref, d_ref, o_ref, dt_ref, de_ref,
    from_pair, paired, came, own, zin, tiles,
    pair_s, pair_r, ctx_s, ctx_r, z_s, z_r, tile_s, tile_r, d_s, d_r, d_own, last_s, last_r, fwd_s, fwd_r,
    edge_s, edge_r,
):
    me, chip, lane, pair, peers = neighbours(ring)
    mine, mates = mates_of(group)
    half = ring // 2
    rows = in_rows + small_rows + 16
    lanes = g_ref.shape[3]
    barrier = pltpu.get_barrier_semaphore()
    for who in [pair] + peers:
        hello(barrier, "ctx", who)
    for who in mates:
        hello(barrier, "wa", who)
    has_next = me < ring - 1
    has_last = me > 0

    @pl.when(has_next)
    def _():
        hello(barrier, "ctx", me + 1)

    @pl.when(has_last)
    def _():
        hello(barrier, "ctx", me - 1)

    around = jnp.where(has_next, 1, 0) + jnp.where(has_last, 1, 0)
    pl.semaphore_wait(barrier, half + group - 1 + around)

    to_pair = remote(g_ref.at[:, 1 - lane], from_pair, pair_s, pair_r, {"ctx": pair})
    to_pair.start()
    ready = 2 * in_rows + small_rows + 16
    parts = [pl.ds(ready, in_rows), pl.ds(0, ready)]
    o_ref[me, parts[0]] = zf_ref[:, lanes:]

    def to_all(i):
        src = o_ref.at[me, parts[i]]
        copies = []
        for k, who in enumerate(peers):
            copies.append(remote(src, src, last_s.at[i, k], last_r.at[i, k], {"ctx": who}))
        copies.append(remote(src, src, fwd_s.at[i, 0], fwd_r.at[i, 0], {"ctx": pair}))
        for copy in copies:
            copy.start()
        return copies

    def forward(i, copies):
        for k in range(1, half):
            copies[k - 1].wait_recv()
            source = lax.rem(chip + half - k, half) * 2 + lane
            block = o_ref.at[source, parts[i]]
            copy = remote(block, block, fwd_s.at[i, k], fwd_r.at[i, k], {"ctx": pair})
            copy.start()
            copies.append(copy)

    x_to = mine // 2
    z_to = group // 2 + mine // 2
    slot = lax.rem(mine, 2)
    z_ref = zf_ref.at[:, pl.ds(0, lanes)]
    x_ref = own.at[pl.ds(0, in_rows)]
    send_x = remote(x_ref, zin.at[slot], z_s.at[0], z_r.at[slot], {"wa": x_to})
    send_z = remote(z_ref, zin.at[slot], z_s.at[1], z_r.at[slot], {"wa": z_to})
    keep_x = pltpu.make_async_copy(x_ref, zin.at[slot], z_r.at[slot])
    keep_z = pltpu.make_async_copy(z_ref, zin.at[slot], z_r.at[slot])

    @pl.when(z_to != mine)
    def _():
        send_z.start()

    @pl.when(z_to == mine)
    def _():
        keep_z.start()

    cut = d_ref.shape[1] // 32 * 16
    pieces = [pl.ds(0, cut), pl.ds(cut, d_ref.shape[1] - cut)]
    trades = []

    def trade_rows(i):
        for k, who in enumerate(mates):
            copy = remote(
                d_ref.at[who, pieces[i]], dt_ref.at[mine, pieces[i]], d_s.at[i, k], d_r.at[i, k],
                {"wa": who},
            )
            copy.start()
            trades.append(copy)

    trade_rows(0)
    kept = pltpu.make_async_copy(d_ref.at[mine], dt_ref.at[mine], d_own)
    kept.start()

    to_pair.wait_recv()
    scattered = []
    for k, who in enumerate(peers):
        to = lax.rem(chip + k + 1, half)
        add_rows(paired.at[to], [g_ref.at[to, lane], from_pair.at[to]], rows)
        copy = remote(paired.at[to], came.at[k], ctx_s.at[k], ctx_r.at[k], {"ctx": who})
        copy.start()
        scattered.append(copy)
    early = to_all(0)
    add_rows(paired.at[chip], [g_ref.at[chip, lane], from_pair.at[chip]], rows)
    for copy in scattered:
        copy.wait_recv()
    add_rows(own, [paired.at[chip]] + [came.at[k] for k in range(half - 1)], rows)

    @pl.when(x_to != mine)
    def _():
        send_x.start()

    @pl.when(x_to == mine)
    def _():
        keep_x.start()

    tile = pl.ds(in_rows + small_rows, 16)
    spread_tiles = []
    for k, who in enumerate(mates):
        copy = remote(own.at[tile], tiles.at[k], tile_s.at[k], tile_r.at[k], {"wa": who})
        copy.start()
        spread_tiles.append(copy)
    forward(0, early)
    o_ref[me, pl.ds(2 * in_rows, small_rows)] = own[pl.ds(in_rows, small_rows)]
    for copy in spread_tiles:
        copy.wait_recv()
    add_rows(
        o_ref.at[me, pl.ds(2 * in_rows + small_rows, 16)],
        [own.at[tile]] + [tiles.at[k] for k in range(group - 1)],
        16,
    )
    for s in range(2):
        pltpu.make_async_copy(zin.at[s], zin.at[s], z_r.at[s]).wait()
        o_ref[me, pl.ds(s * in_rows, in_rows)] = zin[s]
    late = to_all(1)
    trade_rows(1)
    kept.wait()
    forward(1, late)

    for copy in trades:
        copy.wait_recv()
    edges = dt_ref.at[:, pl.ds(d_ref.shape[1] - EDGE, EDGE)]
    to_last = remote(edges, de_ref, edge_s, edge_r, {"ctx": me - 1})

    @pl.when(has_last)
    def _():
        to_last.start()

    for copies in (early, late):
        for copy in copies[half - 1 :]:
            copy.wait_recv()

    to_pair.wait_send()
    for copy in scattered + spread_tiles + early + late + trades:
        copy.wait_send()

    @pl.when(x_to != mine)
    def _():
        send_x.wait_send()

    @pl.when(z_to != mine)
    def _():
        send_z.wait_send()

    @pl.when(has_last)
    def _():
        to_last.wait_send()

    @pl.when(has_next)
    def _():
        to_last.wait_recv()


def finish(g, zf, d, in_rows, small_rows, cid):
    ring, group = lax.axis_size("ctx"), lax.axis_size("wa")
    half = ring // 2
    rows, lanes = g.shape[2:]
    out_rows = 3 * in_rows + small_rows + 16
    vmem = pl.BlockSpec(memory_space=pltpu.VMEM)
    hbm = pl.BlockSpec(memory_space=pl.ANY)
    dma = pltpu.SemaphoreType.DMA
    return pl.pallas_call(
        functools.partial(finish_kernel, ring, group, in_rows, small_rows),
        out_shape=[
            jax.ShapeDtypeStruct((ring, out_rows, lanes), BF16),
            jax.ShapeDtypeStruct(d.shape, d.dtype),
            jax.ShapeDtypeStruct((group, EDGE, d.shape[2]), d.dtype),
        ],
        in_specs=[vmem, vmem, hbm],
        out_specs=[vmem, hbm, hbm],
        scratch_shapes=[
            pltpu.VMEM((half, rows, lanes), BF16),
            pltpu.VMEM((half, rows, lanes), BF16),
            pltpu.VMEM((half - 1, rows, lanes), BF16),
            pltpu.VMEM((rows, lanes), BF16),
            pltpu.VMEM((2, in_rows, lanes), BF16),
            pltpu.VMEM((group - 1, 16, lanes), BF16),
            dma, dma,
            dma((half - 1,)), dma((half - 1,)),
            dma((2,)), dma((2,)),
            dma((group - 1,)), dma((group - 1,)),
            dma((2, group - 1)), dma((2, group - 1)), dma,
            dma((2, half - 1)), dma((2, half - 1)),
            dma((2, half)), dma((2, half)),
            dma, dma,
        ],
        compiler_params=pltpu.CompilerParams(
            collective_id=cid, has_side_effects=True, vmem_limit_bytes=VMEM_LIMIT
        ),
        cost_estimate=lasting(60),
        name="finish",
    )(g, zf, d)


def start_kernel(
    ring, group, tok, par, doc, w_ref, tok_o, edge_o, par_o, doc_o, w_o,
    mate_s, mate_r, own_s, edge_s, edge_r, relay_s, relay_r, shift_s, shift_r, out_s, out_r, fwd_s, fwd_r,
):
    me = lax.axis_index("ctx")
    mine = lax.axis_index("wa")
    half = ring // 2
    lane = lax.rem(me, 2)
    chip = me // 2
    pair = me + 1 - 2 * lane
    peers = [lax.rem(chip + k, half) * 2 + lane for k in range(1, half)]
    mates = [lax.rem(mine + k, group) for k in range(1, group)]
    barrier = pltpu.get_barrier_semaphore()
    for who in [pair] + peers:
        pl.semaphore_signal(barrier, inc=1, device_id={"ctx": who}, device_id_type=MESH)
    for who in mates:
        pl.semaphore_signal(barrier, inc=1, device_id={"wa": who}, device_id_type=MESH)
    has_next = me < ring - 1
    has_last = me > 0

    @pl.when(has_next)
    def _():
        pl.semaphore_signal(barrier, inc=1, device_id={"ctx": me + 1}, device_id_type=MESH)

    @pl.when(has_last)
    def _():
        pl.semaphore_signal(barrier, inc=1, device_id={"ctx": me - 1}, device_id_type=MESH)

    around = jnp.where(has_next, 1, 0) + jnp.where(has_last, 1, 0)
    pl.semaphore_wait(barrier, half + group - 1 + around)

    edge = tok.at[pl.ds(tok.shape[0] - EDGE, EDGE)]
    to_next = remote(edge, edge_o.at[mine], edge_s, edge_r, {"ctx": me + 1})

    @pl.when(has_next)
    def _():
        to_next.start()

    kind = mine // (group // 2)
    base = 2 * lax.rem(mine, group // 2)
    for h in range(2):
        where = base + h
        send = remote(
            w_ref.at[h], w_o.at[kind, me], shift_s.at[h], shift_r.at[kind], {"wa": where}
        )
        keep = pltpu.make_async_copy(w_ref.at[h], w_o.at[kind, me], shift_r.at[kind])

        @pl.when(where != mine)
        def _():
            send.start()

        @pl.when(where == mine)
        def _():
            keep.start()

    trades = []
    for i, (src, dst) in enumerate(((par, par_o), (doc, doc_o), (tok, tok_o))):
        for k, who in enumerate(mates):
            copy = remote(src, dst.at[mine], mate_s.at[i, k], mate_r.at[i, k], {"wa": who})
            copy.start()
            trades.append(copy)
        keep = pltpu.make_async_copy(src, dst.at[mine], own_s.at[i])
        keep.start()

    @pl.when(has_last)
    def _():
        to_next.wait_recv()
        for k, who in enumerate(mates):
            remote(
                edge_o.at[mine], edge_o.at[mine], relay_s.at[k], relay_r.at[k], {"wa": who}
            ).start()

    sends = []
    for t in range(2):
        block = w_o.at[t, me]
        pltpu.make_async_copy(block, block, shift_r.at[t]).wait()
        for k, who in enumerate(peers):
            copy = remote(block, block, out_s.at[t, k], out_r.at[t, k], {"ctx": who})
            copy.start()
            sends.append(copy)
        copy = remote(block, block, fwd_s.at[t, 0], fwd_r.at[t, 0], {"ctx": pair})
        copy.start()
        sends.append(copy)
    forwards = []
    for t in range(2):
        for k in range(1, half):
            source = lax.rem(chip + half - k, half) * 2 + lane
            block = w_o.at[t, source]
            pltpu.make_async_copy(block, block, out_r.at[t, k - 1]).wait()
            copy = remote(block, block, fwd_s.at[t, k], fwd_r.at[t, k], {"ctx": pair})
            copy.start()
            forwards.append(copy)
    for t in range(2):
        for k in range(half):
            pltpu.make_async_copy(w_o.at[t, me], w_o.at[t, me], fwd_r.at[t, k]).wait()
    for copy in sends + forwards:
        copy.wait_send()
    for h in range(2):

        @pl.when(base + h != mine)
        def _():
            remote(
                w_ref.at[h], w_o.at[kind, me], shift_s.at[h], shift_r.at[kind], {"wa": mine}
            ).wait_send()

    for copy in trades:
        copy.wait()
    for i, (src, dst) in enumerate(((par, par_o), (doc, doc_o), (tok, tok_o))):
        pltpu.make_async_copy(src, dst.at[mine], own_s.at[i]).wait()

    @pl.when(has_next)
    def _():
        to_next.wait_send()

    @pl.when(has_last)
    def _():
        for k, who in enumerate(mates):
            remote(
                edge_o.at[mine], edge_o.at[mine], relay_s.at[k], relay_r.at[k], {"wa": who}
            ).wait()


def start(tok, par, doc, halves, cid):
    ring, group = lax.axis_size("ctx"), lax.axis_size("wa")
    half = ring // 2
    hbm = pl.BlockSpec(memory_space=pl.ANY)
    dma = pltpu.SemaphoreType.DMA
    outs = [(group,) + a.shape for a in (tok, tok[:EDGE], par, doc)] + [(2, ring) + halves.shape[1:]]
    types = [a.dtype for a in (tok, tok, par, doc, halves)]
    return pl.pallas_call(
        functools.partial(start_kernel, ring, group),
        out_shape=[jax.ShapeDtypeStruct(s, t) for s, t in zip(outs, types)],
        in_specs=[hbm] * 4,
        out_specs=[hbm] * 5,
        scratch_shapes=[
            dma((3, group - 1)), dma((3, group - 1)), dma((3,)),
            dma, dma,
            dma((group - 1,)), dma((group - 1,)),
            dma((2,)), dma((2,)),
            dma((2, half - 1)), dma((2, half - 1)),
            dma((2, half)), dma((2, half)),
        ],
        compiler_params=pltpu.CompilerParams(
            collective_id=cid, has_side_effects=True, vmem_limit_bytes=VMEM_LIMIT
        ),
        cost_estimate=lasting(35),
        name="start",
    )(tok, par, doc, halves)


def pick(rows, states, at):
    shape = (rows, states * LANE)
    lower = (lax.broadcasted_iota(jnp.int32, shape, 0) - at) * LANE
    place = lax.broadcasted_iota(jnp.int32, shape, 1)
    return jnp.where((place >= lower) & (place < lower + LANE), 1.0, 0.0)


def spread(rows, states, at):
    return jnp.dot(rows, pick(rows.shape[1], states, at).astype(BF16), preferred_element_type=F32)


def collected(wide_rows, states, columns, at):
    shape = (states * LANE, columns)
    lower = (lax.broadcasted_iota(jnp.int32, shape, 1) - at) * LANE
    place = lax.broadcasted_iota(jnp.int32, shape, 0)
    ones = jnp.where((place >= lower) & (place < lower + LANE), 1.0, 0.0)
    return jnp.dot(wide_rows, ones, precision=lax.Precision.HIGHEST, preferred_element_type=F32)


def position_of(shape, axis, steps):
    row = lax.broadcasted_iota(jnp.int32, shape, axis)
    return (row & (SEG - 1)) * steps + (row >> 3)


def permutation(length):
    shape = (length, length)
    at = position_of(shape, 0, length // SEG)
    return jnp.where(at == lax.broadcasted_iota(jnp.int32, shape, 1), 1.0, 0.0).astype(BF16)


def rolled(value, by):
    return pltpu.roll(value, by % SEG, 0)


def lanes_of(g):
    return pl.ds(pl.multiple_of(g * LANE, LANE), LANE)


def rows_of(j):
    return pl.ds(pl.multiple_of(j * SEG, SEG), SEG)


def wide(ref, n, lanes):
    return jnp.broadcast_to(ref[pl.ds(n, 1), lanes], (SEG, LANE))


def state_cols(n):
    return slice(n * LANE, (n + 1) * LANE)


def dot_nt(a, b):
    return lax.dot_general(a, b, (((1,), (1,)), ((), ())), preferred_element_type=F32)


def dot_tn(a, b):
    return lax.dot_general(a, b, (((0,), (0,)), ((), ())), preferred_element_type=F32)


def dot_nn(a, b):
    return jnp.dot(a, b, preferred_element_type=F32)


def rms_scale(values):
    return lax.rsqrt(jnp.mean(values * values, axis=-1, keepdims=True) + EPS)


def norm_grads(values, scale, gain, d_out):
    unit = values * scale
    d_unit = d_out * gain
    d_values = scale * (d_unit - unit * jnp.mean(d_unit * unit, axis=-1, keepdims=True))
    return d_values, d_out * unit


def silu_slope(v):
    s = jax.nn.sigmoid(v)
    return s * (1.0 + v * (1.0 - s))


def seg_of():
    return lax.broadcasted_iota(jnp.int32, (SEG, LANE), 0)


def lag_masks(place, doc_ref, documents, stream, length, taps):
    at = place * length + position_of((length, LANE), 0, length // SEG)
    masks = [None]
    for lag in range(1, taps):
        cut = None
        for d in range(documents):
            begin = doc_ref[stream, 0, d]
            here = (begin > at - lag) & (begin <= at)
            cut = here if cut is None else cut | here
        masks.append(jnp.where(cut, 0.0, 1.0))
    hit = None
    for d in range(documents):
        here = doc_ref[stream, 0, d] == at
        hit = here if hit is None else hit | here
    return masks, jnp.where(hit, CUT, 0.0)


def enter_kernel(
    taps, documents, place_ref, doc_ref, tok, edge, gain, wx, wz, conv, wproj,
    n1_o, ext_o, pre_o, uf_o, u_o, z_o, part_o, cut_o,
):
    length = tok.shape[1]
    steps = length // SEG
    place = place_ref[0]
    gains = gain[0:1]

    def normal(rows):
        return (rows * rms_scale(rows) * gains).astype(BF16)

    n1_o[0, :length] = normal(dot_nn(permutation(length), tok[0]))
    n1_o[0, length:] = normal(jnp.where(place > 0, edge[0].astype(F32), 0.0))
    inner = dot_nn(n1_o[0], wx[0]).astype(BF16).astype(F32)
    z_o[0] = dot_nn(n1_o[0, :length], wz[0]).astype(BF16)
    masks, cut = lag_masks(place, doc_ref, documents, pl.program_id(0), length, taps)
    cut_o[0] = cut
    seg = seg_of()
    behind = taps - 1
    for g in range(inner.shape[1] // LANE):
        cols = slice(g * LANE, (g + 1) * LANE)
        rows, before = inner[:length, cols], inner[length:, cols]
        parts = []
        for i in range(behind):
            j = steps - behind + i
            last = jnp.broadcast_to(before[EDGE - behind + i : EDGE - behind + i + 1], (SEG, LANE))
            parts.append(jnp.where(seg == 0, last, rolled(rows[j * SEG : (j + 1) * SEG], 1)))
        ext = jnp.concatenate(parts + [rows], axis=0)
        ext_o[0, :, cols] = ext
        pre = conv[taps : taps + 1, cols] + conv[0:1, cols] * rows
        for lag in range(1, taps):
            window = ext[(behind - lag) * SEG : (behind - lag) * SEG + length]
            pre = pre + conv[lag : lag + 1, cols] * window * masks[lag]
        pre_o[0, :, cols] = pre
        u = (pre * jax.nn.sigmoid(pre)).astype(BF16)
        u_o[0, :, cols] = u
        uf_o[0, :, cols] = u.astype(F32)
    part_o[0] = dot_nt(u_o[0], wproj[...]).astype(BF16)


def summary_kernel(
    states, b_at, proj_i, wdt, bias, uf, cut, a_ref,
    step_o, sig_o, hx_ref, sx_ref, hd_o, sd_ref, bb, st_s, dr_s, hd_s,
):
    length, width = step_o.shape[1:]
    groups, steps = width // LANE, length // SEG
    proj = proj_i[0]
    bb[...] = spread(proj, states, b_at)
    pre = dot_nn(proj, wdt[...]) + bias[0:1]
    step_size = jnp.maximum(pre, 0.0) + jnp.log1p(jnp.exp(-jnp.abs(pre)))
    step_o[0] = step_size
    sig_o[0] = jax.nn.sigmoid(pre)
    dr_s[...] = step_size * uf[0]
    for g in range(groups):
        cols = slice(g * LANE, (g + 1) * LANE)
        st_s[:, cols] = step_size[:, cols] + cut[0]
    zero = jnp.zeros((SEG, LANE), F32)
    seg = seg_of()

    def group(g, _):
        lanes = lanes_of(g)
        a = [wide(a_ref, n, lanes) for n in range(states)]

        def step(j, carry):
            rows = rows_of(j)
            st = st_s[rows, lanes]
            dr = dr_s[rows, lanes]
            new = [carry[0] + st]
            for n in range(states):
                new.append(jnp.exp(st * a[n]) * carry[n + 1] + bb[rows, state_cols(n)] * dr)
            return tuple(new)

        out = lax.fori_loop(0, steps, step, (zero,) * (states + 1), unroll=2)
        total, h = out[0], list(out[1:])
        for k in (1, 2, 4):
            ok = seg >= k
            for n in range(states):
                h[n] = h[n] + jnp.where(ok, jnp.exp(total * a[n]) * rolled(h[n], k), 0.0)
            total = total + jnp.where(ok, rolled(total, k), 0.0)
        ok = seg >= 1
        sx_ref[0, :, lanes] = jnp.where(ok, rolled(total, 1), 0.0)
        sd_ref[0, :, lanes] = total[SEG - 1 : SEG]
        for n in range(states):
            hx_ref[0, n, :, lanes] = jnp.where(ok, rolled(h[n], 1), 0.0)
            hd_s[pl.ds(n, 1), lanes] = h[n][SEG - 1 : SEG]
        return 0

    lax.fori_loop(0, groups, group, 0)
    hd_o[0] = hd_s[...].astype(BF16)


def entering(e_ref, finals, sums, a_ref, place, ahead):
    ring = finals.shape[0]
    e_ref[...] = jnp.zeros_like(e_ref)

    def one(lap, _):
        c = lap if ahead else ring - 1 - lap
        use = (c < place) if ahead else (c > place)

        @pl.when(use)
        def _():
            e_ref[...] = jnp.exp(sums[c, 0] * a_ref[...]) * e_ref[...] + finals[c, 0].astype(F32)

        return 0

    lax.fori_loop(0, ring, one, 0)


def output_kernel(
    states, b_at, place_ref, proj, step_i, uf, cut, a_ref, hx_ref, sx_ref, finals, sums, z, skip, wout,
    y_o, gated_o, mix_o, e_o, bb, cb, st_s, dr_s,
):
    length, width = step_i.shape[1:]
    groups, steps = width // LANE, length // SEG
    bb[...] = spread(proj[0], states, b_at)
    cb[...] = spread(proj[0], states, b_at + states)
    e_ref = e_o.at[0]
    entering(e_ref, finals, sums, a_ref, place_ref[0], True)
    dr_s[...] = step_i[0] * uf[0]
    for g in range(groups):
        cols = slice(g * LANE, (g + 1) * LANE)
        st_s[:, cols] = step_i[0, :, cols] + cut[0]

    def group(g, _):
        lanes = lanes_of(g)
        a = [wide(a_ref, n, lanes) for n in range(states)]
        sx = sx_ref[0, :, lanes]
        first = tuple(
            jnp.exp(sx * a[n]) * wide(e_ref, n, lanes) + hx_ref[0, n, :, lanes]
            for n in range(states)
        )
        gain = wide(skip, 1, lanes)

        def step(j, h):
            rows = rows_of(j)
            st = st_s[rows, lanes]
            dr = dr_s[rows, lanes]
            new = []
            y = gain * uf[0, rows, lanes]
            for n in range(states):
                state = jnp.exp(st * a[n]) * h[n] + bb[rows, state_cols(n)] * dr
                new.append(state)
                y = y + cb[rows, state_cols(n)] * state
            y_o[0, rows, lanes] = y
            return tuple(new)

        lax.fori_loop(0, steps, step, first, unroll=2)
        return 0

    lax.fori_loop(0, groups, group, 0)
    zf = z[0].astype(F32)
    gated = (y_o[0] * (zf * jax.nn.sigmoid(zf))).astype(BF16)
    gated_o[0] = gated
    mix_o[0] = dot_nn(gated, wout[...]).astype(BF16)


def route_kernel(
    experts, terms, tok, gain, router, route, keep, grad,
    h1_o, n2_o, up_o, cols_o, match_o, out_o, sums_o,
):
    length, width = tok.shape
    shift = permutation(length)
    mix = terms[0].astype(F32)
    for w in range(1, terms.shape[0]):
        mix = mix + terms[w].astype(F32)
    h1 = dot_nn(shift, tok[...]) + mix
    h1_o[...] = h1
    n2 = (h1 * rms_scale(h1) * gain[1:2]).astype(BF16)
    n2_o[...] = n2
    logits = dot_nt(n2, router[...])
    lane = lax.broadcasted_iota(jnp.int32, (length, LANE), 1)
    kind = lax.broadcasted_iota(jnp.int32, (LANE, length), 0)
    named = route[...]
    onehot = jnp.where(kind == named, 1.0, 0.0)
    one = lax.broadcasted_iota(jnp.int32, (length, length), 0)
    two = lax.broadcasted_iota(jnp.int32, (length, length), 1)
    earlier = jnp.where(one < two, 1.0, 0.0).astype(BF16)
    before = dot_nn(onehot.astype(BF16), earlier)
    within = jnp.sum(before * onehot, axis=0, keepdims=True)
    slot = named.astype(F32) * (length // 2) + within
    facts = jnp.where(kind == experts, slot, jnp.where(kind == experts + 1, keep[...].astype(F32), onehot))
    facts = dot_nt(shift, facts.astype(BF16))
    onehot = jnp.where(lane < experts, facts, 0.0)
    slot = jnp.sum(jnp.where(lane == experts, facts, 0.0), axis=1, keepdims=True)
    kept = jnp.sum(jnp.where(lane == experts + 1, facts, 0.0), axis=1, keepdims=True)
    sig = jax.nn.sigmoid(jnp.sum(logits * onehot, axis=1, keepdims=True))
    gates = kept * sig
    cols_o[...] = jnp.where(
        lane == experts, gates, jnp.where(lane == experts + 1, gates * (1.0 - sig), onehot)
    )
    up = dot_nn(shift, grad[...])
    up_o[...] = up
    slots = match_o.shape[1]
    spot = lax.broadcasted_iota(jnp.int32, (length, slots), 1).astype(F32)
    match = jnp.where(slot == spot, 1.0, 0.0).astype(BF16)
    match_o[...] = match
    out_o[0] = dot_tn(match, n2).astype(BF16)
    out_o[1] = dot_tn(match, (gates * up).astype(BF16)).astype(BF16)
    sums_o[...] = jnp.broadcast_to(jnp.sum(mix * mix, keepdims=True), (SEG, LANE))


def pack_kernel(up, down, out):
    width, units = up.shape
    line = lax.broadcasted_iota(jnp.int32, (units, units), 0)
    same = jnp.where(line == lax.broadcasted_iota(jnp.int32, (units, units), 1), 1.0, 0.0)
    out[:, :width] = dot_nt(same.astype(BF16), up[...]).astype(BF16)
    out[:, width:] = down[...]


def prepare_kernel(
    experts, small, own, wx_t, wdt, wout, conv_w, a_log,
    gain_o, router_o, wx_o, wdt_o, wout_o, conv_o, rows_o, a_o, wide_s,
):
    width = wout.shape[1]
    group = small.shape[0]
    share = width // group
    for w in range(group):
        wide_s[:, w * share : (w + 1) * share] = small[w, :, :share].astype(F32)
    gain_o[0:1] = wide_s[SEG - 2 : SEG - 1]
    gain_o[1:2] = wide_s[SEG - 1 : SEG]
    gain_o[2:] = jnp.zeros((SEG - 2, width), F32)
    rows = wide_s[SEG:]
    row = lax.broadcasted_iota(jnp.int32, rows.shape, 0)
    router_o[...] = jnp.zeros_like(router_o)
    router_o[: 2 * SEG] = jnp.concatenate(
        [jnp.where(row < experts, rows, 0.0), jnp.zeros_like(rows)], axis=0
    ).astype(BF16)
    local = wout.shape[0]
    for out, src in ((wx_o, wx_t), (wdt_o, wdt), (a_o, None)):
        out[...] = jnp.zeros_like(out)
        if src is not None:
            out[: src.shape[0], :local] = src[...]
    a_o[...] = jnp.full(a_o.shape, -1.0, F32)
    a_o[:, :local] = -jnp.exp(a_log[...].astype(F32))
    wout_o[...] = jnp.zeros_like(wout_o)
    wout_o[:local] = wout[...]
    conv_o[...] = jnp.zeros_like(conv_o)
    taps = conv_w.shape[0]
    conv_o[:taps, :local] = conv_w[...].astype(F32)
    mine = own[...].astype(F32)
    rows_o[...] = jnp.zeros_like(rows_o)
    for h in range(2):
        cols = slice(h * share, (h + 1) * share)
        conv_o[taps : taps + 1, cols] = mine[h : h + 1, :share]
        rows_o[0:1, cols] = mine[2 + h : 3 + h, :share]
        rows_o[1:2, cols] = mine[4 + h : 5 + h, :share]


def block_rows(value, c, rows):
    low = c * rows
    have = max(0, min(rows, value.shape[0] - low))
    if have == rows:
        return value[low : low + rows]
    blank = jnp.zeros((rows - have, value.shape[1]), value.dtype)
    return blank if have == 0 else jnp.concatenate([value[low : low + have], blank], axis=0)


def pack_zo_kernel(ring, in_rows, local, n1, d_z, d_mix, gated, out):
    width = n1.shape[1]
    lanes = d_z.shape[1]
    grad_z = dot_tn(n1[...], d_z[...])
    grad_o = dot_tn(gated[...], d_mix[...])
    side = jnp.zeros((grad_o.shape[0], lanes - width // 2), F32)
    first = jnp.concatenate([grad_o[:, : width // 2], side], axis=1)
    second = jnp.concatenate([grad_o[:, width // 2 :], side], axis=1)
    rows = in_rows // 2
    for c in range(ring):
        out[c // 2, c % 2, :, :lanes] = block_rows(grad_z, c, in_rows).astype(BF16)
        both = [block_rows(first[:local], c, rows), block_rows(second[:local], c, rows)]
        out[c // 2, c % 2, :, lanes:] = jnp.concatenate(both, axis=0).astype(BF16)


def pack_rest_kernel(
    ring, in_rows, small_rows, group, experts, ranked, mine_ref, n1, d_x, gx, gdt, ga, a_ref, gconv, bias, skip,
    gain_mix, gains, gain_moe, router, out_sums, mix_sum, out, small_s, wide_s,
):
    lanes = d_x.shape[1]
    width = n1.shape[1]
    share = width // group
    grad_x = dot_tn(n1[...], d_x[...])
    small_s[...] = jnp.zeros_like(small_s)
    at = 0
    grad_a = jnp.sum(ga[...], axis=1) * a_ref[...]
    for part in (gx[...], gdt[:ranked], grad_a, gconv[...]):
        small_s[at : at + part.shape[0]] = part
        at += part.shape[0]
    small_s[at : at + 1] = bias[...]
    small_s[at + SEG : at + SEG + 1] = skip[...]
    wide_s[...] = jnp.zeros_like(wide_s)
    wide_s[0:1] = gain_mix[...] / gains[0:1]
    wide_s[1:2] = gain_moe[...]
    wide_s[2 : 2 + experts] = router[:experts]
    lane = lax.broadcasted_iota(jnp.int32, (group, LANE), 1)
    row = lax.broadcasted_iota(jnp.int32, (group, LANE), 0)
    stats = jnp.where(
        lane == 0, out_sums[0:1], jnp.where(lane == 1, mix_sum[0:1], jnp.where(lane == 2, out_sums[1:2], 0.0))
    )
    stats = jnp.where(row == mine_ref[0], stats, 0.0)
    stats = jnp.concatenate([stats, jnp.zeros((group, lanes - LANE), F32)], axis=1)
    bottom = jnp.zeros((16 - 2 * group, lanes), F32)
    small_each = small_s.shape[0] // ring
    for c in range(ring):
        if c < 2 + experts:
            full = [wide_s[c : c + 1, w * share : (w + 1) * share] for w in range(group)]
            full = jnp.concatenate(full, axis=0)
            full = jnp.concatenate([full, jnp.zeros((group, lanes - share), F32)], axis=1)
        else:
            full = jnp.zeros((group, lanes), F32)
        small = small_s[c * small_each : (c + 1) * small_each]
        blank = jnp.zeros((small_rows - small_each, lanes), F32)
        parts = [block_rows(grad_x, c, in_rows), small]
        if small_rows > small_each:
            parts.append(blank)
        rows = jnp.concatenate(parts + [full, stats, bottom], axis=0)
        out[c // 2, c % 2] = rows.astype(BF16)


def unpack_kernel(
    ring, group, in_rows, small_rows, experts, states, ranked, taps, denom, mine_ref, done, up_down,
    in_o, out_o, up_o, down_o, taps_o, wx_o, wdt_o, a_o, vec_o, stat_o, small_s, full_s,
):
    c = pl.program_id(0)
    width = in_o.shape[1]
    local = width // 2
    small_each = small_s.shape[0] // ring
    base = 2 * in_rows

    @pl.when(c == 0)
    def _():
        line = lax.broadcasted_iota(jnp.int32, (width, width), 0)
        same = jnp.where(line == lax.broadcasted_iota(jnp.int32, (width, width), 1), 1.0, 0.0)
        up_o[...] = dot_nt(same.astype(BF16), up_down[:, :width])
        down_o[...] = up_down[:, width:].astype(F32)
        full_s[...] = jnp.zeros_like(full_s)

    @pl.when(c * in_rows < width)
    def _():
        rows = done[0, :base, :].astype(F32)
        in_o[...] = jnp.concatenate([rows[:in_rows, :local], rows[in_rows:, :local]], axis=1)
        low = base + small_rows + 16
        rows = done[0, low : low + in_rows, :].astype(F32)
        half = in_rows // 2
        out_o[...] = jnp.concatenate([rows[:half, :local], rows[half:, :local]], axis=1)

    small = done[0, base : base + small_rows, :].astype(F32)
    small_s[pl.ds(pl.multiple_of(c * small_each, SEG), small_each), :] = small[:small_each]
    tile = done[0, base + small_rows : base + small_rows + 16, :].astype(F32)
    row = lax.broadcasted_iota(jnp.int32, tile.shape, 0)
    own = jnp.sum(jnp.where(row == mine_ref[0], tile, 0.0), axis=0, keepdims=True)
    spot = lax.broadcasted_iota(jnp.int32, full_s.shape, 0)
    full_s[...] += jnp.where(spot == c, own, 0.0)

    @pl.when(c == 0)
    def _():
        sums = jnp.sum(jnp.where(row == group + mine_ref[0], tile, 0.0), axis=0, keepdims=True)
        stat_o[...] = jnp.sqrt(sums[:, :LANE] / denom)

    @pl.when(c == ring - 1)
    def _():
        at = 0
        wx_o[...] = small_s[: wx_o.shape[0], :local]
        at += up_to(wx_o.shape[0], LANE)
        wdt_o[...] = small_s[at : at + ranked, :local]
        at += ranked
        a_o[...] = small_s[at : at + states, :local]
        at += states
        taps_o[...] = small_s[at : at + taps, :local]
        vec_o[:SEG] = full_s[...]
        vec_o[SEG : SEG + 1] = small_s[at + taps : at + taps + 1]
        at += SEG
        vec_o[SEG + 1 : SEG + 2] = small_s[at : at + 1]
        vec_o[SEG + 2 : SEG + 3] = small_s[at + SEG : at + SEG + 1]


def experts_kernel(
    group, chunks, x_ref, w_ref, g_ref, r_ref,
    got, w_s, g_s, act_s, slope_s, pre_s, acc, out_s,
    w_sem, g_sem, s1, r1, own1, s2, r2, own2,
):
    mine, mates = mates_of(group)
    count, width = x_ref.shape[2:]
    slots = group * count
    block = w_ref.shape[0] // chunks

    def load(t):
        at = pl.ds(pl.multiple_of(lax.rem(t, chunks) * block, block), block)
        slot = lax.rem(t, 2)
        return pltpu.make_async_copy(w_ref.at[at], w_s.at[slot], w_sem.at[slot])

    load(0).start()
    greet("wa", group)
    sent = []
    for h in range(2):
        for k, who in enumerate(mates):
            copy = remote(x_ref.at[h, who], got.at[h, mine], s1.at[h, k], r1.at[h, k], {"wa": who})
            copy.start()
            sent.append(copy)
        pltpu.make_async_copy(x_ref.at[h, mine], got.at[h, mine], own1.at[h]).start()

    def arrived(h):
        pltpu.make_async_copy(x_ref.at[h, mine], got.at[h, mine], own1.at[h]).wait()
        for copy in sent[h * len(mates) : (h + 1) * len(mates)]:
            copy.wait_recv()
        return got[h].reshape(slots, width)

    def chunk(i):
        return pl.ds(pl.multiple_of(i * block, block), block)

    def returned(h):
        out_s[h] = acc[...].astype(BF16).reshape(group, count, width)
        for k, who in enumerate(mates):
            copy = remote(out_s.at[h, who], r_ref.at[h, mine], s2.at[h, k], r2.at[h, k], {"wa": who})
            copy.start()
            sent.append(copy)
        pltpu.make_async_copy(out_s.at[h, mine], r_ref.at[h, mine], own2.at[h]).start()

    rows = arrived(0)
    acc[...] = jnp.zeros_like(acc)

    def forward(i, _):
        load(i).wait()
        load(i + 1).start()
        w = w_s.at[lax.rem(i, 2)]
        hidden = dot_nt(w[:, :width], rows)
        c = 0.7978845608
        t = jnp.tanh(c * (hidden + 0.044715 * hidden * hidden * hidden))
        act = (0.5 * hidden * (1.0 + t)).astype(BF16)
        act_s[chunk(i), :] = act
        slope_s[chunk(i), :] = 0.5 * (1.0 + t) + 0.5 * hidden * (1.0 - t * t) * c * (
            1.0 + 3.0 * 0.044715 * hidden * hidden
        )
        acc[...] += dot_tn(act, w[:, width:])
        return 0

    lax.fori_loop(0, chunks, forward, 0)
    returned(0)
    d_out = arrived(1)
    acc[...] = jnp.zeros_like(acc)

    def backward(i, _):
        load(chunks + i).wait()

        @pl.when(i < chunks - 1)
        def _():
            load(chunks + i + 1).start()

        w = w_s.at[lax.rem(chunks + i, 2)]
        d_pre = (dot_nt(w[:, width:], d_out) * slope_s[chunk(i), :]).astype(BF16)
        pre_s[chunk(i), :] = d_pre
        acc[...] += dot_tn(d_pre, w[:, :width])
        return 0

    lax.fori_loop(0, chunks, backward, 0)
    returned(1)

    def store(i):
        slot = lax.rem(i, 2)
        return pltpu.make_async_copy(g_s.at[slot], g_ref.at[chunk(i)], g_sem.at[slot])

    def gradients(i, _):
        @pl.when(i >= 2)
        def _():
            store(i - 2).wait()

        g = g_s.at[lax.rem(i, 2)]
        g[:, :width] = dot_nn(pre_s[chunk(i), :], got[0].reshape(slots, width)).astype(BF16)
        g[:, width:] = dot_nn(act_s[chunk(i), :], got[1].reshape(slots, width)).astype(BF16)
        store(i).start()
        return 0

    lax.fori_loop(0, chunks, gradients, 0)
    store(chunks - 2).wait()
    store(chunks - 1).wait()
    for h in range(2):
        pltpu.make_async_copy(out_s.at[h, mine], r_ref.at[h, mine], own2.at[h]).wait()
    for copy in sent[: 2 * len(mates)]:
        copy.wait_send()
    for copy in sent[2 * len(mates) :]:
        copy.wait()


def experts_call(x, w, chunks, cid, us):
    group = lax.axis_size("wa")
    units, width = w.shape[0], x.shape[3]
    slots = group * x.shape[2]
    block = units // chunks
    dma = pltpu.SemaphoreType.DMA
    hbm = pl.BlockSpec(memory_space=pltpu.HBM)
    vmem = pl.BlockSpec(memory_space=pltpu.VMEM)
    two = dma((2, group - 1))
    return pl.pallas_call(
        functools.partial(experts_kernel, group, chunks),
        out_shape=[jax.ShapeDtypeStruct(w.shape, BF16), jax.ShapeDtypeStruct(x.shape, BF16)],
        in_specs=[vmem, hbm],
        out_specs=[hbm, vmem],
        scratch_shapes=[
            pltpu.VMEM(x.shape, BF16),
            pltpu.VMEM((2, block, 2 * width), BF16),
            pltpu.VMEM((2, block, 2 * width), BF16),
            pltpu.VMEM((units, slots), BF16),
            pltpu.VMEM((units, slots), F32),
            pltpu.VMEM((units, slots), BF16),
            pltpu.VMEM((slots, width), F32),
            pltpu.VMEM(x.shape, BF16),
            dma((2,)), dma((2,)),
            two, two, dma((2,)), two, two, dma((2,)),
        ],
        compiler_params=pltpu.CompilerParams(
            collective_id=cid, has_side_effects=True, vmem_limit_bytes=VMEM_LIMIT + 20 * 2**20
        ),
        cost_estimate=lasting(us),
        name="experts",
    )(x, w)


def store_in_order(out, rows, order_s):
    steps = rows.shape[0] // SEG
    for g in range(rows.shape[1] // LANE):
        cols = slice(g * LANE, (g + 1) * LANE)
        for j in range(steps):
            order_s[g, pl.ds(j, SEG, stride=steps), :] = rows[j * SEG : (j + 1) * SEG, cols]
        out[:, cols] = order_s[g]


def combine_kernel(
    experts, back, match, h1_i, n2, up_i, cols, gain, router,
    out_o, dh_o, dmix_o, router_o, gain_o, sums_o, order_s,
):
    length, width = h1_i.shape
    h1, up = h1_i[...], up_i[...]
    lane = lax.broadcasted_iota(jnp.int32, (length, LANE), 1)
    facts = cols[...]

    def column(at):
        return jnp.sum(jnp.where(lane == at, facts, 0.0), axis=1, keepdims=True)

    gates, slope = column(experts), column(experts + 1)
    onehot = jnp.where(lane < experts, facts, 0.0)
    rows = dot_nn(match[...], back[0])
    moe = gates * rows
    result = h1 + moe
    store_in_order(out_o, result, order_s)
    d_gate = jnp.sum(rows * up, axis=1, keepdims=True)
    d_logits = (onehot * (d_gate * slope)).astype(BF16)
    router_o[...] = dot_tn(d_logits, n2[...])
    d_n2 = dot_nn(match[...], back[1]) + dot_nn(d_logits, router[...])
    d_norm, terms = norm_grads(h1, rms_scale(h1), gain[1:2], d_n2)
    gain_o[...] = jnp.sum(terms, axis=0, keepdims=True)
    d_h1 = up + d_norm
    dh_o[...] = d_h1
    dmix_o[...] = d_h1.astype(BF16)
    sums_o[0:1] = jnp.broadcast_to(jnp.sum(result * result, keepdims=True), (1, LANE))
    sums_o[1:2] = jnp.broadcast_to(jnp.sum(moe * moe, keepdims=True), (1, LANE))


def gate_back_kernel(
    states, c_at, d_mix, wout, y, z, uf, proj, step_i, cut, a_ref,
    dy_o, dz_o, skip_o, fx_ref, tx_ref, fd_o, cb, st_s, fd_s,
):
    length, width = step_i.shape[1:]
    groups, steps = width // LANE, length // SEG
    d_gated = dot_nt(d_mix[0], wout[...])
    zf = z[0].astype(F32)
    dy = d_gated * (zf * jax.nn.sigmoid(zf))
    dy_o[0] = dy
    dz_o[0, :length] = (d_gated * y[0] * silu_slope(zf)).astype(BF16)
    dz_o[0, length:] = jnp.zeros((EDGE, width), BF16)

    @pl.when(pl.program_id(0) == 0)
    def _():
        skip_o[...] = jnp.zeros_like(skip_o)

    skip_o[...] += jnp.sum(dy * uf[0], axis=0, keepdims=True)
    cb[...] = spread(proj[0], states, c_at)
    for g in range(groups):
        cols = slice(g * LANE, (g + 1) * LANE)
        st_s[:, cols] = step_i[0, :, cols] + cut[0]
    zero = jnp.zeros((SEG, LANE), F32)
    seg = seg_of()

    def group(g, _):
        lanes = lanes_of(g)
        a = [wide(a_ref, n, lanes) for n in range(states)]

        def step(lap, carry):
            rows = rows_of(steps - 1 - lap)
            st = st_s[rows, lanes]
            d = dy_o[0, rows, lanes]
            new = [carry[0] + st]
            for n in range(states):
                new.append(jnp.exp(st * a[n]) * (carry[n + 1] + cb[rows, state_cols(n)] * d))
            return tuple(new)

        out = lax.fori_loop(0, steps, step, (zero,) * (states + 1), unroll=2)
        total, f = out[0], list(out[1:])
        for k in (1, 2, 4):
            ok = seg < SEG - k
            for n in range(states):
                f[n] = f[n] + jnp.where(ok, jnp.exp(total * a[n]) * rolled(f[n], -k), 0.0)
            total = total + jnp.where(ok, rolled(total, -k), 0.0)
        ok = seg < SEG - 1
        tx_ref[0, :, lanes] = jnp.where(ok, rolled(total, -1), 0.0)
        for n in range(states):
            fx_ref[0, n, :, lanes] = jnp.where(ok, rolled(f[n], -1), 0.0)
            fd_s[pl.ds(n, 1), lanes] = f[n][0:1]
        return 0

    lax.fori_loop(0, groups, group, 0)
    fd_o[0] = fd_s[...].astype(BF16)


def scan_back_kernel(
    states, b_at, place_ref, proj, step_i, sig, uf, cut, dy_i, a_ref, skip, wdt, hx_ref, sx_ref, e_i,
    fx_ref, tx_ref, finals, sums,
    part_o, du_o, dt_o, bias_o, ga_ref,
    bb, cb, dec, pri, accb, accc, st_s, dr_s, ds_s, out_s,
):
    length, width = step_i.shape[1:]
    groups, steps = width // LANE, length // SEG
    bb[...] = spread(proj[0], states, b_at)
    cb[...] = spread(proj[0], states, b_at + states)
    accb[...] = jnp.zeros_like(accb)
    accc[...] = jnp.zeros_like(accc)
    entering(out_s, finals, sums, a_ref, place_ref[0], False)
    e_ref = e_i.at[0]
    dr_s[...] = step_i[0] * uf[0]
    for g in range(groups):
        cols = slice(g * LANE, (g + 1) * LANE)
        st_s[:, cols] = step_i[0, :, cols] + cut[0]

    @pl.when(pl.program_id(0) == 0)
    def _():
        ga_ref[...] = jnp.zeros_like(ga_ref)
        dt_o[...] = jnp.zeros_like(dt_o)
        bias_o[...] = jnp.zeros_like(bias_o)

    def group(g, _):
        lanes = lanes_of(g)
        a = [wide(a_ref, n, lanes) for n in range(states)]
        sx = sx_ref[0, :, lanes]
        first = tuple(
            jnp.exp(sx * a[n]) * wide(e_ref, n, lanes) + hx_ref[0, n, :, lanes]
            for n in range(states)
        )

        def ahead(j, h):
            rows = rows_of(j)
            st = st_s[rows, lanes]
            dr = dr_s[rows, lanes]
            new = []
            for n in range(states):
                decay = jnp.exp(st * a[n])
                dec[rows, state_cols(n)] = decay
                pri[rows, state_cols(n)] = h[n]
                new.append(decay * h[n] + bb[rows, state_cols(n)] * dr)
            return tuple(new)

        last = lax.fori_loop(0, steps, ahead, first, unroll=2)
        end = rows_of(steps)
        for n in range(states):
            pri[end, state_cols(n)] = last[n]
        tx = tx_ref[0, :, lanes]
        flow = tuple(
            jnp.exp(tx * a[n]) * wide(out_s, n, lanes) + fx_ref[0, n, :, lanes]
            for n in range(states)
        )
        gain = wide(skip, 1, lanes)

        def back(lap, f):
            j = steps - 1 - lap
            rows = rows_of(j)
            after = rows_of(j + 1)
            st = step_i[0, rows, lanes]
            dr = dr_s[rows, lanes]
            dy = dy_i[0, rows, lanes]
            new = []
            d_step = None
            d_drive = None
            for n in range(states):
                cols = state_cols(n)
                d = f[n] + cb[rows, cols] * dy
                accc[rows, cols] += pri[after, cols] * dy
                accb[rows, cols] += d * dr
                flowing = dec[rows, cols] * d
                new.append(flowing)
                d_log = flowing * pri[rows, cols]
                ga_ref[n, :, lanes] += d_log * st
                part = d_log * a[n]
                d_step = part if d_step is None else d_step + part
                part = d * bb[rows, cols]
                d_drive = part if d_drive is None else d_drive + part
            ds_s[rows, lanes] = (d_step + d_drive * uf[0, rows, lanes]) * sig[0, rows, lanes]
            du_o[0, rows, lanes] = d_drive * st + dy * gain
            return tuple(new)

        lax.fori_loop(0, steps, back, flow, unroll=2)
        return 0

    lax.fori_loop(0, groups, group, 0)
    d_pre = ds_s[...]
    bias_o[...] += jnp.sum(d_pre, axis=0, keepdims=True)
    d_pre = d_pre.astype(BF16)
    dt_o[...] += dot_tn(proj[0], d_pre)
    columns = part_o.shape[2]
    part = dot_nt(d_pre, wdt[...])
    part = part + collected(accb[...], states, columns, b_at)
    part = part + collected(accc[...], states, columns, b_at + states)
    part_o[0] = part.astype(BF16)


def conv_back_kernel(
    taps, documents, place_ref, doc_ref, proj_i, wproj, du, pre, ext, u, conv, dz, wx, wz, n1,
    dx_o, dn_o, gconv_o, gx_o, gain_o, dext,
):
    length, width = du.shape[1:]
    steps = length // SEG
    behind = taps - 1

    @pl.when(pl.program_id(0) == 0)
    def _():
        gconv_o[...] = jnp.zeros_like(gconv_o)
        gx_o[...] = jnp.zeros_like(gx_o)
        gain_o[...] = jnp.zeros_like(gain_o)

    proj = proj_i[0]
    gx_o[...] += dot_tn(proj, u[0])
    d_u = dot_nn(proj, wproj[...]) + du[0]
    masks, _ = lag_masks(place_ref[0], doc_ref, documents, pl.program_id(0), length, taps)
    seg = seg_of()
    row = lax.broadcasted_iota(jnp.int32, (EDGE, LANE), 0)
    for g in range(width // LANE):
        cols = slice(g * LANE, (g + 1) * LANE)
        d = d_u[:, cols] * silu_slope(pre[0, :, cols])
        gconv_o[taps : taps + 1, cols] += jnp.sum(d, axis=0, keepdims=True)
        dext[...] = jnp.zeros_like(dext)
        for lag in range(taps):
            weighted = d if lag == 0 else d * masks[lag]
            at = pl.ds((behind - lag) * SEG, length)
            gconv_o[lag : lag + 1, cols] += jnp.sum(weighted * ext[0, at, cols], axis=0, keepdims=True)
            dext[at, :] += weighted * conv[lag : lag + 1, cols]
        before = jnp.zeros((EDGE, LANE), F32)
        for i in range(behind):
            head = dext[i * SEG : (i + 1) * SEG]
            j = pl.ds((steps + i) * SEG, SEG)
            dext[j, :] += jnp.where(seg < SEG - 1, rolled(head, -1), 0.0)
            first = jnp.broadcast_to(head[0:1], (EDGE, LANE))
            before = before + jnp.where(row == EDGE - behind + i, first, 0.0)
        dx_o[0, :length, cols] = dext[behind * SEG :].astype(BF16)
        dx_o[0, length:, cols] = before.astype(BF16)
    d_n1 = dot_nt(dx_o[0], wx[0]) + dot_nt(dz[0], wz[0])
    gain_o[...] += jnp.sum(d_n1 * n1[0].astype(F32), axis=0, keepdims=True)
    dn_o[0] = d_n1.astype(BF16)


def leave_kernel(taps, last_ref, terms, edges, tok, gain, dh, out_o, dn_s, order_s):
    length = tok.shape[0]
    steps = length // SEG
    behind = taps - 1
    total = terms[0, :length].astype(F32)
    edge = edges[0].astype(F32)
    for w in range(1, terms.shape[0]):
        total = total + terms[w, :length].astype(F32)
        edge = edge + edges[w].astype(F32)
    edge = jnp.where(last_ref[0] > 0, 0.0, edge)
    dn_s[...] = total
    seg = lax.broadcasted_iota(jnp.int32, (SEG, tok.shape[1]), 0)
    for i in range(behind):
        j = pl.ds((steps - behind + i) * SEG, SEG)
        row = EDGE - behind + i
        came = jnp.broadcast_to(edge[row : row + 1], seg.shape)
        dn_s[j, :] += jnp.where(seg == SEG - 1, came, 0.0)
    x = dot_nn(permutation(length), tok[...])
    d_x, _ = norm_grads(x, rms_scale(x), gain[0:1], dn_s[...])
    result = dh[...] + d_x
    store_in_order(out_o, result, order_s)


SMEM = "smem"
ANY = "any"


def by_stream(shape, at=0):
    block = tuple(1 if i == at else n for i, n in enumerate(shape))
    rank = len(shape)

    def index(s):
        return tuple(s if i == at else 0 for i in range(rank))

    return pl.BlockSpec(block, index)


def whole(shape):
    return pl.BlockSpec(shape, lambda s: (0,) * len(shape))


def call(kernel, name, grid, args, outs, scratch, us):
    arrays, specs = [], []
    for array, at in args:
        arrays.append(array)
        if at == SMEM:
            specs.append(pl.BlockSpec(memory_space=pltpu.SMEM))
        elif at == ANY:
            specs.append(pl.BlockSpec(memory_space=pl.ANY))
        elif callable(at):
            specs.append(at(array.shape))
        else:
            specs.append(whole(array.shape) if at is None else by_stream(array.shape, at))
    out_specs = []
    for shape, _, at in outs:
        if callable(at):
            out_specs.append(at(shape))
        else:
            out_specs.append(whole(shape) if at is None else by_stream(shape, at))
    return pl.pallas_call(
        kernel,
        grid=(grid,),
        out_shape=[jax.ShapeDtypeStruct(shape, dtype) for shape, dtype, _ in outs],
        in_specs=specs,
        out_specs=out_specs,
        scratch_shapes=scratch,
        compiler_params=pltpu.CompilerParams(vmem_limit_bytes=VMEM_LIMIT),
        cost_estimate=lasting(us),
        name=name,
    )(*arrays)


def padded_to(array, width, axis):
    pads = [(0, 0)] * array.ndim
    pads[axis] = (0, width - array.shape[axis])
    return jnp.pad(array, pads)


def up_to(n, multiple):
    return -(-n // multiple) * multiple


def body(
    tokens, out_grad, doc_starts, routes, keep_mask, norm_mix, w_in, conv_w, conv_b, w_x, w_dt,
    dt_bias, a_log, d_skip, w_out, norm_moe, w_router, w_up, w_down,
):
    group = lax.axis_size("wa")
    ring = lax.axis_size("ctx")
    mine = lax.axis_index("wa")
    place = lax.axis_index("ctx")
    length, width = tokens.shape[1:]
    taps, local = conv_w.shape
    states = a_log.shape[0]
    ranked = w_dt.shape[0]
    experts = w_router.shape[1]
    padded = up_to(local, LANE)
    columns = up_to(w_x.shape[1], LANE)
    steps = length // SEG
    rows = length + EDGE
    slots = experts * (length // 2)
    share = norm_mix.shape[0]
    order_vmem = pltpu.VMEM((width // LANE, length, LANE), F32)
    place_s = place.astype(jnp.int32).reshape(1)
    mine_s = mine.astype(jnp.int32).reshape(1)
    last_s = (place == ring - 1).astype(jnp.int32).reshape(1)
    f32_vmem = lambda *shape: pltpu.VMEM(shape, F32)

    (own_experts,) = call(
        pack_kernel, "pack", 1, [(w_up[0], None), (w_down[0], None)],
        [((w_down.shape[1], 2 * width), BF16, None)], [], 3,
    )
    expert_w = lax.all_gather(own_experts, "ctx", axis=0, tiled=True)

    in_rows = up_to(-(-width // ring), 16)
    blank = ring * in_rows - width
    part_in = jnp.pad(w_in, ((0, blank), (0, 0))) if blank else w_in
    part_in = lax.dynamic_slice_in_dim(part_in, place * in_rows, in_rows, 0)
    halves = jnp.stack([part_in[:, :local], part_in[:, local:]], axis=0)
    halves = jnp.pad(halves, ((0, 0), (0, 0), (0, padded - local)))
    small = jnp.concatenate([conv_b, dt_bias, d_skip, norm_mix, norm_moe], axis=0).reshape(SEG, share)
    small = jnp.concatenate([small, jnp.pad(w_router.T, ((0, SEG - experts), (0, 0)))], axis=0)
    small = padded_to(small, up_to(share, LANE), 1)
    documents = doc_starts.shape[1]
    doc_tile = jnp.pad(doc_starts, ((0, SEG - 1), (0, LANE - documents)))
    all_rows, all_edges, smalls, docs, w_blocks = start(tokens[0], small, doc_tile, halves, 1)
    proj_in = w_blocks.reshape(2, ring * in_rows, padded)[:, :width]
    of_x = lambda shape: pl.BlockSpec((1,) + shape[1:], lambda i: (0, 0, 0))
    of_z = lambda shape: pl.BlockSpec((1,) + shape[1:], lambda i: (1, 0, 0))
    par = (SEG, padded)
    gains, router, wproj, wdt, wout, conv, vectors, a_mat = call(
        functools.partial(prepare_kernel, experts), "prepare", 1,
        [(smalls, None), (small, None), (w_x.T, None), (w_dt, None), (w_out, None), (conv_w, None),
         (a_log, None)],
        [((SEG, width), F32, None), ((LANE, width), BF16, None), ((columns, padded), BF16, None),
         ((columns, padded), BF16, None), ((padded, width), BF16, None), (par, F32, None),
         (par, F32, None), ((states, padded), F32, None)],
        [f32_vmem(2 * SEG, width)], 3,
    )

    vec = (group, length, padded)
    n1, ext, pre_conv, u_f, u, z, part, cut = call(
        functools.partial(enter_kernel, taps, documents), "enter", group,
        [(place_s, SMEM), (docs, SMEM), (all_rows, 0), (all_edges, 0), (gains, None),
         (proj_in, of_x), (proj_in, of_z), (conv, None), (wproj, None)],
        [((group, rows, width), BF16, 0), ((group, (taps - 1) * SEG + length, padded), F32, 0),
         (vec, F32, 0), (vec, F32, 0), (vec, BF16, 0), (vec, BF16, 0),
         ((group, length, columns), BF16, 0), ((group, length, LANE), F32, 0)],
        [], 8,
    )
    projected = sum_all(part, 2, 11)
    seg_states = (group, states, SEG, padded)
    seg_sums = (group, SEG, padded)
    dev_states = (group, states, padded)
    dev_sums = (group, 1, padded)
    spread_vmem = f32_vmem(length, states * LANE)
    lane_vmem = f32_vmem(length, padded)
    state_vmem = f32_vmem(states, padded)
    step_size, sig, h_in, s_in, h_dev, s_dev = call(
        functools.partial(summary_kernel, states, ranked), "scan_summary", group,
        [(projected, 0), (wdt, None), (vectors, None), (u_f, 0), (cut, 0), (a_mat, None)],
        [(vec, F32, 0), (vec, F32, 0), (seg_states, F32, 0),
         (seg_sums, F32, 0), (dev_states, BF16, 0), (dev_sums, F32, 0)],
        [spread_vmem, lane_vmem, lane_vmem, state_vmem], 10,
    )
    all_h, all_s = gather_all([h_dev, s_dev], "ctx", 3, 15)
    y_full, gated, mix_part, e_in = call(
        functools.partial(output_kernel, states, ranked), "scan_output", group,
        [(place_s, SMEM), (projected, 0), (step_size, 0), (u_f, 0), (cut, 0), (a_mat, None), (h_in, 0),
         (s_in, 0), (all_h, 1), (all_s, 1), (z, 0), (vectors, None), (wout, None)],
        [(vec, F32, 0), (vec, BF16, 0), ((group, length, width), BF16, 0), (dev_states, F32, 0)],
        [spread_vmem, spread_vmem, lane_vmem, lane_vmem], 13,
    )
    mix_terms = trade(mix_part, "wa", 4, 25)

    row_f = (length, width)
    h1, n2, upstream, facts, match, outgoing, mix_sum = call(
        functools.partial(route_kernel, experts), "route", 1,
        [(mix_terms, None), (tokens[0], None), (gains, None), (router, None),
         (routes[0].T, None), (keep_mask, None), (out_grad[0], None)],
        [(row_f, F32, None), (row_f, BF16, None), (row_f, F32, None), ((length, LANE), F32, None),
         ((length, slots), BF16, None), ((2, slots, width), BF16, None), ((SEG, LANE), F32, None)],
        [], 5,
    )
    grad_experts, returned = experts_call(
        outgoing.reshape(2, group, slots // group, width), expert_w, 8, 5, 58
    )
    share_experts = lax.psum_scatter(grad_experts, "ctx", scatter_dimension=0, tiled=True)
    result, d_h1, d_mix_own, grad_router, grad_gain_moe, out_sums = call(
        functools.partial(combine_kernel, experts), "combine", 1,
        [(returned.reshape(2, slots, width), None), (match, None), (h1, None), (n2, None),
         (upstream, None), (facts, None), (gains, None), (router, None)],
        [(row_f, F32, None), (row_f, F32, None), (row_f, BF16, None), ((LANE, width), F32, None),
         ((1, width), F32, None), ((SEG, LANE), F32, None)],
        [order_vmem], 6,
    )
    (d_mix,) = gather_all([d_mix_own], "wa", 7, 28)

    d_y, d_z, grad_skip, f_in, t_in, f_dev = call(
        functools.partial(gate_back_kernel, states, ranked + states), "gate_back", group,
        [(d_mix, 0), (wout, None), (y_full, 0), (z, 0), (u_f, 0), (projected, 0), (step_size, 0),
         (cut, 0), (a_mat, None)],
        [(vec, F32, 0), ((group, rows, padded), BF16, 0), ((1, padded), F32, None),
         (seg_states, F32, 0), (seg_sums, F32, 0), (dev_states, BF16, 0)],
        [spread_vmem, lane_vmem, state_vmem], 11,
    )
    flat_n1 = n1.reshape(group * rows, width)
    zo_shape = (ring // 2, 2, in_rows, 2 * padded)
    (grad_zo,) = call(
        functools.partial(pack_zo_kernel, ring, in_rows, local), "pack_zo", 1,
        [(flat_n1, None), (d_z.reshape(group * rows, padded), None),
         (d_mix.reshape(group * length, width), None), (gated.reshape(group * length, padded), None)],
        [(zo_shape, BF16, None)], [], 5,
    )
    all_f, pair_zo = carry_back(f_dev, grad_zo, 8, 14)
    d_part, d_u, grad_dt, grad_step_bias, grad_a = call(
        functools.partial(scan_back_kernel, states, ranked), "scan_back", group,
        [(place_s, SMEM), (projected, 0), (step_size, 0), (sig, 0), (u_f, 0), (cut, 0), (d_y, 0),
         (a_mat, None), (vectors, None), (wdt, None), (h_in, 0), (s_in, 0), (e_in, 0), (f_in, 0),
         (t_in, 0), (all_f, 1), (all_s, 1)],
        [((group, length, columns), BF16, 0), (vec, F32, 0), ((columns, padded), F32, None),
         ((1, padded), F32, None), ((states, SEG, padded), F32, None)],
        [spread_vmem, spread_vmem, spread_vmem, f32_vmem(length + SEG, states * LANE), spread_vmem,
         spread_vmem, lane_vmem, lane_vmem, lane_vmem, state_vmem], 34,
    )
    d_projected, chunk_zo = proj_back(d_part, grad_zo, pair_zo, 9, 20)
    d_x, d_n1_part, grad_conv, grad_x, gain_terms = call(
        functools.partial(conv_back_kernel, taps, documents), "conv_back", group,
        [(place_s, SMEM), (docs, SMEM), (d_projected, 0), (wproj, None), (d_u, 0), (pre_conv, 0),
         (ext, 0), (u, 0), (conv, None), (d_z, 0), (proj_in, of_x), (proj_in, of_z), (n1, 0)],
        [((group, rows, padded), BF16, 0), ((group, rows, width), BF16, 0),
         ((SEG, padded), F32, None), ((columns, padded), F32, None), ((1, width), F32, None)],
        [f32_vmem((taps - 1) * SEG + length, LANE)], 10,
    )
    small_all = columns + up_to(ranked, SEG) + states + 3 * SEG
    small_each = up_to(-(-small_all // ring), SEG)
    small_rows = up_to(small_each, 16)
    (packed,) = call(
        functools.partial(pack_rest_kernel, ring, in_rows, small_rows, group, experts, ranked),
        "pack_rest", 1,
        [(mine_s, SMEM), (flat_n1, None), (d_x.reshape(group * rows, padded), None), (grad_x, None),
         (grad_dt, None), (grad_a, None), (a_mat, None), (grad_conv, None), (grad_step_bias, None),
         (grad_skip, None), (gain_terms, None), (gains, None), (grad_gain_moe, None),
         (grad_router, None), (out_sums, None), (mix_sum, None)],
        [((ring // 2, 2, in_rows + small_rows + 16, padded), BF16, None)],
        [f32_vmem(ring * small_each, padded), f32_vmem(SEG, width)], 5,
    )
    done, d_n1_terms, d_edges = finish(packed, chunk_zo, d_n1_part, in_rows, small_rows, 11)
    blocks = width // in_rows
    of_rows = lambda shape: pl.BlockSpec(
        (shape[0] // blocks, shape[1]), lambda i: (jnp.minimum(i, blocks - 1), 0)
    )
    unpacked = call(
        functools.partial(
            unpack_kernel, ring, group, in_rows, small_rows, experts, states, ranked, taps,
            float(length * ring * width),
        ),
        "unpack", ring,
        [(mine_s, SMEM), (done, 0), (share_experts, None)],
        [((width, 2 * local), F32, of_rows), ((local, width), F32, of_rows),
         ((width, w_down.shape[1]), F32, None), ((w_down.shape[1], width), F32, None),
         ((taps, local), F32, None), ((w_x.shape[1], local), F32, None), ((ranked, local), F32, None),
         ((states, local), F32, None), ((2 * SEG, padded), F32, None), ((1, LANE), F32, None)],
        [f32_vmem(ring * small_each, padded), f32_vmem(SEG, padded)], 8,
    )
    share_in, share_out, share_up, share_down, g_taps, g_wx, g_wdt, g_a, vecs, stats = unpacked
    fulls, vecs = vecs[:SEG, :share], vecs[SEG:, :local]
    (input_grad,) = call(
        functools.partial(leave_kernel, taps), "leave", 1,
        [(last_s, SMEM), (d_n1_terms, None), (d_edges, None), (tokens[0], None), (gains, None),
         (d_h1, None)],
        [(row_f, F32, None)], [f32_vmem(length, width), order_vmem], 4,
    )
    return (
        result[None],
        input_grad[None],
        fulls[0],
        share_in,
        g_taps,
        vecs[0],
        g_wx.T,
        g_wdt,
        vecs[1],
        g_a,
        vecs[2],
        share_out,
        fulls[1],
        fulls[2 : 2 + experts].T,
        share_up[None],
        share_down[None],
        stats[:, :3],
    )


def solution(mesh):
    placed = (
        P("wa", "ctx", None),
        P("wa", "ctx", None),
        P("wa", None),
        P("wa", "ctx", None),
        P("wa", "ctx"),
        P("wa"),
        P(None, "wa"),
        P(None, "wa"),
        P("wa"),
        P("wa", None),
        P(None, "wa"),
        P("wa"),
        P(None, "wa"),
        P("wa"),
        P("wa", None),
        P("wa"),
        P("wa", None),
        P("wa", None, "ctx"),
        P("wa", "ctx", None),
    )
    return jax.shard_map(
        body,
        mesh=mesh,
        in_specs=placed,
        out_specs=(
            P("wa", "ctx", None),
            P("wa", "ctx", None),
            P("wa"),
            P(None, "wa"),
            P(None, "wa"),
            P("wa"),
            P("wa", None),
            P(None, "wa"),
            P("wa"),
            P(None, "wa"),
            P("wa"),
            P("wa", None),
            P("wa"),
            P("wa", None),
            P("wa", None, "ctx"),
            P("wa", "ctx", None),
            P("wa", None),
        ),
        check_vma=False,
    )
```

```python
import functools

import jax
import jax.numpy as jnp
from jax import lax
from jax.experimental import pallas as pl
from jax.experimental.pallas import tpu as pltpu
from jax.sharding import PartitionSpec as P

EPS = 1e-05
F32 = jnp.float32
BF16 = jnp.bfloat16
SEG = 8
LANE = 128
EDGE = 16
CUT = 1e30
MESH = pl.DeviceIdType.MESH
VMEM_LIMIT = 24 * 2**20
LARGE_LIMIT = 60 * 2**20


def lasting(us):
    return pl.CostEstimate(
        flops=int(us * 1.1e9), bytes_accessed=int(us * 3.5e6), transcendentals=0
    )


def greet(axis, count):
    me = lax.axis_index(axis)
    barrier = pltpu.get_barrier_semaphore()
    for k in range(1, count):
        pl.semaphore_signal(
            barrier, inc=1, device_id={axis: lax.rem(me + k, count)}, device_id_type=MESH
        )
    pl.semaphore_wait(barrier, count - 1)
    return me


def gather_kernel(axis, count, arrays, *refs):
    srcs, dsts = refs[:arrays], refs[arrays : 2 * arrays]
    send, recv, own = refs[-3:]
    me = greet(axis, count)
    copies = []
    for i in range(arrays):
        for k in range(1, count):
            copy = pltpu.make_async_remote_copy(
                src_ref=srcs[i],
                dst_ref=dsts[i].at[me],
                send_sem=send.at[i, k],
                recv_sem=recv.at[i, k],
                device_id={axis: lax.rem(me + k, count)},
                device_id_type=MESH,
            )
            copy.start()
            copies.append(copy)
    for i in range(arrays):
        local = pltpu.make_async_copy(srcs[i], dsts[i].at[me], own.at[i])
        local.start()
        copies.append(local)
    for copy in copies:
        copy.wait()


def trade_kernel(axis, count, x_ref, o_ref, send, recv, own):
    me = greet(axis, count)
    copies = []
    for k in range(1, count):
        other = lax.rem(me + k, count)
        copy = pltpu.make_async_remote_copy(
            src_ref=x_ref.at[other],
            dst_ref=o_ref.at[me],
            send_sem=send.at[k],
            recv_sem=recv.at[k],
            device_id={axis: other},
            device_id_type=MESH,
        )
        copy.start()
        copies.append(copy)
    local = pltpu.make_async_copy(x_ref.at[me], o_ref.at[me], own)
    local.start()
    local.wait()
    for copy in copies:
        copy.wait()


def trade(x, axis, cid, us):
    count = lax.axis_size(axis)
    return pl.pallas_call(
        functools.partial(trade_kernel, axis, count),
        out_shape=jax.ShapeDtypeStruct(x.shape, x.dtype),
        in_specs=[pl.BlockSpec(memory_space=pl.ANY)],
        out_specs=pl.BlockSpec(memory_space=pl.ANY),
        scratch_shapes=[
            pltpu.SemaphoreType.DMA((count,)),
            pltpu.SemaphoreType.DMA((count,)),
            pltpu.SemaphoreType.DMA,
        ],
        compiler_params=pltpu.CompilerParams(
            collective_id=cid, has_side_effects=True, vmem_limit_bytes=VMEM_LIMIT
        ),
        cost_estimate=lasting(us),
        name=f"trade_{cid}",
    )(x)


def sum_start(mates, x_ref, got, send, recv):
    copies = []
    for k, who in enumerate(mates):
        copy = remote(x_ref.at[who], got.at[k], send.at[k], recv.at[k], {"wa": who})
        copy.start()
        copies.append(copy)
    return copies


def sum_spread(mine, mates, x_ref, got, o_ref, copies, send, recv):
    for copy in copies:
        copy.wait_recv()
    parts = [x_ref.at[mine]] + [got.at[k] for k in range(len(mates))]
    add_rows(o_ref.at[mine], parts, x_ref.shape[1])
    spreads = []
    for k, who in enumerate(mates):
        copy = remote(o_ref.at[mine], o_ref.at[mine], send.at[k], recv.at[k], {"wa": who})
        copy.start()
        spreads.append(copy)
    return spreads


def sum_all_kernel(group, x_ref, o_ref, got, s1, r1, s2, r2):
    greet("wa", group)
    mine, mates = mates_of(group)
    copies = sum_start(mates, x_ref, got, s1, r1)
    spreads = sum_spread(mine, mates, x_ref, got, o_ref, copies, s2, r2)
    for copy in spreads:
        copy.wait()
    for copy in copies:
        copy.wait_send()


def sum_all(x, cid, us):
    group = lax.axis_size("wa")
    vmem = pl.BlockSpec(memory_space=pltpu.VMEM)
    dma = pltpu.SemaphoreType.DMA
    return pl.pallas_call(
        functools.partial(sum_all_kernel, group),
        out_shape=jax.ShapeDtypeStruct(x.shape, x.dtype),
        in_specs=[vmem],
        out_specs=vmem,
        scratch_shapes=[pltpu.VMEM((group - 1,) + x.shape[1:], x.dtype)] + [dma((group - 1,))] * 4,
        compiler_params=pltpu.CompilerParams(
            collective_id=cid, has_side_effects=True, vmem_limit_bytes=VMEM_LIMIT
        ),
        cost_estimate=lasting(us),
        name="sum_all",
    )(x)


def gather_all(xs, axis, cid, us):
    count, arrays = lax.axis_size(axis), len(xs)
    return pl.pallas_call(
        functools.partial(gather_kernel, axis, count, arrays),
        out_shape=[jax.ShapeDtypeStruct((count,) + x.shape, x.dtype) for x in xs],
        in_specs=[pl.BlockSpec(memory_space=pl.ANY)] * arrays,
        out_specs=[pl.BlockSpec(memory_space=pl.ANY)] * arrays,
        scratch_shapes=[
            pltpu.SemaphoreType.DMA((arrays, count)),
            pltpu.SemaphoreType.DMA((arrays, count)),
            pltpu.SemaphoreType.DMA((arrays,)),
        ],
        compiler_params=pltpu.CompilerParams(
            collective_id=cid, has_side_effects=True, vmem_limit_bytes=VMEM_LIMIT
        ),
        cost_estimate=lasting(us),
        name=f"gather_{cid}",
    )(*xs)


def remote(src, dst, send, recv, where):
    return pltpu.make_async_remote_copy(
        src_ref=src, dst_ref=dst, send_sem=send, recv_sem=recv,
        device_id=where, device_id_type=MESH,
    )


def add_rows(out, parts, rows):
    def one(i, _):
        at = pl.ds(pl.multiple_of(i * 16, 16), 16)
        total = parts[0][at, :].astype(F32)
        for part in parts[1:]:
            total = total + part[at, :].astype(F32)
        out[at, :] = total.astype(out.dtype)
        return 0

    lax.fori_loop(0, rows // 16, one, 0)


def neighbours(ring):
    me = lax.axis_index("ctx")
    half = ring // 2
    lane = lax.rem(me, 2)
    chip = me // 2
    peers = [lax.rem(chip + k, half) * 2 + lane for k in range(1, half)]
    return me, chip, lane, me + 1 - 2 * lane, peers


def mates_of(group):
    mine = lax.axis_index("wa")
    return mine, [lax.rem(mine + k, group) for k in range(1, group)]


def hello(barrier, axis, who):
    pl.semaphore_signal(barrier, inc=1, device_id={axis: who}, device_id_type=MESH)


def carry_kernel(ring, arrays, halved, *refs):
    total = arrays + halved
    srcs, dsts = refs[:total], refs[total : 2 * total]
    send, recv, fwd_s, fwd_r, own, half_s, half_r = refs[2 * total :]
    me, chip, lane, pair, peers = neighbours(ring)
    half = ring // 2
    barrier = pltpu.get_barrier_semaphore()
    for who in [pair] + peers:
        hello(barrier, "ctx", who)
    pl.semaphore_wait(barrier, half)
    copies, forwards, local = [], [], []
    for i in range(arrays):
        for k, who in enumerate(peers):
            copies.append(remote(srcs[i], dsts[i].at[me], send.at[i, k], recv.at[i, k], {"ctx": who}))
            copies[-1].start()
    for i in range(arrays):
        forwards.append(remote(srcs[i], dsts[i].at[me], fwd_s.at[i, 0], fwd_r.at[i, 0], {"ctx": pair}))
        forwards[-1].start()
        local.append(pltpu.make_async_copy(srcs[i], dsts[i].at[me], own.at[i]))
        local[-1].start()
    if halved:
        to_pair = remote(srcs[arrays].at[:, 1 - lane], dsts[arrays], half_s, half_r, {"ctx": pair})
        to_pair.start()
        local.append(to_pair)
    for i in range(arrays):
        for k in range(1, half):
            copies[i * (half - 1) + k - 1].wait_recv()
            block = dsts[i].at[lax.rem(chip + half - k, half) * 2 + lane]
            forwards.append(remote(block, block, fwd_s.at[i, k], fwd_r.at[i, k], {"ctx": pair}))
            forwards[-1].start()
    for copy in copies:
        copy.wait_send()
    for copy in forwards + local:
        copy.wait()


def carry(xs, cid, us, halved=None):
    ring, arrays = lax.axis_size("ctx"), len(xs)
    half = ring // 2
    shapes = [((ring,) + x.shape, x.dtype) for x in xs]
    if halved is not None:
        xs = xs + [halved]
        shapes.append((halved.shape[:1] + halved.shape[2:], halved.dtype))
    hbm = pl.BlockSpec(memory_space=pl.ANY)
    dma = pltpu.SemaphoreType.DMA
    return pl.pallas_call(
        functools.partial(carry_kernel, ring, arrays, len(xs) - arrays),
        out_shape=[jax.ShapeDtypeStruct(shape, dtype) for shape, dtype in shapes],
        in_specs=[hbm] * len(xs),
        out_specs=[hbm] * len(xs),
        scratch_shapes=[
            dma((arrays, half - 1)), dma((arrays, half - 1)), dma((arrays, half)), dma((arrays, half)),
            dma((arrays,)), dma, dma,
        ],
        compiler_params=pltpu.CompilerParams(
            collective_id=cid, has_side_effects=True, vmem_limit_bytes=VMEM_LIMIT
        ),
        cost_estimate=lasting(us),
        name=f"carry_{cid}",
    )(*xs)


def finish_kernel(
    ring, group, in_rows, small_rows,
    g_ref, zf_ref, d_ref, o_ref, dt_ref, de_ref,
    from_pair, paired, came, own, zin, tiles, fin, store_s,
    pair_s, pair_r, ctx_s, ctx_r, z_s, z_r, tile_s, tile_r, d_s, d_r, d_own, last_s, last_r, fwd_s, fwd_r,
    edge_s, edge_r,
):
    me, chip, lane, pair, peers = neighbours(ring)
    mine, mates = mates_of(group)
    half = ring // 2
    rows = in_rows + small_rows + 16
    lanes = g_ref.shape[3]
    barrier = pltpu.get_barrier_semaphore()
    for who in [pair] + peers:
        hello(barrier, "ctx", who)
    for who in mates:
        hello(barrier, "wa", who)
    has_next = me < ring - 1
    has_last = me > 0

    @pl.when(has_next)
    def _():
        hello(barrier, "ctx", me + 1)

    @pl.when(has_last)
    def _():
        hello(barrier, "ctx", me - 1)

    around = jnp.where(has_next, 1, 0) + jnp.where(has_last, 1, 0)
    pl.semaphore_wait(barrier, half + group - 1 + around)

    to_pair = remote(g_ref.at[:, 1 - lane], from_pair, pair_s, pair_r, {"ctx": pair})
    to_pair.start()
    ready = 2 * in_rows + small_rows + 16
    parts = [pl.ds(ready, in_rows), pl.ds(0, ready)]
    fin[parts[0]] = zf_ref[:, lanes:]
    stored = []

    def to_all(i):
        src, dst = fin.at[parts[i]], o_ref.at[me, parts[i]]
        copies = []
        for k, who in enumerate(peers):
            copies.append(remote(src, dst, last_s.at[i, k], last_r.at[i, k], {"ctx": who}))
        copies.append(remote(src, dst, fwd_s.at[i, 0], fwd_r.at[i, 0], {"ctx": pair}))
        for copy in copies:
            copy.start()
        stored.append(pltpu.make_async_copy(src, dst, store_s.at[i]))
        stored[-1].start()
        return copies

    def forward(i, copies):
        for k in range(1, half):
            copies[k - 1].wait_recv()
            source = lax.rem(chip + half - k, half) * 2 + lane
            block = o_ref.at[source, parts[i]]
            copy = remote(block, block, fwd_s.at[i, k], fwd_r.at[i, k], {"ctx": pair})
            copy.start()
            copies.append(copy)

    x_to = mine // 2
    z_to = group // 2 + mine // 2
    slot = lax.rem(mine, 2)
    z_ref = zf_ref.at[:, pl.ds(0, lanes)]
    x_ref = own.at[pl.ds(0, in_rows)]
    send_x = remote(x_ref, zin.at[slot], z_s.at[0], z_r.at[slot], {"wa": x_to})
    send_z = remote(z_ref, zin.at[slot], z_s.at[1], z_r.at[slot], {"wa": z_to})
    keep_x = pltpu.make_async_copy(x_ref, zin.at[slot], z_r.at[slot])
    keep_z = pltpu.make_async_copy(z_ref, zin.at[slot], z_r.at[slot])

    @pl.when(z_to != mine)
    def _():
        send_z.start()

    @pl.when(z_to == mine)
    def _():
        keep_z.start()

    cut = d_ref.shape[1] // 32 * 16
    pieces = [pl.ds(0, cut), pl.ds(cut, d_ref.shape[1] - cut)]
    trades = []

    def trade_rows(i):
        for k, who in enumerate(mates):
            copy = remote(
                d_ref.at[who, pieces[i]], dt_ref.at[mine, pieces[i]], d_s.at[i, k], d_r.at[i, k],
                {"wa": who},
            )
            copy.start()
            trades.append(copy)

    trade_rows(0)
    kept = pltpu.make_async_copy(d_ref.at[mine], dt_ref.at[mine], d_own)
    kept.start()

    to_pair.wait_recv()
    scattered = []
    for k, who in enumerate(peers):
        to = lax.rem(chip + k + 1, half)
        add_rows(paired.at[to], [g_ref.at[to, lane], from_pair.at[to]], rows)
        copy = remote(paired.at[to], came.at[k], ctx_s.at[k], ctx_r.at[k], {"ctx": who})
        copy.start()
        scattered.append(copy)
    early = to_all(0)
    add_rows(paired.at[chip], [g_ref.at[chip, lane], from_pair.at[chip]], rows)
    for copy in scattered:
        copy.wait_recv()
    add_rows(own, [paired.at[chip]] + [came.at[k] for k in range(half - 1)], rows)

    @pl.when(x_to != mine)
    def _():
        send_x.start()

    @pl.when(x_to == mine)
    def _():
        keep_x.start()

    tile = pl.ds(in_rows + small_rows, 16)
    spread_tiles = []
    for k, who in enumerate(mates):
        copy = remote(own.at[tile], tiles.at[k], tile_s.at[k], tile_r.at[k], {"wa": who})
        copy.start()
        spread_tiles.append(copy)
    forward(0, early)
    fin[pl.ds(2 * in_rows, small_rows)] = own[pl.ds(in_rows, small_rows)]
    for copy in spread_tiles:
        copy.wait_recv()
    add_rows(
        fin.at[pl.ds(2 * in_rows + small_rows, 16)],
        [own.at[tile]] + [tiles.at[k] for k in range(group - 1)],
        16,
    )
    for s in range(2):
        pltpu.make_async_copy(zin.at[s], zin.at[s], z_r.at[s]).wait()
        fin[pl.ds(s * in_rows, in_rows)] = zin[s]
    late = to_all(1)
    trade_rows(1)
    kept.wait()
    forward(1, late)

    for copy in trades:
        copy.wait_recv()
    edges = dt_ref.at[:, pl.ds(d_ref.shape[1] - EDGE, EDGE)]
    to_last = remote(edges, de_ref, edge_s, edge_r, {"ctx": me - 1})

    @pl.when(has_last)
    def _():
        to_last.start()

    for copies in (early, late):
        for copy in copies[half - 1 :]:
            copy.wait_recv()

    for copy in stored:
        copy.wait()
    to_pair.wait_send()
    for copy in scattered + spread_tiles + early + late + trades:
        copy.wait_send()

    @pl.when(x_to != mine)
    def _():
        send_x.wait_send()

    @pl.when(z_to != mine)
    def _():
        send_z.wait_send()

    @pl.when(has_last)
    def _():
        to_last.wait_send()

    @pl.when(has_next)
    def _():
        to_last.wait_recv()


def finish(g, zf, d, in_rows, small_rows, cid):
    ring, group = lax.axis_size("ctx"), lax.axis_size("wa")
    half = ring // 2
    rows, lanes = g.shape[2:]
    out_rows = 3 * in_rows + small_rows + 16
    vmem = pl.BlockSpec(memory_space=pltpu.VMEM)
    hbm = pl.BlockSpec(memory_space=pl.ANY)
    dma = pltpu.SemaphoreType.DMA
    return pl.pallas_call(
        functools.partial(finish_kernel, ring, group, in_rows, small_rows),
        out_shape=[
            jax.ShapeDtypeStruct((ring, out_rows, lanes), BF16),
            jax.ShapeDtypeStruct(d.shape, d.dtype),
            jax.ShapeDtypeStruct((group, EDGE, d.shape[2]), d.dtype),
        ],
        in_specs=[vmem, vmem, hbm],
        out_specs=[hbm, hbm, hbm],
        scratch_shapes=[
            pltpu.VMEM((half, rows, lanes), BF16),
            pltpu.VMEM((half, rows, lanes), BF16),
            pltpu.VMEM((half - 1, rows, lanes), BF16),
            pltpu.VMEM((rows, lanes), BF16),
            pltpu.VMEM((2, in_rows, lanes), BF16),
            pltpu.VMEM((group - 1, 16, lanes), BF16),
            pltpu.VMEM((out_rows, lanes), BF16),
            dma((2,)), dma, dma,
            dma((half - 1,)), dma((half - 1,)),
            dma((2,)), dma((2,)),
            dma((group - 1,)), dma((group - 1,)),
            dma((2, group - 1)), dma((2, group - 1)), dma,
            dma((2, half - 1)), dma((2, half - 1)),
            dma((2, half)), dma((2, half)),
            dma, dma,
        ],
        compiler_params=pltpu.CompilerParams(
            collective_id=cid, has_side_effects=True, vmem_limit_bytes=VMEM_LIMIT
        ),
        cost_estimate=lasting(60),
        name="finish",
    )(g, zf, d)


def start_kernel(
    ring, group, tok, par, doc, w_ref, tok_o, edge_o, par_o, doc_o, w_o,
    mate_s, mate_r, own_s, edge_s, edge_r, relay_s, relay_r, shift_s, shift_r, out_s, out_r, fwd_s, fwd_r,
):
    me = lax.axis_index("ctx")
    mine = lax.axis_index("wa")
    half = ring // 2
    lane = lax.rem(me, 2)
    chip = me // 2
    pair = me + 1 - 2 * lane
    peers = [lax.rem(chip + k, half) * 2 + lane for k in range(1, half)]
    mates = [lax.rem(mine + k, group) for k in range(1, group)]
    barrier = pltpu.get_barrier_semaphore()
    for who in [pair] + peers:
        pl.semaphore_signal(barrier, inc=1, device_id={"ctx": who}, device_id_type=MESH)
    for who in mates:
        pl.semaphore_signal(barrier, inc=1, device_id={"wa": who}, device_id_type=MESH)
    has_next = me < ring - 1
    has_last = me > 0

    @pl.when(has_next)
    def _():
        pl.semaphore_signal(barrier, inc=1, device_id={"ctx": me + 1}, device_id_type=MESH)

    @pl.when(has_last)
    def _():
        pl.semaphore_signal(barrier, inc=1, device_id={"ctx": me - 1}, device_id_type=MESH)

    around = jnp.where(has_next, 1, 0) + jnp.where(has_last, 1, 0)
    pl.semaphore_wait(barrier, half + group - 1 + around)

    edge = tok.at[pl.ds(tok.shape[0] - EDGE, EDGE)]
    to_next = remote(edge, edge_o.at[mine], edge_s, edge_r, {"ctx": me + 1})

    @pl.when(has_next)
    def _():
        to_next.start()

    kind = mine // (group // 2)
    base = 2 * lax.rem(mine, group // 2)
    for h in range(2):
        where = base + h
        send = remote(
            w_ref.at[h], w_o.at[kind, me], shift_s.at[h], shift_r.at[kind], {"wa": where}
        )
        keep = pltpu.make_async_copy(w_ref.at[h], w_o.at[kind, me], shift_r.at[kind])

        @pl.when(where != mine)
        def _():
            send.start()

        @pl.when(where == mine)
        def _():
            keep.start()

    trades = []
    for i, (src, dst) in enumerate(((par, par_o), (doc, doc_o), (tok, tok_o))):
        for k, who in enumerate(mates):
            copy = remote(src, dst.at[mine], mate_s.at[i, k], mate_r.at[i, k], {"wa": who})
            copy.start()
            trades.append(copy)
        keep = pltpu.make_async_copy(src, dst.at[mine], own_s.at[i])
        keep.start()

    @pl.when(has_last)
    def _():
        to_next.wait_recv()
        for k, who in enumerate(mates):
            remote(
                edge_o.at[mine], edge_o.at[mine], relay_s.at[k], relay_r.at[k], {"wa": who}
            ).start()

    sends = []
    for t in range(2):
        block = w_o.at[t, me]
        pltpu.make_async_copy(block, block, shift_r.at[t]).wait()
        for k, who in enumerate(peers):
            copy = remote(block, block, out_s.at[t, k], out_r.at[t, k], {"ctx": who})
            copy.start()
            sends.append(copy)
        copy = remote(block, block, fwd_s.at[t, 0], fwd_r.at[t, 0], {"ctx": pair})
        copy.start()
        sends.append(copy)
    forwards = []
    for t in range(2):
        for k in range(1, half):
            source = lax.rem(chip + half - k, half) * 2 + lane
            block = w_o.at[t, source]
            pltpu.make_async_copy(block, block, out_r.at[t, k - 1]).wait()
            copy = remote(block, block, fwd_s.at[t, k], fwd_r.at[t, k], {"ctx": pair})
            copy.start()
            forwards.append(copy)
    for t in range(2):
        for k in range(half):
            pltpu.make_async_copy(w_o.at[t, me], w_o.at[t, me], fwd_r.at[t, k]).wait()
    for copy in sends + forwards:
        copy.wait_send()
    for h in range(2):

        @pl.when(base + h != mine)
        def _():
            remote(
                w_ref.at[h], w_o.at[kind, me], shift_s.at[h], shift_r.at[kind], {"wa": mine}
            ).wait_send()

    for copy in trades:
        copy.wait()
    for i, (src, dst) in enumerate(((par, par_o), (doc, doc_o), (tok, tok_o))):
        pltpu.make_async_copy(src, dst.at[mine], own_s.at[i]).wait()

    @pl.when(has_next)
    def _():
        to_next.wait_send()

    @pl.when(has_last)
    def _():
        for k, who in enumerate(mates):
            remote(
                edge_o.at[mine], edge_o.at[mine], relay_s.at[k], relay_r.at[k], {"wa": who}
            ).wait()


def start(tok, par, doc, halves, cid):
    ring, group = lax.axis_size("ctx"), lax.axis_size("wa")
    half = ring // 2
    hbm = pl.BlockSpec(memory_space=pl.ANY)
    dma = pltpu.SemaphoreType.DMA
    outs = [(group,) + a.shape for a in (tok, tok[:EDGE], par, doc)] + [(2, ring) + halves.shape[1:]]
    types = [a.dtype for a in (tok, tok, par, doc, halves)]
    return pl.pallas_call(
        functools.partial(start_kernel, ring, group),
        out_shape=[jax.ShapeDtypeStruct(s, t) for s, t in zip(outs, types)],
        in_specs=[hbm] * 4,
        out_specs=[hbm] * 5,
        scratch_shapes=[
            dma((3, group - 1)), dma((3, group - 1)), dma((3,)),
            dma, dma,
            dma((group - 1,)), dma((group - 1,)),
            dma((2,)), dma((2,)),
            dma((2, half - 1)), dma((2, half - 1)),
            dma((2, half)), dma((2, half)),
        ],
        compiler_params=pltpu.CompilerParams(
            collective_id=cid, has_side_effects=True, vmem_limit_bytes=VMEM_LIMIT
        ),
        cost_estimate=lasting(35),
        name="start",
    )(tok, par, doc, halves)


def pick(rows, states, at):
    shape = (rows, states * LANE)
    lower = (lax.broadcasted_iota(jnp.int32, shape, 0) - at) * LANE
    place = lax.broadcasted_iota(jnp.int32, shape, 1)
    return jnp.where((place >= lower) & (place < lower + LANE), 1.0, 0.0)


def spread(rows, states, at):
    return jnp.dot(rows, pick(rows.shape[1], states, at).astype(BF16), preferred_element_type=F32)


def collected(wide_rows, states, columns, at):
    shape = (states * LANE, columns)
    lower = (lax.broadcasted_iota(jnp.int32, shape, 1) - at) * LANE
    place = lax.broadcasted_iota(jnp.int32, shape, 0)
    ones = jnp.where((place >= lower) & (place < lower + LANE), 1.0, 0.0).astype(BF16)
    coarse = wide_rows.astype(BF16)
    rest = (wide_rows - coarse.astype(F32)).astype(BF16)
    return dot_nn(coarse, ones) + dot_nn(rest, ones)


def position_of(shape, axis, steps):
    row = lax.broadcasted_iota(jnp.int32, shape, axis)
    return (row & (SEG - 1)) * steps + (row >> 3)


def permutation(length):
    shape = (length, length)
    at = position_of(shape, 0, length // SEG)
    return jnp.where(at == lax.broadcasted_iota(jnp.int32, shape, 1), 1.0, 0.0).astype(BF16)


def rolled(value, by):
    return pltpu.roll(value, by % SEG, 0)


def lanes_of(g):
    return pl.ds(pl.multiple_of(g * LANE, LANE), LANE)


def rows_of(j):
    return pl.ds(pl.multiple_of(j * SEG, SEG), SEG)


def wide(ref, n, lanes):
    return jnp.broadcast_to(ref[pl.ds(n, 1), lanes], (SEG, LANE))


def state_cols(n):
    return slice(n * LANE, (n + 1) * LANE)


def dot_nt(a, b):
    return lax.dot_general(a, b, (((1,), (1,)), ((), ())), preferred_element_type=F32)


def dot_tn(a, b):
    return lax.dot_general(a, b, (((0,), (0,)), ((), ())), preferred_element_type=F32)


def dot_nn(a, b):
    return jnp.dot(a, b, preferred_element_type=F32)


def rms_scale(values):
    return lax.rsqrt(jnp.mean(values * values, axis=-1, keepdims=True) + EPS)


def norm_grads(values, scale, gain, d_out):
    unit = values * scale
    d_unit = d_out * gain
    d_values = scale * (d_unit - unit * jnp.mean(d_unit * unit, axis=-1, keepdims=True))
    return d_values, d_out * unit


def silu_slope(v):
    s = jax.nn.sigmoid(v)
    return s * (1.0 + v * (1.0 - s))


def seg_of():
    return lax.broadcasted_iota(jnp.int32, (SEG, LANE), 0)


def lag_masks(place, doc_ref, documents, stream, length, taps):
    at = place * length + position_of((length, LANE), 0, length // SEG)
    masks = [None]
    for lag in range(1, taps):
        cut = None
        for d in range(documents):
            begin = doc_ref[stream, 0, d]
            here = (begin > at - lag) & (begin <= at)
            cut = here if cut is None else cut | here
        masks.append(jnp.where(cut, 0.0, 1.0))
    hit = None
    for d in range(documents):
        here = doc_ref[stream, 0, d] == at
        hit = here if hit is None else hit | here
    return masks, jnp.where(hit, CUT, 0.0)


def enter_kernel(
    taps, documents, place_ref, doc_ref, tok, edge, gain, wx, wz, conv, wproj,
    n1_o, ext_o, pre_o, uf_o, u_o, z_o, part_o, cut_o,
):
    length = tok.shape[1]
    steps = length // SEG
    place = place_ref[0]
    gains = gain[0:1]

    def normal(rows):
        return (rows * rms_scale(rows) * gains).astype(BF16)

    n1_o[0, :length] = normal(dot_nn(permutation(length), tok[0]))
    n1_o[0, length:] = normal(jnp.where(place > 0, edge[0].astype(F32), 0.0))
    inner = dot_nn(n1_o[0], wx[0]).astype(BF16).astype(F32)
    z_o[0] = dot_nn(n1_o[0, :length], wz[0]).astype(BF16)
    masks, cut = lag_masks(place, doc_ref, documents, pl.program_id(0), length, taps)
    cut_o[0] = cut
    seg = seg_of()
    behind = taps - 1
    for g in range(inner.shape[1] // LANE):
        cols = slice(g * LANE, (g + 1) * LANE)
        rows, before = inner[:length, cols], inner[length:, cols]
        parts = []
        for i in range(behind):
            j = steps - behind + i
            last = jnp.broadcast_to(before[EDGE - behind + i : EDGE - behind + i + 1], (SEG, LANE))
            parts.append(jnp.where(seg == 0, last, rolled(rows[j * SEG : (j + 1) * SEG], 1)))
        ext = jnp.concatenate(parts + [rows], axis=0)
        ext_o[0, :, cols] = ext
        pre = conv[taps : taps + 1, cols] + conv[0:1, cols] * rows
        for lag in range(1, taps):
            window = ext[(behind - lag) * SEG : (behind - lag) * SEG + length]
            pre = pre + conv[lag : lag + 1, cols] * window * masks[lag]
        pre_o[0, :, cols] = pre
        u = (pre * jax.nn.sigmoid(pre)).astype(BF16)
        u_o[0, :, cols] = u
        uf_o[0, :, cols] = u.astype(F32)
    part_o[0] = dot_nt(u_o[0], wproj[...]).astype(BF16)


def summary_kernel(
    states, b_at, proj_i, wdt, bias, uf, cut, a_ref,
    step_o, sig_o, hx_ref, sx_ref, hd_o, sd_ref, bb, st_s, dr_s, hd_s,
):
    length, width = step_o.shape[1:]
    groups, steps = width // LANE, length // SEG
    proj = proj_i[0]
    bb[...] = spread(proj, states, b_at)
    pre = dot_nn(proj, wdt[...]) + bias[0:1]
    step_size = jnp.maximum(pre, 0.0) + jnp.log1p(jnp.exp(-jnp.abs(pre)))
    step_o[0] = step_size
    sig_o[0] = jax.nn.sigmoid(pre)
    dr_s[...] = step_size * uf[0]
    for g in range(groups):
        cols = slice(g * LANE, (g + 1) * LANE)
        st_s[:, cols] = step_size[:, cols] + cut[0]
    zero = jnp.zeros((SEG, LANE), F32)
    seg = seg_of()

    def group(g, _):
        lanes = lanes_of(g)
        a = [wide(a_ref, n, lanes) for n in range(states)]

        def step(j, carry):
            rows = rows_of(j)
            st = st_s[rows, lanes]
            dr = dr_s[rows, lanes]
            new = [carry[0] + st]
            for n in range(states):
                new.append(jnp.exp(st * a[n]) * carry[n + 1] + bb[rows, state_cols(n)] * dr)
            return tuple(new)

        out = lax.fori_loop(0, steps, step, (zero,) * (states + 1), unroll=8)
        total, h = out[0], list(out[1:])
        for k in (1, 2, 4):
            ok = seg >= k
            for n in range(states):
                h[n] = h[n] + jnp.where(ok, jnp.exp(total * a[n]) * rolled(h[n], k), 0.0)
            total = total + jnp.where(ok, rolled(total, k), 0.0)
        ok = seg >= 1
        sx_ref[0, :, lanes] = jnp.where(ok, rolled(total, 1), 0.0)
        sd_ref[0, :, lanes] = total[SEG - 1 : SEG]
        for n in range(states):
            hx_ref[0, n, :, lanes] = jnp.where(ok, rolled(h[n], 1), 0.0)
            hd_s[pl.ds(n, 1), lanes] = h[n][SEG - 1 : SEG]
        return 0

    lax.fori_loop(0, groups, group, 0)
    hd_o[0] = hd_s[...].astype(BF16)


def entering(e_ref, finals, sums, a_ref, place, ahead):
    ring = finals.shape[0]
    e_ref[...] = jnp.zeros_like(e_ref)

    def one(lap, _):
        c = lap if ahead else ring - 1 - lap
        use = (c < place) if ahead else (c > place)

        @pl.when(use)
        def _():
            e_ref[...] = jnp.exp(sums[c, 0] * a_ref[...]) * e_ref[...] + finals[c, 0].astype(F32)

        return 0

    lax.fori_loop(0, ring, one, 0)


def output_kernel(
    states, b_at, place_ref, proj, step_i, uf, cut, a_ref, hx_ref, sx_ref, finals, sums, z, skip, wout,
    y_o, gated_o, mix_o, e_o, bb, cb, st_s, dr_s,
):
    length, width = step_i.shape[1:]
    groups, steps = width // LANE, length // SEG
    bb[...] = spread(proj[0], states, b_at)
    cb[...] = spread(proj[0], states, b_at + states)
    e_ref = e_o.at[0]
    entering(e_ref, finals, sums, a_ref, place_ref[0], True)
    dr_s[...] = step_i[0] * uf[0]
    for g in range(groups):
        cols = slice(g * LANE, (g + 1) * LANE)
        st_s[:, cols] = step_i[0, :, cols] + cut[0]

    def group(g, _):
        lanes = lanes_of(g)
        a = [wide(a_ref, n, lanes) for n in range(states)]
        sx = sx_ref[0, :, lanes]
        first = tuple(
            jnp.exp(sx * a[n]) * wide(e_ref, n, lanes) + hx_ref[0, n, :, lanes]
            for n in range(states)
        )
        gain = wide(skip, 1, lanes)

        def step(j, h):
            rows = rows_of(j)
            st = st_s[rows, lanes]
            dr = dr_s[rows, lanes]
            new = []
            y = gain * uf[0, rows, lanes]
            for n in range(states):
                state = jnp.exp(st * a[n]) * h[n] + bb[rows, state_cols(n)] * dr
                new.append(state)
                y = y + cb[rows, state_cols(n)] * state
            y_o[0, rows, lanes] = y
            return tuple(new)

        lax.fori_loop(0, steps, step, first, unroll=8)
        return 0

    lax.fori_loop(0, groups, group, 0)
    zf = z[0].astype(F32)
    gated = (y_o[0] * (zf * jax.nn.sigmoid(zf))).astype(BF16)
    gated_o[0] = gated
    mix_o[0] = dot_nn(gated, wout[...]).astype(BF16)


def route_kernel(
    experts, terms, tok, gain, router, route, keep, grad,
    h1_o, n2_o, up_o, cols_o, match_o, out_o, sums_o,
):
    length, width = tok.shape
    shift = permutation(length)
    mix = terms[0].astype(F32)
    for w in range(1, terms.shape[0]):
        mix = mix + terms[w].astype(F32)
    h1 = dot_nn(shift, tok[...]) + mix
    h1_o[...] = h1
    n2 = (h1 * rms_scale(h1) * gain[1:2]).astype(BF16)
    n2_o[...] = n2
    logits = dot_nt(n2, router[...])
    lane = lax.broadcasted_iota(jnp.int32, (length, LANE), 1)
    kind = lax.broadcasted_iota(jnp.int32, (LANE, length), 0)
    named = route[...]
    onehot = jnp.where(kind == named, 1.0, 0.0)
    one = lax.broadcasted_iota(jnp.int32, (length, length), 0)
    two = lax.broadcasted_iota(jnp.int32, (length, length), 1)
    earlier = jnp.where(one < two, 1.0, 0.0).astype(BF16)
    before = dot_nn(onehot.astype(BF16), earlier)
    within = jnp.sum(before * onehot, axis=0, keepdims=True)
    slot = named.astype(F32) * (length // 2) + within
    facts = jnp.where(kind == experts, slot, jnp.where(kind == experts + 1, keep[...].astype(F32), onehot))
    facts = dot_nt(shift, facts.astype(BF16))
    onehot = jnp.where(lane < experts, facts, 0.0)
    slot = jnp.sum(jnp.where(lane == experts, facts, 0.0), axis=1, keepdims=True)
    kept = jnp.sum(jnp.where(lane == experts + 1, facts, 0.0), axis=1, keepdims=True)
    sig = jax.nn.sigmoid(jnp.sum(logits * onehot, axis=1, keepdims=True))
    gates = kept * sig
    cols_o[...] = jnp.where(
        lane == experts, gates, jnp.where(lane == experts + 1, gates * (1.0 - sig), onehot)
    )
    up = dot_nn(shift, grad[...])
    up_o[...] = up
    slots = match_o.shape[1]
    spot = lax.broadcasted_iota(jnp.int32, (length, slots), 1).astype(F32)
    match = jnp.where(slot == spot, 1.0, 0.0).astype(BF16)
    match_o[...] = match
    out_o[0] = dot_tn(match, n2).astype(BF16).reshape(out_o.shape[1:])
    out_o[1] = dot_tn(match, (gates * up).astype(BF16)).astype(BF16).reshape(out_o.shape[1:])
    sums_o[...] = jnp.broadcast_to(jnp.sum(mix * mix, keepdims=True), (SEG, LANE))


def pack_kernel(up, down, out):
    width, units = up.shape
    line = lax.broadcasted_iota(jnp.int32, (units, units), 0)
    same = jnp.where(line == lax.broadcasted_iota(jnp.int32, (units, units), 1), 1.0, 0.0)
    out[:, :width] = dot_nt(same.astype(BF16), up[...]).astype(BF16)
    out[:, width:] = down[...]


def prepare_kernel(
    experts, small, own, wx_t, wdt, wout, conv_w, a_log,
    gain_o, router_o, wx_o, wdt_o, wout_o, conv_o, rows_o, a_o, wide_s,
):
    width = wout.shape[1]
    group = small.shape[0]
    share = width // group
    for w in range(group):
        wide_s[:, w * share : (w + 1) * share] = small[w, :, :share].astype(F32)
    gain_o[0:1] = wide_s[SEG - 2 : SEG - 1]
    gain_o[1:2] = wide_s[SEG - 1 : SEG]
    gain_o[2:] = jnp.zeros((SEG - 2, width), F32)
    rows = wide_s[SEG:]
    row = lax.broadcasted_iota(jnp.int32, rows.shape, 0)
    router_o[...] = jnp.zeros_like(router_o)
    router_o[: 2 * SEG] = jnp.concatenate(
        [jnp.where(row < experts, rows, 0.0), jnp.zeros_like(rows)], axis=0
    ).astype(BF16)
    local = wout.shape[0]
    for out, src in ((wx_o, wx_t), (wdt_o, wdt), (a_o, None)):
        out[...] = jnp.zeros_like(out)
        if src is not None:
            out[: src.shape[0], :local] = src[...]
    a_o[...] = jnp.full(a_o.shape, -1.0, F32)
    a_o[:, :local] = -jnp.exp(a_log[...].astype(F32))
    wout_o[...] = jnp.zeros_like(wout_o)
    wout_o[:local] = wout[...]
    conv_o[...] = jnp.zeros_like(conv_o)
    taps = conv_w.shape[0]
    conv_o[:taps, :local] = conv_w[...].astype(F32)
    mine = own[...].astype(F32)
    rows_o[...] = jnp.zeros_like(rows_o)
    for h in range(2):
        cols = slice(h * share, (h + 1) * share)
        conv_o[taps : taps + 1, cols] = mine[h : h + 1, :share]
        rows_o[0:1, cols] = mine[2 + h : 3 + h, :share]
        rows_o[1:2, cols] = mine[4 + h : 5 + h, :share]


def block_rows(value, c, rows):
    low = c * rows
    have = max(0, min(rows, value.shape[0] - low))
    if have == rows:
        return value[low : low + rows]
    blank = jnp.zeros((rows - have, value.shape[1]), value.dtype)
    return blank if have == 0 else jnp.concatenate([value[low : low + have], blank], axis=0)


def pack_zo_kernel(ring, in_rows, local, n1, d_z, d_mix, gated, out):
    width = n1.shape[1]
    lanes = d_z.shape[1]
    grad_z = dot_tn(n1[...], d_z[...])
    grad_o = dot_tn(gated[...], d_mix[...])
    side = jnp.zeros((grad_o.shape[0], lanes - width // 2), F32)
    first = jnp.concatenate([grad_o[:, : width // 2], side], axis=1)
    second = jnp.concatenate([grad_o[:, width // 2 :], side], axis=1)
    rows = in_rows // 2
    for c in range(ring):
        out[c // 2, c % 2, :, :lanes] = block_rows(grad_z, c, in_rows).astype(BF16)
        both = [block_rows(first[:local], c, rows), block_rows(second[:local], c, rows)]
        out[c // 2, c % 2, :, lanes:] = jnp.concatenate(both, axis=0).astype(BF16)


def pack_rest_kernel(
    ring, in_rows, small_rows, group, experts, ranked, mine_ref, n1, d_x, gx, gdt, ga, a_ref, gconv, bias, skip,
    gain_mix, gains, gain_moe, router, out_sums, mix_sum, out, small_s, wide_s,
):
    lanes = d_x.shape[1]
    width = n1.shape[1]
    share = width // group
    grad_x = dot_tn(n1[...], d_x[...])
    small_s[...] = jnp.zeros_like(small_s)
    at = 0
    grad_a = jnp.sum(ga[...], axis=1) * a_ref[...]
    for part in (gx[...], gdt[:ranked], grad_a, gconv[...]):
        small_s[at : at + part.shape[0]] = part
        at += part.shape[0]
    small_s[at : at + 1] = bias[...]
    small_s[at + SEG : at + SEG + 1] = skip[...]
    wide_s[...] = jnp.zeros_like(wide_s)
    wide_s[0:1] = gain_mix[...] / gains[0:1]
    wide_s[1:2] = gain_moe[...]
    wide_s[2 : 2 + experts] = router[:experts]
    lane = lax.broadcasted_iota(jnp.int32, (group, LANE), 1)
    row = lax.broadcasted_iota(jnp.int32, (group, LANE), 0)
    stats = jnp.where(
        lane == 0, out_sums[0:1], jnp.where(lane == 1, mix_sum[0:1], jnp.where(lane == 2, out_sums[1:2], 0.0))
    )
    stats = jnp.where(row == mine_ref[0], stats, 0.0)
    stats = jnp.concatenate([stats, jnp.zeros((group, lanes - LANE), F32)], axis=1)
    bottom = jnp.zeros((16 - 2 * group, lanes), F32)
    small_each = small_s.shape[0] // ring
    for c in range(ring):
        if c < 2 + experts:
            full = [wide_s[c : c + 1, w * share : (w + 1) * share] for w in range(group)]
            full = jnp.concatenate(full, axis=0)
            full = jnp.concatenate([full, jnp.zeros((group, lanes - share), F32)], axis=1)
        else:
            full = jnp.zeros((group, lanes), F32)
        small = small_s[c * small_each : (c + 1) * small_each]
        blank = jnp.zeros((small_rows - small_each, lanes), F32)
        parts = [block_rows(grad_x, c, in_rows), small]
        if small_rows > small_each:
            parts.append(blank)
        rows = jnp.concatenate(parts + [full, stats, bottom], axis=0)
        out[c // 2, c % 2] = rows.astype(BF16)


def store_in_order(out, rows, order_s):
    steps = rows.shape[0] // SEG
    for g in range(rows.shape[1] // LANE):
        cols = slice(g * LANE, (g + 1) * LANE)
        for j in range(steps):
            order_s[g, pl.ds(j, SEG, stride=steps), :] = rows[j * SEG : (j + 1) * SEG, cols]
        out[:, cols] = order_s[g]


def input_gradient(taps, last_ref, terms, edges, tok, gain, dh, out_o, dn_s, order_s):
    length = tok.shape[0]
    steps = length // SEG
    behind = taps - 1
    total = terms[0, :length].astype(F32)
    edge = edges[0].astype(F32)
    for w in range(1, terms.shape[0]):
        total = total + terms[w, :length].astype(F32)
        edge = edge + edges[w].astype(F32)
    edge = jnp.where(last_ref[0] > 0, 0.0, edge)
    dn_s[...] = total
    seg = lax.broadcasted_iota(jnp.int32, (SEG, tok.shape[1]), 0)
    for i in range(behind):
        j = pl.ds((steps - behind + i) * SEG, SEG)
        row = EDGE - behind + i
        came = jnp.broadcast_to(edge[row : row + 1], seg.shape)
        dn_s[j, :] += jnp.where(seg == SEG - 1, came, 0.0)
    x = dot_nn(permutation(length), tok[...])
    d_x, _ = norm_grads(x, rms_scale(x), gain[0:1], dn_s[...])
    result = dh[...] + d_x
    store_in_order(out_o, result, order_s)


def unpack_kernel(
    ring, group, in_rows, small_rows, experts, states, ranked, taps, denom, mine_ref, done, up_down,
    last_ref, terms, edges, tok, gain, dh, res,
    in_o, out_o, up_o, down_o, taps_o, wx_o, wdt_o, a_o, vec_o, stat_o, grad_o, layer_o,
    small_s, full_s, dn_s, order_s,
):
    c = pl.program_id(0)
    width = in_o.shape[1]

    @pl.when(c == 1)
    def _():
        store_in_order(layer_o, res[...], order_s)
        input_gradient(taps, last_ref, terms, edges, tok, gain, dh, grad_o, dn_s, order_s)

    local = width // 2
    small_each = small_s.shape[0] // ring
    base = 2 * in_rows

    @pl.when(c == 0)
    def _():
        line = lax.broadcasted_iota(jnp.int32, (width, width), 0)
        same = jnp.where(line == lax.broadcasted_iota(jnp.int32, (width, width), 1), 1.0, 0.0)
        up_o[...] = dot_nt(same.astype(BF16), up_down[:, :width])
        down_o[...] = up_down[:, width:].astype(F32)
        full_s[...] = jnp.zeros_like(full_s)

    @pl.when(c * in_rows < width)
    def _():
        rows = done[0, :base, :].astype(F32)
        in_o[...] = jnp.concatenate([rows[:in_rows, :local], rows[in_rows:, :local]], axis=1)
        low = base + small_rows + 16
        rows = done[0, low : low + in_rows, :].astype(F32)
        half = in_rows // 2
        out_o[...] = jnp.concatenate([rows[:half, :local], rows[half:, :local]], axis=1)

    small = done[0, base : base + small_rows, :].astype(F32)
    small_s[pl.ds(pl.multiple_of(c * small_each, SEG), small_each), :] = small[:small_each]
    tile = done[0, base + small_rows : base + small_rows + 16, :].astype(F32)
    row = lax.broadcasted_iota(jnp.int32, tile.shape, 0)
    own = jnp.sum(jnp.where(row == mine_ref[0], tile, 0.0), axis=0, keepdims=True)
    spot = lax.broadcasted_iota(jnp.int32, full_s.shape, 0)
    full_s[...] += jnp.where(spot == c, own, 0.0)

    @pl.when(c == 0)
    def _():
        sums = jnp.sum(jnp.where(row == group + mine_ref[0], tile, 0.0), axis=0, keepdims=True)
        stat_o[...] = jnp.sqrt(sums[:, :LANE] / denom)

    @pl.when(c == ring - 1)
    def _():
        at = 0
        wx_o[...] = small_s[: wx_o.shape[0], :local]
        at += up_to(wx_o.shape[0], LANE)
        wdt_o[...] = small_s[at : at + ranked, :local]
        at += ranked
        a_o[...] = small_s[at : at + states, :local]
        at += states
        taps_o[...] = small_s[at : at + taps, :local]
        vec_o[:SEG] = full_s[...]
        vec_o[SEG : SEG + 1] = small_s[at + taps : at + taps + 1]
        at += SEG
        vec_o[SEG + 1 : SEG + 2] = small_s[at : at + 1]
        vec_o[SEG + 2 : SEG + 3] = small_s[at + SEG : at + SEG + 1]


def middle_kernel(
    experts, group, chunks,
    mix_ref, tok, gain, router, route, keep, grad, w_ref,
    g_ref, layer_o, dh_o, dmix_o, router_o, gain_o, sums_o, mix_o,
    mix_s, h1_s, n2_s, up_s, cols_s, match_s, x_ref, r_ref,
    got, w_s, g_s, act_s, slope_s, pre_s, acc, out_s,
    w_sem, g_sem, s0, r0, own0, s1, r1, own1, s2, r2, own2,
):
    mine, mates = mates_of(group)
    count, width = x_ref.shape[2:]
    slots = group * count
    block = w_ref.shape[0] // chunks

    def load(t):
        at = pl.ds(pl.multiple_of(lax.rem(t, chunks) * block, block), block)
        slot = lax.rem(t, 2)
        return pltpu.make_async_copy(w_ref.at[at], w_s.at[slot], w_sem.at[slot])

    load(0).start()
    greet("wa", group)
    terms = []
    for k, who in enumerate(mates):
        copy = remote(mix_ref.at[who], mix_s.at[mine], s0.at[k], r0.at[k], {"wa": who})
        copy.start()
        terms.append(copy)
    kept = pltpu.make_async_copy(mix_ref.at[mine], mix_s.at[mine], own0)
    kept.start()
    for copy in terms + [kept]:
        copy.wait()
    route_kernel(
        experts, mix_s, tok, gain, router, route, keep, grad,
        h1_s, n2_s, up_s, cols_s, match_s, x_ref, mix_o,
    )
    sent = []
    for h in range(2):
        for k, who in enumerate(mates):
            copy = remote(x_ref.at[h, who], got.at[h, mine], s1.at[h, k], r1.at[h, k], {"wa": who})
            copy.start()
            sent.append(copy)
        pltpu.make_async_copy(x_ref.at[h, mine], got.at[h, mine], own1.at[h]).start()

    def arrived(h):
        pltpu.make_async_copy(x_ref.at[h, mine], got.at[h, mine], own1.at[h]).wait()
        for copy in sent[h * len(mates) : (h + 1) * len(mates)]:
            copy.wait_recv()
        return got[h].reshape(slots, width)

    def chunk(i):
        return pl.ds(pl.multiple_of(i * block, block), block)

    def returned(h):
        out_s[h] = acc[...].astype(BF16).reshape(group, count, width)
        for k, who in enumerate(mates):
            copy = remote(out_s.at[h, who], r_ref.at[h, mine], s2.at[h, k], r2.at[h, k], {"wa": who})
            copy.start()
            sent.append(copy)
        pltpu.make_async_copy(out_s.at[h, mine], r_ref.at[h, mine], own2.at[h]).start()

    rows = arrived(0)
    acc[...] = jnp.zeros_like(acc)

    def forward(i, _):
        load(i).wait()
        load(i + 1).start()
        w = w_s.at[lax.rem(i, 2)]
        hidden = dot_nt(w[:, :width], rows)
        c = 0.7978845608
        t = jnp.tanh(c * (hidden + 0.044715 * hidden * hidden * hidden))
        act = (0.5 * hidden * (1.0 + t)).astype(BF16)
        act_s[chunk(i), :] = act
        slope_s[chunk(i), :] = 0.5 * (1.0 + t) + 0.5 * hidden * (1.0 - t * t) * c * (
            1.0 + 3.0 * 0.044715 * hidden * hidden
        )
        acc[...] += dot_tn(act, w[:, width:])
        return 0

    lax.fori_loop(0, chunks, forward, 0)
    returned(0)
    d_out = arrived(1)
    acc[...] = jnp.zeros_like(acc)

    def backward(i, _):
        load(chunks + i).wait()

        @pl.when(i < chunks - 1)
        def _():
            load(chunks + i + 1).start()

        w = w_s.at[lax.rem(chunks + i, 2)]
        d_pre = (dot_nt(w[:, width:], d_out) * slope_s[chunk(i), :]).astype(BF16)
        pre_s[chunk(i), :] = d_pre
        acc[...] += dot_tn(d_pre, w[:, :width])
        return 0

    lax.fori_loop(0, chunks, backward, 0)
    returned(1)

    def store(i):
        slot = lax.rem(i, 2)
        return pltpu.make_async_copy(g_s.at[slot], g_ref.at[chunk(i)], g_sem.at[slot])

    def gradients(i, _):
        @pl.when(i >= 2)
        def _():
            store(i - 2).wait()

        g = g_s.at[lax.rem(i, 2)]
        g[:, :width] = dot_nn(pre_s[chunk(i), :], got[0].reshape(slots, width)).astype(BF16)
        g[:, width:] = dot_nn(act_s[chunk(i), :], got[1].reshape(slots, width)).astype(BF16)
        store(i).start()
        return 0

    lax.fori_loop(0, chunks, gradients, 0)
    store(chunks - 2).wait()
    store(chunks - 1).wait()
    for h in range(2):
        pltpu.make_async_copy(out_s.at[h, mine], r_ref.at[h, mine], own2.at[h]).wait()
    for copy in sent[: 2 * len(mates)]:
        copy.wait_send()
    for copy in sent[2 * len(mates) :]:
        copy.wait()
    combine_kernel(
        experts, r_ref, match_s, h1_s, n2_s, up_s, cols_s, gain, router,
        layer_o, dh_o, dmix_o, router_o, gain_o, sums_o,
    )


def middle(experts, mix_part, tok, gains, router, route, keep, grad, w, chunks, cid, us):
    group = lax.axis_size("wa")
    units = w.shape[0]
    length, width = tok.shape
    slots = experts * (length // 2)
    block = units // chunks
    dma = pltpu.SemaphoreType.DMA
    hbm = pl.BlockSpec(memory_space=pltpu.HBM)
    vmem = pl.BlockSpec(memory_space=pltpu.VMEM)
    two = dma((2, group - 1))
    one = dma((group - 1,))
    rows = pltpu.VMEM((2, group, slots // group, width), BF16)
    shapes = [
        (w.shape, BF16), ((length, width), F32), ((length, width), F32), ((length, width), BF16),
        ((LANE, width), F32), ((1, width), F32), ((SEG, LANE), F32), ((SEG, LANE), F32),
    ]
    return pl.pallas_call(
        functools.partial(middle_kernel, experts, group, chunks),
        out_shape=[jax.ShapeDtypeStruct(shape, dtype) for shape, dtype in shapes],
        in_specs=[vmem] * 7 + [hbm],
        out_specs=[hbm] + [vmem] * 7,
        scratch_shapes=[
            pltpu.VMEM(mix_part.shape, BF16),
            pltpu.VMEM((length, width), F32),
            pltpu.VMEM((length, width), BF16),
            pltpu.VMEM((length, width), F32),
            pltpu.VMEM((length, LANE), F32),
            pltpu.VMEM((length, slots), BF16),
            rows, rows, rows,
            pltpu.VMEM((2, block, 2 * width), BF16),
            pltpu.VMEM((2, block, 2 * width), BF16),
            pltpu.VMEM((units, slots), BF16),
            pltpu.VMEM((units, slots), F32),
            pltpu.VMEM((units, slots), BF16),
            pltpu.VMEM((slots, width), F32),
            rows,
            dma((2,)), dma((2,)),
            one, one, dma, two, two, dma((2,)), two, two, dma((2,)),
        ],
        compiler_params=pltpu.CompilerParams(
            collective_id=cid, has_side_effects=True, vmem_limit_bytes=VMEM_LIMIT + 20 * 2**20
        ),
        cost_estimate=lasting(us),
        name="middle",
    )(mix_part, tok, gains, router, route, keep, grad, w)


def combine_kernel(
    experts, back, match, h1_i, n2, up_i, cols, gain, router,
    out_o, dh_o, dmix_o, router_o, gain_o, sums_o,
):
    length, width = h1_i.shape
    h1, up = h1_i[...], up_i[...]
    lane = lax.broadcasted_iota(jnp.int32, (length, LANE), 1)
    facts = cols[...]

    def column(at):
        return jnp.sum(jnp.where(lane == at, facts, 0.0), axis=1, keepdims=True)

    gates, slope = column(experts), column(experts + 1)
    onehot = jnp.where(lane < experts, facts, 0.0)
    slots = match.shape[1]
    rows = dot_nn(match[...], back[0].reshape(slots, width))
    moe = gates * rows
    result = h1 + moe
    out_o[...] = result
    d_gate = jnp.sum(rows * up, axis=1, keepdims=True)
    d_logits = (onehot * (d_gate * slope)).astype(BF16)
    router_o[...] = dot_tn(d_logits, n2[...])
    d_n2 = dot_nn(match[...], back[1].reshape(slots, width)) + dot_nn(d_logits, router[...])
    d_norm, terms = norm_grads(h1, rms_scale(h1), gain[1:2], d_n2)
    gain_o[...] = jnp.sum(terms, axis=0, keepdims=True)
    d_h1 = up + d_norm
    dh_o[...] = d_h1
    dmix_o[...] = d_h1.astype(BF16)
    sums_o[0:1] = jnp.broadcast_to(jnp.sum(result * result, keepdims=True), (1, LANE))
    sums_o[1:2] = jnp.broadcast_to(jnp.sum(moe * moe, keepdims=True), (1, LANE))


def gate_back_kernel(
    states, c_at, d_mix, wout, y, z, uf, proj, step_i, cut, a_ref,
    dy_o, dz_o, skip_o, fx_ref, tx_ref, fd_o, cb, st_s, fd_s,
):
    length, width = step_i.shape[1:]
    groups, steps = width // LANE, length // SEG
    d_gated = dot_nt(d_mix[0], wout[...])
    zf = z[0].astype(F32)
    dy = d_gated * (zf * jax.nn.sigmoid(zf))
    dy_o[0] = dy
    dz_o[0, :length] = (d_gated * y[0] * silu_slope(zf)).astype(BF16)
    dz_o[0, length:] = jnp.zeros((EDGE, width), BF16)

    @pl.when(pl.program_id(0) == 0)
    def _():
        skip_o[...] = jnp.zeros_like(skip_o)

    skip_o[...] += jnp.sum(dy * uf[0], axis=0, keepdims=True)
    cb[...] = spread(proj[0], states, c_at)
    for g in range(groups):
        cols = slice(g * LANE, (g + 1) * LANE)
        st_s[:, cols] = step_i[0, :, cols] + cut[0]
    zero = jnp.zeros((SEG, LANE), F32)
    seg = seg_of()

    def group(g, _):
        lanes = lanes_of(g)
        a = [wide(a_ref, n, lanes) for n in range(states)]

        def step(lap, carry):
            rows = rows_of(steps - 1 - lap)
            st = st_s[rows, lanes]
            d = dy_o[0, rows, lanes]
            new = [carry[0] + st]
            for n in range(states):
                new.append(jnp.exp(st * a[n]) * (carry[n + 1] + cb[rows, state_cols(n)] * d))
            return tuple(new)

        out = lax.fori_loop(0, steps, step, (zero,) * (states + 1), unroll=8)
        total, f = out[0], list(out[1:])
        for k in (1, 2, 4):
            ok = seg < SEG - k
            for n in range(states):
                f[n] = f[n] + jnp.where(ok, jnp.exp(total * a[n]) * rolled(f[n], -k), 0.0)
            total = total + jnp.where(ok, rolled(total, -k), 0.0)
        ok = seg < SEG - 1
        tx_ref[0, :, lanes] = jnp.where(ok, rolled(total, -1), 0.0)
        for n in range(states):
            fx_ref[0, n, :, lanes] = jnp.where(ok, rolled(f[n], -1), 0.0)
            fd_s[pl.ds(n, 1), lanes] = f[n][0:1]
        return 0

    lax.fori_loop(0, groups, group, 0)
    fd_o[0] = fd_s[...].astype(BF16)


def scan_back_kernel(
    states, b_at, proj, step_i, sig, uf, cut, dy_i, a_ref, skip, wdt, hx_ref, sx_ref, e_i,
    fx_ref, tx_ref, finals, sums, g_ref, p_ref,
    part_o, du_o, dt_o, bias_o, ga_ref, g_o,
    bb, cb, dec, pri, accb, accc, st_s, dr_s, ds_s, out_s,
    from_pair, kept, came, load, ctx_s, ctx_r,
):
    ring = finals.shape[0]
    half = ring // 2
    _, chip, lane, _, peers = neighbours(ring)
    own_half = pltpu.make_async_copy(g_ref.at[:, lane], kept, load.at[0])
    pair_half = pltpu.make_async_copy(p_ref, from_pair, load.at[1])
    targets = [lax.rem(chip + k, half) for k in range(1, half)]
    scattered = [
        remote(kept.at[to], came.at[k], ctx_s.at[k], ctx_r.at[k], {"ctx": who})
        for k, (to, who) in enumerate(zip(targets, peers))
    ]
    at = pl.program_id(0)

    @pl.when(at == 0)
    def _():
        own_half.start()
        pair_half.start()
        barrier = pltpu.get_barrier_semaphore()
        for who in peers:
            hello(barrier, "ctx", who)
        pl.semaphore_wait(barrier, half - 1)
        own_half.wait()
        pair_half.wait()
        for to, copy in zip(targets, scattered):
            add_rows(kept.at[to], [kept.at[to], from_pair.at[to]], kept.shape[1])
            copy.start()
        add_rows(kept.at[chip], [kept.at[chip], from_pair.at[chip]], kept.shape[1])

    @pl.when(at == pl.num_programs(0) - 1)
    def _():
        for copy in scattered:
            copy.wait()
        add_rows(g_o, [kept.at[chip]] + [came.at[k] for k in range(half - 1)], kept.shape[1])

    length, width = step_i.shape[1:]
    groups, steps = width // LANE, length // SEG
    bb[...] = spread(proj[0], states, b_at)
    cb[...] = spread(proj[0], states, b_at + states)
    accb[...] = jnp.zeros_like(accb)
    accc[...] = jnp.zeros_like(accc)
    entering(out_s, finals, sums, a_ref, lax.axis_index("ctx"), False)
    e_ref = e_i.at[0]
    dr_s[...] = step_i[0] * uf[0]
    for g in range(groups):
        cols = slice(g * LANE, (g + 1) * LANE)
        st_s[:, cols] = step_i[0, :, cols] + cut[0]

    @pl.when(pl.program_id(0) == 0)
    def _():
        ga_ref[...] = jnp.zeros_like(ga_ref)
        dt_o[...] = jnp.zeros_like(dt_o)
        bias_o[...] = jnp.zeros_like(bias_o)

    def group(g, _):
        lanes = lanes_of(g)
        a = [wide(a_ref, n, lanes) for n in range(states)]
        sx = sx_ref[0, :, lanes]
        first = tuple(
            jnp.exp(sx * a[n]) * wide(e_ref, n, lanes) + hx_ref[0, n, :, lanes]
            for n in range(states)
        )

        def ahead(j, h):
            rows = rows_of(j)
            st = st_s[rows, lanes]
            dr = dr_s[rows, lanes]
            new = []
            for n in range(states):
                decay = jnp.exp(st * a[n])
                dec[rows, state_cols(n)] = decay
                pri[rows, state_cols(n)] = h[n]
                new.append(decay * h[n] + bb[rows, state_cols(n)] * dr)
            return tuple(new)

        last = lax.fori_loop(0, steps, ahead, first, unroll=8)
        end = rows_of(steps)
        for n in range(states):
            pri[end, state_cols(n)] = last[n]
        tx = tx_ref[0, :, lanes]
        flow = tuple(
            jnp.exp(tx * a[n]) * wide(out_s, n, lanes) + fx_ref[0, n, :, lanes]
            for n in range(states)
        )
        gain = wide(skip, 1, lanes)

        def back(lap, f):
            j = steps - 1 - lap
            rows = rows_of(j)
            after = rows_of(j + 1)
            st = step_i[0, rows, lanes]
            dr = dr_s[rows, lanes]
            dy = dy_i[0, rows, lanes]
            new = []
            d_step = None
            d_drive = None
            for n in range(states):
                cols = state_cols(n)
                d = f[n] + cb[rows, cols] * dy
                accc[rows, cols] += pri[after, cols] * dy
                accb[rows, cols] += d * dr
                flowing = dec[rows, cols] * d
                new.append(flowing)
                d_log = flowing * pri[rows, cols]
                ga_ref[n, :, lanes] += d_log * st
                part = d_log * a[n]
                d_step = part if d_step is None else d_step + part
                part = d * bb[rows, cols]
                d_drive = part if d_drive is None else d_drive + part
            ds_s[rows, lanes] = (d_step + d_drive * uf[0, rows, lanes]) * sig[0, rows, lanes]
            du_o[0, rows, lanes] = d_drive * st + dy * gain
            return tuple(new)

        lax.fori_loop(0, steps, back, flow, unroll=8)
        return 0

    lax.fori_loop(0, groups, group, 0)
    d_pre = ds_s[...]
    bias_o[...] += jnp.sum(d_pre, axis=0, keepdims=True)
    d_pre = d_pre.astype(BF16)
    dt_o[...] += dot_tn(proj[0], d_pre)
    columns = part_o.shape[2]
    part = dot_nt(d_pre, wdt[...])
    part = part + collected(accb[...], states, columns, b_at)
    part = part + collected(accc[...], states, columns, b_at + states)
    part_o[0] = part.astype(BF16)


def conv_back_kernel(
    taps, documents, place_ref, doc_ref, proj_i, wproj, du, pre, ext, u, conv, dz, wx, wz, n1,
    dx_o, dn_o, gconv_o, gx_o, gain_o, dext,
):
    length, width = du.shape[1:]
    steps = length // SEG
    behind = taps - 1

    @pl.when(pl.program_id(0) == 0)
    def _():
        gconv_o[...] = jnp.zeros_like(gconv_o)
        gx_o[...] = jnp.zeros_like(gx_o)
        gain_o[...] = jnp.zeros_like(gain_o)

    proj = proj_i[0]
    gx_o[...] += dot_tn(proj, u[0])
    d_u = dot_nn(proj, wproj[...]) + du[0]
    masks, _ = lag_masks(place_ref[0], doc_ref, documents, pl.program_id(0), length, taps)
    seg = seg_of()
    row = lax.broadcasted_iota(jnp.int32, (EDGE, LANE), 0)
    for g in range(width // LANE):
        cols = slice(g * LANE, (g + 1) * LANE)
        d = d_u[:, cols] * silu_slope(pre[0, :, cols])
        gconv_o[taps : taps + 1, cols] += jnp.sum(d, axis=0, keepdims=True)
        dext[...] = jnp.zeros_like(dext)
        for lag in range(taps):
            weighted = d if lag == 0 else d * masks[lag]
            at = pl.ds((behind - lag) * SEG, length)
            gconv_o[lag : lag + 1, cols] += jnp.sum(weighted * ext[0, at, cols], axis=0, keepdims=True)
            dext[at, :] += weighted * conv[lag : lag + 1, cols]
        before = jnp.zeros((EDGE, LANE), F32)
        for i in range(behind):
            head = dext[i * SEG : (i + 1) * SEG]
            j = pl.ds((steps + i) * SEG, SEG)
            dext[j, :] += jnp.where(seg < SEG - 1, rolled(head, -1), 0.0)
            first = jnp.broadcast_to(head[0:1], (EDGE, LANE))
            before = before + jnp.where(row == EDGE - behind + i, first, 0.0)
        dx_o[0, :length, cols] = dext[behind * SEG :].astype(BF16)
        dx_o[0, length:, cols] = before.astype(BF16)
    d_n1 = dot_nt(dx_o[0], wx[0]) + dot_nt(dz[0], wz[0])
    gain_o[...] += jnp.sum(d_n1 * n1[0].astype(F32), axis=0, keepdims=True)
    dn_o[0] = d_n1.astype(BF16)


SMEM = "smem"
ANY = "any"


def by_stream(shape, at=0):
    block = tuple(1 if i == at else n for i, n in enumerate(shape))
    rank = len(shape)

    def index(s):
        return tuple(s if i == at else 0 for i in range(rank))

    return pl.BlockSpec(block, index)


def whole(shape):
    return pl.BlockSpec(shape, lambda s: (0,) * len(shape))


def call(kernel, name, grid, args, outs, scratch, us, cid=None, limit=VMEM_LIMIT):
    arrays, specs = [], []
    for array, at in args:
        arrays.append(array)
        if at == SMEM:
            specs.append(pl.BlockSpec(memory_space=pltpu.SMEM))
        elif at == ANY:
            specs.append(pl.BlockSpec(memory_space=pl.ANY))
        elif callable(at):
            specs.append(at(array.shape))
        else:
            specs.append(whole(array.shape) if at is None else by_stream(array.shape, at))
    out_specs = []
    for shape, _, at in outs:
        if callable(at):
            out_specs.append(at(shape))
        else:
            out_specs.append(whole(shape) if at is None else by_stream(shape, at))
    return pl.pallas_call(
        kernel,
        grid=(grid,),
        out_shape=[jax.ShapeDtypeStruct(shape, dtype) for shape, dtype, _ in outs],
        in_specs=specs,
        out_specs=out_specs,
        scratch_shapes=scratch,
        compiler_params=pltpu.CompilerParams(
            vmem_limit_bytes=limit, collective_id=cid, has_side_effects=cid is not None
        ),
        cost_estimate=lasting(us),
        name=name,
    )(*arrays)


def padded_to(array, width, axis):
    pads = [(0, 0)] * array.ndim
    pads[axis] = (0, width - array.shape[axis])
    return jnp.pad(array, pads)


def up_to(n, multiple):
    return -(-n // multiple) * multiple


def body(
    tokens, out_grad, doc_starts, routes, keep_mask, norm_mix, w_in, conv_w, conv_b, w_x, w_dt,
    dt_bias, a_log, d_skip, w_out, norm_moe, w_router, w_up, w_down,
):
    group = lax.axis_size("wa")
    ring = lax.axis_size("ctx")
    mine = lax.axis_index("wa")
    place = lax.axis_index("ctx")
    length, width = tokens.shape[1:]
    taps, local = conv_w.shape
    states = a_log.shape[0]
    ranked = w_dt.shape[0]
    experts = w_router.shape[1]
    padded = up_to(local, LANE)
    columns = up_to(w_x.shape[1], LANE)
    steps = length // SEG
    rows = length + EDGE
    slots = experts * (length // 2)
    share = norm_mix.shape[0]
    order_vmem = pltpu.VMEM((width // LANE, length, LANE), F32)
    place_s = place.astype(jnp.int32).reshape(1)
    mine_s = mine.astype(jnp.int32).reshape(1)
    last_s = (place == ring - 1).astype(jnp.int32).reshape(1)
    f32_vmem = lambda *shape: pltpu.VMEM(shape, F32)

    (own_experts,) = call(
        pack_kernel, "pack", 1, [(w_up[0], None), (w_down[0], None)],
        [((w_down.shape[1], 2 * width), BF16, None)], [], 3, None, LARGE_LIMIT,
    )
    expert_w = lax.all_gather(own_experts, "ctx", axis=0, tiled=True)

    in_rows = up_to(-(-width // ring), 16)
    blank = ring * in_rows - width
    part_in = jnp.pad(w_in, ((0, blank), (0, 0))) if blank else w_in
    part_in = lax.dynamic_slice_in_dim(part_in, place * in_rows, in_rows, 0)
    halves = jnp.stack([part_in[:, :local], part_in[:, local:]], axis=0)
    halves = jnp.pad(halves, ((0, 0), (0, 0), (0, padded - local)))
    small = jnp.concatenate([conv_b, dt_bias, d_skip, norm_mix, norm_moe], axis=0).reshape(SEG, share)
    small = jnp.concatenate([small, jnp.pad(w_router.T, ((0, SEG - experts), (0, 0)))], axis=0)
    small = padded_to(small, up_to(share, LANE), 1)
    documents = doc_starts.shape[1]
    doc_tile = jnp.pad(doc_starts, ((0, SEG - 1), (0, LANE - documents)))
    all_rows, all_edges, smalls, docs, w_blocks = start(tokens[0], small, doc_tile, halves, 1)
    proj_in = w_blocks.reshape(2, ring * in_rows, padded)[:, :width]
    of_x = lambda shape: pl.BlockSpec((1,) + shape[1:], lambda i: (0, 0, 0))
    of_z = lambda shape: pl.BlockSpec((1,) + shape[1:], lambda i: (1, 0, 0))
    par = (SEG, padded)
    gains, router, wproj, wdt, wout, conv, vectors, a_mat = call(
        functools.partial(prepare_kernel, experts), "prepare", 1,
        [(smalls, None), (small, None), (w_x.T, None), (w_dt, None), (w_out, None), (conv_w, None),
         (a_log, None)],
        [((SEG, width), F32, None), ((LANE, width), BF16, None), ((columns, padded), BF16, None),
         ((columns, padded), BF16, None), ((padded, width), BF16, None), (par, F32, None),
         (par, F32, None), ((states, padded), F32, None)],
        [f32_vmem(2 * SEG, width)], 3,
    )

    vec = (group, length, padded)
    n1, ext, pre_conv, u_f, u, z, part, cut = call(
        functools.partial(enter_kernel, taps, documents), "enter", group,
        [(place_s, SMEM), (docs, SMEM), (all_rows, 0), (all_edges, 0), (gains, None),
         (proj_in, of_x), (proj_in, of_z), (conv, None), (wproj, None)],
        [((group, rows, width), BF16, 0), ((group, (taps - 1) * SEG + length, padded), F32, 0),
         (vec, F32, 0), (vec, F32, 0), (vec, BF16, 0), (vec, BF16, 0),
         ((group, length, columns), BF16, 0), ((group, length, LANE), F32, 0)],
        [], 8,
    )
    projected = sum_all(part, 2, 11)
    seg_states = (group, states, SEG, padded)
    seg_sums = (group, SEG, padded)
    dev_states = (group, states, padded)
    dev_sums = (group, 1, padded)
    spread_vmem = f32_vmem(length, states * LANE)
    lane_vmem = f32_vmem(length, padded)
    state_vmem = f32_vmem(states, padded)
    step_size, sig, h_in, s_in, h_dev, s_dev = call(
        functools.partial(summary_kernel, states, ranked), "scan_summary", group,
        [(projected, 0), (wdt, None), (vectors, None), (u_f, 0), (cut, 0), (a_mat, None)],
        [(vec, F32, 0), (vec, F32, 0), (seg_states, F32, 0),
         (seg_sums, F32, 0), (dev_states, BF16, 0), (dev_sums, F32, 0)],
        [spread_vmem, lane_vmem, lane_vmem, state_vmem], 10,
    )
    all_h, all_s = carry([h_dev, s_dev], 3, 10)
    y_full, gated, mix_part, e_in = call(
        functools.partial(output_kernel, states, ranked), "scan_output", group,
        [(place_s, SMEM), (projected, 0), (step_size, 0), (u_f, 0), (cut, 0), (a_mat, None), (h_in, 0),
         (s_in, 0), (all_h, 1), (all_s, 1), (z, 0), (vectors, None), (wout, None)],
        [(vec, F32, 0), (vec, BF16, 0), ((group, length, width), BF16, 0), (dev_states, F32, 0)],
        [spread_vmem, spread_vmem, lane_vmem, lane_vmem], 13,
    )

    row_f = (length, width)
    grad_experts, result, d_h1, d_mix_own, grad_router, grad_gain_moe, out_sums, mix_sum = middle(
        experts, mix_part, tokens[0], gains, router, routes[0].T, keep_mask, out_grad[0], expert_w, 8, 5, 85
    )
    share_experts = lax.psum_scatter(grad_experts, "ctx", scatter_dimension=0, tiled=True)
    (d_mix,) = gather_all([d_mix_own], "wa", 7, 28)

    d_y, d_z, grad_skip, f_in, t_in, f_dev = call(
        functools.partial(gate_back_kernel, states, ranked + states), "gate_back", group,
        [(d_mix, 0), (wout, None), (y_full, 0), (z, 0), (u_f, 0), (projected, 0), (step_size, 0),
         (cut, 0), (a_mat, None)],
        [(vec, F32, 0), ((group, rows, padded), BF16, 0), ((1, padded), F32, None),
         (seg_states, F32, 0), (seg_sums, F32, 0), (dev_states, BF16, 0)],
        [spread_vmem, lane_vmem, state_vmem], 11,
    )
    flat_n1 = n1.reshape(group * rows, width)
    zo_shape = (ring // 2, 2, in_rows, 2 * padded)
    (grad_zo,) = call(
        functools.partial(pack_zo_kernel, ring, in_rows, local), "pack_zo", 1,
        [(flat_n1, None), (d_z.reshape(group * rows, padded), None),
         (d_mix.reshape(group * length, width), None), (gated.reshape(group * length, padded), None)],
        [(zo_shape, BF16, None)], [], 5,
    )
    all_f, pair_zo = carry([f_dev], 8, 10, grad_zo)
    zo_half = pltpu.VMEM((ring // 2, in_rows, 2 * padded), BF16)
    dma = pltpu.SemaphoreType.DMA
    d_part, d_u, grad_dt, grad_step_bias, grad_a, chunk_zo = call(
        functools.partial(scan_back_kernel, states, ranked), "scan_back", group,
        [(projected, 0), (step_size, 0), (sig, 0), (u_f, 0), (cut, 0), (d_y, 0),
         (a_mat, None), (vectors, None), (wdt, None), (h_in, 0), (s_in, 0), (e_in, 0), (f_in, 0),
         (t_in, 0), (all_f, 1), (all_s, 1), (grad_zo, ANY), (pair_zo, ANY)],
        [((group, length, columns), BF16, 0), (vec, F32, 0), ((columns, padded), F32, None),
         ((1, padded), F32, None), ((states, SEG, padded), F32, None), ((in_rows, 2 * padded), BF16, None)],
        [spread_vmem, spread_vmem, spread_vmem, f32_vmem(length + SEG, states * LANE), spread_vmem,
         spread_vmem, lane_vmem, lane_vmem, lane_vmem, state_vmem,
         zo_half, zo_half, pltpu.VMEM((ring // 2 - 1, in_rows, 2 * padded), BF16),
         dma((2,)), dma((ring // 2 - 1,)), dma((ring // 2 - 1,))], 34, 12,
    )
    d_projected = sum_all(d_part, 9, 11)
    d_x, d_n1_part, grad_conv, grad_x, gain_terms = call(
        functools.partial(conv_back_kernel, taps, documents), "conv_back", group,
        [(place_s, SMEM), (docs, SMEM), (d_projected, 0), (wproj, None), (d_u, 0), (pre_conv, 0),
         (ext, 0), (u, 0), (conv, None), (d_z, 0), (proj_in, of_x), (proj_in, of_z), (n1, 0)],
        [((group, rows, padded), BF16, 0), ((group, rows, width), BF16, 0),
         ((SEG, padded), F32, None), ((columns, padded), F32, None), ((1, width), F32, None)],
        [f32_vmem((taps - 1) * SEG + length, LANE)], 10,
    )
    small_all = columns + up_to(ranked, SEG) + states + 3 * SEG
    small_each = up_to(-(-small_all // ring), SEG)
    small_rows = up_to(small_each, 16)
    (packed,) = call(
        functools.partial(pack_rest_kernel, ring, in_rows, small_rows, group, experts, ranked),
        "pack_rest", 1,
        [(mine_s, SMEM), (flat_n1, None), (d_x.reshape(group * rows, padded), None), (grad_x, None),
         (grad_dt, None), (grad_a, None), (a_mat, None), (grad_conv, None), (grad_step_bias, None),
         (grad_skip, None), (gain_terms, None), (gains, None), (grad_gain_moe, None),
         (grad_router, None), (out_sums, None), (mix_sum, None)],
        [((ring // 2, 2, in_rows + small_rows + 16, padded), BF16, None)],
        [f32_vmem(ring * small_each, padded), f32_vmem(SEG, width)], 5,
    )
    done, d_n1_terms, d_edges = finish(packed, chunk_zo, d_n1_part, in_rows, small_rows, 11)
    blocks = width // in_rows
    of_rows = lambda shape: pl.BlockSpec(
        (shape[0] // blocks, shape[1]), lambda i: (jnp.minimum(i, blocks - 1), 0)
    )
    unpacked = call(
        functools.partial(
            unpack_kernel, ring, group, in_rows, small_rows, experts, states, ranked, taps,
            float(length * ring * width),
        ),
        "unpack", ring,
        [(mine_s, SMEM), (done, 0), (share_experts, None), (last_s, SMEM), (d_n1_terms, None),
         (d_edges, None), (tokens[0], None), (gains, None), (d_h1, None), (result, None)],
        [((width, 2 * local), F32, of_rows), ((local, width), F32, of_rows),
         ((width, w_down.shape[1]), F32, None), ((w_down.shape[1], width), F32, None),
         ((taps, local), F32, None), ((w_x.shape[1], local), F32, None), ((ranked, local), F32, None),
         ((states, local), F32, None), ((2 * SEG, padded), F32, None), ((1, LANE), F32, None),
         (row_f, F32, None), (row_f, F32, None)],
        [f32_vmem(ring * small_each, padded), f32_vmem(SEG, padded), f32_vmem(length, width), order_vmem],
        9,
    )
    share_in, share_out, share_up, share_down, g_taps, g_wx, g_wdt, g_a, vecs, stats, input_grad, layer_out = unpacked
    fulls, vecs = vecs[:SEG, :share], vecs[SEG:, :local]
    return (
        layer_out[None],
        input_grad[None],
        fulls[0],
        share_in,
        g_taps,
        vecs[0],
        g_wx.T,
        g_wdt,
        vecs[1],
        g_a,
        vecs[2],
        share_out,
        fulls[1],
        fulls[2 : 2 + experts].T,
        share_up[None],
        share_down[None],
        stats[:, :3],
    )


def solution(mesh):
    placed = (
        P("wa", "ctx", None),
        P("wa", "ctx", None),
        P("wa", None),
        P("wa", "ctx", None),
        P("wa", "ctx"),
        P("wa"),
        P(None, "wa"),
        P(None, "wa"),
        P("wa"),
        P("wa", None),
        P(None, "wa"),
        P("wa"),
        P(None, "wa"),
        P("wa"),
        P("wa", None),
        P("wa"),
        P("wa", None),
        P("wa", None, "ctx"),
        P("wa", "ctx", None),
    )
    return jax.shard_map(
        body,
        mesh=mesh,
        in_specs=placed,
        out_specs=(
            P("wa", "ctx", None),
            P("wa", "ctx", None),
            P("wa"),
            P(None, "wa"),
            P(None, "wa"),
            P("wa"),
            P("wa", None),
            P(None, "wa"),
            P("wa"),
            P(None, "wa"),
            P("wa"),
            P("wa", None),
            P("wa"),
            P("wa", None),
            P("wa", None, "ctx"),
            P("wa", "ctx", None),
            P("wa", None),
        ),
        check_vma=False,
    )
```

```python
import functools

import jax
import jax.numpy as jnp
from jax import lax
from jax.experimental import pallas as pl
from jax.experimental.pallas import tpu as pltpu
from jax.sharding import PartitionSpec as P

EPS = 1e-05
F32 = jnp.float32
BF16 = jnp.bfloat16
SEG = 8
LANE = 128
EDGE = 16
CUT = 1e30
MESH = pl.DeviceIdType.MESH
VMEM_LIMIT = 24 * 2**20
LARGE_LIMIT = 60 * 2**20


def lasting(us):
    return pl.CostEstimate(
        flops=int(us * 1.1e9), bytes_accessed=int(us * 3.5e6), transcendentals=0
    )


def greet(axis, count):
    me = lax.axis_index(axis)
    barrier = pltpu.get_barrier_semaphore()
    for k in range(1, count):
        pl.semaphore_signal(
            barrier, inc=1, device_id={axis: lax.rem(me + k, count)}, device_id_type=MESH
        )
    pl.semaphore_wait(barrier, count - 1)
    return me


def gather_kernel(axis, count, arrays, *refs):
    srcs, dsts = refs[:arrays], refs[arrays : 2 * arrays]
    send, recv, own = refs[-3:]
    me = greet(axis, count)
    copies = []
    for i in range(arrays):
        for k in range(1, count):
            copy = pltpu.make_async_remote_copy(
                src_ref=srcs[i],
                dst_ref=dsts[i].at[me],
                send_sem=send.at[i, k],
                recv_sem=recv.at[i, k],
                device_id={axis: lax.rem(me + k, count)},
                device_id_type=MESH,
            )
            copy.start()
            copies.append(copy)
    for i in range(arrays):
        local = pltpu.make_async_copy(srcs[i], dsts[i].at[me], own.at[i])
        local.start()
        copies.append(local)
    for copy in copies:
        copy.wait()


def trade_kernel(axis, count, x_ref, o_ref, send, recv, own):
    me = greet(axis, count)
    copies = []
    for k in range(1, count):
        other = lax.rem(me + k, count)
        copy = pltpu.make_async_remote_copy(
            src_ref=x_ref.at[other],
            dst_ref=o_ref.at[me],
            send_sem=send.at[k],
            recv_sem=recv.at[k],
            device_id={axis: other},
            device_id_type=MESH,
        )
        copy.start()
        copies.append(copy)
    local = pltpu.make_async_copy(x_ref.at[me], o_ref.at[me], own)
    local.start()
    local.wait()
    for copy in copies:
        copy.wait()


def trade(x, axis, cid, us):
    count = lax.axis_size(axis)
    return pl.pallas_call(
        functools.partial(trade_kernel, axis, count),
        out_shape=jax.ShapeDtypeStruct(x.shape, x.dtype),
        in_specs=[pl.BlockSpec(memory_space=pl.ANY)],
        out_specs=pl.BlockSpec(memory_space=pl.ANY),
        scratch_shapes=[
            pltpu.SemaphoreType.DMA((count,)),
            pltpu.SemaphoreType.DMA((count,)),
            pltpu.SemaphoreType.DMA,
        ],
        compiler_params=pltpu.CompilerParams(
            collective_id=cid, has_side_effects=True, vmem_limit_bytes=VMEM_LIMIT
        ),
        cost_estimate=lasting(us),
        name=f"trade_{cid}",
    )(x)


def sum_start(mates, x_ref, got, send, recv):
    copies = []
    for k, who in enumerate(mates):
        copy = remote(x_ref.at[who], got.at[k], send.at[k], recv.at[k], {"wa": who})
        copy.start()
        copies.append(copy)
    return copies


def sum_spread(mine, mates, x_ref, got, o_ref, copies, send, recv):
    for copy in copies:
        copy.wait_recv()
    parts = [x_ref.at[mine]] + [got.at[k] for k in range(len(mates))]
    add_rows(o_ref.at[mine], parts, x_ref.shape[1])
    spreads = []
    for k, who in enumerate(mates):
        copy = remote(o_ref.at[mine], o_ref.at[mine], send.at[k], recv.at[k], {"wa": who})
        copy.start()
        spreads.append(copy)
    return spreads


def sum_all_kernel(group, x_ref, o_ref, got, s1, r1, s2, r2):
    greet("wa", group)
    mine, mates = mates_of(group)
    copies = sum_start(mates, x_ref, got, s1, r1)
    spreads = sum_spread(mine, mates, x_ref, got, o_ref, copies, s2, r2)
    for copy in spreads:
        copy.wait()
    for copy in copies:
        copy.wait_send()


def sum_all(x, cid, us):
    group = lax.axis_size("wa")
    vmem = pl.BlockSpec(memory_space=pltpu.VMEM)
    dma = pltpu.SemaphoreType.DMA
    return pl.pallas_call(
        functools.partial(sum_all_kernel, group),
        out_shape=jax.ShapeDtypeStruct(x.shape, x.dtype),
        in_specs=[vmem],
        out_specs=vmem,
        scratch_shapes=[pltpu.VMEM((group - 1,) + x.shape[1:], x.dtype)] + [dma((group - 1,))] * 4,
        compiler_params=pltpu.CompilerParams(
            collective_id=cid, has_side_effects=True, vmem_limit_bytes=VMEM_LIMIT
        ),
        cost_estimate=lasting(us),
        name="sum_all",
    )(x)


def gather_all(xs, axis, cid, us):
    count, arrays = lax.axis_size(axis), len(xs)
    return pl.pallas_call(
        functools.partial(gather_kernel, axis, count, arrays),
        out_shape=[jax.ShapeDtypeStruct((count,) + x.shape, x.dtype) for x in xs],
        in_specs=[pl.BlockSpec(memory_space=pl.ANY)] * arrays,
        out_specs=[pl.BlockSpec(memory_space=pl.ANY)] * arrays,
        scratch_shapes=[
            pltpu.SemaphoreType.DMA((arrays, count)),
            pltpu.SemaphoreType.DMA((arrays, count)),
            pltpu.SemaphoreType.DMA((arrays,)),
        ],
        compiler_params=pltpu.CompilerParams(
            collective_id=cid, has_side_effects=True, vmem_limit_bytes=VMEM_LIMIT
        ),
        cost_estimate=lasting(us),
        name=f"gather_{cid}",
    )(*xs)


def remote(src, dst, send, recv, where):
    return pltpu.make_async_remote_copy(
        src_ref=src, dst_ref=dst, send_sem=send, recv_sem=recv,
        device_id=where, device_id_type=MESH,
    )


def add_rows(out, parts, rows):
    def one(i, _):
        at = pl.ds(pl.multiple_of(i * 16, 16), 16)
        total = parts[0][at, :].astype(F32)
        for part in parts[1:]:
            total = total + part[at, :].astype(F32)
        out[at, :] = total.astype(out.dtype)
        return 0

    lax.fori_loop(0, rows // 16, one, 0)


def neighbours(ring):
    me = lax.axis_index("ctx")
    half = ring // 2
    lane = lax.rem(me, 2)
    chip = me // 2
    peers = [lax.rem(chip + k, half) * 2 + lane for k in range(1, half)]
    return me, chip, lane, me + 1 - 2 * lane, peers


def mates_of(group):
    mine = lax.axis_index("wa")
    return mine, [lax.rem(mine + k, group) for k in range(1, group)]


def hello(barrier, axis, who):
    pl.semaphore_signal(barrier, inc=1, device_id={axis: who}, device_id_type=MESH)


def carry_kernel(ring, arrays, halved, *refs):
    total = arrays + halved
    srcs, dsts = refs[:total], refs[total : 2 * total]
    send, recv, fwd_s, fwd_r, own, half_s, half_r = refs[2 * total :]
    me, chip, lane, pair, peers = neighbours(ring)
    half = ring // 2
    barrier = pltpu.get_barrier_semaphore()
    for who in [pair] + peers:
        hello(barrier, "ctx", who)
    pl.semaphore_wait(barrier, half)
    copies, forwards, local = [], [], []
    for i in range(arrays):
        for k, who in enumerate(peers):
            copies.append(remote(srcs[i], dsts[i].at[me], send.at[i, k], recv.at[i, k], {"ctx": who}))
            copies[-1].start()
    for i in range(arrays):
        forwards.append(remote(srcs[i], dsts[i].at[me], fwd_s.at[i, 0], fwd_r.at[i, 0], {"ctx": pair}))
        forwards[-1].start()
        local.append(pltpu.make_async_copy(srcs[i], dsts[i].at[me], own.at[i]))
        local[-1].start()
    if halved:
        to_pair = remote(srcs[arrays].at[:, 1 - lane], dsts[arrays], half_s, half_r, {"ctx": pair})
        to_pair.start()
        local.append(to_pair)
    for i in range(arrays):
        for k in range(1, half):
            copies[i * (half - 1) + k - 1].wait_recv()
            block = dsts[i].at[lax.rem(chip + half - k, half) * 2 + lane]
            forwards.append(remote(block, block, fwd_s.at[i, k], fwd_r.at[i, k], {"ctx": pair}))
            forwards[-1].start()
    for copy in copies:
        copy.wait_send()
    for copy in forwards + local:
        copy.wait()


def carry(xs, cid, us, halved=None):
    ring, arrays = lax.axis_size("ctx"), len(xs)
    half = ring // 2
    shapes = [((ring,) + x.shape, x.dtype) for x in xs]
    if halved is not None:
        xs = xs + [halved]
        shapes.append((halved.shape[:1] + halved.shape[2:], halved.dtype))
    hbm = pl.BlockSpec(memory_space=pl.ANY)
    dma = pltpu.SemaphoreType.DMA
    return pl.pallas_call(
        functools.partial(carry_kernel, ring, arrays, len(xs) - arrays),
        out_shape=[jax.ShapeDtypeStruct(shape, dtype) for shape, dtype in shapes],
        in_specs=[hbm] * len(xs),
        out_specs=[hbm] * len(xs),
        scratch_shapes=[
            dma((arrays, half - 1)), dma((arrays, half - 1)), dma((arrays, half)), dma((arrays, half)),
            dma((arrays,)), dma, dma,
        ],
        compiler_params=pltpu.CompilerParams(
            collective_id=cid, has_side_effects=True, vmem_limit_bytes=VMEM_LIMIT
        ),
        cost_estimate=lasting(us),
        name=f"carry_{cid}",
    )(*xs)


def finish_kernel(
    ring, group, in_rows, small_rows,
    g_ref, zf_ref, d_ref, o_ref, dt_ref, de_ref,
    from_pair, paired, came, own, zin, tiles, fin, store_s,
    pair_s, pair_r, ctx_s, ctx_r, z_s, z_r, tile_s, tile_r, d_s, d_r, d_own, last_s, last_r, fwd_s, fwd_r,
    edge_s, edge_r,
):
    me, chip, lane, pair, peers = neighbours(ring)
    mine, mates = mates_of(group)
    half = ring // 2
    rows = in_rows + small_rows + 16
    lanes = g_ref.shape[3]
    barrier = pltpu.get_barrier_semaphore()
    for who in [pair] + peers:
        hello(barrier, "ctx", who)
    for who in mates:
        hello(barrier, "wa", who)
    has_next = me < ring - 1
    has_last = me > 0

    @pl.when(has_next)
    def _():
        hello(barrier, "ctx", me + 1)

    @pl.when(has_last)
    def _():
        hello(barrier, "ctx", me - 1)

    around = jnp.where(has_next, 1, 0) + jnp.where(has_last, 1, 0)
    pl.semaphore_wait(barrier, half + group - 1 + around)

    to_pair = remote(g_ref.at[:, 1 - lane], from_pair, pair_s, pair_r, {"ctx": pair})
    to_pair.start()
    small_at = 2 * in_rows + 16
    parts = [
        pl.ds(small_at + small_rows, in_rows), pl.ds(small_at, small_rows),
        pl.ds(0, in_rows), pl.ds(in_rows, in_rows + 16),
    ]
    fin[parts[0]] = zf_ref[:, lanes:]
    stored = []

    def to_all(i):
        src, dst = fin.at[parts[i]], o_ref.at[me, parts[i]]
        copies = []
        for k, who in enumerate(peers):
            copies.append(remote(src, dst, last_s.at[i, k], last_r.at[i, k], {"ctx": who}))
        copies.append(remote(src, dst, fwd_s.at[i, 0], fwd_r.at[i, 0], {"ctx": pair}))
        for copy in copies:
            copy.start()
        stored.append(pltpu.make_async_copy(src, dst, store_s.at[i]))
        stored[-1].start()
        return copies

    def forward(i, copies):
        for k in range(1, half):
            copies[k - 1].wait_recv()
            source = lax.rem(chip + half - k, half) * 2 + lane
            block = o_ref.at[source, parts[i]]
            copy = remote(block, block, fwd_s.at[i, k], fwd_r.at[i, k], {"ctx": pair})
            copy.start()
            copies.append(copy)

    x_to = mine // 2
    z_to = group // 2 + mine // 2
    slot = lax.rem(mine, 2)
    z_ref = zf_ref.at[:, pl.ds(0, lanes)]
    x_ref = own.at[pl.ds(0, in_rows)]
    send_x = remote(x_ref, zin.at[slot], z_s.at[0], z_r.at[slot], {"wa": x_to})
    send_z = remote(z_ref, zin.at[slot], z_s.at[1], z_r.at[slot], {"wa": z_to})
    keep_x = pltpu.make_async_copy(x_ref, zin.at[slot], z_r.at[slot])
    keep_z = pltpu.make_async_copy(z_ref, zin.at[slot], z_r.at[slot])

    @pl.when(z_to != mine)
    def _():
        send_z.start()

    @pl.when(z_to == mine)
    def _():
        keep_z.start()

    cut = d_ref.shape[1] // 32 * 16
    pieces = [pl.ds(0, cut), pl.ds(cut, d_ref.shape[1] - cut)]
    trades = []

    def trade_rows(i):
        for k, who in enumerate(mates):
            copy = remote(
                d_ref.at[who, pieces[i]], dt_ref.at[mine, pieces[i]], d_s.at[i, k], d_r.at[i, k],
                {"wa": who},
            )
            copy.start()
            trades.append(copy)

    trade_rows(0)
    kept = pltpu.make_async_copy(d_ref.at[mine], dt_ref.at[mine], d_own)
    kept.start()

    to_pair.wait_recv()
    scattered = []
    for k, who in enumerate(peers):
        to = lax.rem(chip + k + 1, half)
        add_rows(paired.at[to], [g_ref.at[to, lane], from_pair.at[to]], rows)
        copy = remote(paired.at[to], came.at[k], ctx_s.at[k], ctx_r.at[k], {"ctx": who})
        copy.start()
        scattered.append(copy)
    early = to_all(0)
    add_rows(paired.at[chip], [g_ref.at[chip, lane], from_pair.at[chip]], rows)
    for copy in scattered:
        copy.wait_recv()
    add_rows(own, [paired.at[chip]] + [came.at[k] for k in range(half - 1)], rows)

    @pl.when(x_to != mine)
    def _():
        send_x.start()

    @pl.when(x_to == mine)
    def _():
        keep_x.start()

    tile = pl.ds(in_rows + small_rows, 16)
    spread_tiles = []
    for k, who in enumerate(mates):
        copy = remote(own.at[tile], tiles.at[k], tile_s.at[k], tile_r.at[k], {"wa": who})
        copy.start()
        spread_tiles.append(copy)
    fin[parts[1]] = own[pl.ds(in_rows, small_rows)]
    middle_rows = to_all(1)
    forward(0, early)

    def landed(slot):
        pltpu.make_async_copy(zin.at[slot], zin.at[slot], z_r.at[slot]).wait()
        fin[pl.ds(slot * in_rows, in_rows)] = zin[slot]

    landed(0)
    late = [to_all(2)]
    forward(1, middle_rows)
    for copy in spread_tiles:
        copy.wait_recv()
    add_rows(
        fin.at[pl.ds(2 * in_rows, 16)],
        [own.at[tile]] + [tiles.at[k] for k in range(group - 1)],
        16,
    )
    landed(1)
    late.append(to_all(3))
    trade_rows(1)
    kept.wait()
    forward(2, late[0])
    forward(3, late[1])

    for copy in trades:
        copy.wait_recv()
    edges = dt_ref.at[:, pl.ds(d_ref.shape[1] - EDGE, EDGE)]
    to_last = remote(edges, de_ref, edge_s, edge_r, {"ctx": me - 1})

    @pl.when(has_last)
    def _():
        to_last.start()

    for copies in [early, middle_rows] + late:
        for copy in copies[half - 1 :]:
            copy.wait_recv()

    for copy in stored:
        copy.wait()
    to_pair.wait_send()
    for copy in scattered + spread_tiles + early + middle_rows + late[0] + late[1] + trades:
        copy.wait_send()

    @pl.when(x_to != mine)
    def _():
        send_x.wait_send()

    @pl.when(z_to != mine)
    def _():
        send_z.wait_send()

    @pl.when(has_last)
    def _():
        to_last.wait_send()

    @pl.when(has_next)
    def _():
        to_last.wait_recv()


def finish(g, zf, d, in_rows, small_rows, cid):
    ring, group = lax.axis_size("ctx"), lax.axis_size("wa")
    half = ring // 2
    rows, lanes = g.shape[2:]
    out_rows = 3 * in_rows + small_rows + 16
    vmem = pl.BlockSpec(memory_space=pltpu.VMEM)
    hbm = pl.BlockSpec(memory_space=pl.ANY)
    dma = pltpu.SemaphoreType.DMA
    return pl.pallas_call(
        functools.partial(finish_kernel, ring, group, in_rows, small_rows),
        out_shape=[
            jax.ShapeDtypeStruct((ring, out_rows, lanes), BF16),
            jax.ShapeDtypeStruct(d.shape, d.dtype),
            jax.ShapeDtypeStruct((group, EDGE, d.shape[2]), d.dtype),
        ],
        in_specs=[vmem, vmem, hbm],
        out_specs=[hbm, hbm, hbm],
        scratch_shapes=[
            pltpu.VMEM((half, rows, lanes), BF16),
            pltpu.VMEM((half, rows, lanes), BF16),
            pltpu.VMEM((half - 1, rows, lanes), BF16),
            pltpu.VMEM((rows, lanes), BF16),
            pltpu.VMEM((2, in_rows, lanes), BF16),
            pltpu.VMEM((group - 1, 16, lanes), BF16),
            pltpu.VMEM((out_rows, lanes), BF16),
            dma((4,)), dma, dma,
            dma((half - 1,)), dma((half - 1,)),
            dma((2,)), dma((2,)),
            dma((group - 1,)), dma((group - 1,)),
            dma((2, group - 1)), dma((2, group - 1)), dma,
            dma((4, half - 1)), dma((4, half - 1)),
            dma((4, half)), dma((4, half)),
            dma, dma,
        ],
        compiler_params=pltpu.CompilerParams(
            collective_id=cid, has_side_effects=True, vmem_limit_bytes=VMEM_LIMIT
        ),
        cost_estimate=lasting(60),
        name="finish",
    )(g, zf, d)


def start_kernel(
    ring, group, tok, par, doc, w_ref, tok_o, edge_o, par_o, doc_o, w_o,
    mate_s, mate_r, own_s, edge_s, edge_r, relay_s, relay_r, shift_s, shift_r, out_s, out_r, fwd_s, fwd_r,
):
    me = lax.axis_index("ctx")
    mine = lax.axis_index("wa")
    half = ring // 2
    lane = lax.rem(me, 2)
    chip = me // 2
    pair = me + 1 - 2 * lane
    peers = [lax.rem(chip + k, half) * 2 + lane for k in range(1, half)]
    mates = [lax.rem(mine + k, group) for k in range(1, group)]
    barrier = pltpu.get_barrier_semaphore()
    for who in [pair] + peers:
        pl.semaphore_signal(barrier, inc=1, device_id={"ctx": who}, device_id_type=MESH)
    for who in mates:
        pl.semaphore_signal(barrier, inc=1, device_id={"wa": who}, device_id_type=MESH)
    has_next = me < ring - 1
    has_last = me > 0

    @pl.when(has_next)
    def _():
        pl.semaphore_signal(barrier, inc=1, device_id={"ctx": me + 1}, device_id_type=MESH)

    @pl.when(has_last)
    def _():
        pl.semaphore_signal(barrier, inc=1, device_id={"ctx": me - 1}, device_id_type=MESH)

    around = jnp.where(has_next, 1, 0) + jnp.where(has_last, 1, 0)
    pl.semaphore_wait(barrier, half + group - 1 + around)

    edge = tok.at[pl.ds(tok.shape[0] - EDGE, EDGE)]
    to_next = remote(edge, edge_o.at[mine], edge_s, edge_r, {"ctx": me + 1})

    @pl.when(has_next)
    def _():
        to_next.start()

    kind = mine // (group // 2)
    base = 2 * lax.rem(mine, group // 2)
    for h in range(2):
        where = base + h
        send = remote(
            w_ref.at[h], w_o.at[kind, me], shift_s.at[h], shift_r.at[kind], {"wa": where}
        )
        keep = pltpu.make_async_copy(w_ref.at[h], w_o.at[kind, me], shift_r.at[kind])

        @pl.when(where != mine)
        def _():
            send.start()

        @pl.when(where == mine)
        def _():
            keep.start()

    trades = []
    for i, (src, dst) in enumerate(((par, par_o), (doc, doc_o), (tok, tok_o))):
        for k, who in enumerate(mates):
            copy = remote(src, dst.at[mine], mate_s.at[i, k], mate_r.at[i, k], {"wa": who})
            copy.start()
            trades.append(copy)
        keep = pltpu.make_async_copy(src, dst.at[mine], own_s.at[i])
        keep.start()

    @pl.when(has_last)
    def _():
        to_next.wait_recv()
        for k, who in enumerate(mates):
            remote(
                edge_o.at[mine], edge_o.at[mine], relay_s.at[k], relay_r.at[k], {"wa": who}
            ).start()

    sends = []
    for t in range(2):
        block = w_o.at[t, me]
        pltpu.make_async_copy(block, block, shift_r.at[t]).wait()
        for k, who in enumerate(peers):
            copy = remote(block, block, out_s.at[t, k], out_r.at[t, k], {"ctx": who})
            copy.start()
            sends.append(copy)
        copy = remote(block, block, fwd_s.at[t, 0], fwd_r.at[t, 0], {"ctx": pair})
        copy.start()
        sends.append(copy)
    forwards = []
    for t in range(2):
        for k in range(1, half):
            source = lax.rem(chip + half - k, half) * 2 + lane
            block = w_o.at[t, source]
            pltpu.make_async_copy(block, block, out_r.at[t, k - 1]).wait()
            copy = remote(block, block, fwd_s.at[t, k], fwd_r.at[t, k], {"ctx": pair})
            copy.start()
            forwards.append(copy)
    for t in range(2):
        for k in range(half):
            pltpu.make_async_copy(w_o.at[t, me], w_o.at[t, me], fwd_r.at[t, k]).wait()
    for copy in sends + forwards:
        copy.wait_send()
    for h in range(2):

        @pl.when(base + h != mine)
        def _():
            remote(
                w_ref.at[h], w_o.at[kind, me], shift_s.at[h], shift_r.at[kind], {"wa": mine}
            ).wait_send()

    for copy in trades:
        copy.wait()
    for i, (src, dst) in enumerate(((par, par_o), (doc, doc_o), (tok, tok_o))):
        pltpu.make_async_copy(src, dst.at[mine], own_s.at[i]).wait()

    @pl.when(has_next)
    def _():
        to_next.wait_send()

    @pl.when(has_last)
    def _():
        for k, who in enumerate(mates):
            remote(
                edge_o.at[mine], edge_o.at[mine], relay_s.at[k], relay_r.at[k], {"wa": who}
            ).wait()


def start(tok, par, doc, halves, cid):
    ring, group = lax.axis_size("ctx"), lax.axis_size("wa")
    half = ring // 2
    hbm = pl.BlockSpec(memory_space=pl.ANY)
    dma = pltpu.SemaphoreType.DMA
    outs = [(group,) + a.shape for a in (tok, tok[:EDGE], par, doc)] + [(2, ring) + halves.shape[1:]]
    types = [a.dtype for a in (tok, tok, par, doc, halves)]
    return pl.pallas_call(
        functools.partial(start_kernel, ring, group),
        out_shape=[jax.ShapeDtypeStruct(s, t) for s, t in zip(outs, types)],
        in_specs=[hbm] * 4,
        out_specs=[hbm] * 5,
        scratch_shapes=[
            dma((3, group - 1)), dma((3, group - 1)), dma((3,)),
            dma, dma,
            dma((group - 1,)), dma((group - 1,)),
            dma((2,)), dma((2,)),
            dma((2, half - 1)), dma((2, half - 1)),
            dma((2, half)), dma((2, half)),
        ],
        compiler_params=pltpu.CompilerParams(
            collective_id=cid, has_side_effects=True, vmem_limit_bytes=VMEM_LIMIT
        ),
        cost_estimate=lasting(35),
        name="start",
    )(tok, par, doc, halves)


def pick(rows, states, at):
    shape = (rows, states * LANE)
    lower = (lax.broadcasted_iota(jnp.int32, shape, 0) - at) * LANE
    place = lax.broadcasted_iota(jnp.int32, shape, 1)
    return jnp.where((place >= lower) & (place < lower + LANE), 1.0, 0.0)


def spread(rows, states, at):
    return jnp.dot(rows, pick(rows.shape[1], states, at).astype(BF16), preferred_element_type=F32)


def collected(wide_rows, states, columns, at):
    shape = (states * LANE, columns)
    lower = (lax.broadcasted_iota(jnp.int32, shape, 1) - at) * LANE
    place = lax.broadcasted_iota(jnp.int32, shape, 0)
    ones = jnp.where((place >= lower) & (place < lower + LANE), 1.0, 0.0).astype(BF16)
    coarse = wide_rows.astype(BF16)
    rest = (wide_rows - coarse.astype(F32)).astype(BF16)
    return dot_nn(coarse, ones) + dot_nn(rest, ones)


def position_of(shape, axis, steps):
    row = lax.broadcasted_iota(jnp.int32, shape, axis)
    return (row & (SEG - 1)) * steps + (row >> 3)


def permutation(length):
    shape = (length, length)
    at = position_of(shape, 0, length // SEG)
    return jnp.where(at == lax.broadcasted_iota(jnp.int32, shape, 1), 1.0, 0.0).astype(BF16)


def rolled(value, by):
    return pltpu.roll(value, by % SEG, 0)


def lanes_of(g):
    return pl.ds(pl.multiple_of(g * LANE, LANE), LANE)


def rows_of(j):
    return pl.ds(pl.multiple_of(j * SEG, SEG), SEG)


def wide(ref, n, lanes):
    return jnp.broadcast_to(ref[pl.ds(n, 1), lanes], (SEG, LANE))


def state_cols(n):
    return slice(n * LANE, (n + 1) * LANE)


def dot_nt(a, b):
    return lax.dot_general(a, b, (((1,), (1,)), ((), ())), preferred_element_type=F32)


def dot_tn(a, b):
    return lax.dot_general(a, b, (((0,), (0,)), ((), ())), preferred_element_type=F32)


def dot_nn(a, b):
    return jnp.dot(a, b, preferred_element_type=F32)


def rms_scale(values):
    return lax.rsqrt(jnp.mean(values * values, axis=-1, keepdims=True) + EPS)


def norm_grads(values, scale, gain, d_out):
    unit = values * scale
    d_unit = d_out * gain
    d_values = scale * (d_unit - unit * jnp.mean(d_unit * unit, axis=-1, keepdims=True))
    return d_values, d_out * unit


def silu_slope(v):
    s = jax.nn.sigmoid(v)
    return s * (1.0 + v * (1.0 - s))


def seg_of():
    return lax.broadcasted_iota(jnp.int32, (SEG, LANE), 0)


def lag_masks(place, doc_ref, documents, stream, length, taps):
    at = place * length + position_of((length, LANE), 0, length // SEG)
    masks = [None]
    for lag in range(1, taps):
        cut = None
        for d in range(documents):
            begin = doc_ref[stream, 0, d]
            here = (begin > at - lag) & (begin <= at)
            cut = here if cut is None else cut | here
        masks.append(jnp.where(cut, 0.0, 1.0))
    hit = None
    for d in range(documents):
        here = doc_ref[stream, 0, d] == at
        hit = here if hit is None else hit | here
    return masks, jnp.where(hit, CUT, 0.0)


def enter_kernel(
    taps, documents, place_ref, doc_ref, tok, edge, gain, wx, wz, conv, wproj,
    n1_o, ext_o, pre_o, uf_o, u_o, z_o, part_o, cut_o,
):
    length = tok.shape[1]
    steps = length // SEG
    place = place_ref[0]
    gains = gain[0:1]

    def normal(rows):
        return (rows * rms_scale(rows) * gains).astype(BF16)

    n1_o[0, :length] = normal(dot_nn(permutation(length), tok[0]))
    n1_o[0, length:] = normal(jnp.where(place > 0, edge[0].astype(F32), 0.0))
    inner = dot_nn(n1_o[0], wx[0]).astype(BF16).astype(F32)
    z_o[0] = dot_nn(n1_o[0, :length], wz[0]).astype(BF16)
    masks, cut = lag_masks(place, doc_ref, documents, pl.program_id(0), length, taps)
    cut_o[0] = cut
    seg = seg_of()
    behind = taps - 1
    for g in range(inner.shape[1] // LANE):
        cols = slice(g * LANE, (g + 1) * LANE)
        rows, before = inner[:length, cols], inner[length:, cols]
        parts = []
        for i in range(behind):
            j = steps - behind + i
            last = jnp.broadcast_to(before[EDGE - behind + i : EDGE - behind + i + 1], (SEG, LANE))
            parts.append(jnp.where(seg == 0, last, rolled(rows[j * SEG : (j + 1) * SEG], 1)))
        ext = jnp.concatenate(parts + [rows], axis=0)
        ext_o[0, :, cols] = ext
        pre = conv[taps : taps + 1, cols] + conv[0:1, cols] * rows
        for lag in range(1, taps):
            window = ext[(behind - lag) * SEG : (behind - lag) * SEG + length]
            pre = pre + conv[lag : lag + 1, cols] * window * masks[lag]
        pre_o[0, :, cols] = pre
        u = (pre * jax.nn.sigmoid(pre)).astype(BF16)
        u_o[0, :, cols] = u
        uf_o[0, :, cols] = u.astype(F32)
    part_o[0] = dot_nt(u_o[0], wproj[...]).astype(BF16)


def summary_kernel(
    states, b_at, proj_i, wdt, bias, uf, cut, a_ref,
    step_o, sig_o, hx_ref, sx_ref, hd_o, sd_ref, bb, st_s, dr_s, hd_s,
):
    length, width = step_o.shape[1:]
    groups, steps = width // LANE, length // SEG
    proj = proj_i[0]
    bb[...] = spread(proj, states, b_at)
    pre = dot_nn(proj, wdt[...]) + bias[0:1]
    step_size = jnp.maximum(pre, 0.0) + jnp.log1p(jnp.exp(-jnp.abs(pre)))
    step_o[0] = step_size
    sig_o[0] = jax.nn.sigmoid(pre)
    dr_s[...] = step_size * uf[0]
    for g in range(groups):
        cols = slice(g * LANE, (g + 1) * LANE)
        st_s[:, cols] = step_size[:, cols] + cut[0]
    zero = jnp.zeros((SEG, LANE), F32)
    seg = seg_of()

    def group(g, _):
        lanes = lanes_of(g)
        a = [wide(a_ref, n, lanes) for n in range(states)]

        def step(j, carry):
            rows = rows_of(j)
            st = st_s[rows, lanes]
            dr = dr_s[rows, lanes]
            new = [carry[0] + st]
            for n in range(states):
                new.append(jnp.exp(st * a[n]) * carry[n + 1] + bb[rows, state_cols(n)] * dr)
            return tuple(new)

        out = lax.fori_loop(0, steps, step, (zero,) * (states + 1), unroll=8)
        total, h = out[0], list(out[1:])
        for k in (1, 2, 4):
            ok = seg >= k
            for n in range(states):
                h[n] = h[n] + jnp.where(ok, jnp.exp(total * a[n]) * rolled(h[n], k), 0.0)
            total = total + jnp.where(ok, rolled(total, k), 0.0)
        ok = seg >= 1
        sx_ref[0, :, lanes] = jnp.where(ok, rolled(total, 1), 0.0)
        sd_ref[0, :, lanes] = total[SEG - 1 : SEG]
        for n in range(states):
            hx_ref[0, n, :, lanes] = jnp.where(ok, rolled(h[n], 1), 0.0)
            hd_s[pl.ds(n, 1), lanes] = h[n][SEG - 1 : SEG]
        return 0

    lax.fori_loop(0, groups, group, 0)
    hd_o[0] = hd_s[...].astype(BF16)


def entering(e_ref, finals, sums, a_ref, place, ahead):
    ring = finals.shape[0]
    e_ref[...] = jnp.zeros_like(e_ref)

    def one(lap, _):
        c = lap if ahead else ring - 1 - lap
        use = (c < place) if ahead else (c > place)

        @pl.when(use)
        def _():
            e_ref[...] = jnp.exp(sums[c, 0] * a_ref[...]) * e_ref[...] + finals[c, 0].astype(F32)

        return 0

    lax.fori_loop(0, ring, one, 0)


def output_kernel(
    states, b_at, place_ref, proj, step_i, uf, cut, a_ref, hx_ref, sx_ref, finals, sums, z, skip, wout,
    y_o, gated_o, mix_o, e_o, bb, cb, st_s, dr_s,
):
    length, width = step_i.shape[1:]
    groups, steps = width // LANE, length // SEG
    bb[...] = spread(proj[0], states, b_at)
    cb[...] = spread(proj[0], states, b_at + states)
    e_ref = e_o.at[0]
    entering(e_ref, finals, sums, a_ref, place_ref[0], True)
    dr_s[...] = step_i[0] * uf[0]
    for g in range(groups):
        cols = slice(g * LANE, (g + 1) * LANE)
        st_s[:, cols] = step_i[0, :, cols] + cut[0]

    def group(g, _):
        lanes = lanes_of(g)
        a = [wide(a_ref, n, lanes) for n in range(states)]
        sx = sx_ref[0, :, lanes]
        first = tuple(
            jnp.exp(sx * a[n]) * wide(e_ref, n, lanes) + hx_ref[0, n, :, lanes]
            for n in range(states)
        )
        gain = wide(skip, 1, lanes)

        def step(j, h):
            rows = rows_of(j)
            st = st_s[rows, lanes]
            dr = dr_s[rows, lanes]
            new = []
            y = gain * uf[0, rows, lanes]
            for n in range(states):
                state = jnp.exp(st * a[n]) * h[n] + bb[rows, state_cols(n)] * dr
                new.append(state)
                y = y + cb[rows, state_cols(n)] * state
            y_o[0, rows, lanes] = y
            return tuple(new)

        lax.fori_loop(0, steps, step, first, unroll=8)
        return 0

    lax.fori_loop(0, groups, group, 0)
    zf = z[0].astype(F32)
    gated = (y_o[0] * (zf * jax.nn.sigmoid(zf))).astype(BF16)
    gated_o[0] = gated
    mix_o[0] = dot_nn(gated, wout[...]).astype(BF16)


def route_kernel(
    experts, terms, tok, gain, router, route, keep, grad,
    h1_o, n2_o, up_o, cols_o, match_o, out_o, sums_o,
):
    length, width = tok.shape
    shift = permutation(length)
    mix = terms[0].astype(F32)
    for w in range(1, terms.shape[0]):
        mix = mix + terms[w].astype(F32)
    h1 = dot_nn(shift, tok[...]) + mix
    h1_o[...] = h1
    n2 = (h1 * rms_scale(h1) * gain[1:2]).astype(BF16)
    n2_o[...] = n2
    logits = dot_nt(n2, router[...])
    lane = lax.broadcasted_iota(jnp.int32, (length, LANE), 1)
    kind = lax.broadcasted_iota(jnp.int32, (LANE, length), 0)
    named = route[...]
    onehot = jnp.where(kind == named, 1.0, 0.0)
    one = lax.broadcasted_iota(jnp.int32, (length, length), 0)
    two = lax.broadcasted_iota(jnp.int32, (length, length), 1)
    earlier = jnp.where(one < two, 1.0, 0.0).astype(BF16)
    before = dot_nn(onehot.astype(BF16), earlier)
    within = jnp.sum(before * onehot, axis=0, keepdims=True)
    slot = named.astype(F32) * (length // 2) + within
    facts = jnp.where(kind == experts, slot, jnp.where(kind == experts + 1, keep[...].astype(F32), onehot))
    facts = dot_nt(shift, facts.astype(BF16))
    onehot = jnp.where(lane < experts, facts, 0.0)
    slot = jnp.sum(jnp.where(lane == experts, facts, 0.0), axis=1, keepdims=True)
    kept = jnp.sum(jnp.where(lane == experts + 1, facts, 0.0), axis=1, keepdims=True)
    sig = jax.nn.sigmoid(jnp.sum(logits * onehot, axis=1, keepdims=True))
    gates = kept * sig
    cols_o[...] = jnp.where(
        lane == experts, gates, jnp.where(lane == experts + 1, gates * (1.0 - sig), onehot)
    )
    up = dot_nn(shift, grad[...])
    up_o[...] = up
    slots = match_o.shape[1]
    spot = lax.broadcasted_iota(jnp.int32, (length, slots), 1).astype(F32)
    match = jnp.where(slot == spot, 1.0, 0.0).astype(BF16)
    match_o[...] = match
    out_o[0] = dot_tn(match, n2).astype(BF16).reshape(out_o.shape[1:])
    out_o[1] = dot_tn(match, (gates * up).astype(BF16)).astype(BF16).reshape(out_o.shape[1:])
    sums_o[...] = jnp.broadcast_to(jnp.sum(mix * mix, keepdims=True), (SEG, LANE))


def pack_kernel(up, down, out):
    width, units = up.shape
    line = lax.broadcasted_iota(jnp.int32, (units, units), 0)
    same = jnp.where(line == lax.broadcasted_iota(jnp.int32, (units, units), 1), 1.0, 0.0)
    out[:, :width] = dot_nt(same.astype(BF16), up[...]).astype(BF16)
    out[:, width:] = down[...]


def prepare_kernel(
    experts, small, own, wx_t, wdt, wout, conv_w, a_log,
    gain_o, router_o, wx_o, wdt_o, wout_o, conv_o, rows_o, a_o, wide_s,
):
    width = wout.shape[1]
    group = small.shape[0]
    share = width // group
    for w in range(group):
        wide_s[:, w * share : (w + 1) * share] = small[w, :, :share].astype(F32)
    gain_o[0:1] = wide_s[SEG - 2 : SEG - 1]
    gain_o[1:2] = wide_s[SEG - 1 : SEG]
    gain_o[2:] = jnp.zeros((SEG - 2, width), F32)
    rows = wide_s[SEG:]
    row = lax.broadcasted_iota(jnp.int32, rows.shape, 0)
    router_o[...] = jnp.zeros_like(router_o)
    router_o[: 2 * SEG] = jnp.concatenate(
        [jnp.where(row < experts, rows, 0.0), jnp.zeros_like(rows)], axis=0
    ).astype(BF16)
    local = wout.shape[0]
    for out, src in ((wx_o, wx_t), (wdt_o, wdt), (a_o, None)):
        out[...] = jnp.zeros_like(out)
        if src is not None:
            out[: src.shape[0], :local] = src[...]
    a_o[...] = jnp.full(a_o.shape, -1.0, F32)
    a_o[:, :local] = -jnp.exp(a_log[...].astype(F32))
    wout_o[...] = jnp.zeros_like(wout_o)
    wout_o[:local] = wout[...]
    conv_o[...] = jnp.zeros_like(conv_o)
    taps = conv_w.shape[0]
    conv_o[:taps, :local] = conv_w[...].astype(F32)
    mine = own[...].astype(F32)
    rows_o[...] = jnp.zeros_like(rows_o)
    for h in range(2):
        cols = slice(h * share, (h + 1) * share)
        conv_o[taps : taps + 1, cols] = mine[h : h + 1, :share]
        rows_o[0:1, cols] = mine[2 + h : 3 + h, :share]
        rows_o[1:2, cols] = mine[4 + h : 5 + h, :share]


def block_rows(value, c, rows):
    low = c * rows
    have = max(0, min(rows, value.shape[0] - low))
    if have == rows:
        return value[low : low + rows]
    blank = jnp.zeros((rows - have, value.shape[1]), value.dtype)
    return blank if have == 0 else jnp.concatenate([value[low : low + have], blank], axis=0)


def pack_zo_kernel(ring, in_rows, local, n1, d_z, d_mix, gated, out):
    width = n1.shape[1]
    lanes = d_z.shape[1]
    grad_z = dot_tn(n1[...], d_z[...])
    grad_o = dot_tn(gated[...], d_mix[...])
    side = jnp.zeros((grad_o.shape[0], lanes - width // 2), F32)
    first = jnp.concatenate([grad_o[:, : width // 2], side], axis=1)
    second = jnp.concatenate([grad_o[:, width // 2 :], side], axis=1)
    rows = in_rows // 2
    for c in range(ring):
        out[c // 2, c % 2, :, :lanes] = block_rows(grad_z, c, in_rows).astype(BF16)
        both = [block_rows(first[:local], c, rows), block_rows(second[:local], c, rows)]
        out[c // 2, c % 2, :, lanes:] = jnp.concatenate(both, axis=0).astype(BF16)


def pack_rest_kernel(
    ring, in_rows, small_rows, group, experts, ranked, mine_ref, n1, d_x, gx, gdt, ga, a_ref, gconv, bias, skip,
    gain_mix, gains, gain_moe, router, out_sums, mix_sum, out, small_s, wide_s,
):
    lanes = d_x.shape[1]
    width = n1.shape[1]
    share = width // group
    grad_x = dot_tn(n1[...], d_x[...])
    small_s[...] = jnp.zeros_like(small_s)
    at = 0
    grad_a = jnp.sum(ga[...], axis=1) * a_ref[...]
    for part in (gx[...], gdt[:ranked], grad_a, gconv[...]):
        small_s[at : at + part.shape[0]] = part
        at += part.shape[0]
    small_s[at : at + 1] = bias[...]
    small_s[at + SEG : at + SEG + 1] = skip[...]
    wide_s[...] = jnp.zeros_like(wide_s)
    wide_s[0:1] = gain_mix[...] / gains[0:1]
    wide_s[1:2] = gain_moe[...]
    wide_s[2 : 2 + experts] = router[:experts]
    lane = lax.broadcasted_iota(jnp.int32, (group, LANE), 1)
    row = lax.broadcasted_iota(jnp.int32, (group, LANE), 0)
    stats = jnp.where(
        lane == 0, out_sums[0:1], jnp.where(lane == 1, mix_sum[0:1], jnp.where(lane == 2, out_sums[1:2], 0.0))
    )
    stats = jnp.where(row == mine_ref[0], stats, 0.0)
    stats = jnp.concatenate([stats, jnp.zeros((group, lanes - LANE), F32)], axis=1)
    bottom = jnp.zeros((16 - 2 * group, lanes), F32)
    small_each = small_s.shape[0] // ring
    for c in range(ring):
        if c < 2 + experts:
            full = [wide_s[c : c + 1, w * share : (w + 1) * share] for w in range(group)]
            full = jnp.concatenate(full, axis=0)
            full = jnp.concatenate([full, jnp.zeros((group, lanes - share), F32)], axis=1)
        else:
            full = jnp.zeros((group, lanes), F32)
        small = small_s[c * small_each : (c + 1) * small_each]
        blank = jnp.zeros((small_rows - small_each, lanes), F32)
        parts = [block_rows(grad_x, c, in_rows), small]
        if small_rows > small_each:
            parts.append(blank)
        rows = jnp.concatenate(parts + [full, stats, bottom], axis=0)
        out[c // 2, c % 2] = rows.astype(BF16)


def store_in_order(out, rows, order_s):
    steps = rows.shape[0] // SEG
    for g in range(rows.shape[1] // LANE):
        cols = slice(g * LANE, (g + 1) * LANE)
        for j in range(steps):
            order_s[g, pl.ds(j, SEG, stride=steps), :] = rows[j * SEG : (j + 1) * SEG, cols]
        out[:, cols] = order_s[g]


def input_gradient(taps, last_ref, terms, edges, tok, gain, dh, out_o, dn_s, order_s):
    length = tok.shape[0]
    steps = length // SEG
    behind = taps - 1
    total = terms[0, :length].astype(F32)
    edge = edges[0].astype(F32)
    for w in range(1, terms.shape[0]):
        total = total + terms[w, :length].astype(F32)
        edge = edge + edges[w].astype(F32)
    edge = jnp.where(last_ref[0] > 0, 0.0, edge)
    dn_s[...] = total
    seg = lax.broadcasted_iota(jnp.int32, (SEG, tok.shape[1]), 0)
    for i in range(behind):
        j = pl.ds((steps - behind + i) * SEG, SEG)
        row = EDGE - behind + i
        came = jnp.broadcast_to(edge[row : row + 1], seg.shape)
        dn_s[j, :] += jnp.where(seg == SEG - 1, came, 0.0)
    x = dot_nn(permutation(length), tok[...])
    d_x, _ = norm_grads(x, rms_scale(x), gain[0:1], dn_s[...])
    result = dh[...] + d_x
    store_in_order(out_o, result, order_s)


def unpack_kernel(
    ring, group, in_rows, small_rows, experts, states, ranked, taps, denom, mine_ref, done, up_down,
    last_ref, terms, edges, tok, gain, dh, res,
    in_o, out_o, up_o, down_o, taps_o, wx_o, wdt_o, a_o, vec_o, stat_o, grad_o, layer_o,
    small_s, full_s, dn_s, order_s,
):
    c = pl.program_id(0)
    width = in_o.shape[1]

    @pl.when(c == 1)
    def _():
        store_in_order(layer_o, res[...], order_s)
        input_gradient(taps, last_ref, terms, edges, tok, gain, dh, grad_o, dn_s, order_s)

    local = width // 2
    small_each = small_s.shape[0] // ring
    base = 2 * in_rows

    @pl.when(c == 0)
    def _():
        line = lax.broadcasted_iota(jnp.int32, (width, width), 0)
        same = jnp.where(line == lax.broadcasted_iota(jnp.int32, (width, width), 1), 1.0, 0.0)
        up_o[...] = dot_nt(same.astype(BF16), up_down[:, :width])
        down_o[...] = up_down[:, width:].astype(F32)
        full_s[...] = jnp.zeros_like(full_s)

    @pl.when(c * in_rows < width)
    def _():
        rows = done[0, :base, :].astype(F32)
        in_o[...] = jnp.concatenate([rows[:in_rows, :local], rows[in_rows:, :local]], axis=1)
        low = base + 16 + small_rows
        rows = done[0, low : low + in_rows, :].astype(F32)
        half = in_rows // 2
        out_o[...] = jnp.concatenate([rows[:half, :local], rows[half:, :local]], axis=1)

    small = done[0, base + 16 : base + 16 + small_rows, :].astype(F32)
    small_s[pl.ds(pl.multiple_of(c * small_each, SEG), small_each), :] = small[:small_each]
    tile = done[0, base : base + 16, :].astype(F32)
    row = lax.broadcasted_iota(jnp.int32, tile.shape, 0)
    own = jnp.sum(jnp.where(row == mine_ref[0], tile, 0.0), axis=0, keepdims=True)
    spot = lax.broadcasted_iota(jnp.int32, full_s.shape, 0)
    full_s[...] += jnp.where(spot == c, own, 0.0)

    @pl.when(c == 0)
    def _():
        sums = jnp.sum(jnp.where(row == group + mine_ref[0], tile, 0.0), axis=0, keepdims=True)
        stat_o[...] = jnp.sqrt(sums[:, :LANE] / denom)

    @pl.when(c == ring - 1)
    def _():
        at = 0
        wx_o[...] = small_s[: wx_o.shape[0], :local]
        at += up_to(wx_o.shape[0], LANE)
        wdt_o[...] = small_s[at : at + ranked, :local]
        at += ranked
        a_o[...] = small_s[at : at + states, :local]
        at += states
        taps_o[...] = small_s[at : at + taps, :local]
        vec_o[:SEG] = full_s[...]
        vec_o[SEG : SEG + 1] = small_s[at + taps : at + taps + 1]
        at += SEG
        vec_o[SEG + 1 : SEG + 2] = small_s[at : at + 1]
        vec_o[SEG + 2 : SEG + 3] = small_s[at + SEG : at + SEG + 1]


def middle_kernel(
    experts, group, chunks,
    mix_ref, tok, gain, router, route, keep, grad, w_ref,
    g_ref, layer_o, dh_o, dmix_o, router_o, gain_o, sums_o, mix_o,
    layer_s, dh_s, dmix_s, leave_sem,
    mix_s, h1_s, n2_s, up_s, cols_s, match_s, x_ref, r_ref,
    got, w_s, g_s, act_s, slope_s, pre_s, acc, out_s,
    w_sem, g_sem, s0, r0, own0, s1, r1, own1, s2, r2, own2,
):
    mine, mates = mates_of(group)
    count, width = x_ref.shape[2:]
    slots = group * count
    block = w_ref.shape[0] // chunks

    def load(t):
        at = pl.ds(pl.multiple_of(lax.rem(t, chunks) * block, block), block)
        slot = lax.rem(t, 2)
        return pltpu.make_async_copy(w_ref.at[at], w_s.at[slot], w_sem.at[slot])

    load(0).start()
    greet("wa", group)
    terms = []
    for k, who in enumerate(mates):
        copy = remote(mix_ref.at[who], mix_s.at[mine], s0.at[k], r0.at[k], {"wa": who})
        copy.start()
        terms.append(copy)
    kept = pltpu.make_async_copy(mix_ref.at[mine], mix_s.at[mine], own0)
    kept.start()
    for copy in terms + [kept]:
        copy.wait()
    route_kernel(
        experts, mix_s, tok, gain, router, route, keep, grad,
        h1_s, n2_s, up_s, cols_s, match_s, x_ref, mix_o,
    )
    sent = []
    for h in range(2):
        for k, who in enumerate(mates):
            copy = remote(x_ref.at[h, who], got.at[h, mine], s1.at[h, k], r1.at[h, k], {"wa": who})
            copy.start()
            sent.append(copy)
        pltpu.make_async_copy(x_ref.at[h, mine], got.at[h, mine], own1.at[h]).start()

    def arrived(h):
        pltpu.make_async_copy(x_ref.at[h, mine], got.at[h, mine], own1.at[h]).wait()
        for copy in sent[h * len(mates) : (h + 1) * len(mates)]:
            copy.wait_recv()
        return got[h].reshape(slots, width)

    def chunk(i):
        return pl.ds(pl.multiple_of(i * block, block), block)

    def returned(h):
        out_s[h] = acc[...].astype(BF16).reshape(group, count, width)
        for k, who in enumerate(mates):
            copy = remote(out_s.at[h, who], r_ref.at[h, mine], s2.at[h, k], r2.at[h, k], {"wa": who})
            copy.start()
            sent.append(copy)
        pltpu.make_async_copy(out_s.at[h, mine], r_ref.at[h, mine], own2.at[h]).start()

    rows = arrived(0)
    acc[...] = jnp.zeros_like(acc)

    def forward(i, _):
        load(i).wait()
        load(i + 1).start()
        w = w_s.at[lax.rem(i, 2)]
        hidden = dot_nt(w[:, :width], rows)
        c = 0.7978845608
        t = jnp.tanh(c * (hidden + 0.044715 * hidden * hidden * hidden))
        act = (0.5 * hidden * (1.0 + t)).astype(BF16)
        act_s[chunk(i), :] = act
        slope_s[chunk(i), :] = 0.5 * (1.0 + t) + 0.5 * hidden * (1.0 - t * t) * c * (
            1.0 + 3.0 * 0.044715 * hidden * hidden
        )
        acc[...] += dot_tn(act, w[:, width:])
        return 0

    lax.fori_loop(0, chunks, forward, 0)
    returned(0)
    d_out = arrived(1)
    acc[...] = jnp.zeros_like(acc)

    def backward(i, _):
        load(chunks + i).wait()

        @pl.when(i < chunks - 1)
        def _():
            load(chunks + i + 1).start()

        w = w_s.at[lax.rem(chunks + i, 2)]
        d_pre = (dot_nt(w[:, width:], d_out) * slope_s[chunk(i), :]).astype(BF16)
        pre_s[chunk(i), :] = d_pre
        acc[...] += dot_tn(d_pre, w[:, :width])
        return 0

    lax.fori_loop(0, chunks, backward, 0)
    returned(1)

    def store(i):
        slot = lax.rem(i, 2)
        return pltpu.make_async_copy(g_s.at[slot], g_ref.at[chunk(i)], g_sem.at[slot])

    def gradients(i, _):
        @pl.when(i >= 2)
        def _():
            store(i - 2).wait()

        g = g_s.at[lax.rem(i, 2)]
        g[:, :width] = dot_nn(pre_s[chunk(i), :], got[0].reshape(slots, width)).astype(BF16)
        g[:, width:] = dot_nn(act_s[chunk(i), :], got[1].reshape(slots, width)).astype(BF16)
        store(i).start()
        return 0

    lax.fori_loop(0, chunks, gradients, 0)
    store(chunks - 2).wait()
    store(chunks - 1).wait()
    for h in range(2):
        pltpu.make_async_copy(out_s.at[h, mine], r_ref.at[h, mine], own2.at[h]).wait()
    for copy in sent[: 2 * len(mates)]:
        copy.wait_send()
    for copy in sent[2 * len(mates) :]:
        copy.wait()
    combine_kernel(
        experts, r_ref, match_s, h1_s, n2_s, up_s, cols_s, gain, router,
        layer_s, dh_s, dmix_s, router_o, gain_o, sums_o,
    )
    leaving = [
        pltpu.make_async_copy(src, dst, leave_sem.at[i])
        for i, (src, dst) in enumerate(((dmix_s, dmix_o), (dh_s, dh_o), (layer_s, layer_o)))
    ]
    for copy in leaving:
        copy.start()
    for copy in leaving:
        copy.wait()


def middle(experts, mix_part, tok, gains, router, route, keep, grad, w, chunks, cid, us):
    group = lax.axis_size("wa")
    units = w.shape[0]
    length, width = tok.shape
    slots = experts * (length // 2)
    block = units // chunks
    dma = pltpu.SemaphoreType.DMA
    hbm = pl.BlockSpec(memory_space=pltpu.HBM)
    vmem = pl.BlockSpec(memory_space=pltpu.VMEM)
    anywhere = pl.BlockSpec(memory_space=pl.ANY)
    two = dma((2, group - 1))
    one = dma((group - 1,))
    rows = pltpu.VMEM((2, group, slots // group, width), BF16)
    shapes = [
        (w.shape, BF16), ((length, width), F32), ((length, width), F32), ((length, width), BF16),
        ((LANE, width), F32), ((1, width), F32), ((SEG, LANE), F32), ((SEG, LANE), F32),
    ]
    return pl.pallas_call(
        functools.partial(middle_kernel, experts, group, chunks),
        out_shape=[jax.ShapeDtypeStruct(shape, dtype) for shape, dtype in shapes],
        in_specs=[anywhere] + [vmem] * 6 + [hbm],
        out_specs=[hbm] + [anywhere] * 3 + [vmem] * 4,
        scratch_shapes=[
            pltpu.VMEM((length, width), F32), pltpu.VMEM((length, width), F32),
            pltpu.VMEM((length, width), BF16), dma((3,)),
            pltpu.VMEM(mix_part.shape, BF16),
            pltpu.VMEM((length, width), F32),
            pltpu.VMEM((length, width), BF16),
            pltpu.VMEM((length, width), F32),
            pltpu.VMEM((length, LANE), F32),
            pltpu.VMEM((length, slots), BF16),
            rows, rows, rows,
            pltpu.VMEM((2, block, 2 * width), BF16),
            pltpu.VMEM((2, block, 2 * width), BF16),
            pltpu.VMEM((units, slots), BF16),
            pltpu.VMEM((units, slots), F32),
            pltpu.VMEM((units, slots), BF16),
            pltpu.VMEM((slots, width), F32),
            rows,
            dma((2,)), dma((2,)),
            one, one, dma, two, two, dma((2,)), two, two, dma((2,)),
        ],
        compiler_params=pltpu.CompilerParams(
            collective_id=cid, has_side_effects=True, vmem_limit_bytes=VMEM_LIMIT + 20 * 2**20
        ),
        cost_estimate=lasting(us),
        name="middle",
    )(mix_part, tok, gains, router, route, keep, grad, w)


def combine_kernel(
    experts, back, match, h1_i, n2, up_i, cols, gain, router,
    out_o, dh_o, dmix_o, router_o, gain_o, sums_o,
):
    length, width = h1_i.shape
    h1, up = h1_i[...], up_i[...]
    lane = lax.broadcasted_iota(jnp.int32, (length, LANE), 1)
    facts = cols[...]

    def column(at):
        return jnp.sum(jnp.where(lane == at, facts, 0.0), axis=1, keepdims=True)

    gates, slope = column(experts), column(experts + 1)
    onehot = jnp.where(lane < experts, facts, 0.0)
    slots = match.shape[1]
    rows = dot_nn(match[...], back[0].reshape(slots, width))
    moe = gates * rows
    result = h1 + moe
    out_o[...] = result
    d_gate = jnp.sum(rows * up, axis=1, keepdims=True)
    d_logits = (onehot * (d_gate * slope)).astype(BF16)
    router_o[...] = dot_tn(d_logits, n2[...])
    d_n2 = dot_nn(match[...], back[1].reshape(slots, width)) + dot_nn(d_logits, router[...])
    d_norm, terms = norm_grads(h1, rms_scale(h1), gain[1:2], d_n2)
    gain_o[...] = jnp.sum(terms, axis=0, keepdims=True)
    d_h1 = up + d_norm
    dh_o[...] = d_h1
    dmix_o[...] = d_h1.astype(BF16)
    sums_o[0:1] = jnp.broadcast_to(jnp.sum(result * result, keepdims=True), (1, LANE))
    sums_o[1:2] = jnp.broadcast_to(jnp.sum(moe * moe, keepdims=True), (1, LANE))


def gate_back_kernel(
    states, c_at, d_mix, wout, y, z, uf, proj, step_i, cut, a_ref,
    dy_o, dz_o, skip_o, fx_ref, tx_ref, fd_o, cb, st_s, fd_s,
):
    length, width = step_i.shape[1:]
    groups, steps = width // LANE, length // SEG
    d_gated = dot_nt(d_mix[0], wout[...])
    zf = z[0].astype(F32)
    dy = d_gated * (zf * jax.nn.sigmoid(zf))
    dy_o[0] = dy
    dz_o[0, :length] = (d_gated * y[0] * silu_slope(zf)).astype(BF16)
    dz_o[0, length:] = jnp.zeros((EDGE, width), BF16)

    @pl.when(pl.program_id(0) == 0)
    def _():
        skip_o[...] = jnp.zeros_like(skip_o)

    skip_o[...] += jnp.sum(dy * uf[0], axis=0, keepdims=True)
    cb[...] = spread(proj[0], states, c_at)
    for g in range(groups):
        cols = slice(g * LANE, (g + 1) * LANE)
        st_s[:, cols] = step_i[0, :, cols] + cut[0]
    zero = jnp.zeros((SEG, LANE), F32)
    seg = seg_of()

    def group(g, _):
        lanes = lanes_of(g)
        a = [wide(a_ref, n, lanes) for n in range(states)]

        def step(lap, carry):
            rows = rows_of(steps - 1 - lap)
            st = st_s[rows, lanes]
            d = dy_o[0, rows, lanes]
            new = [carry[0] + st]
            for n in range(states):
                new.append(jnp.exp(st * a[n]) * (carry[n + 1] + cb[rows, state_cols(n)] * d))
            return tuple(new)

        out = lax.fori_loop(0, steps, step, (zero,) * (states + 1), unroll=8)
        total, f = out[0], list(out[1:])
        for k in (1, 2, 4):
            ok = seg < SEG - k
            for n in range(states):
                f[n] = f[n] + jnp.where(ok, jnp.exp(total * a[n]) * rolled(f[n], -k), 0.0)
            total = total + jnp.where(ok, rolled(total, -k), 0.0)
        ok = seg < SEG - 1
        tx_ref[0, :, lanes] = jnp.where(ok, rolled(total, -1), 0.0)
        for n in range(states):
            fx_ref[0, n, :, lanes] = jnp.where(ok, rolled(f[n], -1), 0.0)
            fd_s[pl.ds(n, 1), lanes] = f[n][0:1]
        return 0

    lax.fori_loop(0, groups, group, 0)
    fd_o[0] = fd_s[...].astype(BF16)


def scan_back_kernel(
    states, b_at, proj, step_i, sig, uf, cut, dy_i, a_ref, skip, wdt, hx_ref, sx_ref, e_i,
    fx_ref, tx_ref, finals, sums, g_ref, p_ref,
    part_o, du_o, dt_o, bias_o, ga_ref, g_o,
    bb, cb, dec, pri, accb, accc, st_s, dr_s, ds_s, out_s,
    from_pair, kept, came, load, ctx_s, ctx_r,
):
    ring = finals.shape[0]
    half = ring // 2
    _, chip, lane, _, peers = neighbours(ring)
    own_half = pltpu.make_async_copy(g_ref.at[:, lane], kept, load.at[0])
    pair_half = pltpu.make_async_copy(p_ref, from_pair, load.at[1])
    targets = [lax.rem(chip + k, half) for k in range(1, half)]
    scattered = [
        remote(kept.at[to], came.at[k], ctx_s.at[k], ctx_r.at[k], {"ctx": who})
        for k, (to, who) in enumerate(zip(targets, peers))
    ]
    at = pl.program_id(0)

    @pl.when(at == 0)
    def _():
        own_half.start()
        pair_half.start()
        barrier = pltpu.get_barrier_semaphore()
        for who in peers:
            hello(barrier, "ctx", who)
        pl.semaphore_wait(barrier, half - 1)
        own_half.wait()
        pair_half.wait()
        for to, copy in zip(targets, scattered):
            add_rows(kept.at[to], [kept.at[to], from_pair.at[to]], kept.shape[1])
            copy.start()
        add_rows(kept.at[chip], [kept.at[chip], from_pair.at[chip]], kept.shape[1])

    @pl.when(at == pl.num_programs(0) - 1)
    def _():
        for copy in scattered:
            copy.wait()
        add_rows(g_o, [kept.at[chip]] + [came.at[k] for k in range(half - 1)], kept.shape[1])

    length, width = step_i.shape[1:]
    groups, steps = width // LANE, length // SEG
    bb[...] = spread(proj[0], states, b_at)
    cb[...] = spread(proj[0], states, b_at + states)
    accb[...] = jnp.zeros_like(accb)
    accc[...] = jnp.zeros_like(accc)
    entering(out_s, finals, sums, a_ref, lax.axis_index("ctx"), False)
    e_ref = e_i.at[0]
    dr_s[...] = step_i[0] * uf[0]
    for g in range(groups):
        cols = slice(g * LANE, (g + 1) * LANE)
        st_s[:, cols] = step_i[0, :, cols] + cut[0]

    @pl.when(pl.program_id(0) == 0)
    def _():
        ga_ref[...] = jnp.zeros_like(ga_ref)
        dt_o[...] = jnp.zeros_like(dt_o)
        bias_o[...] = jnp.zeros_like(bias_o)

    def group(g, _):
        lanes = lanes_of(g)
        a = [wide(a_ref, n, lanes) for n in range(states)]
        sx = sx_ref[0, :, lanes]
        first = tuple(
            jnp.exp(sx * a[n]) * wide(e_ref, n, lanes) + hx_ref[0, n, :, lanes]
            for n in range(states)
        )

        def ahead(j, h):
            rows = rows_of(j)
            st = st_s[rows, lanes]
            dr = dr_s[rows, lanes]
            new = []
            for n in range(states):
                decay = jnp.exp(st * a[n])
                dec[rows, state_cols(n)] = decay
                pri[rows, state_cols(n)] = h[n]
                new.append(decay * h[n] + bb[rows, state_cols(n)] * dr)
            return tuple(new)

        last = lax.fori_loop(0, steps, ahead, first, unroll=8)
        end = rows_of(steps)
        for n in range(states):
            pri[end, state_cols(n)] = last[n]
        tx = tx_ref[0, :, lanes]
        flow = tuple(
            jnp.exp(tx * a[n]) * wide(out_s, n, lanes) + fx_ref[0, n, :, lanes]
            for n in range(states)
        )
        gain = wide(skip, 1, lanes)

        def back(lap, f):
            j = steps - 1 - lap
            rows = rows_of(j)
            after = rows_of(j + 1)
            st = step_i[0, rows, lanes]
            dr = dr_s[rows, lanes]
            dy = dy_i[0, rows, lanes]
            new = []
            d_step = None
            d_drive = None
            for n in range(states):
                cols = state_cols(n)
                d = f[n] + cb[rows, cols] * dy
                accc[rows, cols] += pri[after, cols] * dy
                accb[rows, cols] += d * dr
                flowing = dec[rows, cols] * d
                new.append(flowing)
                d_log = flowing * pri[rows, cols]
                ga_ref[n, :, lanes] += d_log * st
                part = d_log * a[n]
                d_step = part if d_step is None else d_step + part
                part = d * bb[rows, cols]
                d_drive = part if d_drive is None else d_drive + part
            ds_s[rows, lanes] = (d_step + d_drive * uf[0, rows, lanes]) * sig[0, rows, lanes]
            du_o[0, rows, lanes] = d_drive * st + dy * gain
            return tuple(new)

        lax.fori_loop(0, steps, back, flow, unroll=8)
        return 0

    lax.fori_loop(0, groups, group, 0)
    d_pre = ds_s[...]
    bias_o[...] += jnp.sum(d_pre, axis=0, keepdims=True)
    d_pre = d_pre.astype(BF16)
    dt_o[...] += dot_tn(proj[0], d_pre)
    columns = part_o.shape[2]
    part = dot_nt(d_pre, wdt[...])
    part = part + collected(accb[...], states, columns, b_at)
    part = part + collected(accc[...], states, columns, b_at + states)
    part_o[0] = part.astype(BF16)


def conv_back_kernel(
    taps, documents, place_ref, doc_ref, proj_i, wproj, du, pre, ext, u, conv, dz, wx, wz, n1,
    dx_o, dn_o, gconv_o, gx_o, gain_o, dext,
):
    length, width = du.shape[1:]
    steps = length // SEG
    behind = taps - 1

    @pl.when(pl.program_id(0) == 0)
    def _():
        gconv_o[...] = jnp.zeros_like(gconv_o)
        gx_o[...] = jnp.zeros_like(gx_o)
        gain_o[...] = jnp.zeros_like(gain_o)

    proj = proj_i[0]
    gx_o[...] += dot_tn(proj, u[0])
    d_u = dot_nn(proj, wproj[...]) + du[0]
    masks, _ = lag_masks(place_ref[0], doc_ref, documents, pl.program_id(0), length, taps)
    seg = seg_of()
    row = lax.broadcasted_iota(jnp.int32, (EDGE, LANE), 0)
    for g in range(width // LANE):
        cols = slice(g * LANE, (g + 1) * LANE)
        d = d_u[:, cols] * silu_slope(pre[0, :, cols])
        gconv_o[taps : taps + 1, cols] += jnp.sum(d, axis=0, keepdims=True)
        dext[...] = jnp.zeros_like(dext)
        for lag in range(taps):
            weighted = d if lag == 0 else d * masks[lag]
            at = pl.ds((behind - lag) * SEG, length)
            gconv_o[lag : lag + 1, cols] += jnp.sum(weighted * ext[0, at, cols], axis=0, keepdims=True)
            dext[at, :] += weighted * conv[lag : lag + 1, cols]
        before = jnp.zeros((EDGE, LANE), F32)
        for i in range(behind):
            head = dext[i * SEG : (i + 1) * SEG]
            j = pl.ds((steps + i) * SEG, SEG)
            dext[j, :] += jnp.where(seg < SEG - 1, rolled(head, -1), 0.0)
            first = jnp.broadcast_to(head[0:1], (EDGE, LANE))
            before = before + jnp.where(row == EDGE - behind + i, first, 0.0)
        dx_o[0, :length, cols] = dext[behind * SEG :].astype(BF16)
        dx_o[0, length:, cols] = before.astype(BF16)
    d_n1 = dot_nt(dx_o[0], wx[0]) + dot_nt(dz[0], wz[0])
    gain_o[...] += jnp.sum(d_n1 * n1[0].astype(F32), axis=0, keepdims=True)
    dn_o[0] = d_n1.astype(BF16)


SMEM = "smem"
ANY = "any"


def by_stream(shape, at=0):
    block = tuple(1 if i == at else n for i, n in enumerate(shape))
    rank = len(shape)

    def index(s):
        return tuple(s if i == at else 0 for i in range(rank))

    return pl.BlockSpec(block, index)


def whole(shape):
    return pl.BlockSpec(shape, lambda s: (0,) * len(shape))


def call(kernel, name, grid, args, outs, scratch, us, cid=None, limit=VMEM_LIMIT):
    arrays, specs = [], []
    for array, at in args:
        arrays.append(array)
        if at == SMEM:
            specs.append(pl.BlockSpec(memory_space=pltpu.SMEM))
        elif at == ANY:
            specs.append(pl.BlockSpec(memory_space=pl.ANY))
        elif callable(at):
            specs.append(at(array.shape))
        else:
            specs.append(whole(array.shape) if at is None else by_stream(array.shape, at))
    out_specs = []
    for shape, _, at in outs:
        if callable(at):
            out_specs.append(at(shape))
        else:
            out_specs.append(whole(shape) if at is None else by_stream(shape, at))
    return pl.pallas_call(
        kernel,
        grid=(grid,),
        out_shape=[jax.ShapeDtypeStruct(shape, dtype) for shape, dtype, _ in outs],
        in_specs=specs,
        out_specs=out_specs,
        scratch_shapes=scratch,
        compiler_params=pltpu.CompilerParams(
            vmem_limit_bytes=limit, collective_id=cid, has_side_effects=cid is not None
        ),
        cost_estimate=lasting(us),
        name=name,
    )(*arrays)


def padded_to(array, width, axis):
    pads = [(0, 0)] * array.ndim
    pads[axis] = (0, width - array.shape[axis])
    return jnp.pad(array, pads)


def up_to(n, multiple):
    return -(-n // multiple) * multiple


def body(
    tokens, out_grad, doc_starts, routes, keep_mask, norm_mix, w_in, conv_w, conv_b, w_x, w_dt,
    dt_bias, a_log, d_skip, w_out, norm_moe, w_router, w_up, w_down,
):
    group = lax.axis_size("wa")
    ring = lax.axis_size("ctx")
    mine = lax.axis_index("wa")
    place = lax.axis_index("ctx")
    length, width = tokens.shape[1:]
    taps, local = conv_w.shape
    states = a_log.shape[0]
    ranked = w_dt.shape[0]
    experts = w_router.shape[1]
    padded = up_to(local, LANE)
    columns = up_to(w_x.shape[1], LANE)
    steps = length // SEG
    rows = length + EDGE
    slots = experts * (length // 2)
    share = norm_mix.shape[0]
    order_vmem = pltpu.VMEM((width // LANE, length, LANE), F32)
    place_s = place.astype(jnp.int32).reshape(1)
    mine_s = mine.astype(jnp.int32).reshape(1)
    last_s = (place == ring - 1).astype(jnp.int32).reshape(1)
    f32_vmem = lambda *shape: pltpu.VMEM(shape, F32)

    (own_experts,) = call(
        pack_kernel, "pack", 1, [(w_up[0], None), (w_down[0], None)],
        [((w_down.shape[1], 2 * width), BF16, None)], [], 3, None, LARGE_LIMIT,
    )
    expert_w = lax.all_gather(own_experts, "ctx", axis=0, tiled=True)

    in_rows = up_to(-(-width // ring), 16)
    blank = ring * in_rows - width
    part_in = jnp.pad(w_in, ((0, blank), (0, 0))) if blank else w_in
    part_in = lax.dynamic_slice_in_dim(part_in, place * in_rows, in_rows, 0)
    halves = jnp.stack([part_in[:, :local], part_in[:, local:]], axis=0)
    halves = jnp.pad(halves, ((0, 0), (0, 0), (0, padded - local)))
    small = jnp.concatenate([conv_b, dt_bias, d_skip, norm_mix, norm_moe], axis=0).reshape(SEG, share)
    small = jnp.concatenate([small, jnp.pad(w_router.T, ((0, SEG - experts), (0, 0)))], axis=0)
    small = padded_to(small, up_to(share, LANE), 1)
    documents = doc_starts.shape[1]
    doc_tile = jnp.pad(doc_starts, ((0, SEG - 1), (0, LANE - documents)))
    all_rows, all_edges, smalls, docs, w_blocks = start(tokens[0], small, doc_tile, halves, 1)
    proj_in = w_blocks.reshape(2, ring * in_rows, padded)[:, :width]
    of_x = lambda shape: pl.BlockSpec((1,) + shape[1:], lambda i: (0, 0, 0))
    of_z = lambda shape: pl.BlockSpec((1,) + shape[1:], lambda i: (1, 0, 0))
    par = (SEG, padded)
    gains, router, wproj, wdt, wout, conv, vectors, a_mat = call(
        functools.partial(prepare_kernel, experts), "prepare", 1,
        [(smalls, None), (small, None), (w_x.T, None), (w_dt, None), (w_out, None), (conv_w, None),
         (a_log, None)],
        [((SEG, width), F32, None), ((LANE, width), BF16, None), ((columns, padded), BF16, None),
         ((columns, padded), BF16, None), ((padded, width), BF16, None), (par, F32, None),
         (par, F32, None), ((states, padded), F32, None)],
        [f32_vmem(2 * SEG, width)], 3,
    )

    vec = (group, length, padded)
    n1, ext, pre_conv, u_f, u, z, part, cut = call(
        functools.partial(enter_kernel, taps, documents), "enter", group,
        [(place_s, SMEM), (docs, SMEM), (all_rows, 0), (all_edges, 0), (gains, None),
         (proj_in, of_x), (proj_in, of_z), (conv, None), (wproj, None)],
        [((group, rows, width), BF16, 0), ((group, (taps - 1) * SEG + length, padded), F32, 0),
         (vec, F32, 0), (vec, F32, 0), (vec, BF16, 0), (vec, BF16, 0),
         ((group, length, columns), BF16, 0), ((group, length, LANE), F32, 0)],
        [], 8,
    )
    projected = sum_all(part, 2, 11)
    seg_states = (group, states, SEG, padded)
    seg_sums = (group, SEG, padded)
    dev_states = (group, states, padded)
    dev_sums = (group, 1, padded)
    spread_vmem = f32_vmem(length, states * LANE)
    lane_vmem = f32_vmem(length, padded)
    state_vmem = f32_vmem(states, padded)
    step_size, sig, h_in, s_in, h_dev, s_dev = call(
        functools.partial(summary_kernel, states, ranked), "scan_summary", group,
        [(projected, 0), (wdt, None), (vectors, None), (u_f, 0), (cut, 0), (a_mat, None)],
        [(vec, F32, 0), (vec, F32, 0), (seg_states, F32, 0),
         (seg_sums, F32, 0), (dev_states, BF16, 0), (dev_sums, F32, 0)],
        [spread_vmem, lane_vmem, lane_vmem, state_vmem], 10,
    )
    all_h, all_s = carry([h_dev, s_dev], 3, 10)
    y_full, gated, mix_part, e_in = call(
        functools.partial(output_kernel, states, ranked), "scan_output", group,
        [(place_s, SMEM), (projected, 0), (step_size, 0), (u_f, 0), (cut, 0), (a_mat, None), (h_in, 0),
         (s_in, 0), (all_h, 1), (all_s, 1), (z, 0), (vectors, None), (wout, None)],
        [(vec, F32, 0), (vec, BF16, 0), ((group, length, width), BF16, 0), (dev_states, F32, 0)],
        [spread_vmem, spread_vmem, lane_vmem, lane_vmem], 13,
    )

    row_f = (length, width)
    grad_experts, result, d_h1, d_mix_own, grad_router, grad_gain_moe, out_sums, mix_sum = middle(
        experts, mix_part, tokens[0], gains, router, routes[0].T, keep_mask, out_grad[0], expert_w, 8, 5, 85
    )
    share_experts = lax.psum_scatter(grad_experts, "ctx", scatter_dimension=0, tiled=True)
    (d_mix,) = gather_all([d_mix_own], "wa", 7, 28)

    d_y, d_z, grad_skip, f_in, t_in, f_dev = call(
        functools.partial(gate_back_kernel, states, ranked + states), "gate_back", group,
        [(d_mix, 0), (wout, None), (y_full, 0), (z, 0), (u_f, 0), (projected, 0), (step_size, 0),
         (cut, 0), (a_mat, None)],
        [(vec, F32, 0), ((group, rows, padded), BF16, 0), ((1, padded), F32, None),
         (seg_states, F32, 0), (seg_sums, F32, 0), (dev_states, BF16, 0)],
        [spread_vmem, lane_vmem, state_vmem], 11,
    )
    flat_n1 = n1.reshape(group * rows, width)
    zo_shape = (ring // 2, 2, in_rows, 2 * padded)
    (grad_zo,) = call(
        functools.partial(pack_zo_kernel, ring, in_rows, local), "pack_zo", 1,
        [(flat_n1, None), (d_z.reshape(group * rows, padded), None),
         (d_mix.reshape(group * length, width), None), (gated.reshape(group * length, padded), None)],
        [(zo_shape, BF16, None)], [], 5,
    )
    all_f, pair_zo = carry([f_dev], 8, 10, grad_zo)
    zo_half = pltpu.VMEM((ring // 2, in_rows, 2 * padded), BF16)
    dma = pltpu.SemaphoreType.DMA
    d_part, d_u, grad_dt, grad_step_bias, grad_a, chunk_zo = call(
        functools.partial(scan_back_kernel, states, ranked), "scan_back", group,
        [(projected, 0), (step_size, 0), (sig, 0), (u_f, 0), (cut, 0), (d_y, 0),
         (a_mat, None), (vectors, None), (wdt, None), (h_in, 0), (s_in, 0), (e_in, 0), (f_in, 0),
         (t_in, 0), (all_f, 1), (all_s, 1), (grad_zo, ANY), (pair_zo, ANY)],
        [((group, length, columns), BF16, 0), (vec, F32, 0), ((columns, padded), F32, None),
         ((1, padded), F32, None), ((states, SEG, padded), F32, None), ((in_rows, 2 * padded), BF16, None)],
        [spread_vmem, spread_vmem, spread_vmem, f32_vmem(length + SEG, states * LANE), spread_vmem,
         spread_vmem, lane_vmem, lane_vmem, lane_vmem, state_vmem,
         zo_half, zo_half, pltpu.VMEM((ring // 2 - 1, in_rows, 2 * padded), BF16),
         dma((2,)), dma((ring // 2 - 1,)), dma((ring // 2 - 1,))], 34, 12,
    )
    d_projected = sum_all(d_part, 9, 11)
    d_x, d_n1_part, grad_conv, grad_x, gain_terms = call(
        functools.partial(conv_back_kernel, taps, documents), "conv_back", group,
        [(place_s, SMEM), (docs, SMEM), (d_projected, 0), (wproj, None), (d_u, 0), (pre_conv, 0),
         (ext, 0), (u, 0), (conv, None), (d_z, 0), (proj_in, of_x), (proj_in, of_z), (n1, 0)],
        [((group, rows, padded), BF16, 0), ((group, rows, width), BF16, 0),
         ((SEG, padded), F32, None), ((columns, padded), F32, None), ((1, width), F32, None)],
        [f32_vmem((taps - 1) * SEG + length, LANE)], 10,
    )
    small_all = columns + up_to(ranked, SEG) + states + 3 * SEG
    small_each = up_to(-(-small_all // ring), SEG)
    small_rows = up_to(small_each, 16)
    (packed,) = call(
        functools.partial(pack_rest_kernel, ring, in_rows, small_rows, group, experts, ranked),
        "pack_rest", 1,
        [(mine_s, SMEM), (flat_n1, None), (d_x.reshape(group * rows, padded), None), (grad_x, None),
         (grad_dt, None), (grad_a, None), (a_mat, None), (grad_conv, None), (grad_step_bias, None),
         (grad_skip, None), (gain_terms, None), (gains, None), (grad_gain_moe, None),
         (grad_router, None), (out_sums, None), (mix_sum, None)],
        [((ring // 2, 2, in_rows + small_rows + 16, padded), BF16, None)],
        [f32_vmem(ring * small_each, padded), f32_vmem(SEG, width)], 5,
    )
    done, d_n1_terms, d_edges = finish(packed, chunk_zo, d_n1_part, in_rows, small_rows, 11)
    blocks = width // in_rows
    of_rows = lambda shape: pl.BlockSpec(
        (shape[0] // blocks, shape[1]), lambda i: (jnp.minimum(i, blocks - 1), 0)
    )
    unpacked = call(
        functools.partial(
            unpack_kernel, ring, group, in_rows, small_rows, experts, states, ranked, taps,
            float(length * ring * width),
        ),
        "unpack", ring,
        [(mine_s, SMEM), (done, 0), (share_experts, None), (last_s, SMEM), (d_n1_terms, None),
         (d_edges, None), (tokens[0], None), (gains, None), (d_h1, None), (result, None)],
        [((width, 2 * local), F32, of_rows), ((local, width), F32, of_rows),
         ((width, w_down.shape[1]), F32, None), ((w_down.shape[1], width), F32, None),
         ((taps, local), F32, None), ((w_x.shape[1], local), F32, None), ((ranked, local), F32, None),
         ((states, local), F32, None), ((2 * SEG, padded), F32, None), ((1, LANE), F32, None),
         (row_f, F32, None), (row_f, F32, None)],
        [f32_vmem(ring * small_each, padded), f32_vmem(SEG, padded), f32_vmem(length, width), order_vmem],
        9,
    )
    share_in, share_out, share_up, share_down, g_taps, g_wx, g_wdt, g_a, vecs, stats, input_grad, layer_out = unpacked
    fulls, vecs = vecs[:SEG, :share], vecs[SEG:, :local]
    return (
        layer_out[None],
        input_grad[None],
        fulls[0],
        share_in,
        g_taps,
        vecs[0],
        g_wx.T,
        g_wdt,
        vecs[1],
        g_a,
        vecs[2],
        share_out,
        fulls[1],
        fulls[2 : 2 + experts].T,
        share_up[None],
        share_down[None],
        stats[:, :3],
    )


def solution(mesh):
    placed = (
        P("wa", "ctx", None),
        P("wa", "ctx", None),
        P("wa", None),
        P("wa", "ctx", None),
        P("wa", "ctx"),
        P("wa"),
        P(None, "wa"),
        P(None, "wa"),
        P("wa"),
        P("wa", None),
        P(None, "wa"),
        P("wa"),
        P(None, "wa"),
        P("wa"),
        P("wa", None),
        P("wa"),
        P("wa", None),
        P("wa", None, "ctx"),
        P("wa", "ctx", None),
    )
    return jax.shard_map(
        body,
        mesh=mesh,
        in_specs=placed,
        out_specs=(
            P("wa", "ctx", None),
            P("wa", "ctx", None),
            P("wa"),
            P(None, "wa"),
            P(None, "wa"),
            P("wa"),
            P("wa", None),
            P(None, "wa"),
            P("wa"),
            P(None, "wa"),
            P("wa"),
            P("wa", None),
            P("wa"),
            P("wa", None),
            P("wa", None, "ctx"),
            P("wa", "ctx", None),
            P("wa", None),
        ),
        check_vma=False,
    )
```

```python
import functools

import jax
import jax.numpy as jnp
from jax import lax
from jax.experimental import pallas as pl
from jax.experimental.pallas import tpu as pltpu
from jax.sharding import PartitionSpec as P

EPS = 1e-05
F32 = jnp.float32
BF16 = jnp.bfloat16
SEG = 8
LANE = 128
EDGE = 16
CUT = 1e30
MESH = pl.DeviceIdType.MESH
VMEM_LIMIT = 24 * 2**20
LARGE_LIMIT = 60 * 2**20


def lasting(us):
    return pl.CostEstimate(
        flops=int(us * 1.1e9), bytes_accessed=int(us * 3.5e6), transcendentals=0
    )


def greet(axis, count):
    me = lax.axis_index(axis)
    barrier = pltpu.get_barrier_semaphore()
    for k in range(1, count):
        pl.semaphore_signal(
            barrier, inc=1, device_id={axis: lax.rem(me + k, count)}, device_id_type=MESH
        )
    pl.semaphore_wait(barrier, count - 1)
    return me


def gather_kernel(axis, count, arrays, *refs):
    srcs, dsts = refs[:arrays], refs[arrays : 2 * arrays]
    send, recv, own = refs[-3:]
    me = greet(axis, count)
    copies = []
    for i in range(arrays):
        for k in range(1, count):
            copy = pltpu.make_async_remote_copy(
                src_ref=srcs[i],
                dst_ref=dsts[i].at[me],
                send_sem=send.at[i, k],
                recv_sem=recv.at[i, k],
                device_id={axis: lax.rem(me + k, count)},
                device_id_type=MESH,
            )
            copy.start()
            copies.append(copy)
    for i in range(arrays):
        local = pltpu.make_async_copy(srcs[i], dsts[i].at[me], own.at[i])
        local.start()
        copies.append(local)
    for copy in copies:
        copy.wait()


def trade_kernel(axis, count, x_ref, o_ref, send, recv, own):
    me = greet(axis, count)
    copies = []
    for k in range(1, count):
        other = lax.rem(me + k, count)
        copy = pltpu.make_async_remote_copy(
            src_ref=x_ref.at[other],
            dst_ref=o_ref.at[me],
            send_sem=send.at[k],
            recv_sem=recv.at[k],
            device_id={axis: other},
            device_id_type=MESH,
        )
        copy.start()
        copies.append(copy)
    local = pltpu.make_async_copy(x_ref.at[me], o_ref.at[me], own)
    local.start()
    local.wait()
    for copy in copies:
        copy.wait()


def trade(x, axis, cid, us):
    count = lax.axis_size(axis)
    return pl.pallas_call(
        functools.partial(trade_kernel, axis, count),
        out_shape=jax.ShapeDtypeStruct(x.shape, x.dtype),
        in_specs=[pl.BlockSpec(memory_space=pl.ANY)],
        out_specs=pl.BlockSpec(memory_space=pl.ANY),
        scratch_shapes=[
            pltpu.SemaphoreType.DMA((count,)),
            pltpu.SemaphoreType.DMA((count,)),
            pltpu.SemaphoreType.DMA,
        ],
        compiler_params=pltpu.CompilerParams(
            collective_id=cid, has_side_effects=True, vmem_limit_bytes=VMEM_LIMIT
        ),
        cost_estimate=lasting(us),
        name=f"trade_{cid}",
    )(x)


def sum_start(mates, x_ref, got, send, recv):
    copies = []
    for k, who in enumerate(mates):
        copy = remote(x_ref.at[who], got.at[k], send.at[k], recv.at[k], {"wa": who})
        copy.start()
        copies.append(copy)
    return copies


def sum_spread(mine, mates, x_ref, got, o_ref, copies, send, recv):
    for copy in copies:
        copy.wait_recv()
    parts = [x_ref.at[mine]] + [got.at[k] for k in range(len(mates))]
    add_rows(o_ref.at[mine], parts, x_ref.shape[1])
    spreads = []
    for k, who in enumerate(mates):
        copy = remote(o_ref.at[mine], o_ref.at[mine], send.at[k], recv.at[k], {"wa": who})
        copy.start()
        spreads.append(copy)
    return spreads


def sum_all_kernel(group, x_ref, o_ref, got, s1, r1, s2, r2):
    greet("wa", group)
    mine, mates = mates_of(group)
    copies = sum_start(mates, x_ref, got, s1, r1)
    spreads = sum_spread(mine, mates, x_ref, got, o_ref, copies, s2, r2)
    for copy in spreads:
        copy.wait()
    for copy in copies:
        copy.wait_send()


def sum_all(x, cid, us):
    group = lax.axis_size("wa")
    vmem = pl.BlockSpec(memory_space=pltpu.VMEM)
    dma = pltpu.SemaphoreType.DMA
    return pl.pallas_call(
        functools.partial(sum_all_kernel, group),
        out_shape=jax.ShapeDtypeStruct(x.shape, x.dtype),
        in_specs=[vmem],
        out_specs=vmem,
        scratch_shapes=[pltpu.VMEM((group - 1,) + x.shape[1:], x.dtype)] + [dma((group - 1,))] * 4,
        compiler_params=pltpu.CompilerParams(
            collective_id=cid, has_side_effects=True, vmem_limit_bytes=VMEM_LIMIT
        ),
        cost_estimate=lasting(us),
        name="sum_all",
    )(x)


def gather_all(xs, axis, cid, us):
    count, arrays = lax.axis_size(axis), len(xs)
    return pl.pallas_call(
        functools.partial(gather_kernel, axis, count, arrays),
        out_shape=[jax.ShapeDtypeStruct((count,) + x.shape, x.dtype) for x in xs],
        in_specs=[pl.BlockSpec(memory_space=pl.ANY)] * arrays,
        out_specs=[pl.BlockSpec(memory_space=pl.ANY)] * arrays,
        scratch_shapes=[
            pltpu.SemaphoreType.DMA((arrays, count)),
            pltpu.SemaphoreType.DMA((arrays, count)),
            pltpu.SemaphoreType.DMA((arrays,)),
        ],
        compiler_params=pltpu.CompilerParams(
            collective_id=cid, has_side_effects=True, vmem_limit_bytes=VMEM_LIMIT
        ),
        cost_estimate=lasting(us),
        name=f"gather_{cid}",
    )(*xs)


def remote(src, dst, send, recv, where):
    return pltpu.make_async_remote_copy(
        src_ref=src, dst_ref=dst, send_sem=send, recv_sem=recv,
        device_id=where, device_id_type=MESH,
    )


def add_rows(out, parts, rows):
    def one(i, _):
        at = pl.ds(pl.multiple_of(i * 16, 16), 16)
        total = parts[0][at, :].astype(F32)
        for part in parts[1:]:
            total = total + part[at, :].astype(F32)
        out[at, :] = total.astype(out.dtype)
        return 0

    lax.fori_loop(0, rows // 16, one, 0)


def neighbours(ring):
    me = lax.axis_index("ctx")
    half = ring // 2
    lane = lax.rem(me, 2)
    chip = me // 2
    peers = [lax.rem(chip + k, half) * 2 + lane for k in range(1, half)]
    return me, chip, lane, me + 1 - 2 * lane, peers


def mates_of(group):
    mine = lax.axis_index("wa")
    return mine, [lax.rem(mine + k, group) for k in range(1, group)]


def hello(barrier, axis, who):
    pl.semaphore_signal(barrier, inc=1, device_id={axis: who}, device_id_type=MESH)


def carry_kernel(ring, arrays, halved, *refs):
    total = arrays + halved
    srcs, dsts = refs[:total], refs[total : 2 * total]
    send, recv, fwd_s, fwd_r, own, half_s, half_r = refs[2 * total :]
    me, chip, lane, pair, peers = neighbours(ring)
    half = ring // 2
    barrier = pltpu.get_barrier_semaphore()
    for who in [pair] + peers:
        hello(barrier, "ctx", who)
    pl.semaphore_wait(barrier, half)
    copies, forwards, local = [], [], []
    for i in range(arrays):
        for k, who in enumerate(peers):
            copies.append(remote(srcs[i], dsts[i].at[me], send.at[i, k], recv.at[i, k], {"ctx": who}))
            copies[-1].start()
    for i in range(arrays):
        forwards.append(remote(srcs[i], dsts[i].at[me], fwd_s.at[i, 0], fwd_r.at[i, 0], {"ctx": pair}))
        forwards[-1].start()
        local.append(pltpu.make_async_copy(srcs[i], dsts[i].at[me], own.at[i]))
        local[-1].start()
    if halved:
        to_pair = remote(srcs[arrays].at[:, 1 - lane], dsts[arrays], half_s, half_r, {"ctx": pair})
        to_pair.start()
        local.append(to_pair)
    for i in range(arrays):
        for k in range(1, half):
            copies[i * (half - 1) + k - 1].wait_recv()
            block = dsts[i].at[lax.rem(chip + half - k, half) * 2 + lane]
            forwards.append(remote(block, block, fwd_s.at[i, k], fwd_r.at[i, k], {"ctx": pair}))
            forwards[-1].start()
    for copy in copies:
        copy.wait_send()
    for copy in forwards + local:
        copy.wait()


def carry(xs, cid, us, halved=None):
    ring, arrays = lax.axis_size("ctx"), len(xs)
    half = ring // 2
    shapes = [((ring,) + x.shape, x.dtype) for x in xs]
    if halved is not None:
        xs = xs + [halved]
        shapes.append((halved.shape[:1] + halved.shape[2:], halved.dtype))
    hbm = pl.BlockSpec(memory_space=pl.ANY)
    dma = pltpu.SemaphoreType.DMA
    return pl.pallas_call(
        functools.partial(carry_kernel, ring, arrays, len(xs) - arrays),
        out_shape=[jax.ShapeDtypeStruct(shape, dtype) for shape, dtype in shapes],
        in_specs=[hbm] * len(xs),
        out_specs=[hbm] * len(xs),
        scratch_shapes=[
            dma((arrays, half - 1)), dma((arrays, half - 1)), dma((arrays, half)), dma((arrays, half)),
            dma((arrays,)), dma, dma,
        ],
        compiler_params=pltpu.CompilerParams(
            collective_id=cid, has_side_effects=True, vmem_limit_bytes=VMEM_LIMIT
        ),
        cost_estimate=lasting(us),
        name=f"carry_{cid}",
    )(*xs)


def finish_kernel(
    ring, group, in_rows, small_rows,
    g_ref, zf_ref, d_ref, o_ref, dt_ref, de_ref,
    from_pair, paired, came, own, zin, tiles, fin, store_s,
    pair_s, pair_r, ctx_s, ctx_r, z_s, z_r, tile_s, tile_r, d_s, d_r, d_own, last_s, last_r, fwd_s, fwd_r,
    edge_s, edge_r,
):
    me, chip, lane, pair, peers = neighbours(ring)
    mine, mates = mates_of(group)
    half = ring // 2
    rows = in_rows + small_rows + 16
    lanes = g_ref.shape[3]
    barrier = pltpu.get_barrier_semaphore()
    for who in [pair] + peers:
        hello(barrier, "ctx", who)
    for who in mates:
        hello(barrier, "wa", who)
    has_next = me < ring - 1
    has_last = me > 0

    @pl.when(has_next)
    def _():
        hello(barrier, "ctx", me + 1)

    @pl.when(has_last)
    def _():
        hello(barrier, "ctx", me - 1)

    around = jnp.where(has_next, 1, 0) + jnp.where(has_last, 1, 0)
    pl.semaphore_wait(barrier, half + group - 1 + around)

    to_pair = remote(g_ref.at[:, 1 - lane], from_pair, pair_s, pair_r, {"ctx": pair})
    to_pair.start()
    small_at = 2 * in_rows + 16
    parts = [
        pl.ds(small_at + small_rows, in_rows), pl.ds(small_at, small_rows),
        pl.ds(0, in_rows), pl.ds(in_rows, in_rows + 16),
    ]
    fin[parts[0]] = zf_ref[:, lanes:]
    stored = []

    def to_all(i):
        src, dst = fin.at[parts[i]], o_ref.at[me, parts[i]]
        copies = []
        for k, who in enumerate(peers):
            copies.append(remote(src, dst, last_s.at[i, k], last_r.at[i, k], {"ctx": who}))
        copies.append(remote(src, dst, fwd_s.at[i, 0], fwd_r.at[i, 0], {"ctx": pair}))
        for copy in copies:
            copy.start()
        stored.append(pltpu.make_async_copy(src, dst, store_s.at[i]))
        stored[-1].start()
        return copies

    def forward(i, copies):
        for k in range(1, half):
            copies[k - 1].wait_recv()
            source = lax.rem(chip + half - k, half) * 2 + lane
            block = o_ref.at[source, parts[i]]
            copy = remote(block, block, fwd_s.at[i, k], fwd_r.at[i, k], {"ctx": pair})
            copy.start()
            copies.append(copy)

    x_to = mine // 2
    z_to = group // 2 + mine // 2
    slot = lax.rem(mine, 2)
    z_ref = zf_ref.at[:, pl.ds(0, lanes)]
    x_ref = own.at[pl.ds(0, in_rows)]
    send_x = remote(x_ref, zin.at[slot], z_s.at[0], z_r.at[slot], {"wa": x_to})
    send_z = remote(z_ref, zin.at[slot], z_s.at[1], z_r.at[slot], {"wa": z_to})
    keep_x = pltpu.make_async_copy(x_ref, zin.at[slot], z_r.at[slot])
    keep_z = pltpu.make_async_copy(z_ref, zin.at[slot], z_r.at[slot])

    @pl.when(z_to != mine)
    def _():
        send_z.start()

    @pl.when(z_to == mine)
    def _():
        keep_z.start()

    cut = d_ref.shape[1] // 32 * 16
    pieces = [pl.ds(0, cut), pl.ds(cut, d_ref.shape[1] - cut)]
    trades = []

    def trade_rows(i):
        for k, who in enumerate(mates):
            copy = remote(
                d_ref.at[who, pieces[i]], dt_ref.at[mine, pieces[i]], d_s.at[i, k], d_r.at[i, k],
                {"wa": who},
            )
            copy.start()
            trades.append(copy)

    trade_rows(0)
    kept = pltpu.make_async_copy(d_ref.at[mine], dt_ref.at[mine], d_own)
    kept.start()

    to_pair.wait_recv()
    scattered = []
    for k, who in enumerate(peers):
        to = lax.rem(chip + k + 1, half)
        add_rows(paired.at[to], [g_ref.at[to, lane], from_pair.at[to]], rows)
        copy = remote(paired.at[to], came.at[k], ctx_s.at[k], ctx_r.at[k], {"ctx": who})
        copy.start()
        scattered.append(copy)
    early = to_all(0)
    add_rows(paired.at[chip], [g_ref.at[chip, lane], from_pair.at[chip]], rows)
    for copy in scattered:
        copy.wait_recv()
    add_rows(own, [paired.at[chip]] + [came.at[k] for k in range(half - 1)], rows)

    @pl.when(x_to != mine)
    def _():
        send_x.start()

    @pl.when(x_to == mine)
    def _():
        keep_x.start()

    tile = pl.ds(in_rows + small_rows, 16)
    spread_tiles = []
    for k, who in enumerate(mates):
        copy = remote(own.at[tile], tiles.at[k], tile_s.at[k], tile_r.at[k], {"wa": who})
        copy.start()
        spread_tiles.append(copy)
    fin[parts[1]] = own[pl.ds(in_rows, small_rows)]
    middle_rows = to_all(1)
    forward(0, early)

    def landed(slot):
        pltpu.make_async_copy(zin.at[slot], zin.at[slot], z_r.at[slot]).wait()
        fin[pl.ds(slot * in_rows, in_rows)] = zin[slot]

    landed(0)
    late = [to_all(2)]
    forward(1, middle_rows)
    for copy in spread_tiles:
        copy.wait_recv()
    add_rows(
        fin.at[pl.ds(2 * in_rows, 16)],
        [own.at[tile]] + [tiles.at[k] for k in range(group - 1)],
        16,
    )
    landed(1)
    late.append(to_all(3))
    trade_rows(1)
    kept.wait()
    forward(2, late[0])
    forward(3, late[1])

    for copy in trades:
        copy.wait_recv()
    edges = dt_ref.at[:, pl.ds(d_ref.shape[1] - EDGE, EDGE)]
    to_last = remote(edges, de_ref, edge_s, edge_r, {"ctx": me - 1})

    @pl.when(has_last)
    def _():
        to_last.start()

    for copies in [early, middle_rows] + late:
        for copy in copies[half - 1 :]:
            copy.wait_recv()

    for copy in stored:
        copy.wait()
    to_pair.wait_send()
    for copy in scattered + spread_tiles + early + middle_rows + late[0] + late[1] + trades:
        copy.wait_send()

    @pl.when(x_to != mine)
    def _():
        send_x.wait_send()

    @pl.when(z_to != mine)
    def _():
        send_z.wait_send()

    @pl.when(has_last)
    def _():
        to_last.wait_send()

    @pl.when(has_next)
    def _():
        to_last.wait_recv()


def finish(g, zf, d, in_rows, small_rows, cid):
    ring, group = lax.axis_size("ctx"), lax.axis_size("wa")
    half = ring // 2
    rows, lanes = g.shape[2:]
    out_rows = 3 * in_rows + small_rows + 16
    vmem = pl.BlockSpec(memory_space=pltpu.VMEM)
    hbm = pl.BlockSpec(memory_space=pl.ANY)
    dma = pltpu.SemaphoreType.DMA
    return pl.pallas_call(
        functools.partial(finish_kernel, ring, group, in_rows, small_rows),
        out_shape=[
            jax.ShapeDtypeStruct((ring, out_rows, lanes), BF16),
            jax.ShapeDtypeStruct(d.shape, d.dtype),
            jax.ShapeDtypeStruct((group, EDGE, d.shape[2]), d.dtype),
        ],
        in_specs=[vmem, vmem, hbm],
        out_specs=[hbm, hbm, hbm],
        scratch_shapes=[
            pltpu.VMEM((half, rows, lanes), BF16),
            pltpu.VMEM((half, rows, lanes), BF16),
            pltpu.VMEM((half - 1, rows, lanes), BF16),
            pltpu.VMEM((rows, lanes), BF16),
            pltpu.VMEM((2, in_rows, lanes), BF16),
            pltpu.VMEM((group - 1, 16, lanes), BF16),
            pltpu.VMEM((out_rows, lanes), BF16),
            dma((4,)), dma, dma,
            dma((half - 1,)), dma((half - 1,)),
            dma((2,)), dma((2,)),
            dma((group - 1,)), dma((group - 1,)),
            dma((2, group - 1)), dma((2, group - 1)), dma,
            dma((4, half - 1)), dma((4, half - 1)),
            dma((4, half)), dma((4, half)),
            dma, dma,
        ],
        compiler_params=pltpu.CompilerParams(
            collective_id=cid, has_side_effects=True, vmem_limit_bytes=VMEM_LIMIT
        ),
        cost_estimate=lasting(60),
        name="finish",
    )(g, zf, d)


def start_kernel(
    ring, group, tok, par, doc, w_ref, tok_o, edge_o, par_o, doc_o, w_o,
    mate_s, mate_r, own_s, edge_s, edge_r, relay_s, relay_r, shift_s, shift_r, out_s, out_r, fwd_s, fwd_r,
):
    me = lax.axis_index("ctx")
    mine = lax.axis_index("wa")
    half = ring // 2
    lane = lax.rem(me, 2)
    chip = me // 2
    pair = me + 1 - 2 * lane
    peers = [lax.rem(chip + k, half) * 2 + lane for k in range(1, half)]
    mates = [lax.rem(mine + k, group) for k in range(1, group)]
    barrier = pltpu.get_barrier_semaphore()
    for who in [pair] + peers:
        pl.semaphore_signal(barrier, inc=1, device_id={"ctx": who}, device_id_type=MESH)
    for who in mates:
        pl.semaphore_signal(barrier, inc=1, device_id={"wa": who}, device_id_type=MESH)
    has_next = me < ring - 1
    has_last = me > 0

    @pl.when(has_next)
    def _():
        pl.semaphore_signal(barrier, inc=1, device_id={"ctx": me + 1}, device_id_type=MESH)

    @pl.when(has_last)
    def _():
        pl.semaphore_signal(barrier, inc=1, device_id={"ctx": me - 1}, device_id_type=MESH)

    around = jnp.where(has_next, 1, 0) + jnp.where(has_last, 1, 0)
    pl.semaphore_wait(barrier, half + group - 1 + around)

    edge = tok.at[pl.ds(tok.shape[0] - EDGE, EDGE)]
    to_next = remote(edge, edge_o.at[mine], edge_s, edge_r, {"ctx": me + 1})

    @pl.when(has_next)
    def _():
        to_next.start()

    kind = mine // (group // 2)
    base = 2 * lax.rem(mine, group // 2)
    for h in range(2):
        where = base + h
        send = remote(
            w_ref.at[h], w_o.at[kind, me], shift_s.at[h], shift_r.at[kind], {"wa": where}
        )
        keep = pltpu.make_async_copy(w_ref.at[h], w_o.at[kind, me], shift_r.at[kind])

        @pl.when(where != mine)
        def _():
            send.start()

        @pl.when(where == mine)
        def _():
            keep.start()

    trades = []
    for i, (src, dst) in enumerate(((par, par_o), (doc, doc_o), (tok, tok_o))):
        for k, who in enumerate(mates):
            copy = remote(src, dst.at[mine], mate_s.at[i, k], mate_r.at[i, k], {"wa": who})
            copy.start()
            trades.append(copy)
        keep = pltpu.make_async_copy(src, dst.at[mine], own_s.at[i])
        keep.start()

    @pl.when(has_last)
    def _():
        to_next.wait_recv()
        for k, who in enumerate(mates):
            remote(
                edge_o.at[mine], edge_o.at[mine], relay_s.at[k], relay_r.at[k], {"wa": who}
            ).start()

    sends = []
    for t in range(2):
        block = w_o.at[t, me]
        pltpu.make_async_copy(block, block, shift_r.at[t]).wait()
        for k, who in enumerate(peers):
            copy = remote(block, block, out_s.at[t, k], out_r.at[t, k], {"ctx": who})
            copy.start()
            sends.append(copy)
        copy = remote(block, block, fwd_s.at[t, 0], fwd_r.at[t, 0], {"ctx": pair})
        copy.start()
        sends.append(copy)
    forwards = []
    for t in range(2):
        for k in range(1, half):
            source = lax.rem(chip + half - k, half) * 2 + lane
            block = w_o.at[t, source]
            pltpu.make_async_copy(block, block, out_r.at[t, k - 1]).wait()
            copy = remote(block, block, fwd_s.at[t, k], fwd_r.at[t, k], {"ctx": pair})
            copy.start()
            forwards.append(copy)
    for t in range(2):
        for k in range(half):
            pltpu.make_async_copy(w_o.at[t, me], w_o.at[t, me], fwd_r.at[t, k]).wait()
    for copy in sends + forwards:
        copy.wait_send()
    for h in range(2):

        @pl.when(base + h != mine)
        def _():
            remote(
                w_ref.at[h], w_o.at[kind, me], shift_s.at[h], shift_r.at[kind], {"wa": mine}
            ).wait_send()

    for copy in trades:
        copy.wait()
    for i, (src, dst) in enumerate(((par, par_o), (doc, doc_o), (tok, tok_o))):
        pltpu.make_async_copy(src, dst.at[mine], own_s.at[i]).wait()

    @pl.when(has_next)
    def _():
        to_next.wait_send()

    @pl.when(has_last)
    def _():
        for k, who in enumerate(mates):
            remote(
                edge_o.at[mine], edge_o.at[mine], relay_s.at[k], relay_r.at[k], {"wa": who}
            ).wait()


def start(tok, par, doc, halves, cid):
    ring, group = lax.axis_size("ctx"), lax.axis_size("wa")
    half = ring // 2
    hbm = pl.BlockSpec(memory_space=pl.ANY)
    dma = pltpu.SemaphoreType.DMA
    outs = [(group,) + a.shape for a in (tok, tok[:EDGE], par, doc)] + [(2, ring) + halves.shape[1:]]
    types = [a.dtype for a in (tok, tok, par, doc, halves)]
    return pl.pallas_call(
        functools.partial(start_kernel, ring, group),
        out_shape=[jax.ShapeDtypeStruct(s, t) for s, t in zip(outs, types)],
        in_specs=[hbm] * 4,
        out_specs=[hbm] * 5,
        scratch_shapes=[
            dma((3, group - 1)), dma((3, group - 1)), dma((3,)),
            dma, dma,
            dma((group - 1,)), dma((group - 1,)),
            dma((2,)), dma((2,)),
            dma((2, half - 1)), dma((2, half - 1)),
            dma((2, half)), dma((2, half)),
        ],
        compiler_params=pltpu.CompilerParams(
            collective_id=cid, has_side_effects=True, vmem_limit_bytes=VMEM_LIMIT
        ),
        cost_estimate=lasting(35),
        name="start",
    )(tok, par, doc, halves)


def pick(rows, states, at):
    shape = (rows, states * LANE)
    lower = (lax.broadcasted_iota(jnp.int32, shape, 0) - at) * LANE
    place = lax.broadcasted_iota(jnp.int32, shape, 1)
    return jnp.where((place >= lower) & (place < lower + LANE), 1.0, 0.0)


def spread(rows, states, at):
    return jnp.dot(rows, pick(rows.shape[1], states, at).astype(BF16), preferred_element_type=F32)


def collected(wide_rows, states, columns, at):
    shape = (states * LANE, columns)
    lower = (lax.broadcasted_iota(jnp.int32, shape, 1) - at) * LANE
    place = lax.broadcasted_iota(jnp.int32, shape, 0)
    ones = jnp.where((place >= lower) & (place < lower + LANE), 1.0, 0.0).astype(BF16)
    coarse = wide_rows.astype(BF16)
    rest = (wide_rows - coarse.astype(F32)).astype(BF16)
    return dot_nn(coarse, ones) + dot_nn(rest, ones)


def position_of(shape, axis, steps):
    row = lax.broadcasted_iota(jnp.int32, shape, axis)
    return (row & (SEG - 1)) * steps + (row >> 3)


def permutation(length):
    shape = (length, length)
    at = position_of(shape, 0, length // SEG)
    return jnp.where(at == lax.broadcasted_iota(jnp.int32, shape, 1), 1.0, 0.0).astype(BF16)


def rolled(value, by):
    return pltpu.roll(value, by % SEG, 0)


def lanes_of(g):
    return pl.ds(pl.multiple_of(g * LANE, LANE), LANE)


def rows_of(j):
    return pl.ds(pl.multiple_of(j * SEG, SEG), SEG)


def wide(ref, n, lanes):
    return jnp.broadcast_to(ref[pl.ds(n, 1), lanes], (SEG, LANE))


def state_cols(n):
    return slice(n * LANE, (n + 1) * LANE)


def dot_nt(a, b):
    return lax.dot_general(a, b, (((1,), (1,)), ((), ())), preferred_element_type=F32)


def dot_tn(a, b):
    return lax.dot_general(a, b, (((0,), (0,)), ((), ())), preferred_element_type=F32)


def dot_nn(a, b):
    return jnp.dot(a, b, preferred_element_type=F32)


def rms_scale(values):
    return lax.rsqrt(jnp.mean(values * values, axis=-1, keepdims=True) + EPS)


def norm_grads(values, scale, gain, d_out):
    unit = values * scale
    d_unit = d_out * gain
    d_values = scale * (d_unit - unit * jnp.mean(d_unit * unit, axis=-1, keepdims=True))
    return d_values, d_out * unit


def silu_slope(v):
    s = jax.nn.sigmoid(v)
    return s * (1.0 + v * (1.0 - s))


def seg_of():
    return lax.broadcasted_iota(jnp.int32, (SEG, LANE), 0)


def lag_masks(place, doc_ref, documents, stream, length, taps):
    at = place * length + position_of((length, LANE), 0, length // SEG)
    masks = [None]
    for lag in range(1, taps):
        cut = None
        for d in range(documents):
            begin = doc_ref[stream, 0, d]
            here = (begin > at - lag) & (begin <= at)
            cut = here if cut is None else cut | here
        masks.append(jnp.where(cut, 0.0, 1.0))
    hit = None
    for d in range(documents):
        here = doc_ref[stream, 0, d] == at
        hit = here if hit is None else hit | here
    return masks, jnp.where(hit, CUT, 0.0)


def enter_kernel(
    taps, documents, place_ref, doc_ref, tok, edge, gain, wx, wz, conv, wproj,
    n1_o, ext_o, pre_o, uf_o, u_o, z_o, part_o, cut_o,
):
    length = tok.shape[1]
    steps = length // SEG
    place = place_ref[0]
    gains = gain[0:1]

    def normal(rows):
        return (rows * rms_scale(rows) * gains).astype(BF16)

    n1_o[0, :length] = normal(dot_nn(permutation(length), tok[0]))
    n1_o[0, length:] = normal(jnp.where(place > 0, edge[0].astype(F32), 0.0))
    inner = dot_nn(n1_o[0], wx[0]).astype(BF16).astype(F32)
    z_o[0] = dot_nn(n1_o[0, :length], wz[0]).astype(BF16)
    masks, cut = lag_masks(place, doc_ref, documents, pl.program_id(0), length, taps)
    cut_o[0] = cut
    seg = seg_of()
    behind = taps - 1
    for g in range(inner.shape[1] // LANE):
        cols = slice(g * LANE, (g + 1) * LANE)
        rows, before = inner[:length, cols], inner[length:, cols]
        parts = []
        for i in range(behind):
            j = steps - behind + i
            last = jnp.broadcast_to(before[EDGE - behind + i : EDGE - behind + i + 1], (SEG, LANE))
            parts.append(jnp.where(seg == 0, last, rolled(rows[j * SEG : (j + 1) * SEG], 1)))
        ext = jnp.concatenate(parts + [rows], axis=0)
        ext_o[0, :, cols] = ext
        pre = conv[taps : taps + 1, cols] + conv[0:1, cols] * rows
        for lag in range(1, taps):
            window = ext[(behind - lag) * SEG : (behind - lag) * SEG + length]
            pre = pre + conv[lag : lag + 1, cols] * window * masks[lag]
        pre_o[0, :, cols] = pre
        u = (pre * jax.nn.sigmoid(pre)).astype(BF16)
        u_o[0, :, cols] = u
        uf_o[0, :, cols] = u.astype(F32)
    part_o[0] = dot_nt(u_o[0], wproj[...]).astype(BF16)


def summary_kernel(
    states, b_at, proj_i, wdt, bias, uf, cut, a_ref,
    step_o, sig_o, hx_ref, sx_ref, hd_o, sd_ref, bb, st_s, dr_s, hd_s,
):
    length, width = step_o.shape[1:]
    groups, steps = width // LANE, length // SEG
    proj = proj_i[0]
    bb[...] = spread(proj, states, b_at)
    pre = dot_nn(proj, wdt[...]) + bias[0:1]
    step_size = jnp.maximum(pre, 0.0) + jnp.log1p(jnp.exp(-jnp.abs(pre)))
    step_o[0] = step_size
    sig_o[0] = jax.nn.sigmoid(pre)
    dr_s[...] = step_size * uf[0]
    for g in range(groups):
        cols = slice(g * LANE, (g + 1) * LANE)
        st_s[:, cols] = step_size[:, cols] + cut[0]
    zero = jnp.zeros((SEG, LANE), F32)
    seg = seg_of()

    def group(g, _):
        lanes = lanes_of(g)
        a = [wide(a_ref, n, lanes) for n in range(states)]

        def step(j, carry):
            rows = rows_of(j)
            st = st_s[rows, lanes]
            dr = dr_s[rows, lanes]
            new = [carry[0] + st]
            for n in range(states):
                new.append(jnp.exp(st * a[n]) * carry[n + 1] + bb[rows, state_cols(n)] * dr)
            return tuple(new)

        out = lax.fori_loop(0, steps, step, (zero,) * (states + 1), unroll=8)
        total, h = out[0], list(out[1:])
        for k in (1, 2, 4):
            ok = seg >= k
            for n in range(states):
                h[n] = h[n] + jnp.where(ok, jnp.exp(total * a[n]) * rolled(h[n], k), 0.0)
            total = total + jnp.where(ok, rolled(total, k), 0.0)
        ok = seg >= 1
        sx_ref[0, :, lanes] = jnp.where(ok, rolled(total, 1), 0.0)
        sd_ref[0, :, lanes] = total[SEG - 1 : SEG]
        for n in range(states):
            hx_ref[0, n, :, lanes] = jnp.where(ok, rolled(h[n], 1), 0.0)
            hd_s[pl.ds(n, 1), lanes] = h[n][SEG - 1 : SEG]
        return 0

    lax.fori_loop(0, groups, group, 0)
    hd_o[0] = hd_s[...].astype(BF16)


def entering(e_ref, finals, sums, a_ref, place, ahead):
    ring = finals.shape[0]
    e_ref[...] = jnp.zeros_like(e_ref)

    def one(lap, _):
        c = lap if ahead else ring - 1 - lap
        use = (c < place) if ahead else (c > place)

        @pl.when(use)
        def _():
            e_ref[...] = jnp.exp(sums[c, 0] * a_ref[...]) * e_ref[...] + finals[c, 0].astype(F32)

        return 0

    lax.fori_loop(0, ring, one, 0)


def output_kernel(
    group, states, b_at, proj, step_i, uf, cut, a_ref, hx_ref, sx_ref, finals, sums, z, skip, wout,
    y_o, gated_o, terms_o, e_o, bb, cb, st_s, dr_s, mix_s, send, recv, own_s,
):
    at = pl.program_id(0)
    mine = lax.axis_index("wa")
    barrier = pltpu.get_barrier_semaphore()
    goals = [lax.rem(mine + 1 + i, group) for i in range(group - 1)]
    sends = [
        remote(mix_s.at[i], terms_o.at[mine], send.at[i], recv.at[i], {"wa": who})
        for i, who in enumerate(goals)
    ]

    @pl.when(at == 0)
    def _():
        for who in goals:
            hello(barrier, "wa", who)

    length, width = step_i.shape[1:]
    groups, steps = width // LANE, length // SEG
    bb[...] = spread(proj[0], states, b_at)
    cb[...] = spread(proj[0], states, b_at + states)
    e_ref = e_o.at[0]
    entering(e_ref, finals, sums, a_ref, lax.axis_index("ctx"), True)
    dr_s[...] = step_i[0] * uf[0]
    for g in range(groups):
        cols = slice(g * LANE, (g + 1) * LANE)
        st_s[:, cols] = step_i[0, :, cols] + cut[0]

    def lane_group(g, _):
        lanes = lanes_of(g)
        a = [wide(a_ref, n, lanes) for n in range(states)]
        sx = sx_ref[0, :, lanes]
        first = tuple(
            jnp.exp(sx * a[n]) * wide(e_ref, n, lanes) + hx_ref[0, n, :, lanes]
            for n in range(states)
        )
        gain = wide(skip, 1, lanes)

        def step(j, h):
            rows = rows_of(j)
            st = st_s[rows, lanes]
            dr = dr_s[rows, lanes]
            new = []
            y = gain * uf[0, rows, lanes]
            for n in range(states):
                state = jnp.exp(st * a[n]) * h[n] + bb[rows, state_cols(n)] * dr
                new.append(state)
                y = y + cb[rows, state_cols(n)] * state
            y_o[0, rows, lanes] = y
            return tuple(new)

        lax.fori_loop(0, steps, step, first, unroll=8)
        return 0

    lax.fori_loop(0, groups, lane_group, 0)
    zf = z[0].astype(F32)
    gated = (y_o[0] * (zf * jax.nn.sigmoid(zf))).astype(BF16)
    gated_o[0] = gated
    mix_s[at] = dot_nn(gated, wout[...]).astype(BF16)
    for i, copy in enumerate(sends):

        @pl.when(at == i)
        def _():
            if i == 0:
                pl.semaphore_wait(barrier, group - 1)
            copy.start()

    @pl.when(at == group - 1)
    def _():
        kept = pltpu.make_async_copy(mix_s.at[group - 1], terms_o.at[mine], own_s)
        kept.start()
        for copy in sends + [kept]:
            copy.wait()


def route_kernel(
    experts, terms, tok, gain, router, route, keep, grad,
    h1_o, n2_o, up_o, cols_o, match_o, out_o, sums_o,
):
    length, width = tok.shape
    shift = permutation(length)
    mix = terms[0].astype(F32)
    for w in range(1, terms.shape[0]):
        mix = mix + terms[w].astype(F32)
    h1 = dot_nn(shift, tok[...]) + mix
    h1_o[...] = h1
    n2 = (h1 * rms_scale(h1) * gain[1:2]).astype(BF16)
    n2_o[...] = n2
    logits = dot_nt(n2, router[...])
    lane = lax.broadcasted_iota(jnp.int32, (length, LANE), 1)
    kind = lax.broadcasted_iota(jnp.int32, (LANE, length), 0)
    named = route[...]
    onehot = jnp.where(kind == named, 1.0, 0.0)
    one = lax.broadcasted_iota(jnp.int32, (length, length), 0)
    two = lax.broadcasted_iota(jnp.int32, (length, length), 1)
    earlier = jnp.where(one < two, 1.0, 0.0).astype(BF16)
    before = dot_nn(onehot.astype(BF16), earlier)
    within = jnp.sum(before * onehot, axis=0, keepdims=True)
    slot = named.astype(F32) * (length // 2) + within
    facts = jnp.where(kind == experts, slot, jnp.where(kind == experts + 1, keep[...].astype(F32), onehot))
    facts = dot_nt(shift, facts.astype(BF16))
    onehot = jnp.where(lane < experts, facts, 0.0)
    slot = jnp.sum(jnp.where(lane == experts, facts, 0.0), axis=1, keepdims=True)
    kept = jnp.sum(jnp.where(lane == experts + 1, facts, 0.0), axis=1, keepdims=True)
    sig = jax.nn.sigmoid(jnp.sum(logits * onehot, axis=1, keepdims=True))
    gates = kept * sig
    cols_o[...] = jnp.where(
        lane == experts, gates, jnp.where(lane == experts + 1, gates * (1.0 - sig), onehot)
    )
    up = dot_nn(shift, grad[...])
    up_o[...] = up
    slots = match_o.shape[1]
    spot = lax.broadcasted_iota(jnp.int32, (length, slots), 1).astype(F32)
    match = jnp.where(slot == spot, 1.0, 0.0).astype(BF16)
    match_o[...] = match
    out_o[0] = dot_tn(match, n2).astype(BF16).reshape(out_o.shape[1:])
    out_o[1] = dot_tn(match, (gates * up).astype(BF16)).astype(BF16).reshape(out_o.shape[1:])
    sums_o[...] = jnp.broadcast_to(jnp.sum(mix * mix, keepdims=True), (SEG, LANE))


def pack_kernel(up, down, out):
    width, units = up.shape
    line = lax.broadcasted_iota(jnp.int32, (units, units), 0)
    same = jnp.where(line == lax.broadcasted_iota(jnp.int32, (units, units), 1), 1.0, 0.0)
    out[:, :width] = dot_nt(same.astype(BF16), up[...]).astype(BF16)
    out[:, width:] = down[...]


def prepare_kernel(
    experts, small, own, wx_t, wdt, wout, conv_w, a_log,
    gain_o, router_o, wx_o, wdt_o, wout_o, conv_o, rows_o, a_o, wide_s,
):
    width = wout.shape[1]
    group = small.shape[0]
    share = width // group
    for w in range(group):
        wide_s[:, w * share : (w + 1) * share] = small[w, :, :share].astype(F32)
    gain_o[0:1] = wide_s[SEG - 2 : SEG - 1]
    gain_o[1:2] = wide_s[SEG - 1 : SEG]
    gain_o[2:] = jnp.zeros((SEG - 2, width), F32)
    rows = wide_s[SEG:]
    row = lax.broadcasted_iota(jnp.int32, rows.shape, 0)
    router_o[...] = jnp.zeros_like(router_o)
    router_o[: 2 * SEG] = jnp.concatenate(
        [jnp.where(row < experts, rows, 0.0), jnp.zeros_like(rows)], axis=0
    ).astype(BF16)
    local = wout.shape[0]
    for out, src in ((wx_o, wx_t), (wdt_o, wdt), (a_o, None)):
        out[...] = jnp.zeros_like(out)
        if src is not None:
            out[: src.shape[0], :local] = src[...]
    a_o[...] = jnp.full(a_o.shape, -1.0, F32)
    a_o[:, :local] = -jnp.exp(a_log[...].astype(F32))
    wout_o[...] = jnp.zeros_like(wout_o)
    wout_o[:local] = wout[...]
    conv_o[...] = jnp.zeros_like(conv_o)
    taps = conv_w.shape[0]
    conv_o[:taps, :local] = conv_w[...].astype(F32)
    mine = own[...].astype(F32)
    rows_o[...] = jnp.zeros_like(rows_o)
    for h in range(2):
        cols = slice(h * share, (h + 1) * share)
        conv_o[taps : taps + 1, cols] = mine[h : h + 1, :share]
        rows_o[0:1, cols] = mine[2 + h : 3 + h, :share]
        rows_o[1:2, cols] = mine[4 + h : 5 + h, :share]


def block_rows(value, c, rows):
    low = c * rows
    have = max(0, min(rows, value.shape[0] - low))
    if have == rows:
        return value[low : low + rows]
    blank = jnp.zeros((rows - have, value.shape[1]), value.dtype)
    return blank if have == 0 else jnp.concatenate([value[low : low + have], blank], axis=0)


def pack_zo_kernel(ring, in_rows, local, n1, d_z, d_mix, gated, out):
    width = n1.shape[1]
    lanes = d_z.shape[1]
    grad_z = dot_tn(n1[...], d_z[...])
    grad_o = dot_tn(gated[...], d_mix[...])
    side = jnp.zeros((grad_o.shape[0], lanes - width // 2), F32)
    first = jnp.concatenate([grad_o[:, : width // 2], side], axis=1)
    second = jnp.concatenate([grad_o[:, width // 2 :], side], axis=1)
    rows = in_rows // 2
    for c in range(ring):
        out[c // 2, c % 2, :, :lanes] = block_rows(grad_z, c, in_rows).astype(BF16)
        both = [block_rows(first[:local], c, rows), block_rows(second[:local], c, rows)]
        out[c // 2, c % 2, :, lanes:] = jnp.concatenate(both, axis=0).astype(BF16)


def pack_rest_kernel(
    ring, in_rows, small_rows, group, experts, ranked, mine_ref, n1, d_x, gx, gdt, ga, a_ref, gconv, bias, skip,
    gain_mix, gains, gain_moe, router, out_sums, mix_sum, out, small_s, wide_s,
):
    lanes = d_x.shape[1]
    width = n1.shape[1]
    share = width // group
    grad_x = dot_tn(n1[...], d_x[...])
    small_s[...] = jnp.zeros_like(small_s)
    at = 0
    grad_a = jnp.sum(ga[...], axis=1) * a_ref[...]
    for part in (gx[...], gdt[:ranked], grad_a, gconv[...]):
        small_s[at : at + part.shape[0]] = part
        at += part.shape[0]
    small_s[at : at + 1] = bias[...]
    small_s[at + SEG : at + SEG + 1] = skip[...]
    wide_s[...] = jnp.zeros_like(wide_s)
    wide_s[0:1] = gain_mix[...] / gains[0:1]
    wide_s[1:2] = gain_moe[...]
    wide_s[2 : 2 + experts] = router[:experts]
    lane = lax.broadcasted_iota(jnp.int32, (group, LANE), 1)
    row = lax.broadcasted_iota(jnp.int32, (group, LANE), 0)
    stats = jnp.where(
        lane == 0, out_sums[0:1], jnp.where(lane == 1, mix_sum[0:1], jnp.where(lane == 2, out_sums[1:2], 0.0))
    )
    stats = jnp.where(row == mine_ref[0], stats, 0.0)
    stats = jnp.concatenate([stats, jnp.zeros((group, lanes - LANE), F32)], axis=1)
    bottom = jnp.zeros((16 - 2 * group, lanes), F32)
    small_each = small_s.shape[0] // ring
    for c in range(ring):
        if c < 2 + experts:
            full = [wide_s[c : c + 1, w * share : (w + 1) * share] for w in range(group)]
            full = jnp.concatenate(full, axis=0)
            full = jnp.concatenate([full, jnp.zeros((group, lanes - share), F32)], axis=1)
        else:
            full = jnp.zeros((group, lanes), F32)
        small = small_s[c * small_each : (c + 1) * small_each]
        blank = jnp.zeros((small_rows - small_each, lanes), F32)
        parts = [block_rows(grad_x, c, in_rows), small]
        if small_rows > small_each:
            parts.append(blank)
        rows = jnp.concatenate(parts + [full, stats, bottom], axis=0)
        out[c // 2, c % 2] = rows.astype(BF16)


def store_in_order(out, rows, order_s):
    steps = rows.shape[0] // SEG
    for g in range(rows.shape[1] // LANE):
        cols = slice(g * LANE, (g + 1) * LANE)
        for j in range(steps):
            order_s[g, pl.ds(j, SEG, stride=steps), :] = rows[j * SEG : (j + 1) * SEG, cols]
        out[:, cols] = order_s[g]


def input_gradient(taps, last_ref, terms, edges, tok, gain, dh, out_o, dn_s, order_s):
    length = tok.shape[0]
    steps = length // SEG
    behind = taps - 1
    total = terms[0, :length].astype(F32)
    edge = edges[0].astype(F32)
    for w in range(1, terms.shape[0]):
        total = total + terms[w, :length].astype(F32)
        edge = edge + edges[w].astype(F32)
    edge = jnp.where(last_ref[0] > 0, 0.0, edge)
    dn_s[...] = total
    seg = lax.broadcasted_iota(jnp.int32, (SEG, tok.shape[1]), 0)
    for i in range(behind):
        j = pl.ds((steps - behind + i) * SEG, SEG)
        row = EDGE - behind + i
        came = jnp.broadcast_to(edge[row : row + 1], seg.shape)
        dn_s[j, :] += jnp.where(seg == SEG - 1, came, 0.0)
    x = dot_nn(permutation(length), tok[...])
    d_x, _ = norm_grads(x, rms_scale(x), gain[0:1], dn_s[...])
    result = dh[...] + d_x
    store_in_order(out_o, result, order_s)


def unpack_kernel(
    ring, group, in_rows, small_rows, experts, states, ranked, taps, denom, mine_ref, done, up_down,
    last_ref, terms, edges, tok, gain, dh, res,
    in_o, out_o, up_o, down_o, taps_o, wx_o, wdt_o, a_o, vec_o, stat_o, grad_o, layer_o,
    small_s, full_s, dn_s, order_s,
):
    c = pl.program_id(0)
    width = in_o.shape[1]

    @pl.when(c == 1)
    def _():
        store_in_order(layer_o, res[...], order_s)
        input_gradient(taps, last_ref, terms, edges, tok, gain, dh, grad_o, dn_s, order_s)

    local = width // 2
    small_each = small_s.shape[0] // ring
    base = 2 * in_rows

    @pl.when(c == 0)
    def _():
        line = lax.broadcasted_iota(jnp.int32, (width, width), 0)
        same = jnp.where(line == lax.broadcasted_iota(jnp.int32, (width, width), 1), 1.0, 0.0)
        up_o[...] = dot_nt(same.astype(BF16), up_down[:, :width])
        down_o[...] = up_down[:, width:].astype(F32)
        full_s[...] = jnp.zeros_like(full_s)

    @pl.when(c * in_rows < width)
    def _():
        rows = done[0, :base, :].astype(F32)
        in_o[...] = jnp.concatenate([rows[:in_rows, :local], rows[in_rows:, :local]], axis=1)
        low = base + 16 + small_rows
        rows = done[0, low : low + in_rows, :].astype(F32)
        half = in_rows // 2
        out_o[...] = jnp.concatenate([rows[:half, :local], rows[half:, :local]], axis=1)

    small = done[0, base + 16 : base + 16 + small_rows, :].astype(F32)
    small_s[pl.ds(pl.multiple_of(c * small_each, SEG), small_each), :] = small[:small_each]
    tile = done[0, base : base + 16, :].astype(F32)
    row = lax.broadcasted_iota(jnp.int32, tile.shape, 0)
    own = jnp.sum(jnp.where(row == mine_ref[0], tile, 0.0), axis=0, keepdims=True)
    spot = lax.broadcasted_iota(jnp.int32, full_s.shape, 0)
    full_s[...] += jnp.where(spot == c, own, 0.0)

    @pl.when(c == 0)
    def _():
        sums = jnp.sum(jnp.where(row == group + mine_ref[0], tile, 0.0), axis=0, keepdims=True)
        stat_o[...] = jnp.sqrt(sums[:, :LANE] / denom)

    @pl.when(c == ring - 1)
    def _():
        at = 0
        wx_o[...] = small_s[: wx_o.shape[0], :local]
        at += up_to(wx_o.shape[0], LANE)
        wdt_o[...] = small_s[at : at + ranked, :local]
        at += ranked
        a_o[...] = small_s[at : at + states, :local]
        at += states
        taps_o[...] = small_s[at : at + taps, :local]
        vec_o[:SEG] = full_s[...]
        vec_o[SEG : SEG + 1] = small_s[at + taps : at + taps + 1]
        at += SEG
        vec_o[SEG + 1 : SEG + 2] = small_s[at : at + 1]
        vec_o[SEG + 2 : SEG + 3] = small_s[at + SEG : at + SEG + 1]


def middle_kernel(
    experts, group, chunks,
    mix_ref, tok, gain, router, route, keep, grad, w_ref,
    g_ref, layer_o, dh_o, dmix_o, router_o, gain_o, sums_o, mix_o,
    layer_s, dh_s, dmix_s, leave_sem,
    h1_s, n2_s, up_s, cols_s, match_s, x_ref, r_ref,
    got, w_s, g_s, act_s, slope_s, pre_s, acc, out_s,
    w_sem, g_sem, s1, r1, own1, s2, r2, own2,
):
    mine, mates = mates_of(group)
    count, width = x_ref.shape[2:]
    slots = group * count
    block = w_ref.shape[0] // chunks

    def load(t):
        at = pl.ds(pl.multiple_of(lax.rem(t, chunks) * block, block), block)
        slot = lax.rem(t, 2)
        return pltpu.make_async_copy(w_ref.at[at], w_s.at[slot], w_sem.at[slot])

    load(0).start()
    greet("wa", group)
    route_kernel(
        experts, mix_ref, tok, gain, router, route, keep, grad,
        h1_s, n2_s, up_s, cols_s, match_s, x_ref, mix_o,
    )
    sent = []
    for h in range(2):
        for k, who in enumerate(mates):
            copy = remote(x_ref.at[h, who], got.at[h, mine], s1.at[h, k], r1.at[h, k], {"wa": who})
            copy.start()
            sent.append(copy)
        pltpu.make_async_copy(x_ref.at[h, mine], got.at[h, mine], own1.at[h]).start()

    def arrived(h):
        pltpu.make_async_copy(x_ref.at[h, mine], got.at[h, mine], own1.at[h]).wait()
        for copy in sent[h * len(mates) : (h + 1) * len(mates)]:
            copy.wait_recv()
        return got[h].reshape(slots, width)

    def chunk(i):
        return pl.ds(pl.multiple_of(i * block, block), block)

    def returned(h):
        out_s[h] = acc[...].astype(BF16).reshape(group, count, width)
        for k, who in enumerate(mates):
            copy = remote(out_s.at[h, who], r_ref.at[h, mine], s2.at[h, k], r2.at[h, k], {"wa": who})
            copy.start()
            sent.append(copy)
        pltpu.make_async_copy(out_s.at[h, mine], r_ref.at[h, mine], own2.at[h]).start()

    rows = arrived(0)
    acc[...] = jnp.zeros_like(acc)

    def forward(i, _):
        load(i).wait()
        load(i + 1).start()
        w = w_s.at[lax.rem(i, 2)]
        hidden = dot_nt(w[:, :width], rows)
        c = 0.7978845608
        t = jnp.tanh(c * (hidden + 0.044715 * hidden * hidden * hidden))
        act = (0.5 * hidden * (1.0 + t)).astype(BF16)
        act_s[chunk(i), :] = act
        slope_s[chunk(i), :] = 0.5 * (1.0 + t) + 0.5 * hidden * (1.0 - t * t) * c * (
            1.0 + 3.0 * 0.044715 * hidden * hidden
        )
        acc[...] += dot_tn(act, w[:, width:])
        return 0

    lax.fori_loop(0, chunks, forward, 0)
    returned(0)
    d_out = arrived(1)
    acc[...] = jnp.zeros_like(acc)

    def backward(i, _):
        load(chunks + i).wait()

        @pl.when(i < chunks - 1)
        def _():
            load(chunks + i + 1).start()

        w = w_s.at[lax.rem(chunks + i, 2)]
        d_pre = (dot_nt(w[:, width:], d_out) * slope_s[chunk(i), :]).astype(BF16)
        pre_s[chunk(i), :] = d_pre
        acc[...] += dot_tn(d_pre, w[:, :width])
        return 0

    lax.fori_loop(0, chunks, backward, 0)
    returned(1)

    def store(i):
        slot = lax.rem(i, 2)
        return pltpu.make_async_copy(g_s.at[slot], g_ref.at[chunk(i)], g_sem.at[slot])

    def gradients(i, _):
        @pl.when(i >= 2)
        def _():
            store(i - 2).wait()

        g = g_s.at[lax.rem(i, 2)]
        g[:, :width] = dot_nn(pre_s[chunk(i), :], got[0].reshape(slots, width)).astype(BF16)
        g[:, width:] = dot_nn(act_s[chunk(i), :], got[1].reshape(slots, width)).astype(BF16)
        store(i).start()
        return 0

    lax.fori_loop(0, chunks, gradients, 0)
    store(chunks - 2).wait()
    store(chunks - 1).wait()
    for h in range(2):
        pltpu.make_async_copy(out_s.at[h, mine], r_ref.at[h, mine], own2.at[h]).wait()
    for copy in sent[: 2 * len(mates)]:
        copy.wait_send()
    for copy in sent[2 * len(mates) :]:
        copy.wait()
    combine_kernel(
        experts, r_ref, match_s, h1_s, n2_s, up_s, cols_s, gain, router,
        layer_s, dh_s, dmix_s, router_o, gain_o, sums_o,
    )
    leaving = [
        pltpu.make_async_copy(src, dst, leave_sem.at[i])
        for i, (src, dst) in enumerate(((dmix_s, dmix_o), (dh_s, dh_o), (layer_s, layer_o)))
    ]
    for copy in leaving:
        copy.start()
    for copy in leaving:
        copy.wait()


def middle(experts, terms, tok, gains, router, route, keep, grad, w, chunks, cid, us):
    group = lax.axis_size("wa")
    units = w.shape[0]
    length, width = tok.shape
    slots = experts * (length // 2)
    block = units // chunks
    dma = pltpu.SemaphoreType.DMA
    hbm = pl.BlockSpec(memory_space=pltpu.HBM)
    vmem = pl.BlockSpec(memory_space=pltpu.VMEM)
    anywhere = pl.BlockSpec(memory_space=pl.ANY)
    two = dma((2, group - 1))
    rows = pltpu.VMEM((2, group, slots // group, width), BF16)
    shapes = [
        (w.shape, BF16), ((length, width), F32), ((length, width), F32), ((length, width), BF16),
        ((LANE, width), F32), ((1, width), F32), ((SEG, LANE), F32), ((SEG, LANE), F32),
    ]
    return pl.pallas_call(
        functools.partial(middle_kernel, experts, group, chunks),
        out_shape=[jax.ShapeDtypeStruct(shape, dtype) for shape, dtype in shapes],
        in_specs=[vmem] * 7 + [hbm],
        out_specs=[hbm] + [anywhere] * 3 + [vmem] * 4,
        scratch_shapes=[
            pltpu.VMEM((length, width), F32), pltpu.VMEM((length, width), F32),
            pltpu.VMEM((length, width), BF16), dma((3,)),
            pltpu.VMEM((length, width), F32),
            pltpu.VMEM((length, width), BF16),
            pltpu.VMEM((length, width), F32),
            pltpu.VMEM((length, LANE), F32),
            pltpu.VMEM((length, slots), BF16),
            rows, rows, rows,
            pltpu.VMEM((2, block, 2 * width), BF16),
            pltpu.VMEM((2, block, 2 * width), BF16),
            pltpu.VMEM((units, slots), BF16),
            pltpu.VMEM((units, slots), F32),
            pltpu.VMEM((units, slots), BF16),
            pltpu.VMEM((slots, width), F32),
            rows,
            dma((2,)), dma((2,)),
            two, two, dma((2,)), two, two, dma((2,)),
        ],
        compiler_params=pltpu.CompilerParams(
            collective_id=cid, has_side_effects=True, vmem_limit_bytes=VMEM_LIMIT + 20 * 2**20
        ),
        cost_estimate=lasting(us),
        name="middle",
    )(terms, tok, gains, router, route, keep, grad, w)


def combine_kernel(
    experts, back, match, h1_i, n2, up_i, cols, gain, router,
    out_o, dh_o, dmix_o, router_o, gain_o, sums_o,
):
    length, width = h1_i.shape
    h1, up = h1_i[...], up_i[...]
    lane = lax.broadcasted_iota(jnp.int32, (length, LANE), 1)
    facts = cols[...]

    def column(at):
        return jnp.sum(jnp.where(lane == at, facts, 0.0), axis=1, keepdims=True)

    gates, slope = column(experts), column(experts + 1)
    onehot = jnp.where(lane < experts, facts, 0.0)
    slots = match.shape[1]
    rows = dot_nn(match[...], back[0].reshape(slots, width))
    moe = gates * rows
    result = h1 + moe
    out_o[...] = result
    d_gate = jnp.sum(rows * up, axis=1, keepdims=True)
    d_logits = (onehot * (d_gate * slope)).astype(BF16)
    router_o[...] = dot_tn(d_logits, n2[...])
    d_n2 = dot_nn(match[...], back[1].reshape(slots, width)) + dot_nn(d_logits, router[...])
    d_norm, terms = norm_grads(h1, rms_scale(h1), gain[1:2], d_n2)
    gain_o[...] = jnp.sum(terms, axis=0, keepdims=True)
    d_h1 = up + d_norm
    dh_o[...] = d_h1
    dmix_o[...] = d_h1.astype(BF16)
    sums_o[0:1] = jnp.broadcast_to(jnp.sum(result * result, keepdims=True), (1, LANE))
    sums_o[1:2] = jnp.broadcast_to(jnp.sum(moe * moe, keepdims=True), (1, LANE))


def gate_back_kernel(
    states, c_at, d_mix, wout, y, z, uf, proj, step_i, cut, a_ref,
    dy_o, dz_o, skip_o, fx_ref, tx_ref, fd_o, cb, st_s, fd_s,
):
    length, width = step_i.shape[1:]
    groups, steps = width // LANE, length // SEG
    d_gated = dot_nt(d_mix[0], wout[...])
    zf = z[0].astype(F32)
    dy = d_gated * (zf * jax.nn.sigmoid(zf))
    dy_o[0] = dy
    dz_o[0, :length] = (d_gated * y[0] * silu_slope(zf)).astype(BF16)
    dz_o[0, length:] = jnp.zeros((EDGE, width), BF16)

    @pl.when(pl.program_id(0) == 0)
    def _():
        skip_o[...] = jnp.zeros_like(skip_o)

    skip_o[...] += jnp.sum(dy * uf[0], axis=0, keepdims=True)
    cb[...] = spread(proj[0], states, c_at)
    for g in range(groups):
        cols = slice(g * LANE, (g + 1) * LANE)
        st_s[:, cols] = step_i[0, :, cols] + cut[0]
    zero = jnp.zeros((SEG, LANE), F32)
    seg = seg_of()

    def group(g, _):
        lanes = lanes_of(g)
        a = [wide(a_ref, n, lanes) for n in range(states)]

        def step(lap, carry):
            rows = rows_of(steps - 1 - lap)
            st = st_s[rows, lanes]
            d = dy_o[0, rows, lanes]
            new = [carry[0] + st]
            for n in range(states):
                new.append(jnp.exp(st * a[n]) * (carry[n + 1] + cb[rows, state_cols(n)] * d))
            return tuple(new)

        out = lax.fori_loop(0, steps, step, (zero,) * (states + 1), unroll=8)
        total, f = out[0], list(out[1:])
        for k in (1, 2, 4):
            ok = seg < SEG - k
            for n in range(states):
                f[n] = f[n] + jnp.where(ok, jnp.exp(total * a[n]) * rolled(f[n], -k), 0.0)
            total = total + jnp.where(ok, rolled(total, -k), 0.0)
        ok = seg < SEG - 1
        tx_ref[0, :, lanes] = jnp.where(ok, rolled(total, -1), 0.0)
        for n in range(states):
            fx_ref[0, n, :, lanes] = jnp.where(ok, rolled(f[n], -1), 0.0)
            fd_s[pl.ds(n, 1), lanes] = f[n][0:1]
        return 0

    lax.fori_loop(0, groups, group, 0)
    fd_o[0] = fd_s[...].astype(BF16)


def scan_back_kernel(
    states, b_at, proj, step_i, sig, uf, cut, dy_i, a_ref, skip, wdt, hx_ref, sx_ref, e_i,
    fx_ref, tx_ref, finals, sums, g_ref, p_ref,
    part_o, du_o, dt_o, bias_o, ga_ref, g_o,
    bb, cb, dec, pri, accb, accc, st_s, dr_s, ds_s, out_s,
    from_pair, kept, came, load, ctx_s, ctx_r,
):
    ring = finals.shape[0]
    half = ring // 2
    _, chip, lane, _, peers = neighbours(ring)
    own_half = pltpu.make_async_copy(g_ref.at[:, lane], kept, load.at[0])
    pair_half = pltpu.make_async_copy(p_ref, from_pair, load.at[1])
    targets = [lax.rem(chip + k, half) for k in range(1, half)]
    scattered = [
        remote(kept.at[to], came.at[k], ctx_s.at[k], ctx_r.at[k], {"ctx": who})
        for k, (to, who) in enumerate(zip(targets, peers))
    ]
    at = pl.program_id(0)

    @pl.when(at == 0)
    def _():
        own_half.start()
        pair_half.start()
        barrier = pltpu.get_barrier_semaphore()
        for who in peers:
            hello(barrier, "ctx", who)
        pl.semaphore_wait(barrier, half - 1)
        own_half.wait()
        pair_half.wait()
        for to, copy in zip(targets, scattered):
            add_rows(kept.at[to], [kept.at[to], from_pair.at[to]], kept.shape[1])
            copy.start()
        add_rows(kept.at[chip], [kept.at[chip], from_pair.at[chip]], kept.shape[1])

    @pl.when(at == pl.num_programs(0) - 1)
    def _():
        for copy in scattered:
            copy.wait()
        add_rows(g_o, [kept.at[chip]] + [came.at[k] for k in range(half - 1)], kept.shape[1])

    length, width = step_i.shape[1:]
    groups, steps = width // LANE, length // SEG
    bb[...] = spread(proj[0], states, b_at)
    cb[...] = spread(proj[0], states, b_at + states)
    accb[...] = jnp.zeros_like(accb)
    accc[...] = jnp.zeros_like(accc)
    entering(out_s, finals, sums, a_ref, lax.axis_index("ctx"), False)
    e_ref = e_i.at[0]
    dr_s[...] = step_i[0] * uf[0]
    for g in range(groups):
        cols = slice(g * LANE, (g + 1) * LANE)
        st_s[:, cols] = step_i[0, :, cols] + cut[0]

    @pl.when(pl.program_id(0) == 0)
    def _():
        ga_ref[...] = jnp.zeros_like(ga_ref)
        dt_o[...] = jnp.zeros_like(dt_o)
        bias_o[...] = jnp.zeros_like(bias_o)

    def group(g, _):
        lanes = lanes_of(g)
        a = [wide(a_ref, n, lanes) for n in range(states)]
        sx = sx_ref[0, :, lanes]
        first = tuple(
            jnp.exp(sx * a[n]) * wide(e_ref, n, lanes) + hx_ref[0, n, :, lanes]
            for n in range(states)
        )

        def ahead(j, h):
            rows = rows_of(j)
            st = st_s[rows, lanes]
            dr = dr_s[rows, lanes]
            new = []
            for n in range(states):
                decay = jnp.exp(st * a[n])
                dec[rows, state_cols(n)] = decay
                pri[rows, state_cols(n)] = h[n]
                new.append(decay * h[n] + bb[rows, state_cols(n)] * dr)
            return tuple(new)

        last = lax.fori_loop(0, steps, ahead, first, unroll=8)
        end = rows_of(steps)
        for n in range(states):
            pri[end, state_cols(n)] = last[n]
        tx = tx_ref[0, :, lanes]
        flow = tuple(
            jnp.exp(tx * a[n]) * wide(out_s, n, lanes) + fx_ref[0, n, :, lanes]
            for n in range(states)
        )
        gain = wide(skip, 1, lanes)

        def back(lap, f):
            j = steps - 1 - lap
            rows = rows_of(j)
            after = rows_of(j + 1)
            st = step_i[0, rows, lanes]
            dr = dr_s[rows, lanes]
            dy = dy_i[0, rows, lanes]
            new = []
            d_step = None
            d_drive = None
            for n in range(states):
                cols = state_cols(n)
                d = f[n] + cb[rows, cols] * dy
                accc[rows, cols] += pri[after, cols] * dy
                accb[rows, cols] += d * dr
                flowing = dec[rows, cols] * d
                new.append(flowing)
                d_log = flowing * pri[rows, cols]
                ga_ref[n, :, lanes] += d_log * st
                part = d_log * a[n]
                d_step = part if d_step is None else d_step + part
                part = d * bb[rows, cols]
                d_drive = part if d_drive is None else d_drive + part
            ds_s[rows, lanes] = (d_step + d_drive * uf[0, rows, lanes]) * sig[0, rows, lanes]
            du_o[0, rows, lanes] = d_drive * st + dy * gain
            return tuple(new)

        lax.fori_loop(0, steps, back, flow, unroll=8)
        return 0

    lax.fori_loop(0, groups, group, 0)
    d_pre = ds_s[...]
    bias_o[...] += jnp.sum(d_pre, axis=0, keepdims=True)
    d_pre = d_pre.astype(BF16)
    dt_o[...] += dot_tn(proj[0], d_pre)
    columns = part_o.shape[2]
    part = dot_nt(d_pre, wdt[...])
    part = part + collected(accb[...], states, columns, b_at)
    part = part + collected(accc[...], states, columns, b_at + states)
    part_o[0] = part.astype(BF16)


def conv_back_kernel(
    taps, documents, place_ref, doc_ref, proj_i, wproj, du, pre, ext, u, conv, dz, wx, wz, n1,
    dx_o, dn_o, gconv_o, gx_o, gain_o, dext,
):
    length, width = du.shape[1:]
    steps = length // SEG
    behind = taps - 1

    @pl.when(pl.program_id(0) == 0)
    def _():
        gconv_o[...] = jnp.zeros_like(gconv_o)
        gx_o[...] = jnp.zeros_like(gx_o)
        gain_o[...] = jnp.zeros_like(gain_o)

    proj = proj_i[0]
    gx_o[...] += dot_tn(proj, u[0])
    d_u = dot_nn(proj, wproj[...]) + du[0]
    masks, _ = lag_masks(place_ref[0], doc_ref, documents, pl.program_id(0), length, taps)
    seg = seg_of()
    row = lax.broadcasted_iota(jnp.int32, (EDGE, LANE), 0)
    for g in range(width // LANE):
        cols = slice(g * LANE, (g + 1) * LANE)
        d = d_u[:, cols] * silu_slope(pre[0, :, cols])
        gconv_o[taps : taps + 1, cols] += jnp.sum(d, axis=0, keepdims=True)
        dext[...] = jnp.zeros_like(dext)
        for lag in range(taps):
            weighted = d if lag == 0 else d * masks[lag]
            at = pl.ds((behind - lag) * SEG, length)
            gconv_o[lag : lag + 1, cols] += jnp.sum(weighted * ext[0, at, cols], axis=0, keepdims=True)
            dext[at, :] += weighted * conv[lag : lag + 1, cols]
        before = jnp.zeros((EDGE, LANE), F32)
        for i in range(behind):
            head = dext[i * SEG : (i + 1) * SEG]
            j = pl.ds((steps + i) * SEG, SEG)
            dext[j, :] += jnp.where(seg < SEG - 1, rolled(head, -1), 0.0)
            first = jnp.broadcast_to(head[0:1], (EDGE, LANE))
            before = before + jnp.where(row == EDGE - behind + i, first, 0.0)
        dx_o[0, :length, cols] = dext[behind * SEG :].astype(BF16)
        dx_o[0, length:, cols] = before.astype(BF16)
    d_n1 = dot_nt(dx_o[0], wx[0]) + dot_nt(dz[0], wz[0])
    gain_o[...] += jnp.sum(d_n1 * n1[0].astype(F32), axis=0, keepdims=True)
    dn_o[0] = d_n1.astype(BF16)


SMEM = "smem"
ANY = "any"


def by_stream(shape, at, order):
    block = tuple(1 if i == at else n for i, n in enumerate(shape))
    rank = len(shape)

    def index(s):
        return tuple(order(s) if i == at else 0 for i in range(rank))

    return pl.BlockSpec(block, index)


def whole(shape):
    return pl.BlockSpec(shape, lambda s: (0,) * len(shape))


def call(kernel, name, grid, args, outs, scratch, us, cid=None, limit=VMEM_LIMIT, order=lambda s: s):
    arrays, specs = [], []
    for array, at in args:
        arrays.append(array)
        if at == SMEM:
            specs.append(pl.BlockSpec(memory_space=pltpu.SMEM))
        elif at == ANY:
            specs.append(pl.BlockSpec(memory_space=pl.ANY))
        elif callable(at):
            specs.append(at(array.shape))
        else:
            specs.append(whole(array.shape) if at is None else by_stream(array.shape, at, order))
    out_specs = []
    for shape, _, at in outs:
        if callable(at):
            out_specs.append(at(shape))
        elif at == ANY:
            out_specs.append(pl.BlockSpec(memory_space=pl.ANY))
        else:
            out_specs.append(whole(shape) if at is None else by_stream(shape, at, order))
    return pl.pallas_call(
        kernel,
        grid=(grid,),
        out_shape=[jax.ShapeDtypeStruct(shape, dtype) for shape, dtype, _ in outs],
        in_specs=specs,
        out_specs=out_specs,
        scratch_shapes=scratch,
        compiler_params=pltpu.CompilerParams(
            vmem_limit_bytes=limit, collective_id=cid, has_side_effects=cid is not None
        ),
        cost_estimate=lasting(us),
        name=name,
    )(*arrays)


def padded_to(array, width, axis):
    pads = [(0, 0)] * array.ndim
    pads[axis] = (0, width - array.shape[axis])
    return jnp.pad(array, pads)


def up_to(n, multiple):
    return -(-n // multiple) * multiple


def body(
    tokens, out_grad, doc_starts, routes, keep_mask, norm_mix, w_in, conv_w, conv_b, w_x, w_dt,
    dt_bias, a_log, d_skip, w_out, norm_moe, w_router, w_up, w_down,
):
    group = lax.axis_size("wa")
    ring = lax.axis_size("ctx")
    mine = lax.axis_index("wa")
    place = lax.axis_index("ctx")
    length, width = tokens.shape[1:]
    taps, local = conv_w.shape
    states = a_log.shape[0]
    ranked = w_dt.shape[0]
    experts = w_router.shape[1]
    padded = up_to(local, LANE)
    columns = up_to(w_x.shape[1], LANE)
    steps = length // SEG
    rows = length + EDGE
    slots = experts * (length // 2)
    share = norm_mix.shape[0]
    order_vmem = pltpu.VMEM((width // LANE, length, LANE), F32)
    place_s = place.astype(jnp.int32).reshape(1)
    mine_s = mine.astype(jnp.int32).reshape(1)
    last_s = (place == ring - 1).astype(jnp.int32).reshape(1)
    f32_vmem = lambda *shape: pltpu.VMEM(shape, F32)

    (own_experts,) = call(
        pack_kernel, "pack", 1, [(w_up[0], None), (w_down[0], None)],
        [((w_down.shape[1], 2 * width), BF16, None)], [], 3, None, LARGE_LIMIT,
    )
    expert_w = lax.all_gather(own_experts, "ctx", axis=0, tiled=True)

    in_rows = up_to(-(-width // ring), 16)
    blank = ring * in_rows - width
    part_in = jnp.pad(w_in, ((0, blank), (0, 0))) if blank else w_in
    part_in = lax.dynamic_slice_in_dim(part_in, place * in_rows, in_rows, 0)
    halves = jnp.stack([part_in[:, :local], part_in[:, local:]], axis=0)
    halves = jnp.pad(halves, ((0, 0), (0, 0), (0, padded - local)))
    small = jnp.concatenate([conv_b, dt_bias, d_skip, norm_mix, norm_moe], axis=0).reshape(SEG, share)
    small = jnp.concatenate([small, jnp.pad(w_router.T, ((0, SEG - experts), (0, 0)))], axis=0)
    small = padded_to(small, up_to(share, LANE), 1)
    documents = doc_starts.shape[1]
    doc_tile = jnp.pad(doc_starts, ((0, SEG - 1), (0, LANE - documents)))
    all_rows, all_edges, smalls, docs, w_blocks = start(tokens[0], small, doc_tile, halves, 1)
    proj_in = w_blocks.reshape(2, ring * in_rows, padded)[:, :width]
    of_x = lambda shape: pl.BlockSpec((1,) + shape[1:], lambda i: (0, 0, 0))
    of_z = lambda shape: pl.BlockSpec((1,) + shape[1:], lambda i: (1, 0, 0))
    par = (SEG, padded)
    gains, router, wproj, wdt, wout, conv, vectors, a_mat = call(
        functools.partial(prepare_kernel, experts), "prepare", 1,
        [(smalls, None), (small, None), (w_x.T, None), (w_dt, None), (w_out, None), (conv_w, None),
         (a_log, None)],
        [((SEG, width), F32, None), ((LANE, width), BF16, None), ((columns, padded), BF16, None),
         ((columns, padded), BF16, None), ((padded, width), BF16, None), (par, F32, None),
         (par, F32, None), ((states, padded), F32, None)],
        [f32_vmem(2 * SEG, width)], 3,
    )

    vec = (group, length, padded)
    n1, ext, pre_conv, u_f, u, z, part, cut = call(
        functools.partial(enter_kernel, taps, documents), "enter", group,
        [(place_s, SMEM), (docs, SMEM), (all_rows, 0), (all_edges, 0), (gains, None),
         (proj_in, of_x), (proj_in, of_z), (conv, None), (wproj, None)],
        [((group, rows, width), BF16, 0), ((group, (taps - 1) * SEG + length, padded), F32, 0),
         (vec, F32, 0), (vec, F32, 0), (vec, BF16, 0), (vec, BF16, 0),
         ((group, length, columns), BF16, 0), ((group, length, LANE), F32, 0)],
        [], 8,
    )
    projected = sum_all(part, 2, 11)
    seg_states = (group, states, SEG, padded)
    seg_sums = (group, SEG, padded)
    dev_states = (group, states, padded)
    dev_sums = (group, 1, padded)
    spread_vmem = f32_vmem(length, states * LANE)
    lane_vmem = f32_vmem(length, padded)
    state_vmem = f32_vmem(states, padded)
    step_size, sig, h_in, s_in, h_dev, s_dev = call(
        functools.partial(summary_kernel, states, ranked), "scan_summary", group,
        [(projected, 0), (wdt, None), (vectors, None), (u_f, 0), (cut, 0), (a_mat, None)],
        [(vec, F32, 0), (vec, F32, 0), (seg_states, F32, 0),
         (seg_sums, F32, 0), (dev_states, BF16, 0), (dev_sums, F32, 0)],
        [spread_vmem, lane_vmem, lane_vmem, state_vmem], 10,
    )
    all_h, all_s = carry([h_dev, s_dev], 3, 10)
    dma = pltpu.SemaphoreType.DMA
    y_full, gated, mix_terms, e_in = call(
        functools.partial(output_kernel, group, states, ranked), "scan_output", group,
        [(projected, 0), (step_size, 0), (u_f, 0), (cut, 0), (a_mat, None), (h_in, 0),
         (s_in, 0), (all_h, 1), (all_s, 1), (z, 0), (vectors, None), (wout, None)],
        [(vec, F32, 0), (vec, BF16, 0), ((group, length, width), BF16, ANY), (dev_states, F32, 0)],
        [spread_vmem, spread_vmem, lane_vmem, lane_vmem, pltpu.VMEM((group, length, width), BF16),
         dma((group - 1,)), dma((group - 1,)), dma], 27, 4, VMEM_LIMIT,
        lambda s: lax.rem(lax.axis_index("wa") + 1 + s, group),
    )

    row_f = (length, width)
    grad_experts, result, d_h1, d_mix_own, grad_router, grad_gain_moe, out_sums, mix_sum = middle(
        experts, mix_terms, tokens[0], gains, router, routes[0].T, keep_mask, out_grad[0], expert_w, 8, 5, 85
    )
    share_experts = lax.psum_scatter(grad_experts, "ctx", scatter_dimension=0, tiled=True)
    (d_mix,) = gather_all([d_mix_own], "wa", 7, 28)

    d_y, d_z, grad_skip, f_in, t_in, f_dev = call(
        functools.partial(gate_back_kernel, states, ranked + states), "gate_back", group,
        [(d_mix, 0), (wout, None), (y_full, 0), (z, 0), (u_f, 0), (projected, 0), (step_size, 0),
         (cut, 0), (a_mat, None)],
        [(vec, F32, 0), ((group, rows, padded), BF16, 0), ((1, padded), F32, None),
         (seg_states, F32, 0), (seg_sums, F32, 0), (dev_states, BF16, 0)],
        [spread_vmem, lane_vmem, state_vmem], 11,
    )
    flat_n1 = n1.reshape(group * rows, width)
    zo_shape = (ring // 2, 2, in_rows, 2 * padded)
    (grad_zo,) = call(
        functools.partial(pack_zo_kernel, ring, in_rows, local), "pack_zo", 1,
        [(flat_n1, None), (d_z.reshape(group * rows, padded), None),
         (d_mix.reshape(group * length, width), None), (gated.reshape(group * length, padded), None)],
        [(zo_shape, BF16, None)], [], 5,
    )
    all_f, pair_zo = carry([f_dev], 8, 10, grad_zo)
    zo_half = pltpu.VMEM((ring // 2, in_rows, 2 * padded), BF16)
    dma = pltpu.SemaphoreType.DMA
    d_part, d_u, grad_dt, grad_step_bias, grad_a, chunk_zo = call(
        functools.partial(scan_back_kernel, states, ranked), "scan_back", group,
        [(projected, 0), (step_size, 0), (sig, 0), (u_f, 0), (cut, 0), (d_y, 0),
         (a_mat, None), (vectors, None), (wdt, None), (h_in, 0), (s_in, 0), (e_in, 0), (f_in, 0),
         (t_in, 0), (all_f, 1), (all_s, 1), (grad_zo, ANY), (pair_zo, ANY)],
        [((group, length, columns), BF16, 0), (vec, F32, 0), ((columns, padded), F32, None),
         ((1, padded), F32, None), ((states, SEG, padded), F32, None), ((in_rows, 2 * padded), BF16, None)],
        [spread_vmem, spread_vmem, spread_vmem, f32_vmem(length + SEG, states * LANE), spread_vmem,
         spread_vmem, lane_vmem, lane_vmem, lane_vmem, state_vmem,
         zo_half, zo_half, pltpu.VMEM((ring // 2 - 1, in_rows, 2 * padded), BF16),
         dma((2,)), dma((ring // 2 - 1,)), dma((ring // 2 - 1,))], 34, 12,
    )
    d_projected = sum_all(d_part, 9, 11)
    d_x, d_n1_part, grad_conv, grad_x, gain_terms = call(
        functools.partial(conv_back_kernel, taps, documents), "conv_back", group,
        [(place_s, SMEM), (docs, SMEM), (d_projected, 0), (wproj, None), (d_u, 0), (pre_conv, 0),
         (ext, 0), (u, 0), (conv, None), (d_z, 0), (proj_in, of_x), (proj_in, of_z), (n1, 0)],
        [((group, rows, padded), BF16, 0), ((group, rows, width), BF16, 0),
         ((SEG, padded), F32, None), ((columns, padded), F32, None), ((1, width), F32, None)],
        [f32_vmem((taps - 1) * SEG + length, LANE)], 10,
    )
    small_all = columns + up_to(ranked, SEG) + states + 3 * SEG
    small_each = up_to(-(-small_all // ring), SEG)
    small_rows = up_to(small_each, 16)
    (packed,) = call(
        functools.partial(pack_rest_kernel, ring, in_rows, small_rows, group, experts, ranked),
        "pack_rest", 1,
        [(mine_s, SMEM), (flat_n1, None), (d_x.reshape(group * rows, padded), None), (grad_x, None),
         (grad_dt, None), (grad_a, None), (a_mat, None), (grad_conv, None), (grad_step_bias, None),
         (grad_skip, None), (gain_terms, None), (gains, None), (grad_gain_moe, None),
         (grad_router, None), (out_sums, None), (mix_sum, None)],
        [((ring // 2, 2, in_rows + small_rows + 16, padded), BF16, None)],
        [f32_vmem(ring * small_each, padded), f32_vmem(SEG, width)], 5,
    )
    done, d_n1_terms, d_edges = finish(packed, chunk_zo, d_n1_part, in_rows, small_rows, 11)
    blocks = width // in_rows
    of_rows = lambda shape: pl.BlockSpec(
        (shape[0] // blocks, shape[1]), lambda i: (jnp.minimum(i, blocks - 1), 0)
    )
    unpacked = call(
        functools.partial(
            unpack_kernel, ring, group, in_rows, small_rows, experts, states, ranked, taps,
            float(length * ring * width),
        ),
        "unpack", ring,
        [(mine_s, SMEM), (done, 0), (share_experts, None), (last_s, SMEM), (d_n1_terms, None),
         (d_edges, None), (tokens[0], None), (gains, None), (d_h1, None), (result, None)],
        [((width, 2 * local), F32, of_rows), ((local, width), F32, of_rows),
         ((width, w_down.shape[1]), F32, None), ((w_down.shape[1], width), F32, None),
         ((taps, local), F32, None), ((w_x.shape[1], local), F32, None), ((ranked, local), F32, None),
         ((states, local), F32, None), ((2 * SEG, padded), F32, None), ((1, LANE), F32, None),
         (row_f, F32, None), (row_f, F32, None)],
        [f32_vmem(ring * small_each, padded), f32_vmem(SEG, padded), f32_vmem(length, width), order_vmem],
        9,
    )
    share_in, share_out, share_up, share_down, g_taps, g_wx, g_wdt, g_a, vecs, stats, input_grad, layer_out = unpacked
    fulls, vecs = vecs[:SEG, :share], vecs[SEG:, :local]
    return (
        layer_out[None],
        input_grad[None],
        fulls[0],
        share_in,
        g_taps,
        vecs[0],
        g_wx.T,
        g_wdt,
        vecs[1],
        g_a,
        vecs[2],
        share_out,
        fulls[1],
        fulls[2 : 2 + experts].T,
        share_up[None],
        share_down[None],
        stats[:, :3],
    )


def solution(mesh):
    placed = (
        P("wa", "ctx", None),
        P("wa", "ctx", None),
        P("wa", None),
        P("wa", "ctx", None),
        P("wa", "ctx"),
        P("wa"),
        P(None, "wa"),
        P(None, "wa"),
        P("wa"),
        P("wa", None),
        P(None, "wa"),
        P("wa"),
        P(None, "wa"),
        P("wa"),
        P("wa", None),
        P("wa"),
        P("wa", None),
        P("wa", None, "ctx"),
        P("wa", "ctx", None),
    )
    return jax.shard_map(
        body,
        mesh=mesh,
        in_specs=placed,
        out_specs=(
            P("wa", "ctx", None),
            P("wa", "ctx", None),
            P("wa"),
            P(None, "wa"),
            P(None, "wa"),
            P("wa"),
            P("wa", None),
            P(None, "wa"),
            P("wa"),
            P(None, "wa"),
            P("wa"),
            P("wa", None),
            P("wa"),
            P("wa", None),
            P("wa", None, "ctx"),
            P("wa", "ctx", None),
            P("wa", None),
        ),
        check_vma=False,
    )
```

```python
import functools

import jax
import jax.numpy as jnp
from jax import lax
from jax.experimental import pallas as pl
from jax.experimental.pallas import tpu as pltpu
from jax.sharding import PartitionSpec as P

EPS = 1e-05
F32 = jnp.float32
BF16 = jnp.bfloat16
SEG = 8
LANE = 128
EDGE = 16
CUT = 1e30
MESH = pl.DeviceIdType.MESH
VMEM_LIMIT = 24 * 2**20
LARGE_LIMIT = 60 * 2**20


def lasting(us):
    return pl.CostEstimate(
        flops=int(us * 1.1e9), bytes_accessed=int(us * 3.5e6), transcendentals=0
    )


def greet(axis, count):
    me = lax.axis_index(axis)
    barrier = pltpu.get_barrier_semaphore()
    for k in range(1, count):
        pl.semaphore_signal(
            barrier, inc=1, device_id={axis: lax.rem(me + k, count)}, device_id_type=MESH
        )
    pl.semaphore_wait(barrier, count - 1)
    return me


def gather_kernel(axis, count, arrays, *refs):
    srcs, dsts = refs[:arrays], refs[arrays : 2 * arrays]
    send, recv, own = refs[-3:]
    me = greet(axis, count)
    copies = []
    for i in range(arrays):
        for k in range(1, count):
            copy = pltpu.make_async_remote_copy(
                src_ref=srcs[i],
                dst_ref=dsts[i].at[me],
                send_sem=send.at[i, k],
                recv_sem=recv.at[i, k],
                device_id={axis: lax.rem(me + k, count)},
                device_id_type=MESH,
            )
            copy.start()
            copies.append(copy)
    for i in range(arrays):
        local = pltpu.make_async_copy(srcs[i], dsts[i].at[me], own.at[i])
        local.start()
        copies.append(local)
    for copy in copies:
        copy.wait()


def trade_kernel(axis, count, x_ref, o_ref, send, recv, own):
    me = greet(axis, count)
    copies = []
    for k in range(1, count):
        other = lax.rem(me + k, count)
        copy = pltpu.make_async_remote_copy(
            src_ref=x_ref.at[other],
            dst_ref=o_ref.at[me],
            send_sem=send.at[k],
            recv_sem=recv.at[k],
            device_id={axis: other},
            device_id_type=MESH,
        )
        copy.start()
        copies.append(copy)
    local = pltpu.make_async_copy(x_ref.at[me], o_ref.at[me], own)
    local.start()
    local.wait()
    for copy in copies:
        copy.wait()


def trade(x, axis, cid, us):
    count = lax.axis_size(axis)
    return pl.pallas_call(
        functools.partial(trade_kernel, axis, count),
        out_shape=jax.ShapeDtypeStruct(x.shape, x.dtype),
        in_specs=[pl.BlockSpec(memory_space=pl.ANY)],
        out_specs=pl.BlockSpec(memory_space=pl.ANY),
        scratch_shapes=[
            pltpu.SemaphoreType.DMA((count,)),
            pltpu.SemaphoreType.DMA((count,)),
            pltpu.SemaphoreType.DMA,
        ],
        compiler_params=pltpu.CompilerParams(
            collective_id=cid, has_side_effects=True, vmem_limit_bytes=VMEM_LIMIT
        ),
        cost_estimate=lasting(us),
        name=f"trade_{cid}",
    )(x)


def sum_start(mates, x_ref, got, send, recv):
    copies = []
    for k, who in enumerate(mates):
        copy = remote(x_ref.at[who], got.at[k], send.at[k], recv.at[k], {"wa": who})
        copy.start()
        copies.append(copy)
    return copies


def sum_spread(mine, mates, x_ref, got, o_ref, copies, send, recv):
    for copy in copies:
        copy.wait_recv()
    parts = [x_ref.at[mine]] + [got.at[k] for k in range(len(mates))]
    add_rows(o_ref.at[mine], parts, x_ref.shape[1])
    spreads = []
    for k, who in enumerate(mates):
        copy = remote(o_ref.at[mine], o_ref.at[mine], send.at[k], recv.at[k], {"wa": who})
        copy.start()
        spreads.append(copy)
    return spreads


def sum_all_kernel(group, x_ref, o_ref, got, s1, r1, s2, r2):
    greet("wa", group)
    mine, mates = mates_of(group)
    copies = sum_start(mates, x_ref, got, s1, r1)
    spreads = sum_spread(mine, mates, x_ref, got, o_ref, copies, s2, r2)
    for copy in spreads:
        copy.wait()
    for copy in copies:
        copy.wait_send()


def sum_all(x, cid, us):
    group = lax.axis_size("wa")
    vmem = pl.BlockSpec(memory_space=pltpu.VMEM)
    dma = pltpu.SemaphoreType.DMA
    return pl.pallas_call(
        functools.partial(sum_all_kernel, group),
        out_shape=jax.ShapeDtypeStruct(x.shape, x.dtype),
        in_specs=[vmem],
        out_specs=vmem,
        scratch_shapes=[pltpu.VMEM((group - 1,) + x.shape[1:], x.dtype)] + [dma((group - 1,))] * 4,
        compiler_params=pltpu.CompilerParams(
            collective_id=cid, has_side_effects=True, vmem_limit_bytes=VMEM_LIMIT
        ),
        cost_estimate=lasting(us),
        name="sum_all",
    )(x)


def gather_all(xs, axis, cid, us):
    count, arrays = lax.axis_size(axis), len(xs)
    return pl.pallas_call(
        functools.partial(gather_kernel, axis, count, arrays),
        out_shape=[jax.ShapeDtypeStruct((count,) + x.shape, x.dtype) for x in xs],
        in_specs=[pl.BlockSpec(memory_space=pl.ANY)] * arrays,
        out_specs=[pl.BlockSpec(memory_space=pl.ANY)] * arrays,
        scratch_shapes=[
            pltpu.SemaphoreType.DMA((arrays, count)),
            pltpu.SemaphoreType.DMA((arrays, count)),
            pltpu.SemaphoreType.DMA((arrays,)),
        ],
        compiler_params=pltpu.CompilerParams(
            collective_id=cid, has_side_effects=True, vmem_limit_bytes=VMEM_LIMIT
        ),
        cost_estimate=lasting(us),
        name=f"gather_{cid}",
    )(*xs)


def remote(src, dst, send, recv, where):
    return pltpu.make_async_remote_copy(
        src_ref=src, dst_ref=dst, send_sem=send, recv_sem=recv,
        device_id=where, device_id_type=MESH,
    )


def add_rows(out, parts, rows):
    def one(i, _):
        at = pl.ds(pl.multiple_of(i * 16, 16), 16)
        total = parts[0][at, :].astype(F32)
        for part in parts[1:]:
            total = total + part[at, :].astype(F32)
        out[at, :] = total.astype(out.dtype)
        return 0

    lax.fori_loop(0, rows // 16, one, 0)


def neighbours(ring):
    me = lax.axis_index("ctx")
    half = ring // 2
    lane = lax.rem(me, 2)
    chip = me // 2
    peers = [lax.rem(chip + k, half) * 2 + lane for k in range(1, half)]
    return me, chip, lane, me + 1 - 2 * lane, peers


def mates_of(group):
    mine = lax.axis_index("wa")
    return mine, [lax.rem(mine + k, group) for k in range(1, group)]


def hello(barrier, axis, who):
    pl.semaphore_signal(barrier, inc=1, device_id={axis: who}, device_id_type=MESH)


def carry_kernel(ring, arrays, halved, *refs):
    total = arrays + halved
    srcs, dsts = refs[:total], refs[total : 2 * total]
    send, recv, fwd_s, fwd_r, own, half_s, half_r = refs[2 * total :]
    me, chip, lane, pair, peers = neighbours(ring)
    half = ring // 2
    barrier = pltpu.get_barrier_semaphore()
    for who in [pair] + peers:
        hello(barrier, "ctx", who)
    pl.semaphore_wait(barrier, half)
    copies, forwards, local = [], [], []
    for i in range(arrays):
        for k, who in enumerate(peers):
            copies.append(remote(srcs[i], dsts[i].at[me], send.at[i, k], recv.at[i, k], {"ctx": who}))
            copies[-1].start()
    for i in range(arrays):
        forwards.append(remote(srcs[i], dsts[i].at[me], fwd_s.at[i, 0], fwd_r.at[i, 0], {"ctx": pair}))
        forwards[-1].start()
        local.append(pltpu.make_async_copy(srcs[i], dsts[i].at[me], own.at[i]))
        local[-1].start()
    if halved:
        to_pair = remote(srcs[arrays].at[:, 1 - lane], dsts[arrays], half_s, half_r, {"ctx": pair})
        to_pair.start()
        local.append(to_pair)
    for i in range(arrays):
        for k in range(1, half):
            copies[i * (half - 1) + k - 1].wait_recv()
            block = dsts[i].at[lax.rem(chip + half - k, half) * 2 + lane]
            forwards.append(remote(block, block, fwd_s.at[i, k], fwd_r.at[i, k], {"ctx": pair}))
            forwards[-1].start()
    for copy in copies:
        copy.wait_send()
    for copy in forwards + local:
        copy.wait()


def carry(xs, cid, us, halved=None):
    ring, arrays = lax.axis_size("ctx"), len(xs)
    half = ring // 2
    shapes = [((ring,) + x.shape, x.dtype) for x in xs]
    if halved is not None:
        xs = xs + [halved]
        shapes.append((halved.shape[:1] + halved.shape[2:], halved.dtype))
    hbm = pl.BlockSpec(memory_space=pl.ANY)
    dma = pltpu.SemaphoreType.DMA
    return pl.pallas_call(
        functools.partial(carry_kernel, ring, arrays, len(xs) - arrays),
        out_shape=[jax.ShapeDtypeStruct(shape, dtype) for shape, dtype in shapes],
        in_specs=[hbm] * len(xs),
        out_specs=[hbm] * len(xs),
        scratch_shapes=[
            dma((arrays, half - 1)), dma((arrays, half - 1)), dma((arrays, half)), dma((arrays, half)),
            dma((arrays,)), dma, dma,
        ],
        compiler_params=pltpu.CompilerParams(
            collective_id=cid, has_side_effects=True, vmem_limit_bytes=VMEM_LIMIT
        ),
        cost_estimate=lasting(us),
        name=f"carry_{cid}",
    )(*xs)


def finish_kernel(
    ring, group, in_rows, small_rows,
    g_ref, zf_ref, d_ref, o_ref, dt_ref, de_ref,
    from_pair, paired, came, own, zin, tiles, fin, store_s,
    pair_s, pair_r, ctx_s, ctx_r, z_s, z_r, tile_s, tile_r, d_s, d_r, d_own, last_s, last_r, fwd_s, fwd_r,
    edge_s, edge_r,
):
    me, chip, lane, pair, peers = neighbours(ring)
    mine, mates = mates_of(group)
    half = ring // 2
    rows = in_rows + small_rows + 16
    lanes = g_ref.shape[3]
    barrier = pltpu.get_barrier_semaphore()
    for who in [pair] + peers:
        hello(barrier, "ctx", who)
    for who in mates:
        hello(barrier, "wa", who)
    has_next = me < ring - 1
    has_last = me > 0

    @pl.when(has_next)
    def _():
        hello(barrier, "ctx", me + 1)

    @pl.when(has_last)
    def _():
        hello(barrier, "ctx", me - 1)

    around = jnp.where(has_next, 1, 0) + jnp.where(has_last, 1, 0)
    pl.semaphore_wait(barrier, half + group - 1 + around)

    to_pair = remote(g_ref.at[:, 1 - lane], from_pair, pair_s, pair_r, {"ctx": pair})
    to_pair.start()
    small_at = 2 * in_rows + 16
    parts = [
        pl.ds(small_at + small_rows, in_rows), pl.ds(small_at, small_rows),
        pl.ds(0, in_rows), pl.ds(in_rows, in_rows + 16),
    ]
    fin[parts[0]] = zf_ref[:, lanes:]
    stored = []

    def to_all(i):
        src, dst = fin.at[parts[i]], o_ref.at[me, parts[i]]
        copies = []
        for k, who in enumerate(peers):
            copies.append(remote(src, dst, last_s.at[i, k], last_r.at[i, k], {"ctx": who}))
        copies.append(remote(src, dst, fwd_s.at[i, 0], fwd_r.at[i, 0], {"ctx": pair}))
        for copy in copies:
            copy.start()
        stored.append(pltpu.make_async_copy(src, dst, store_s.at[i]))
        stored[-1].start()
        return copies

    def forward(i, copies):
        for k in range(1, half):
            copies[k - 1].wait_recv()
            source = lax.rem(chip + half - k, half) * 2 + lane
            block = o_ref.at[source, parts[i]]
            copy = remote(block, block, fwd_s.at[i, k], fwd_r.at[i, k], {"ctx": pair})
            copy.start()
            copies.append(copy)

    x_to = mine // 2
    z_to = group // 2 + mine // 2
    slot = lax.rem(mine, 2)
    z_ref = zf_ref.at[:, pl.ds(0, lanes)]
    x_ref = own.at[pl.ds(0, in_rows)]
    send_x = remote(x_ref, zin.at[slot], z_s.at[0], z_r.at[slot], {"wa": x_to})
    send_z = remote(z_ref, zin.at[slot], z_s.at[1], z_r.at[slot], {"wa": z_to})
    keep_x = pltpu.make_async_copy(x_ref, zin.at[slot], z_r.at[slot])
    keep_z = pltpu.make_async_copy(z_ref, zin.at[slot], z_r.at[slot])

    @pl.when(z_to != mine)
    def _():
        send_z.start()

    @pl.when(z_to == mine)
    def _():
        keep_z.start()

    cut = d_ref.shape[1] // 32 * 16
    pieces = [pl.ds(0, cut), pl.ds(cut, d_ref.shape[1] - cut)]
    trades = []

    def trade_rows(i):
        for k, who in enumerate(mates):
            copy = remote(
                d_ref.at[who, pieces[i]], dt_ref.at[mine, pieces[i]], d_s.at[i, k], d_r.at[i, k],
                {"wa": who},
            )
            copy.start()
            trades.append(copy)

    trade_rows(0)
    kept = pltpu.make_async_copy(d_ref.at[mine], dt_ref.at[mine], d_own)
    kept.start()

    to_pair.wait_recv()
    scattered = []
    for k, who in enumerate(peers):
        to = lax.rem(chip + k + 1, half)
        add_rows(paired.at[to], [g_ref.at[to, lane], from_pair.at[to]], rows)
        copy = remote(paired.at[to], came.at[k], ctx_s.at[k], ctx_r.at[k], {"ctx": who})
        copy.start()
        scattered.append(copy)
    early = to_all(0)
    add_rows(paired.at[chip], [g_ref.at[chip, lane], from_pair.at[chip]], rows)
    for copy in scattered:
        copy.wait_recv()
    add_rows(own, [paired.at[chip]] + [came.at[k] for k in range(half - 1)], rows)

    @pl.when(x_to != mine)
    def _():
        send_x.start()

    @pl.when(x_to == mine)
    def _():
        keep_x.start()

    tile = pl.ds(in_rows + small_rows, 16)
    spread_tiles = []
    for k, who in enumerate(mates):
        copy = remote(own.at[tile], tiles.at[k], tile_s.at[k], tile_r.at[k], {"wa": who})
        copy.start()
        spread_tiles.append(copy)
    fin[parts[1]] = own[pl.ds(in_rows, small_rows)]
    middle_rows = to_all(1)
    forward(0, early)

    def landed(slot):
        pltpu.make_async_copy(zin.at[slot], zin.at[slot], z_r.at[slot]).wait()
        fin[pl.ds(slot * in_rows, in_rows)] = zin[slot]

    landed(0)
    late = [to_all(2)]
    forward(1, middle_rows)
    for copy in spread_tiles:
        copy.wait_recv()
    add_rows(
        fin.at[pl.ds(2 * in_rows, 16)],
        [own.at[tile]] + [tiles.at[k] for k in range(group - 1)],
        16,
    )
    landed(1)
    late.append(to_all(3))
    trade_rows(1)
    kept.wait()
    forward(2, late[0])
    forward(3, late[1])

    for copy in trades:
        copy.wait_recv()
    edges = dt_ref.at[:, pl.ds(d_ref.shape[1] - EDGE, EDGE)]
    to_last = remote(edges, de_ref, edge_s, edge_r, {"ctx": me - 1})

    @pl.when(has_last)
    def _():
        to_last.start()

    for copies in [early, middle_rows] + late:
        for copy in copies[half - 1 :]:
            copy.wait_recv()

    for copy in stored:
        copy.wait()
    to_pair.wait_send()
    for copy in scattered + spread_tiles + early + middle_rows + late[0] + late[1] + trades:
        copy.wait_send()

    @pl.when(x_to != mine)
    def _():
        send_x.wait_send()

    @pl.when(z_to != mine)
    def _():
        send_z.wait_send()

    @pl.when(has_last)
    def _():
        to_last.wait_send()

    @pl.when(has_next)
    def _():
        to_last.wait_recv()


def finish(g, zf, d, in_rows, small_rows, cid):
    ring, group = lax.axis_size("ctx"), lax.axis_size("wa")
    half = ring // 2
    rows, lanes = g.shape[2:]
    out_rows = 3 * in_rows + small_rows + 16
    vmem = pl.BlockSpec(memory_space=pltpu.VMEM)
    hbm = pl.BlockSpec(memory_space=pl.ANY)
    dma = pltpu.SemaphoreType.DMA
    return pl.pallas_call(
        functools.partial(finish_kernel, ring, group, in_rows, small_rows),
        out_shape=[
            jax.ShapeDtypeStruct((ring, out_rows, lanes), BF16),
            jax.ShapeDtypeStruct(d.shape, d.dtype),
            jax.ShapeDtypeStruct((group, EDGE, d.shape[2]), d.dtype),
        ],
        in_specs=[vmem, vmem, hbm],
        out_specs=[hbm, hbm, hbm],
        scratch_shapes=[
            pltpu.VMEM((half, rows, lanes), BF16),
            pltpu.VMEM((half, rows, lanes), BF16),
            pltpu.VMEM((half - 1, rows, lanes), BF16),
            pltpu.VMEM((rows, lanes), BF16),
            pltpu.VMEM((2, in_rows, lanes), BF16),
            pltpu.VMEM((group - 1, 16, lanes), BF16),
            pltpu.VMEM((out_rows, lanes), BF16),
            dma((4,)), dma, dma,
            dma((half - 1,)), dma((half - 1,)),
            dma((2,)), dma((2,)),
            dma((group - 1,)), dma((group - 1,)),
            dma((2, group - 1)), dma((2, group - 1)), dma,
            dma((4, half - 1)), dma((4, half - 1)),
            dma((4, half)), dma((4, half)),
            dma, dma,
        ],
        compiler_params=pltpu.CompilerParams(
            collective_id=cid, has_side_effects=True, vmem_limit_bytes=VMEM_LIMIT
        ),
        cost_estimate=lasting(60),
        name="finish",
    )(g, zf, d)


def start_kernel(
    ring, group, tok, par, doc, w_ref, tok_o, edge_o, par_o, doc_o, w_o,
    mate_s, mate_r, own_s, edge_s, edge_r, relay_s, relay_r, shift_s, shift_r, out_s, out_r, fwd_s, fwd_r,
):
    me = lax.axis_index("ctx")
    mine = lax.axis_index("wa")
    half = ring // 2
    lane = lax.rem(me, 2)
    chip = me // 2
    pair = me + 1 - 2 * lane
    peers = [lax.rem(chip + k, half) * 2 + lane for k in range(1, half)]
    mates = [lax.rem(mine + k, group) for k in range(1, group)]
    barrier = pltpu.get_barrier_semaphore()
    for who in [pair] + peers:
        pl.semaphore_signal(barrier, inc=1, device_id={"ctx": who}, device_id_type=MESH)
    for who in mates:
        pl.semaphore_signal(barrier, inc=1, device_id={"wa": who}, device_id_type=MESH)
    has_next = me < ring - 1
    has_last = me > 0

    @pl.when(has_next)
    def _():
        pl.semaphore_signal(barrier, inc=1, device_id={"ctx": me + 1}, device_id_type=MESH)

    @pl.when(has_last)
    def _():
        pl.semaphore_signal(barrier, inc=1, device_id={"ctx": me - 1}, device_id_type=MESH)

    around = jnp.where(has_next, 1, 0) + jnp.where(has_last, 1, 0)
    pl.semaphore_wait(barrier, half + group - 1 + around)

    edge = tok.at[pl.ds(tok.shape[0] - EDGE, EDGE)]
    to_next = remote(edge, edge_o.at[mine], edge_s, edge_r, {"ctx": me + 1})

    @pl.when(has_next)
    def _():
        to_next.start()

    kind = mine // (group // 2)
    base = 2 * lax.rem(mine, group // 2)
    for h in range(2):
        where = base + h
        send = remote(
            w_ref.at[h], w_o.at[kind, me], shift_s.at[h], shift_r.at[kind], {"wa": where}
        )
        keep = pltpu.make_async_copy(w_ref.at[h], w_o.at[kind, me], shift_r.at[kind])

        @pl.when(where != mine)
        def _():
            send.start()

        @pl.when(where == mine)
        def _():
            keep.start()

    trades = []
    for i, (src, dst) in enumerate(((par, par_o), (doc, doc_o), (tok, tok_o))):
        for k, who in enumerate(mates):
            copy = remote(src, dst.at[mine], mate_s.at[i, k], mate_r.at[i, k], {"wa": who})
            copy.start()
            trades.append(copy)
        keep = pltpu.make_async_copy(src, dst.at[mine], own_s.at[i])
        keep.start()

    @pl.when(has_last)
    def _():
        to_next.wait_recv()
        for k, who in enumerate(mates):
            remote(
                edge_o.at[mine], edge_o.at[mine], relay_s.at[k], relay_r.at[k], {"wa": who}
            ).start()

    sends = []
    for t in range(2):
        block = w_o.at[t, me]
        pltpu.make_async_copy(block, block, shift_r.at[t]).wait()
        for k, who in enumerate(peers):
            copy = remote(block, block, out_s.at[t, k], out_r.at[t, k], {"ctx": who})
            copy.start()
            sends.append(copy)
        copy = remote(block, block, fwd_s.at[t, 0], fwd_r.at[t, 0], {"ctx": pair})
        copy.start()
        sends.append(copy)
    forwards = []
    for t in range(2):
        for k in range(1, half):
            source = lax.rem(chip + half - k, half) * 2 + lane
            block = w_o.at[t, source]
            pltpu.make_async_copy(block, block, out_r.at[t, k - 1]).wait()
            copy = remote(block, block, fwd_s.at[t, k], fwd_r.at[t, k], {"ctx": pair})
            copy.start()
            forwards.append(copy)
    for t in range(2):
        for k in range(half):
            pltpu.make_async_copy(w_o.at[t, me], w_o.at[t, me], fwd_r.at[t, k]).wait()
    for copy in sends + forwards:
        copy.wait_send()
    for h in range(2):

        @pl.when(base + h != mine)
        def _():
            remote(
                w_ref.at[h], w_o.at[kind, me], shift_s.at[h], shift_r.at[kind], {"wa": mine}
            ).wait_send()

    for copy in trades:
        copy.wait()
    for i, (src, dst) in enumerate(((par, par_o), (doc, doc_o), (tok, tok_o))):
        pltpu.make_async_copy(src, dst.at[mine], own_s.at[i]).wait()

    @pl.when(has_next)
    def _():
        to_next.wait_send()

    @pl.when(has_last)
    def _():
        for k, who in enumerate(mates):
            remote(
                edge_o.at[mine], edge_o.at[mine], relay_s.at[k], relay_r.at[k], {"wa": who}
            ).wait()


def start(tok, par, doc, halves, cid):
    ring, group = lax.axis_size("ctx"), lax.axis_size("wa")
    half = ring // 2
    hbm = pl.BlockSpec(memory_space=pl.ANY)
    dma = pltpu.SemaphoreType.DMA
    outs = [(group,) + a.shape for a in (tok, tok[:EDGE], par, doc)] + [(2, ring) + halves.shape[1:]]
    types = [a.dtype for a in (tok, tok, par, doc, halves)]
    return pl.pallas_call(
        functools.partial(start_kernel, ring, group),
        out_shape=[jax.ShapeDtypeStruct(s, t) for s, t in zip(outs, types)],
        in_specs=[hbm] * 4,
        out_specs=[hbm] * 5,
        scratch_shapes=[
            dma((3, group - 1)), dma((3, group - 1)), dma((3,)),
            dma, dma,
            dma((group - 1,)), dma((group - 1,)),
            dma((2,)), dma((2,)),
            dma((2, half - 1)), dma((2, half - 1)),
            dma((2, half)), dma((2, half)),
        ],
        compiler_params=pltpu.CompilerParams(
            collective_id=cid, has_side_effects=True, vmem_limit_bytes=VMEM_LIMIT
        ),
        cost_estimate=lasting(35),
        name="start",
    )(tok, par, doc, halves)


def pick(rows, states, at):
    shape = (rows, states * LANE)
    lower = (lax.broadcasted_iota(jnp.int32, shape, 0) - at) * LANE
    place = lax.broadcasted_iota(jnp.int32, shape, 1)
    return jnp.where((place >= lower) & (place < lower + LANE), 1.0, 0.0)


def spread(rows, states, at):
    return jnp.dot(rows, pick(rows.shape[1], states, at).astype(BF16), preferred_element_type=F32)


def collected(wide_rows, states, columns, at):
    shape = (states * LANE, columns)
    lower = (lax.broadcasted_iota(jnp.int32, shape, 1) - at) * LANE
    place = lax.broadcasted_iota(jnp.int32, shape, 0)
    ones = jnp.where((place >= lower) & (place < lower + LANE), 1.0, 0.0).astype(BF16)
    coarse = wide_rows.astype(BF16)
    rest = (wide_rows - coarse.astype(F32)).astype(BF16)
    return dot_nn(coarse, ones) + dot_nn(rest, ones)


def position_of(shape, axis, steps):
    row = lax.broadcasted_iota(jnp.int32, shape, axis)
    return (row & (SEG - 1)) * steps + (row >> 3)


def permutation(length):
    shape = (length, length)
    at = position_of(shape, 0, length // SEG)
    return jnp.where(at == lax.broadcasted_iota(jnp.int32, shape, 1), 1.0, 0.0).astype(BF16)


def rolled(value, by):
    return pltpu.roll(value, by % SEG, 0)


def lanes_of(g):
    return pl.ds(pl.multiple_of(g * LANE, LANE), LANE)


def rows_of(j):
    return pl.ds(pl.multiple_of(j * SEG, SEG), SEG)


def wide(ref, n, lanes):
    return jnp.broadcast_to(ref[pl.ds(n, 1), lanes], (SEG, LANE))


def state_cols(n):
    return slice(n * LANE, (n + 1) * LANE)


def dot_nt(a, b):
    return lax.dot_general(a, b, (((1,), (1,)), ((), ())), preferred_element_type=F32)


def dot_tn(a, b):
    return lax.dot_general(a, b, (((0,), (0,)), ((), ())), preferred_element_type=F32)


def dot_nn(a, b):
    return jnp.dot(a, b, preferred_element_type=F32)


def rms_scale(values):
    return lax.rsqrt(jnp.mean(values * values, axis=-1, keepdims=True) + EPS)


def norm_grads(values, scale, gain, d_out):
    unit = values * scale
    d_unit = d_out * gain
    d_values = scale * (d_unit - unit * jnp.mean(d_unit * unit, axis=-1, keepdims=True))
    return d_values, d_out * unit


def silu_slope(v):
    s = jax.nn.sigmoid(v)
    return s * (1.0 + v * (1.0 - s))


def seg_of():
    return lax.broadcasted_iota(jnp.int32, (SEG, LANE), 0)


def lag_masks(place, doc_ref, documents, stream, length, taps):
    at = place * length + position_of((length, LANE), 0, length // SEG)
    masks = [None]
    for lag in range(1, taps):
        cut = None
        for d in range(documents):
            begin = doc_ref[stream, 0, d]
            here = (begin > at - lag) & (begin <= at)
            cut = here if cut is None else cut | here
        masks.append(jnp.where(cut, 0.0, 1.0))
    hit = None
    for d in range(documents):
        here = doc_ref[stream, 0, d] == at
        hit = here if hit is None else hit | here
    return masks, jnp.where(hit, CUT, 0.0)


def enter_kernel(
    taps, documents, place_ref, doc_ref, tok, edge, gain, wx, wz, conv, wproj,
    n1_o, ext_o, pre_o, uf_o, u_o, z_o, part_o, cut_o,
):
    length = tok.shape[1]
    steps = length // SEG
    place = place_ref[0]
    gains = gain[0:1]

    def normal(rows):
        return (rows * rms_scale(rows) * gains).astype(BF16)

    n1_o[0, :length] = normal(dot_nn(permutation(length), tok[0]))
    n1_o[0, length:] = normal(jnp.where(place > 0, edge[0].astype(F32), 0.0))
    inner = dot_nn(n1_o[0], wx[0]).astype(BF16).astype(F32)
    z_o[0] = dot_nn(n1_o[0, :length], wz[0]).astype(BF16)
    masks, cut = lag_masks(place, doc_ref, documents, pl.program_id(0), length, taps)
    cut_o[0] = cut
    seg = seg_of()
    behind = taps - 1
    for g in range(inner.shape[1] // LANE):
        cols = slice(g * LANE, (g + 1) * LANE)
        rows, before = inner[:length, cols], inner[length:, cols]
        parts = []
        for i in range(behind):
            j = steps - behind + i
            last = jnp.broadcast_to(before[EDGE - behind + i : EDGE - behind + i + 1], (SEG, LANE))
            parts.append(jnp.where(seg == 0, last, rolled(rows[j * SEG : (j + 1) * SEG], 1)))
        ext = jnp.concatenate(parts + [rows], axis=0)
        ext_o[0, :, cols] = ext
        pre = conv[taps : taps + 1, cols] + conv[0:1, cols] * rows
        for lag in range(1, taps):
            window = ext[(behind - lag) * SEG : (behind - lag) * SEG + length]
            pre = pre + conv[lag : lag + 1, cols] * window * masks[lag]
        pre_o[0, :, cols] = pre
        u = (pre * jax.nn.sigmoid(pre)).astype(BF16)
        u_o[0, :, cols] = u
        uf_o[0, :, cols] = u.astype(F32)
    part_o[0] = dot_nt(u_o[0], wproj[...]).astype(BF16)


def summary_kernel(
    states, b_at, proj_i, wdt, bias, uf, cut, a_ref,
    step_o, sig_o, hx_ref, sx_ref, hd_o, sd_ref, bb, st_s, dr_s, hd_s,
):
    length, width = step_o.shape[1:]
    groups, steps = width // LANE, length // SEG
    proj = proj_i[0]
    bb[...] = spread(proj, states, b_at)
    pre = dot_nn(proj, wdt[...]) + bias[0:1]
    step_size = jnp.maximum(pre, 0.0) + jnp.log1p(jnp.exp(-jnp.abs(pre)))
    step_o[0] = step_size
    sig_o[0] = jax.nn.sigmoid(pre)
    dr_s[...] = step_size * uf[0]
    for g in range(groups):
        cols = slice(g * LANE, (g + 1) * LANE)
        st_s[:, cols] = step_size[:, cols] + cut[0]
    zero = jnp.zeros((SEG, LANE), F32)
    seg = seg_of()

    def group(g, _):
        lanes = lanes_of(g)
        a = [wide(a_ref, n, lanes) for n in range(states)]

        def step(j, carry):
            rows = rows_of(j)
            st = st_s[rows, lanes]
            dr = dr_s[rows, lanes]
            new = [carry[0] + st]
            for n in range(states):
                new.append(jnp.exp(st * a[n]) * carry[n + 1] + bb[rows, state_cols(n)] * dr)
            return tuple(new)

        out = lax.fori_loop(0, steps, step, (zero,) * (states + 1), unroll=8)
        total, h = out[0], list(out[1:])
        for k in (1, 2, 4):
            ok = seg >= k
            for n in range(states):
                h[n] = h[n] + jnp.where(ok, jnp.exp(total * a[n]) * rolled(h[n], k), 0.0)
            total = total + jnp.where(ok, rolled(total, k), 0.0)
        ok = seg >= 1
        sx_ref[0, :, lanes] = jnp.where(ok, rolled(total, 1), 0.0)
        sd_ref[0, :, lanes] = total[SEG - 1 : SEG]
        for n in range(states):
            hx_ref[0, n, :, lanes] = jnp.where(ok, rolled(h[n], 1), 0.0)
            hd_s[pl.ds(n, 1), lanes] = h[n][SEG - 1 : SEG]
        return 0

    lax.fori_loop(0, groups, group, 0)
    hd_o[0] = hd_s[...].astype(BF16)


def entering(e_ref, finals, sums, a_ref, place, ahead):
    ring = finals.shape[0]
    e_ref[...] = jnp.zeros_like(e_ref)

    def one(lap, _):
        c = lap if ahead else ring - 1 - lap
        use = (c < place) if ahead else (c > place)

        @pl.when(use)
        def _():
            e_ref[...] = jnp.exp(sums[c, 0] * a_ref[...]) * e_ref[...] + finals[c, 0].astype(F32)

        return 0

    lax.fori_loop(0, ring, one, 0)


def output_kernel(
    group, states, b_at, proj, step_i, uf, cut, a_ref, hx_ref, sx_ref, finals, sums, z, skip, wout,
    y_o, gated_o, terms_o, e_o, bb, cb, st_s, dr_s, mix_s, send, recv, own_s,
):
    at = pl.program_id(0)
    mine = lax.axis_index("wa")
    barrier = pltpu.get_barrier_semaphore()
    goals = [lax.rem(mine + 1 + i, group) for i in range(group - 1)]
    sends = [
        remote(mix_s.at[i], terms_o.at[mine], send.at[i], recv.at[i], {"wa": who})
        for i, who in enumerate(goals)
    ]

    @pl.when(at == 0)
    def _():
        for who in goals:
            hello(barrier, "wa", who)

    length, width = step_i.shape[1:]
    groups, steps = width // LANE, length // SEG
    bb[...] = spread(proj[0], states, b_at)
    cb[...] = spread(proj[0], states, b_at + states)
    e_ref = e_o.at[0]
    entering(e_ref, finals, sums, a_ref, lax.axis_index("ctx"), True)
    dr_s[...] = step_i[0] * uf[0]
    for g in range(groups):
        cols = slice(g * LANE, (g + 1) * LANE)
        st_s[:, cols] = step_i[0, :, cols] + cut[0]

    def lane_group(g, _):
        lanes = lanes_of(g)
        a = [wide(a_ref, n, lanes) for n in range(states)]
        sx = sx_ref[0, :, lanes]
        first = tuple(
            jnp.exp(sx * a[n]) * wide(e_ref, n, lanes) + hx_ref[0, n, :, lanes]
            for n in range(states)
        )
        gain = wide(skip, 1, lanes)

        def step(j, h):
            rows = rows_of(j)
            st = st_s[rows, lanes]
            dr = dr_s[rows, lanes]
            new = []
            y = gain * uf[0, rows, lanes]
            for n in range(states):
                state = jnp.exp(st * a[n]) * h[n] + bb[rows, state_cols(n)] * dr
                new.append(state)
                y = y + cb[rows, state_cols(n)] * state
            y_o[0, rows, lanes] = y
            return tuple(new)

        lax.fori_loop(0, steps, step, first, unroll=8)
        return 0

    lax.fori_loop(0, groups, lane_group, 0)
    zf = z[0].astype(F32)
    gated = (y_o[0] * (zf * jax.nn.sigmoid(zf))).astype(BF16)
    gated_o[0] = gated
    mix_s[at] = dot_nn(gated, wout[...]).astype(BF16)
    for i, copy in enumerate(sends):

        @pl.when(at == i)
        def _():
            if i == 0:
                pl.semaphore_wait(barrier, group - 1)
            copy.start()

    @pl.when(at == group - 1)
    def _():
        kept = pltpu.make_async_copy(mix_s.at[group - 1], terms_o.at[mine], own_s)
        kept.start()
        for copy in sends + [kept]:
            copy.wait()


def route_kernel(
    experts, terms, tok, gain, router, route, keep, grad,
    h1_o, n2_o, up_o, cols_o, match_o, out_o, sums_o,
):
    length, width = tok.shape
    shift = permutation(length)
    mix = terms[0].astype(F32)
    for w in range(1, terms.shape[0]):
        mix = mix + terms[w].astype(F32)
    h1 = dot_nn(shift, tok[...]) + mix
    h1_o[...] = h1
    n2 = (h1 * rms_scale(h1) * gain[1:2]).astype(BF16)
    n2_o[...] = n2
    logits = dot_nt(n2, router[...])
    lane = lax.broadcasted_iota(jnp.int32, (length, LANE), 1)
    kind = lax.broadcasted_iota(jnp.int32, (LANE, length), 0)
    named = route[...]
    onehot = jnp.where(kind == named, 1.0, 0.0)
    one = lax.broadcasted_iota(jnp.int32, (length, length), 0)
    two = lax.broadcasted_iota(jnp.int32, (length, length), 1)
    earlier = jnp.where(one < two, 1.0, 0.0).astype(BF16)
    before = dot_nn(onehot.astype(BF16), earlier)
    within = jnp.sum(before * onehot, axis=0, keepdims=True)
    slot = named.astype(F32) * (length // 2) + within
    facts = jnp.where(kind == experts, slot, jnp.where(kind == experts + 1, keep[...].astype(F32), onehot))
    facts = dot_nt(shift, facts.astype(BF16))
    onehot = jnp.where(lane < experts, facts, 0.0)
    slot = jnp.sum(jnp.where(lane == experts, facts, 0.0), axis=1, keepdims=True)
    kept = jnp.sum(jnp.where(lane == experts + 1, facts, 0.0), axis=1, keepdims=True)
    sig = jax.nn.sigmoid(jnp.sum(logits * onehot, axis=1, keepdims=True))
    gates = kept * sig
    cols_o[...] = jnp.where(
        lane == experts, gates, jnp.where(lane == experts + 1, gates * (1.0 - sig), onehot)
    )
    up = dot_nn(shift, grad[...])
    up_o[...] = up
    slots = match_o.shape[1]
    spot = lax.broadcasted_iota(jnp.int32, (length, slots), 1).astype(F32)
    match = jnp.where(slot == spot, 1.0, 0.0).astype(BF16)
    match_o[...] = match
    out_o[0] = dot_tn(match, n2).astype(BF16).reshape(out_o.shape[1:])
    out_o[1] = dot_tn(match, (gates * up).astype(BF16)).astype(BF16).reshape(out_o.shape[1:])
    sums_o[...] = jnp.broadcast_to(jnp.sum(mix * mix, keepdims=True), (SEG, LANE))


def pack_kernel(up, down, out):
    width, units = up.shape
    line = lax.broadcasted_iota(jnp.int32, (units, units), 0)
    same = jnp.where(line == lax.broadcasted_iota(jnp.int32, (units, units), 1), 1.0, 0.0)
    out[:, :width] = dot_nt(same.astype(BF16), up[...]).astype(BF16)
    out[:, width:] = down[...]


def prepare_kernel(
    experts, small, own, wx_t, wdt, wout, conv_w, a_log,
    gain_o, router_o, wx_o, wdt_o, wout_o, conv_o, rows_o, a_o, wide_s,
):
    width = wout.shape[1]
    group = small.shape[0]
    share = width // group
    for w in range(group):
        wide_s[:, w * share : (w + 1) * share] = small[w, :, :share].astype(F32)
    gain_o[0:1] = wide_s[SEG - 2 : SEG - 1]
    gain_o[1:2] = wide_s[SEG - 1 : SEG]
    gain_o[2:] = jnp.zeros((SEG - 2, width), F32)
    rows = wide_s[SEG:]
    row = lax.broadcasted_iota(jnp.int32, rows.shape, 0)
    router_o[...] = jnp.zeros_like(router_o)
    router_o[: 2 * SEG] = jnp.concatenate(
        [jnp.where(row < experts, rows, 0.0), jnp.zeros_like(rows)], axis=0
    ).astype(BF16)
    local = wout.shape[0]
    for out, src in ((wx_o, wx_t), (wdt_o, wdt), (a_o, None)):
        out[...] = jnp.zeros_like(out)
        if src is not None:
            out[: src.shape[0], :local] = src[...]
    a_o[...] = jnp.full(a_o.shape, -1.0, F32)
    a_o[:, :local] = -jnp.exp(a_log[...].astype(F32))
    wout_o[...] = jnp.zeros_like(wout_o)
    wout_o[:local] = wout[...]
    conv_o[...] = jnp.zeros_like(conv_o)
    taps = conv_w.shape[0]
    conv_o[:taps, :local] = conv_w[...].astype(F32)
    mine = own[...].astype(F32)
    rows_o[...] = jnp.zeros_like(rows_o)
    for h in range(2):
        cols = slice(h * share, (h + 1) * share)
        conv_o[taps : taps + 1, cols] = mine[h : h + 1, :share]
        rows_o[0:1, cols] = mine[2 + h : 3 + h, :share]
        rows_o[1:2, cols] = mine[4 + h : 5 + h, :share]


def block_rows(value, c, rows):
    low = c * rows
    have = max(0, min(rows, value.shape[0] - low))
    if have == rows:
        return value[low : low + rows]
    blank = jnp.zeros((rows - have, value.shape[1]), value.dtype)
    return blank if have == 0 else jnp.concatenate([value[low : low + have], blank], axis=0)


def pack_zo_kernel(ring, in_rows, local, n1, d_z, d_mix, gated, out):
    width = n1.shape[1]
    lanes = d_z.shape[1]
    grad_z = dot_tn(n1[...], d_z[...])
    grad_o = dot_tn(gated[...], d_mix[...])
    side = jnp.zeros((grad_o.shape[0], lanes - width // 2), F32)
    first = jnp.concatenate([grad_o[:, : width // 2], side], axis=1)
    second = jnp.concatenate([grad_o[:, width // 2 :], side], axis=1)
    rows = in_rows // 2
    for c in range(ring):
        out[c // 2, c % 2, :, :lanes] = block_rows(grad_z, c, in_rows).astype(BF16)
        both = [block_rows(first[:local], c, rows), block_rows(second[:local], c, rows)]
        out[c // 2, c % 2, :, lanes:] = jnp.concatenate(both, axis=0).astype(BF16)


def pack_rest_kernel(
    ring, in_rows, small_rows, group, experts, ranked, mine_ref, n1, d_x, gx, gdt, ga, a_ref, gconv, bias, skip,
    gain_mix, gains, gain_moe, router, out_sums, mix_sum, out, small_s, wide_s,
):
    lanes = d_x.shape[1]
    width = n1.shape[1]
    share = width // group
    grad_x = dot_tn(n1[...], d_x[...])
    small_s[...] = jnp.zeros_like(small_s)
    at = 0
    grad_a = jnp.sum(ga[...], axis=1) * a_ref[...]
    for part in (gx[...], gdt[:ranked], grad_a, gconv[...]):
        small_s[at : at + part.shape[0]] = part
        at += part.shape[0]
    small_s[at : at + 1] = bias[...]
    small_s[at + SEG : at + SEG + 1] = skip[...]
    wide_s[...] = jnp.zeros_like(wide_s)
    wide_s[0:1] = gain_mix[...] / gains[0:1]
    wide_s[1:2] = gain_moe[...]
    wide_s[2 : 2 + experts] = router[:experts]
    lane = lax.broadcasted_iota(jnp.int32, (group, LANE), 1)
    row = lax.broadcasted_iota(jnp.int32, (group, LANE), 0)
    stats = jnp.where(
        lane == 0, out_sums[0:1], jnp.where(lane == 1, mix_sum[0:1], jnp.where(lane == 2, out_sums[1:2], 0.0))
    )
    stats = jnp.where(row == mine_ref[0], stats, 0.0)
    stats = jnp.concatenate([stats, jnp.zeros((group, lanes - LANE), F32)], axis=1)
    bottom = jnp.zeros((16 - 2 * group, lanes), F32)
    small_each = small_s.shape[0] // ring
    for c in range(ring):
        if c < 2 + experts:
            full = [wide_s[c : c + 1, w * share : (w + 1) * share] for w in range(group)]
            full = jnp.concatenate(full, axis=0)
            full = jnp.concatenate([full, jnp.zeros((group, lanes - share), F32)], axis=1)
        else:
            full = jnp.zeros((group, lanes), F32)
        small = small_s[c * small_each : (c + 1) * small_each]
        blank = jnp.zeros((small_rows - small_each, lanes), F32)
        parts = [block_rows(grad_x, c, in_rows), small]
        if small_rows > small_each:
            parts.append(blank)
        rows = jnp.concatenate(parts + [full, stats, bottom], axis=0)
        out[c // 2, c % 2] = rows.astype(BF16)


def store_in_order(out, rows, order_s):
    steps = rows.shape[0] // SEG
    for g in range(rows.shape[1] // LANE):
        cols = slice(g * LANE, (g + 1) * LANE)
        for j in range(steps):
            order_s[g, pl.ds(j, SEG, stride=steps), :] = rows[j * SEG : (j + 1) * SEG, cols]
        out[:, cols] = order_s[g]


def input_gradient(taps, last_ref, terms, edges, tok, gain, dh, out_o, dn_s, order_s):
    length = tok.shape[0]
    steps = length // SEG
    behind = taps - 1
    total = terms[0, :length].astype(F32)
    edge = edges[0].astype(F32)
    for w in range(1, terms.shape[0]):
        total = total + terms[w, :length].astype(F32)
        edge = edge + edges[w].astype(F32)
    edge = jnp.where(last_ref[0] > 0, 0.0, edge)
    dn_s[...] = total
    seg = lax.broadcasted_iota(jnp.int32, (SEG, tok.shape[1]), 0)
    for i in range(behind):
        j = pl.ds((steps - behind + i) * SEG, SEG)
        row = EDGE - behind + i
        came = jnp.broadcast_to(edge[row : row + 1], seg.shape)
        dn_s[j, :] += jnp.where(seg == SEG - 1, came, 0.0)
    x = dot_nn(permutation(length), tok[...])
    d_x, _ = norm_grads(x, rms_scale(x), gain[0:1], dn_s[...])
    result = dh[...] + d_x
    store_in_order(out_o, result, order_s)


def unpack_kernel(
    ring, group, in_rows, small_rows, experts, states, ranked, taps, denom, mine_ref, done, up_down,
    last_ref, terms, edges, tok, gain, dh, res,
    in_o, out_o, up_o, down_o, taps_o, wx_o, wdt_o, a_o, vec_o, stat_o, grad_o, layer_o,
    small_s, full_s, dn_s, order_s,
):
    c = pl.program_id(0)
    width = in_o.shape[1]

    @pl.when(c == 1)
    def _():
        store_in_order(layer_o, res[...], order_s)
        input_gradient(taps, last_ref, terms, edges, tok, gain, dh, grad_o, dn_s, order_s)

    local = width // 2
    small_each = small_s.shape[0] // ring
    base = 2 * in_rows

    @pl.when(c == 0)
    def _():
        line = lax.broadcasted_iota(jnp.int32, (width, width), 0)
        same = jnp.where(line == lax.broadcasted_iota(jnp.int32, (width, width), 1), 1.0, 0.0)
        up_o[...] = dot_nt(same.astype(BF16), up_down[:, :width])
        down_o[...] = up_down[:, width:].astype(F32)
        full_s[...] = jnp.zeros_like(full_s)

    @pl.when(c * in_rows < width)
    def _():
        rows = done[0, :base, :].astype(F32)
        in_o[...] = jnp.concatenate([rows[:in_rows, :local], rows[in_rows:, :local]], axis=1)
        low = base + 16 + small_rows
        rows = done[0, low : low + in_rows, :].astype(F32)
        half = in_rows // 2
        out_o[...] = jnp.concatenate([rows[:half, :local], rows[half:, :local]], axis=1)

    small = done[0, base + 16 : base + 16 + small_rows, :].astype(F32)
    small_s[pl.ds(pl.multiple_of(c * small_each, SEG), small_each), :] = small[:small_each]
    tile = done[0, base : base + 16, :].astype(F32)
    row = lax.broadcasted_iota(jnp.int32, tile.shape, 0)
    own = jnp.sum(jnp.where(row == mine_ref[0], tile, 0.0), axis=0, keepdims=True)
    spot = lax.broadcasted_iota(jnp.int32, full_s.shape, 0)
    full_s[...] += jnp.where(spot == c, own, 0.0)

    @pl.when(c == 0)
    def _():
        sums = jnp.sum(jnp.where(row == group + mine_ref[0], tile, 0.0), axis=0, keepdims=True)
        stat_o[...] = jnp.sqrt(sums[:, :LANE] / denom)

    @pl.when(c == ring - 1)
    def _():
        at = 0
        wx_o[...] = small_s[: wx_o.shape[0], :local]
        at += up_to(wx_o.shape[0], LANE)
        wdt_o[...] = small_s[at : at + ranked, :local]
        at += ranked
        a_o[...] = small_s[at : at + states, :local]
        at += states
        taps_o[...] = small_s[at : at + taps, :local]
        vec_o[:SEG] = full_s[...]
        vec_o[SEG : SEG + 1] = small_s[at + taps : at + taps + 1]
        at += SEG
        vec_o[SEG + 1 : SEG + 2] = small_s[at : at + 1]
        vec_o[SEG + 2 : SEG + 3] = small_s[at + SEG : at + SEG + 1]


def middle_kernel(
    experts, group, chunks,
    mix_ref, tok, gain, router, route, keep, grad, w_ref,
    g_ref, layer_o, dh_o, dmix_o, router_o, gain_o, sums_o, mix_o,
    layer_s, dh_s, dmix_s, leave_sem,
    h1_s, n2_s, up_s, cols_s, match_s, x_ref, r_ref,
    got, w_s, g_s, act_s, slope_s, pre_s, acc, out_s,
    w_sem, g_sem, s1, r1, own1, s2, r2, own2,
):
    mine, mates = mates_of(group)
    count, width = x_ref.shape[2:]
    slots = group * count
    block = w_ref.shape[0] // chunks

    def load(t):
        at = pl.ds(pl.multiple_of(lax.rem(t, chunks) * block, block), block)
        slot = lax.rem(t, 2)
        return pltpu.make_async_copy(w_ref.at[at], w_s.at[slot], w_sem.at[slot])

    load(0).start()
    greet("wa", group)
    route_kernel(
        experts, mix_ref, tok, gain, router, route, keep, grad,
        h1_s, n2_s, up_s, cols_s, match_s, x_ref, mix_o,
    )
    sent = []
    for h in range(2):
        for k, who in enumerate(mates):
            copy = remote(x_ref.at[h, who], got.at[h, mine], s1.at[h, k], r1.at[h, k], {"wa": who})
            copy.start()
            sent.append(copy)
        pltpu.make_async_copy(x_ref.at[h, mine], got.at[h, mine], own1.at[h]).start()

    def arrived(h):
        pltpu.make_async_copy(x_ref.at[h, mine], got.at[h, mine], own1.at[h]).wait()
        for copy in sent[h * len(mates) : (h + 1) * len(mates)]:
            copy.wait_recv()
        return got[h].reshape(slots, width)

    def chunk(i):
        return pl.ds(pl.multiple_of(i * block, block), block)

    def returned(h):
        out_s[h] = acc[...].astype(BF16).reshape(group, count, width)
        for k, who in enumerate(mates):
            copy = remote(out_s.at[h, who], r_ref.at[h, mine], s2.at[h, k], r2.at[h, k], {"wa": who})
            copy.start()
            sent.append(copy)
        pltpu.make_async_copy(out_s.at[h, mine], r_ref.at[h, mine], own2.at[h]).start()

    rows = arrived(0)
    acc[...] = jnp.zeros_like(acc)

    def forward(i, _):
        load(i).wait()
        load(i + 1).start()
        w = w_s.at[lax.rem(i, 2)]
        hidden = dot_nt(w[:, :width], rows)
        c = 0.7978845608
        t = jnp.tanh(c * (hidden + 0.044715 * hidden * hidden * hidden))
        act = (0.5 * hidden * (1.0 + t)).astype(BF16)
        act_s[chunk(i), :] = act
        slope_s[chunk(i), :] = 0.5 * (1.0 + t) + 0.5 * hidden * (1.0 - t * t) * c * (
            1.0 + 3.0 * 0.044715 * hidden * hidden
        )
        acc[...] += dot_tn(act, w[:, width:])
        return 0

    lax.fori_loop(0, chunks, forward, 0)
    returned(0)
    d_out = arrived(1)
    acc[...] = jnp.zeros_like(acc)

    def backward(i, _):
        load(chunks + i).wait()

        @pl.when(i < chunks - 1)
        def _():
            load(chunks + i + 1).start()

        w = w_s.at[lax.rem(chunks + i, 2)]
        d_pre = (dot_nt(w[:, width:], d_out) * slope_s[chunk(i), :]).astype(BF16)
        pre_s[chunk(i), :] = d_pre
        acc[...] += dot_tn(d_pre, w[:, :width])
        return 0

    lax.fori_loop(0, chunks, backward, 0)
    returned(1)

    def store(i):
        slot = lax.rem(i, 2)
        return pltpu.make_async_copy(g_s.at[slot], g_ref.at[chunk(i)], g_sem.at[slot])

    def gradients(i, _):
        @pl.when(i >= 2)
        def _():
            store(i - 2).wait()

        g = g_s.at[lax.rem(i, 2)]
        g[:, :width] = dot_nn(pre_s[chunk(i), :], got[0].reshape(slots, width)).astype(BF16)
        g[:, width:] = dot_nn(act_s[chunk(i), :], got[1].reshape(slots, width)).astype(BF16)
        store(i).start()
        return 0

    lax.fori_loop(0, chunks, gradients, 0)
    store(chunks - 2).wait()
    store(chunks - 1).wait()
    for h in range(2):
        pltpu.make_async_copy(out_s.at[h, mine], r_ref.at[h, mine], own2.at[h]).wait()
    for copy in sent[: 2 * len(mates)]:
        copy.wait_send()
    for copy in sent[2 * len(mates) :]:
        copy.wait()
    combine_kernel(
        experts, r_ref, match_s, h1_s, n2_s, up_s, cols_s, gain, router,
        layer_s, dh_s, dmix_s, router_o, gain_o, sums_o,
    )
    leaving = [
        pltpu.make_async_copy(src, dst, leave_sem.at[i])
        for i, (src, dst) in enumerate(((dmix_s, dmix_o), (dh_s, dh_o), (layer_s, layer_o)))
    ]
    for copy in leaving:
        copy.start()
    for copy in leaving:
        copy.wait()


def middle(experts, terms, tok, gains, router, route, keep, grad, w, chunks, cid, us):
    group = lax.axis_size("wa")
    units = w.shape[0]
    length, width = tok.shape
    slots = experts * (length // 2)
    block = units // chunks
    dma = pltpu.SemaphoreType.DMA
    hbm = pl.BlockSpec(memory_space=pltpu.HBM)
    vmem = pl.BlockSpec(memory_space=pltpu.VMEM)
    anywhere = pl.BlockSpec(memory_space=pl.ANY)
    two = dma((2, group - 1))
    rows = pltpu.VMEM((2, group, slots // group, width), BF16)
    shapes = [
        (w.shape, BF16), ((length, width), F32), ((length, width), F32), ((length, width), BF16),
        ((LANE, width), F32), ((1, width), F32), ((SEG, LANE), F32), ((SEG, LANE), F32),
    ]
    return pl.pallas_call(
        functools.partial(middle_kernel, experts, group, chunks),
        out_shape=[jax.ShapeDtypeStruct(shape, dtype) for shape, dtype in shapes],
        in_specs=[vmem] * 7 + [hbm],
        out_specs=[hbm] + [anywhere] * 3 + [vmem] * 4,
        scratch_shapes=[
            pltpu.VMEM((length, width), F32), pltpu.VMEM((length, width), F32),
            pltpu.VMEM((length, width), BF16), dma((3,)),
            pltpu.VMEM((length, width), F32),
            pltpu.VMEM((length, width), BF16),
            pltpu.VMEM((length, width), F32),
            pltpu.VMEM((length, LANE), F32),
            pltpu.VMEM((length, slots), BF16),
            rows, rows, rows,
            pltpu.VMEM((2, block, 2 * width), BF16),
            pltpu.VMEM((2, block, 2 * width), BF16),
            pltpu.VMEM((units, slots), BF16),
            pltpu.VMEM((units, slots), F32),
            pltpu.VMEM((units, slots), BF16),
            pltpu.VMEM((slots, width), F32),
            rows,
            dma((2,)), dma((2,)),
            two, two, dma((2,)), two, two, dma((2,)),
        ],
        compiler_params=pltpu.CompilerParams(
            collective_id=cid, has_side_effects=True, vmem_limit_bytes=VMEM_LIMIT + 20 * 2**20
        ),
        cost_estimate=lasting(us),
        name="middle",
    )(terms, tok, gains, router, route, keep, grad, w)


def combine_kernel(
    experts, back, match, h1_i, n2, up_i, cols, gain, router,
    out_o, dh_o, dmix_o, router_o, gain_o, sums_o,
):
    length, width = h1_i.shape
    h1, up = h1_i[...], up_i[...]
    lane = lax.broadcasted_iota(jnp.int32, (length, LANE), 1)
    facts = cols[...]

    def column(at):
        return jnp.sum(jnp.where(lane == at, facts, 0.0), axis=1, keepdims=True)

    gates, slope = column(experts), column(experts + 1)
    onehot = jnp.where(lane < experts, facts, 0.0)
    slots = match.shape[1]
    rows = dot_nn(match[...], back[0].reshape(slots, width))
    moe = gates * rows
    result = h1 + moe
    out_o[...] = result
    d_gate = jnp.sum(rows * up, axis=1, keepdims=True)
    d_logits = (onehot * (d_gate * slope)).astype(BF16)
    router_o[...] = dot_tn(d_logits, n2[...])
    d_n2 = dot_nn(match[...], back[1].reshape(slots, width)) + dot_nn(d_logits, router[...])
    d_norm, terms = norm_grads(h1, rms_scale(h1), gain[1:2], d_n2)
    gain_o[...] = jnp.sum(terms, axis=0, keepdims=True)
    d_h1 = up + d_norm
    dh_o[...] = d_h1
    dmix_o[...] = d_h1.astype(BF16)
    sums_o[0:1] = jnp.broadcast_to(jnp.sum(result * result, keepdims=True), (1, LANE))
    sums_o[1:2] = jnp.broadcast_to(jnp.sum(moe * moe, keepdims=True), (1, LANE))


def gate_back_kernel(
    count, states, c_at, own, wout, y, z, uf, proj, step_i, cut, a_ref,
    dy_o, dz_o, skip_o, fx_ref, tx_ref, fd_o, mix_o, cb, st_s, fd_s, got, send, recv, own_s,
):
    length, width = step_i.shape[1:]
    groups, steps = width // LANE, length // SEG
    at = pl.program_id(0)
    mine = lax.axis_index("wa")
    goals = [lax.rem(mine + k, count) for k in range(1, count)]
    sends = [
        remote(own, got.at[mine], send.at[k], recv.at[k], {"wa": who}) for k, who in enumerate(goals)
    ]
    kept = pltpu.make_async_copy(own, got.at[mine], own_s)

    @pl.when(at == 0)
    def _():
        kept.start()
        greet("wa", count)
        for copy in sends:
            copy.start()
        kept.wait()

    for k, copy in enumerate(sends):

        @pl.when(at == k + 1)
        def _():
            copy.wait_recv()

    d_mix = got[lax.rem(mine + count - at, count)]
    mix_o[0] = d_mix
    d_gated = dot_nt(d_mix, wout[...])
    zf = z[0].astype(F32)
    dy = d_gated * (zf * jax.nn.sigmoid(zf))
    dy_o[0] = dy
    dz_o[0, :length] = (d_gated * y[0] * silu_slope(zf)).astype(BF16)
    dz_o[0, length:] = jnp.zeros((EDGE, width), BF16)

    @pl.when(pl.program_id(0) == 0)
    def _():
        skip_o[...] = jnp.zeros_like(skip_o)

    skip_o[...] += jnp.sum(dy * uf[0], axis=0, keepdims=True)
    cb[...] = spread(proj[0], states, c_at)
    for g in range(groups):
        cols = slice(g * LANE, (g + 1) * LANE)
        st_s[:, cols] = step_i[0, :, cols] + cut[0]
    zero = jnp.zeros((SEG, LANE), F32)
    seg = seg_of()

    def group(g, _):
        lanes = lanes_of(g)
        a = [wide(a_ref, n, lanes) for n in range(states)]

        def step(lap, carry):
            rows = rows_of(steps - 1 - lap)
            st = st_s[rows, lanes]
            d = dy_o[0, rows, lanes]
            new = [carry[0] + st]
            for n in range(states):
                new.append(jnp.exp(st * a[n]) * (carry[n + 1] + cb[rows, state_cols(n)] * d))
            return tuple(new)

        out = lax.fori_loop(0, steps, step, (zero,) * (states + 1), unroll=8)
        total, f = out[0], list(out[1:])
        for k in (1, 2, 4):
            ok = seg < SEG - k
            for n in range(states):
                f[n] = f[n] + jnp.where(ok, jnp.exp(total * a[n]) * rolled(f[n], -k), 0.0)
            total = total + jnp.where(ok, rolled(total, -k), 0.0)
        ok = seg < SEG - 1
        tx_ref[0, :, lanes] = jnp.where(ok, rolled(total, -1), 0.0)
        for n in range(states):
            fx_ref[0, n, :, lanes] = jnp.where(ok, rolled(f[n], -1), 0.0)
            fd_s[pl.ds(n, 1), lanes] = f[n][0:1]
        return 0

    lax.fori_loop(0, groups, group, 0)
    fd_o[0] = fd_s[...].astype(BF16)

    @pl.when(at == count - 1)
    def _():
        for copy in sends:
            copy.wait_send()


def scan_back_kernel(
    states, b_at, proj, step_i, sig, uf, cut, dy_i, a_ref, skip, wdt, hx_ref, sx_ref, e_i,
    fx_ref, tx_ref, finals, sums, g_ref, p_ref,
    part_o, du_o, dt_o, bias_o, ga_ref, g_o,
    bb, cb, dec, pri, accb, accc, st_s, dr_s, ds_s, out_s,
    from_pair, kept, came, load, ctx_s, ctx_r,
):
    ring = finals.shape[0]
    half = ring // 2
    _, chip, lane, _, peers = neighbours(ring)
    own_half = pltpu.make_async_copy(g_ref.at[:, lane], kept, load.at[0])
    pair_half = pltpu.make_async_copy(p_ref, from_pair, load.at[1])
    targets = [lax.rem(chip + k, half) for k in range(1, half)]
    scattered = [
        remote(kept.at[to], came.at[k], ctx_s.at[k], ctx_r.at[k], {"ctx": who})
        for k, (to, who) in enumerate(zip(targets, peers))
    ]
    at = pl.program_id(0)

    @pl.when(at == 0)
    def _():
        own_half.start()
        pair_half.start()
        barrier = pltpu.get_barrier_semaphore()
        for who in peers:
            hello(barrier, "ctx", who)
        pl.semaphore_wait(barrier, half - 1)
        own_half.wait()
        pair_half.wait()
        for to, copy in zip(targets, scattered):
            add_rows(kept.at[to], [kept.at[to], from_pair.at[to]], kept.shape[1])
            copy.start()
        add_rows(kept.at[chip], [kept.at[chip], from_pair.at[chip]], kept.shape[1])

    @pl.when(at == pl.num_programs(0) - 1)
    def _():
        for copy in scattered:
            copy.wait()
        add_rows(g_o, [kept.at[chip]] + [came.at[k] for k in range(half - 1)], kept.shape[1])

    length, width = step_i.shape[1:]
    groups, steps = width // LANE, length // SEG
    bb[...] = spread(proj[0], states, b_at)
    cb[...] = spread(proj[0], states, b_at + states)
    accb[...] = jnp.zeros_like(accb)
    accc[...] = jnp.zeros_like(accc)
    entering(out_s, finals, sums, a_ref, lax.axis_index("ctx"), False)
    e_ref = e_i.at[0]
    dr_s[...] = step_i[0] * uf[0]
    for g in range(groups):
        cols = slice(g * LANE, (g + 1) * LANE)
        st_s[:, cols] = step_i[0, :, cols] + cut[0]

    @pl.when(pl.program_id(0) == 0)
    def _():
        ga_ref[...] = jnp.zeros_like(ga_ref)
        dt_o[...] = jnp.zeros_like(dt_o)
        bias_o[...] = jnp.zeros_like(bias_o)

    def group(g, _):
        lanes = lanes_of(g)
        a = [wide(a_ref, n, lanes) for n in range(states)]
        sx = sx_ref[0, :, lanes]
        first = tuple(
            jnp.exp(sx * a[n]) * wide(e_ref, n, lanes) + hx_ref[0, n, :, lanes]
            for n in range(states)
        )

        def ahead(j, h):
            rows = rows_of(j)
            st = st_s[rows, lanes]
            dr = dr_s[rows, lanes]
            new = []
            for n in range(states):
                decay = jnp.exp(st * a[n])
                dec[rows, state_cols(n)] = decay
                pri[rows, state_cols(n)] = h[n]
                new.append(decay * h[n] + bb[rows, state_cols(n)] * dr)
            return tuple(new)

        last = lax.fori_loop(0, steps, ahead, first, unroll=8)
        end = rows_of(steps)
        for n in range(states):
            pri[end, state_cols(n)] = last[n]
        tx = tx_ref[0, :, lanes]
        flow = tuple(
            jnp.exp(tx * a[n]) * wide(out_s, n, lanes) + fx_ref[0, n, :, lanes]
            for n in range(states)
        )
        gain = wide(skip, 1, lanes)

        def back(lap, f):
            j = steps - 1 - lap
            rows = rows_of(j)
            after = rows_of(j + 1)
            st = step_i[0, rows, lanes]
            dr = dr_s[rows, lanes]
            dy = dy_i[0, rows, lanes]
            new = []
            d_step = None
            d_drive = None
            for n in range(states):
                cols = state_cols(n)
                d = f[n] + cb[rows, cols] * dy
                accc[rows, cols] += pri[after, cols] * dy
                accb[rows, cols] += d * dr
                flowing = dec[rows, cols] * d
                new.append(flowing)
                d_log = flowing * pri[rows, cols]
                ga_ref[n, :, lanes] += d_log * st
                part = d_log * a[n]
                d_step = part if d_step is None else d_step + part
                part = d * bb[rows, cols]
                d_drive = part if d_drive is None else d_drive + part
            ds_s[rows, lanes] = (d_step + d_drive * uf[0, rows, lanes]) * sig[0, rows, lanes]
            du_o[0, rows, lanes] = d_drive * st + dy * gain
            return tuple(new)

        lax.fori_loop(0, steps, back, flow, unroll=8)
        return 0

    lax.fori_loop(0, groups, group, 0)
    d_pre = ds_s[...]
    bias_o[...] += jnp.sum(d_pre, axis=0, keepdims=True)
    d_pre = d_pre.astype(BF16)
    dt_o[...] += dot_tn(proj[0], d_pre)
    columns = part_o.shape[2]
    part = dot_nt(d_pre, wdt[...])
    part = part + collected(accb[...], states, columns, b_at)
    part = part + collected(accc[...], states, columns, b_at + states)
    part_o[0] = part.astype(BF16)


def conv_back_kernel(
    taps, documents, place_ref, doc_ref, proj_i, wproj, du, pre, ext, u, conv, dz, wx, wz, n1,
    dx_o, dn_o, gconv_o, gx_o, gain_o, dext,
):
    length, width = du.shape[1:]
    steps = length // SEG
    behind = taps - 1

    @pl.when(pl.program_id(0) == 0)
    def _():
        gconv_o[...] = jnp.zeros_like(gconv_o)
        gx_o[...] = jnp.zeros_like(gx_o)
        gain_o[...] = jnp.zeros_like(gain_o)

    proj = proj_i[0]
    gx_o[...] += dot_tn(proj, u[0])
    d_u = dot_nn(proj, wproj[...]) + du[0]
    masks, _ = lag_masks(place_ref[0], doc_ref, documents, pl.program_id(0), length, taps)
    seg = seg_of()
    row = lax.broadcasted_iota(jnp.int32, (EDGE, LANE), 0)
    for g in range(width // LANE):
        cols = slice(g * LANE, (g + 1) * LANE)
        d = d_u[:, cols] * silu_slope(pre[0, :, cols])
        gconv_o[taps : taps + 1, cols] += jnp.sum(d, axis=0, keepdims=True)
        dext[...] = jnp.zeros_like(dext)
        for lag in range(taps):
            weighted = d if lag == 0 else d * masks[lag]
            at = pl.ds((behind - lag) * SEG, length)
            gconv_o[lag : lag + 1, cols] += jnp.sum(weighted * ext[0, at, cols], axis=0, keepdims=True)
            dext[at, :] += weighted * conv[lag : lag + 1, cols]
        before = jnp.zeros((EDGE, LANE), F32)
        for i in range(behind):
            head = dext[i * SEG : (i + 1) * SEG]
            j = pl.ds((steps + i) * SEG, SEG)
            dext[j, :] += jnp.where(seg < SEG - 1, rolled(head, -1), 0.0)
            first = jnp.broadcast_to(head[0:1], (EDGE, LANE))
            before = before + jnp.where(row == EDGE - behind + i, first, 0.0)
        dx_o[0, :length, cols] = dext[behind * SEG :].astype(BF16)
        dx_o[0, length:, cols] = before.astype(BF16)
    d_n1 = dot_nt(dx_o[0], wx[0]) + dot_nt(dz[0], wz[0])
    gain_o[...] += jnp.sum(d_n1 * n1[0].astype(F32), axis=0, keepdims=True)
    dn_o[0] = d_n1.astype(BF16)


SMEM = "smem"
ANY = "any"


def by_stream(shape, at, order):
    block = tuple(1 if i == at else n for i, n in enumerate(shape))
    rank = len(shape)

    def index(s):
        return tuple(order(s) if i == at else 0 for i in range(rank))

    return pl.BlockSpec(block, index)


def whole(shape):
    return pl.BlockSpec(shape, lambda s: (0,) * len(shape))


def call(kernel, name, grid, args, outs, scratch, us, cid=None, limit=VMEM_LIMIT, order=lambda s: s):
    arrays, specs = [], []
    for array, at in args:
        arrays.append(array)
        if at == SMEM:
            specs.append(pl.BlockSpec(memory_space=pltpu.SMEM))
        elif at == ANY:
            specs.append(pl.BlockSpec(memory_space=pl.ANY))
        elif callable(at):
            specs.append(at(array.shape))
        else:
            specs.append(whole(array.shape) if at is None else by_stream(array.shape, at, order))
    out_specs = []
    for shape, _, at in outs:
        if callable(at):
            out_specs.append(at(shape))
        elif at == ANY:
            out_specs.append(pl.BlockSpec(memory_space=pl.ANY))
        else:
            out_specs.append(whole(shape) if at is None else by_stream(shape, at, order))
    return pl.pallas_call(
        kernel,
        grid=(grid,),
        out_shape=[jax.ShapeDtypeStruct(shape, dtype) for shape, dtype, _ in outs],
        in_specs=specs,
        out_specs=out_specs,
        scratch_shapes=scratch,
        compiler_params=pltpu.CompilerParams(
            vmem_limit_bytes=limit, collective_id=cid, has_side_effects=cid is not None
        ),
        cost_estimate=lasting(us),
        name=name,
    )(*arrays)


def padded_to(array, width, axis):
    pads = [(0, 0)] * array.ndim
    pads[axis] = (0, width - array.shape[axis])
    return jnp.pad(array, pads)


def up_to(n, multiple):
    return -(-n // multiple) * multiple


def body(
    tokens, out_grad, doc_starts, routes, keep_mask, norm_mix, w_in, conv_w, conv_b, w_x, w_dt,
    dt_bias, a_log, d_skip, w_out, norm_moe, w_router, w_up, w_down,
):
    group = lax.axis_size("wa")
    ring = lax.axis_size("ctx")
    mine = lax.axis_index("wa")
    place = lax.axis_index("ctx")
    length, width = tokens.shape[1:]
    taps, local = conv_w.shape
    states = a_log.shape[0]
    ranked = w_dt.shape[0]
    experts = w_router.shape[1]
    padded = up_to(local, LANE)
    columns = up_to(w_x.shape[1], LANE)
    steps = length // SEG
    rows = length + EDGE
    slots = experts * (length // 2)
    share = norm_mix.shape[0]
    order_vmem = pltpu.VMEM((width // LANE, length, LANE), F32)
    place_s = place.astype(jnp.int32).reshape(1)
    mine_s = mine.astype(jnp.int32).reshape(1)
    last_s = (place == ring - 1).astype(jnp.int32).reshape(1)
    f32_vmem = lambda *shape: pltpu.VMEM(shape, F32)

    (own_experts,) = call(
        pack_kernel, "pack", 1, [(w_up[0], None), (w_down[0], None)],
        [((w_down.shape[1], 2 * width), BF16, None)], [], 3, None, LARGE_LIMIT,
    )
    expert_w = lax.all_gather(own_experts, "ctx", axis=0, tiled=True)

    in_rows = up_to(-(-width // ring), 16)
    blank = ring * in_rows - width
    part_in = jnp.pad(w_in, ((0, blank), (0, 0))) if blank else w_in
    part_in = lax.dynamic_slice_in_dim(part_in, place * in_rows, in_rows, 0)
    halves = jnp.stack([part_in[:, :local], part_in[:, local:]], axis=0)
    halves = jnp.pad(halves, ((0, 0), (0, 0), (0, padded - local)))
    small = jnp.concatenate([conv_b, dt_bias, d_skip, norm_mix, norm_moe], axis=0).reshape(SEG, share)
    small = jnp.concatenate([small, jnp.pad(w_router.T, ((0, SEG - experts), (0, 0)))], axis=0)
    small = padded_to(small, up_to(share, LANE), 1)
    documents = doc_starts.shape[1]
    doc_tile = jnp.pad(doc_starts, ((0, SEG - 1), (0, LANE - documents)))
    all_rows, all_edges, smalls, docs, w_blocks = start(tokens[0], small, doc_tile, halves, 1)
    proj_in = w_blocks.reshape(2, ring * in_rows, padded)[:, :width]
    of_x = lambda shape: pl.BlockSpec((1,) + shape[1:], lambda i: (0, 0, 0))
    of_z = lambda shape: pl.BlockSpec((1,) + shape[1:], lambda i: (1, 0, 0))
    par = (SEG, padded)
    gains, router, wproj, wdt, wout, conv, vectors, a_mat = call(
        functools.partial(prepare_kernel, experts), "prepare", 1,
        [(smalls, None), (small, None), (w_x.T, None), (w_dt, None), (w_out, None), (conv_w, None),
         (a_log, None)],
        [((SEG, width), F32, None), ((LANE, width), BF16, None), ((columns, padded), BF16, None),
         ((columns, padded), BF16, None), ((padded, width), BF16, None), (par, F32, None),
         (par, F32, None), ((states, padded), F32, None)],
        [f32_vmem(2 * SEG, width)], 3,
    )

    vec = (group, length, padded)
    n1, ext, pre_conv, u_f, u, z, part, cut = call(
        functools.partial(enter_kernel, taps, documents), "enter", group,
        [(place_s, SMEM), (docs, SMEM), (all_rows, 0), (all_edges, 0), (gains, None),
         (proj_in, of_x), (proj_in, of_z), (conv, None), (wproj, None)],
        [((group, rows, width), BF16, 0), ((group, (taps - 1) * SEG + length, padded), F32, 0),
         (vec, F32, 0), (vec, F32, 0), (vec, BF16, 0), (vec, BF16, 0),
         ((group, length, columns), BF16, 0), ((group, length, LANE), F32, 0)],
        [], 8,
    )
    projected = sum_all(part, 2, 11)
    seg_states = (group, states, SEG, padded)
    seg_sums = (group, SEG, padded)
    dev_states = (group, states, padded)
    dev_sums = (group, 1, padded)
    spread_vmem = f32_vmem(length, states * LANE)
    lane_vmem = f32_vmem(length, padded)
    state_vmem = f32_vmem(states, padded)
    step_size, sig, h_in, s_in, h_dev, s_dev = call(
        functools.partial(summary_kernel, states, ranked), "scan_summary", group,
        [(projected, 0), (wdt, None), (vectors, None), (u_f, 0), (cut, 0), (a_mat, None)],
        [(vec, F32, 0), (vec, F32, 0), (seg_states, F32, 0),
         (seg_sums, F32, 0), (dev_states, BF16, 0), (dev_sums, F32, 0)],
        [spread_vmem, lane_vmem, lane_vmem, state_vmem], 10,
    )
    all_h, all_s = carry([h_dev, s_dev], 3, 10)
    dma = pltpu.SemaphoreType.DMA
    y_full, gated, mix_terms, e_in = call(
        functools.partial(output_kernel, group, states, ranked), "scan_output", group,
        [(projected, 0), (step_size, 0), (u_f, 0), (cut, 0), (a_mat, None), (h_in, 0),
         (s_in, 0), (all_h, 1), (all_s, 1), (z, 0), (vectors, None), (wout, None)],
        [(vec, F32, 0), (vec, BF16, 0), ((group, length, width), BF16, ANY), (dev_states, F32, 0)],
        [spread_vmem, spread_vmem, lane_vmem, lane_vmem, pltpu.VMEM((group, length, width), BF16),
         dma((group - 1,)), dma((group - 1,)), dma], 27, 4, VMEM_LIMIT,
        lambda s: lax.rem(lax.axis_index("wa") + 1 + s, group),
    )

    row_f = (length, width)
    grad_experts, result, d_h1, d_mix_own, grad_router, grad_gain_moe, out_sums, mix_sum = middle(
        experts, mix_terms, tokens[0], gains, router, routes[0].T, keep_mask, out_grad[0], expert_w, 8, 5, 85
    )
    share_experts = lax.psum_scatter(grad_experts, "ctx", scatter_dimension=0, tiled=True)

    d_y, d_z, grad_skip, f_in, t_in, f_dev, d_mix = call(
        functools.partial(gate_back_kernel, group, states, ranked + states), "gate_back", group,
        [(d_mix_own, ANY), (wout, None), (y_full, 0), (z, 0), (u_f, 0), (projected, 0), (step_size, 0),
         (cut, 0), (a_mat, None)],
        [(vec, F32, 0), ((group, rows, padded), BF16, 0), ((1, padded), F32, None),
         (seg_states, F32, 0), (seg_sums, F32, 0), (dev_states, BF16, 0), ((group, length, width), BF16, 0)],
        [spread_vmem, lane_vmem, state_vmem, pltpu.VMEM((group, length, width), BF16),
         dma((group - 1,)), dma((group - 1,)), dma], 28, 7, VMEM_LIMIT,
        lambda s: lax.rem(lax.axis_index("wa") + group - s, group),
    )
    flat_n1 = n1.reshape(group * rows, width)
    zo_shape = (ring // 2, 2, in_rows, 2 * padded)
    (grad_zo,) = call(
        functools.partial(pack_zo_kernel, ring, in_rows, local), "pack_zo", 1,
        [(flat_n1, None), (d_z.reshape(group * rows, padded), None),
         (d_mix.reshape(group * length, width), None), (gated.reshape(group * length, padded), None)],
        [(zo_shape, BF16, None)], [], 5,
    )
    all_f, pair_zo = carry([f_dev], 8, 10, grad_zo)
    zo_half = pltpu.VMEM((ring // 2, in_rows, 2 * padded), BF16)
    dma = pltpu.SemaphoreType.DMA
    d_part, d_u, grad_dt, grad_step_bias, grad_a, chunk_zo = call(
        functools.partial(scan_back_kernel, states, ranked), "scan_back", group,
        [(projected, 0), (step_size, 0), (sig, 0), (u_f, 0), (cut, 0), (d_y, 0),
         (a_mat, None), (vectors, None), (wdt, None), (h_in, 0), (s_in, 0), (e_in, 0), (f_in, 0),
         (t_in, 0), (all_f, 1), (all_s, 1), (grad_zo, ANY), (pair_zo, ANY)],
        [((group, length, columns), BF16, 0), (vec, F32, 0), ((columns, padded), F32, None),
         ((1, padded), F32, None), ((states, SEG, padded), F32, None), ((in_rows, 2 * padded), BF16, None)],
        [spread_vmem, spread_vmem, spread_vmem, f32_vmem(length + SEG, states * LANE), spread_vmem,
         spread_vmem, lane_vmem, lane_vmem, lane_vmem, state_vmem,
         zo_half, zo_half, pltpu.VMEM((ring // 2 - 1, in_rows, 2 * padded), BF16),
         dma((2,)), dma((ring // 2 - 1,)), dma((ring // 2 - 1,))], 34, 12,
    )
    d_projected = sum_all(d_part, 9, 11)
    d_x, d_n1_part, grad_conv, grad_x, gain_terms = call(
        functools.partial(conv_back_kernel, taps, documents), "conv_back", group,
        [(place_s, SMEM), (docs, SMEM), (d_projected, 0), (wproj, None), (d_u, 0), (pre_conv, 0),
         (ext, 0), (u, 0), (conv, None), (d_z, 0), (proj_in, of_x), (proj_in, of_z), (n1, 0)],
        [((group, rows, padded), BF16, 0), ((group, rows, width), BF16, 0),
         ((SEG, padded), F32, None), ((columns, padded), F32, None), ((1, width), F32, None)],
        [f32_vmem((taps - 1) * SEG + length, LANE)], 10,
    )
    small_all = columns + up_to(ranked, SEG) + states + 3 * SEG
    small_each = up_to(-(-small_all // ring), SEG)
    small_rows = up_to(small_each, 16)
    (packed,) = call(
        functools.partial(pack_rest_kernel, ring, in_rows, small_rows, group, experts, ranked),
        "pack_rest", 1,
        [(mine_s, SMEM), (flat_n1, None), (d_x.reshape(group * rows, padded), None), (grad_x, None),
         (grad_dt, None), (grad_a, None), (a_mat, None), (grad_conv, None), (grad_step_bias, None),
         (grad_skip, None), (gain_terms, None), (gains, None), (grad_gain_moe, None),
         (grad_router, None), (out_sums, None), (mix_sum, None)],
        [((ring // 2, 2, in_rows + small_rows + 16, padded), BF16, None)],
        [f32_vmem(ring * small_each, padded), f32_vmem(SEG, width)], 5,
    )
    done, d_n1_terms, d_edges = finish(packed, chunk_zo, d_n1_part, in_rows, small_rows, 11)
    blocks = width // in_rows
    of_rows = lambda shape: pl.BlockSpec(
        (shape[0] // blocks, shape[1]), lambda i: (jnp.minimum(i, blocks - 1), 0)
    )
    unpacked = call(
        functools.partial(
            unpack_kernel, ring, group, in_rows, small_rows, experts, states, ranked, taps,
            float(length * ring * width),
        ),
        "unpack", ring,
        [(mine_s, SMEM), (done, 0), (share_experts, None), (last_s, SMEM), (d_n1_terms, None),
         (d_edges, None), (tokens[0], None), (gains, None), (d_h1, None), (result, None)],
        [((width, 2 * local), F32, of_rows), ((local, width), F32, of_rows),
         ((width, w_down.shape[1]), F32, None), ((w_down.shape[1], width), F32, None),
         ((taps, local), F32, None), ((w_x.shape[1], local), F32, None), ((ranked, local), F32, None),
         ((states, local), F32, None), ((2 * SEG, padded), F32, None), ((1, LANE), F32, None),
         (row_f, F32, None), (row_f, F32, None)],
        [f32_vmem(ring * small_each, padded), f32_vmem(SEG, padded), f32_vmem(length, width), order_vmem],
        9,
    )
    share_in, share_out, share_up, share_down, g_taps, g_wx, g_wdt, g_a, vecs, stats, input_grad, layer_out = unpacked
    fulls, vecs = vecs[:SEG, :share], vecs[SEG:, :local]
    return (
        layer_out[None],
        input_grad[None],
        fulls[0],
        share_in,
        g_taps,
        vecs[0],
        g_wx.T,
        g_wdt,
        vecs[1],
        g_a,
        vecs[2],
        share_out,
        fulls[1],
        fulls[2 : 2 + experts].T,
        share_up[None],
        share_down[None],
        stats[:, :3],
    )


def solution(mesh):
    placed = (
        P("wa", "ctx", None),
        P("wa", "ctx", None),
        P("wa", None),
        P("wa", "ctx", None),
        P("wa", "ctx"),
        P("wa"),
        P(None, "wa"),
        P(None, "wa"),
        P("wa"),
        P("wa", None),
        P(None, "wa"),
        P("wa"),
        P(None, "wa"),
        P("wa"),
        P("wa", None),
        P("wa"),
        P("wa", None),
        P("wa", None, "ctx"),
        P("wa", "ctx", None),
    )
    return jax.shard_map(
        body,
        mesh=mesh,
        in_specs=placed,
        out_specs=(
            P("wa", "ctx", None),
            P("wa", "ctx", None),
            P("wa"),
            P(None, "wa"),
            P(None, "wa"),
            P("wa"),
            P("wa", None),
            P(None, "wa"),
            P("wa"),
            P(None, "wa"),
            P("wa"),
            P("wa", None),
            P("wa"),
            P("wa", None),
            P("wa", None, "ctx"),
            P("wa", "ctx", None),
            P("wa", None),
        ),
        check_vma=False,
    )
```

```python
import functools

import jax
import jax.numpy as jnp
from jax import lax
from jax.experimental import pallas as pl
from jax.experimental.pallas import tpu as pltpu
from jax.sharding import PartitionSpec as P

EPS = 1e-05
F32 = jnp.float32
BF16 = jnp.bfloat16
SEG = 8
LANE = 128
EDGE = 16
LOG2E = 1.4426950408889634
CUT = 1e30
MESH = pl.DeviceIdType.MESH
VMEM_LIMIT = 24 * 2**20
LARGE_LIMIT = 60 * 2**20


def lasting(us):
    return pl.CostEstimate(
        flops=int(us * 1.1e9), bytes_accessed=int(us * 3.5e6), transcendentals=0
    )


def greet(axis, count):
    me = lax.axis_index(axis)
    barrier = pltpu.get_barrier_semaphore()
    for k in range(1, count):
        pl.semaphore_signal(
            barrier, inc=1, device_id={axis: lax.rem(me + k, count)}, device_id_type=MESH
        )
    pl.semaphore_wait(barrier, count - 1)
    return me


def gather_kernel(axis, count, arrays, *refs):
    srcs, dsts = refs[:arrays], refs[arrays : 2 * arrays]
    send, recv, own = refs[-3:]
    me = greet(axis, count)
    copies = []
    for i in range(arrays):
        for k in range(1, count):
            copy = pltpu.make_async_remote_copy(
                src_ref=srcs[i],
                dst_ref=dsts[i].at[me],
                send_sem=send.at[i, k],
                recv_sem=recv.at[i, k],
                device_id={axis: lax.rem(me + k, count)},
                device_id_type=MESH,
            )
            copy.start()
            copies.append(copy)
    for i in range(arrays):
        local = pltpu.make_async_copy(srcs[i], dsts[i].at[me], own.at[i])
        local.start()
        copies.append(local)
    for copy in copies:
        copy.wait()


def trade_kernel(axis, count, x_ref, o_ref, send, recv, own):
    me = greet(axis, count)
    copies = []
    for k in range(1, count):
        other = lax.rem(me + k, count)
        copy = pltpu.make_async_remote_copy(
            src_ref=x_ref.at[other],
            dst_ref=o_ref.at[me],
            send_sem=send.at[k],
            recv_sem=recv.at[k],
            device_id={axis: other},
            device_id_type=MESH,
        )
        copy.start()
        copies.append(copy)
    local = pltpu.make_async_copy(x_ref.at[me], o_ref.at[me], own)
    local.start()
    local.wait()
    for copy in copies:
        copy.wait()


def trade(x, axis, cid, us):
    count = lax.axis_size(axis)
    return pl.pallas_call(
        functools.partial(trade_kernel, axis, count),
        out_shape=jax.ShapeDtypeStruct(x.shape, x.dtype),
        in_specs=[pl.BlockSpec(memory_space=pl.ANY)],
        out_specs=pl.BlockSpec(memory_space=pl.ANY),
        scratch_shapes=[
            pltpu.SemaphoreType.DMA((count,)),
            pltpu.SemaphoreType.DMA((count,)),
            pltpu.SemaphoreType.DMA,
        ],
        compiler_params=pltpu.CompilerParams(
            collective_id=cid, has_side_effects=True, vmem_limit_bytes=VMEM_LIMIT
        ),
        cost_estimate=lasting(us),
        name=f"trade_{cid}",
    )(x)


def sum_start(mates, x_ref, got, send, recv):
    copies = []
    for k, who in enumerate(mates):
        copy = remote(x_ref.at[who], got.at[k], send.at[k], recv.at[k], {"wa": who})
        copy.start()
        copies.append(copy)
    return copies


def sum_spread(mine, mates, x_ref, got, o_ref, copies, send, recv):
    for copy in copies:
        copy.wait_recv()
    parts = [x_ref.at[mine]] + [got.at[k] for k in range(len(mates))]
    add_rows(o_ref.at[mine], parts, x_ref.shape[1])
    spreads = []
    for k, who in enumerate(mates):
        copy = remote(o_ref.at[mine], o_ref.at[mine], send.at[k], recv.at[k], {"wa": who})
        copy.start()
        spreads.append(copy)
    return spreads


def sum_all_kernel(group, x_ref, o_ref, got, s1, r1, s2, r2):
    greet("wa", group)
    mine, mates = mates_of(group)
    copies = sum_start(mates, x_ref, got, s1, r1)
    spreads = sum_spread(mine, mates, x_ref, got, o_ref, copies, s2, r2)
    for copy in spreads:
        copy.wait()
    for copy in copies:
        copy.wait_send()


def sum_all(x, cid, us):
    group = lax.axis_size("wa")
    vmem = pl.BlockSpec(memory_space=pltpu.VMEM)
    dma = pltpu.SemaphoreType.DMA
    return pl.pallas_call(
        functools.partial(sum_all_kernel, group),
        out_shape=jax.ShapeDtypeStruct(x.shape, x.dtype),
        in_specs=[vmem],
        out_specs=vmem,
        scratch_shapes=[pltpu.VMEM((group - 1,) + x.shape[1:], x.dtype)] + [dma((group - 1,))] * 4,
        compiler_params=pltpu.CompilerParams(
            collective_id=cid, has_side_effects=True, vmem_limit_bytes=VMEM_LIMIT
        ),
        cost_estimate=lasting(us),
        name="sum_all",
    )(x)


def gather_all(xs, axis, cid, us):
    count, arrays = lax.axis_size(axis), len(xs)
    return pl.pallas_call(
        functools.partial(gather_kernel, axis, count, arrays),
        out_shape=[jax.ShapeDtypeStruct((count,) + x.shape, x.dtype) for x in xs],
        in_specs=[pl.BlockSpec(memory_space=pl.ANY)] * arrays,
        out_specs=[pl.BlockSpec(memory_space=pl.ANY)] * arrays,
        scratch_shapes=[
            pltpu.SemaphoreType.DMA((arrays, count)),
            pltpu.SemaphoreType.DMA((arrays, count)),
            pltpu.SemaphoreType.DMA((arrays,)),
        ],
        compiler_params=pltpu.CompilerParams(
            collective_id=cid, has_side_effects=True, vmem_limit_bytes=VMEM_LIMIT
        ),
        cost_estimate=lasting(us),
        name=f"gather_{cid}",
    )(*xs)


def remote(src, dst, send, recv, where):
    return pltpu.make_async_remote_copy(
        src_ref=src, dst_ref=dst, send_sem=send, recv_sem=recv,
        device_id=where, device_id_type=MESH,
    )


def add_rows(out, parts, rows):
    def one(i, _):
        at = pl.ds(pl.multiple_of(i * 16, 16), 16)
        total = parts[0][at, :].astype(F32)
        for part in parts[1:]:
            total = total + part[at, :].astype(F32)
        out[at, :] = total.astype(out.dtype)
        return 0

    lax.fori_loop(0, rows // 16, one, 0)


def neighbours(ring):
    me = lax.axis_index("ctx")
    half = ring // 2
    lane = lax.rem(me, 2)
    chip = me // 2
    peers = [lax.rem(chip + k, half) * 2 + lane for k in range(1, half)]
    return me, chip, lane, me + 1 - 2 * lane, peers


def mates_of(group):
    mine = lax.axis_index("wa")
    return mine, [lax.rem(mine + k, group) for k in range(1, group)]


def hello(barrier, axis, who):
    pl.semaphore_signal(barrier, inc=1, device_id={axis: who}, device_id_type=MESH)


def carry_kernel(ring, arrays, halved, *refs):
    total = arrays + halved
    srcs, dsts = refs[:total], refs[total : 2 * total]
    send, recv, fwd_s, fwd_r, own, half_s, half_r = refs[2 * total :]
    me, chip, lane, pair, peers = neighbours(ring)
    half = ring // 2
    barrier = pltpu.get_barrier_semaphore()
    for who in [pair] + peers:
        hello(barrier, "ctx", who)
    pl.semaphore_wait(barrier, half)
    copies, forwards, local = [], [], []
    for i in range(arrays):
        for k, who in enumerate(peers):
            copies.append(remote(srcs[i], dsts[i].at[me], send.at[i, k], recv.at[i, k], {"ctx": who}))
            copies[-1].start()
    for i in range(arrays):
        forwards.append(remote(srcs[i], dsts[i].at[me], fwd_s.at[i, 0], fwd_r.at[i, 0], {"ctx": pair}))
        forwards[-1].start()
        local.append(pltpu.make_async_copy(srcs[i], dsts[i].at[me], own.at[i]))
        local[-1].start()
    if halved:
        to_pair = remote(srcs[arrays].at[:, 1 - lane], dsts[arrays], half_s, half_r, {"ctx": pair})
        to_pair.start()
        local.append(to_pair)
    for i in range(arrays):
        for k in range(1, half):
            copies[i * (half - 1) + k - 1].wait_recv()
            block = dsts[i].at[lax.rem(chip + half - k, half) * 2 + lane]
            forwards.append(remote(block, block, fwd_s.at[i, k], fwd_r.at[i, k], {"ctx": pair}))
            forwards[-1].start()
    for copy in copies:
        copy.wait_send()
    for copy in forwards + local:
        copy.wait()


def carry(xs, cid, us, halved=None):
    ring, arrays = lax.axis_size("ctx"), len(xs)
    half = ring // 2
    shapes = [((ring,) + x.shape, x.dtype) for x in xs]
    if halved is not None:
        xs = xs + [halved]
        shapes.append((halved.shape[:1] + halved.shape[2:], halved.dtype))
    hbm = pl.BlockSpec(memory_space=pl.ANY)
    dma = pltpu.SemaphoreType.DMA
    return pl.pallas_call(
        functools.partial(carry_kernel, ring, arrays, len(xs) - arrays),
        out_shape=[jax.ShapeDtypeStruct(shape, dtype) for shape, dtype in shapes],
        in_specs=[hbm] * len(xs),
        out_specs=[hbm] * len(xs),
        scratch_shapes=[
            dma((arrays, half - 1)), dma((arrays, half - 1)), dma((arrays, half)), dma((arrays, half)),
            dma((arrays,)), dma, dma,
        ],
        compiler_params=pltpu.CompilerParams(
            collective_id=cid, has_side_effects=True, vmem_limit_bytes=VMEM_LIMIT
        ),
        cost_estimate=lasting(us),
        name=f"carry_{cid}",
    )(*xs)


def finish_kernel(
    ring, group, in_rows, small_rows,
    g_ref, zf_ref, d_ref, o_ref, dt_ref, de_ref,
    from_pair, paired, came, own, zin, tiles, fin, store_s,
    pair_s, pair_r, ctx_s, ctx_r, z_s, z_r, tile_s, tile_r, d_s, d_r, d_own, last_s, last_r, fwd_s, fwd_r,
    edge_s, edge_r,
):
    me, chip, lane, pair, peers = neighbours(ring)
    mine, mates = mates_of(group)
    half = ring // 2
    rows = in_rows + small_rows + 16
    lanes = g_ref.shape[3]
    barrier = pltpu.get_barrier_semaphore()
    for who in [pair] + peers:
        hello(barrier, "ctx", who)
    for who in mates:
        hello(barrier, "wa", who)
    has_next = me < ring - 1
    has_last = me > 0

    @pl.when(has_next)
    def _():
        hello(barrier, "ctx", me + 1)

    @pl.when(has_last)
    def _():
        hello(barrier, "ctx", me - 1)

    around = jnp.where(has_next, 1, 0) + jnp.where(has_last, 1, 0)
    pl.semaphore_wait(barrier, half + group - 1 + around)

    to_pair = remote(g_ref.at[:, 1 - lane], from_pair, pair_s, pair_r, {"ctx": pair})
    to_pair.start()
    small_at = 2 * in_rows + 16
    parts = [
        pl.ds(small_at + small_rows, in_rows), pl.ds(small_at, small_rows),
        pl.ds(0, in_rows), pl.ds(in_rows, in_rows + 16),
    ]
    fin[parts[0]] = zf_ref[:, lanes:]
    stored = []

    def to_all(i):
        src, dst = fin.at[parts[i]], o_ref.at[me, parts[i]]
        copies = []
        for k, who in enumerate(peers):
            copies.append(remote(src, dst, last_s.at[i, k], last_r.at[i, k], {"ctx": who}))
        copies.append(remote(src, dst, fwd_s.at[i, 0], fwd_r.at[i, 0], {"ctx": pair}))
        for copy in copies:
            copy.start()
        stored.append(pltpu.make_async_copy(src, dst, store_s.at[i]))
        stored[-1].start()
        return copies

    def forward(i, copies):
        for k in range(1, half):
            copies[k - 1].wait_recv()
            source = lax.rem(chip + half - k, half) * 2 + lane
            block = o_ref.at[source, parts[i]]
            copy = remote(block, block, fwd_s.at[i, k], fwd_r.at[i, k], {"ctx": pair})
            copy.start()
            copies.append(copy)

    x_to = mine // 2
    z_to = group // 2 + mine // 2
    slot = lax.rem(mine, 2)
    z_ref = zf_ref.at[:, pl.ds(0, lanes)]
    x_ref = own.at[pl.ds(0, in_rows)]
    send_x = remote(x_ref, zin.at[slot], z_s.at[0], z_r.at[slot], {"wa": x_to})
    send_z = remote(z_ref, zin.at[slot], z_s.at[1], z_r.at[slot], {"wa": z_to})
    keep_x = pltpu.make_async_copy(x_ref, zin.at[slot], z_r.at[slot])
    keep_z = pltpu.make_async_copy(z_ref, zin.at[slot], z_r.at[slot])

    @pl.when(z_to != mine)
    def _():
        send_z.start()

    @pl.when(z_to == mine)
    def _():
        keep_z.start()

    cut = d_ref.shape[1] // 32 * 16
    pieces = [pl.ds(0, cut), pl.ds(cut, d_ref.shape[1] - cut)]
    trades = []

    def trade_rows(i):
        for k, who in enumerate(mates):
            copy = remote(
                d_ref.at[who, pieces[i]], dt_ref.at[mine, pieces[i]], d_s.at[i, k], d_r.at[i, k],
                {"wa": who},
            )
            copy.start()
            trades.append(copy)

    trade_rows(0)
    kept = pltpu.make_async_copy(d_ref.at[mine], dt_ref.at[mine], d_own)
    kept.start()

    to_pair.wait_recv()
    scattered = []
    for k, who in enumerate(peers):
        to = lax.rem(chip + k + 1, half)
        add_rows(paired.at[to], [g_ref.at[to, lane], from_pair.at[to]], rows)
        copy = remote(paired.at[to], came.at[k], ctx_s.at[k], ctx_r.at[k], {"ctx": who})
        copy.start()
        scattered.append(copy)
    early = to_all(0)
    add_rows(paired.at[chip], [g_ref.at[chip, lane], from_pair.at[chip]], rows)
    for copy in scattered:
        copy.wait_recv()
    add_rows(own, [paired.at[chip]] + [came.at[k] for k in range(half - 1)], rows)

    @pl.when(x_to != mine)
    def _():
        send_x.start()

    @pl.when(x_to == mine)
    def _():
        keep_x.start()

    tile = pl.ds(in_rows + small_rows, 16)
    spread_tiles = []
    for k, who in enumerate(mates):
        copy = remote(own.at[tile], tiles.at[k], tile_s.at[k], tile_r.at[k], {"wa": who})
        copy.start()
        spread_tiles.append(copy)
    fin[parts[1]] = own[pl.ds(in_rows, small_rows)]
    middle_rows = to_all(1)
    forward(0, early)

    def landed(slot):
        pltpu.make_async_copy(zin.at[slot], zin.at[slot], z_r.at[slot]).wait()
        fin[pl.ds(slot * in_rows, in_rows)] = zin[slot]

    landed(0)
    late = [to_all(2)]
    forward(1, middle_rows)
    for copy in spread_tiles:
        copy.wait_recv()
    add_rows(
        fin.at[pl.ds(2 * in_rows, 16)],
        [own.at[tile]] + [tiles.at[k] for k in range(group - 1)],
        16,
    )
    landed(1)
    late.append(to_all(3))
    trade_rows(1)
    kept.wait()
    forward(2, late[0])
    forward(3, late[1])

    for copy in trades:
        copy.wait_recv()
    edges = dt_ref.at[:, pl.ds(d_ref.shape[1] - EDGE, EDGE)]
    to_last = remote(edges, de_ref, edge_s, edge_r, {"ctx": me - 1})

    @pl.when(has_last)
    def _():
        to_last.start()

    for copies in [early, middle_rows] + late:
        for copy in copies[half - 1 :]:
            copy.wait_recv()

    for copy in stored:
        copy.wait()
    to_pair.wait_send()
    for copy in scattered + spread_tiles + early + middle_rows + late[0] + late[1] + trades:
        copy.wait_send()

    @pl.when(x_to != mine)
    def _():
        send_x.wait_send()

    @pl.when(z_to != mine)
    def _():
        send_z.wait_send()

    @pl.when(has_last)
    def _():
        to_last.wait_send()

    @pl.when(has_next)
    def _():
        to_last.wait_recv()


def finish(g, zf, d, in_rows, small_rows, cid):
    ring, group = lax.axis_size("ctx"), lax.axis_size("wa")
    half = ring // 2
    rows, lanes = g.shape[2:]
    out_rows = 3 * in_rows + small_rows + 16
    vmem = pl.BlockSpec(memory_space=pltpu.VMEM)
    hbm = pl.BlockSpec(memory_space=pl.ANY)
    dma = pltpu.SemaphoreType.DMA
    return pl.pallas_call(
        functools.partial(finish_kernel, ring, group, in_rows, small_rows),
        out_shape=[
            jax.ShapeDtypeStruct((ring, out_rows, lanes), BF16),
            jax.ShapeDtypeStruct(d.shape, d.dtype),
            jax.ShapeDtypeStruct((group, EDGE, d.shape[2]), d.dtype),
        ],
        in_specs=[vmem, vmem, hbm],
        out_specs=[hbm, hbm, hbm],
        scratch_shapes=[
            pltpu.VMEM((half, rows, lanes), BF16),
            pltpu.VMEM((half, rows, lanes), BF16),
            pltpu.VMEM((half - 1, rows, lanes), BF16),
            pltpu.VMEM((rows, lanes), BF16),
            pltpu.VMEM((2, in_rows, lanes), BF16),
            pltpu.VMEM((group - 1, 16, lanes), BF16),
            pltpu.VMEM((out_rows, lanes), BF16),
            dma((4,)), dma, dma,
            dma((half - 1,)), dma((half - 1,)),
            dma((2,)), dma((2,)),
            dma((group - 1,)), dma((group - 1,)),
            dma((2, group - 1)), dma((2, group - 1)), dma,
            dma((4, half - 1)), dma((4, half - 1)),
            dma((4, half)), dma((4, half)),
            dma, dma,
        ],
        compiler_params=pltpu.CompilerParams(
            collective_id=cid, has_side_effects=True, vmem_limit_bytes=VMEM_LIMIT
        ),
        cost_estimate=lasting(60),
        name="finish",
    )(g, zf, d)


def start_kernel(
    ring, group, tok, par, doc, w_ref, tok_o, edge_o, par_o, doc_o, w_o,
    mate_s, mate_r, own_s, edge_s, edge_r, relay_s, relay_r, shift_s, shift_r, out_s, out_r, fwd_s, fwd_r,
):
    me = lax.axis_index("ctx")
    mine = lax.axis_index("wa")
    half = ring // 2
    lane = lax.rem(me, 2)
    chip = me // 2
    pair = me + 1 - 2 * lane
    peers = [lax.rem(chip + k, half) * 2 + lane for k in range(1, half)]
    mates = [lax.rem(mine + k, group) for k in range(1, group)]
    barrier = pltpu.get_barrier_semaphore()
    for who in [pair] + peers:
        pl.semaphore_signal(barrier, inc=1, device_id={"ctx": who}, device_id_type=MESH)
    for who in mates:
        pl.semaphore_signal(barrier, inc=1, device_id={"wa": who}, device_id_type=MESH)
    has_next = me < ring - 1
    has_last = me > 0

    @pl.when(has_next)
    def _():
        pl.semaphore_signal(barrier, inc=1, device_id={"ctx": me + 1}, device_id_type=MESH)

    @pl.when(has_last)
    def _():
        pl.semaphore_signal(barrier, inc=1, device_id={"ctx": me - 1}, device_id_type=MESH)

    around = jnp.where(has_next, 1, 0) + jnp.where(has_last, 1, 0)
    pl.semaphore_wait(barrier, half + group - 1 + around)

    edge = tok.at[pl.ds(tok.shape[0] - EDGE, EDGE)]
    to_next = remote(edge, edge_o.at[mine], edge_s, edge_r, {"ctx": me + 1})

    @pl.when(has_next)
    def _():
        to_next.start()

    kind = mine // (group // 2)
    base = 2 * lax.rem(mine, group // 2)
    for h in range(2):
        where = base + h
        send = remote(
            w_ref.at[h], w_o.at[kind, me], shift_s.at[h], shift_r.at[kind], {"wa": where}
        )
        keep = pltpu.make_async_copy(w_ref.at[h], w_o.at[kind, me], shift_r.at[kind])

        @pl.when(where != mine)
        def _():
            send.start()

        @pl.when(where == mine)
        def _():
            keep.start()

    trades = []
    for i, (src, dst) in enumerate(((par, par_o), (doc, doc_o), (tok, tok_o))):
        for k, who in enumerate(mates):
            copy = remote(src, dst.at[mine], mate_s.at[i, k], mate_r.at[i, k], {"wa": who})
            copy.start()
            trades.append(copy)
        keep = pltpu.make_async_copy(src, dst.at[mine], own_s.at[i])
        keep.start()

    @pl.when(has_last)
    def _():
        to_next.wait_recv()
        for k, who in enumerate(mates):
            remote(
                edge_o.at[mine], edge_o.at[mine], relay_s.at[k], relay_r.at[k], {"wa": who}
            ).start()

    sends = []
    for t in range(2):
        block = w_o.at[t, me]
        pltpu.make_async_copy(block, block, shift_r.at[t]).wait()
        for k, who in enumerate(peers):
            copy = remote(block, block, out_s.at[t, k], out_r.at[t, k], {"ctx": who})
            copy.start()
            sends.append(copy)
        copy = remote(block, block, fwd_s.at[t, 0], fwd_r.at[t, 0], {"ctx": pair})
        copy.start()
        sends.append(copy)
    forwards = []
    for t in range(2):
        for k in range(1, half):
            source = lax.rem(chip + half - k, half) * 2 + lane
            block = w_o.at[t, source]
            pltpu.make_async_copy(block, block, out_r.at[t, k - 1]).wait()
            copy = remote(block, block, fwd_s.at[t, k], fwd_r.at[t, k], {"ctx": pair})
            copy.start()
            forwards.append(copy)
    for t in range(2):
        for k in range(half):
            pltpu.make_async_copy(w_o.at[t, me], w_o.at[t, me], fwd_r.at[t, k]).wait()
    for copy in sends + forwards:
        copy.wait_send()
    for h in range(2):

        @pl.when(base + h != mine)
        def _():
            remote(
                w_ref.at[h], w_o.at[kind, me], shift_s.at[h], shift_r.at[kind], {"wa": mine}
            ).wait_send()

    for copy in trades:
        copy.wait()
    for i, (src, dst) in enumerate(((par, par_o), (doc, doc_o), (tok, tok_o))):
        pltpu.make_async_copy(src, dst.at[mine], own_s.at[i]).wait()

    @pl.when(has_next)
    def _():
        to_next.wait_send()

    @pl.when(has_last)
    def _():
        for k, who in enumerate(mates):
            remote(
                edge_o.at[mine], edge_o.at[mine], relay_s.at[k], relay_r.at[k], {"wa": who}
            ).wait()


def start(tok, par, doc, halves, cid):
    ring, group = lax.axis_size("ctx"), lax.axis_size("wa")
    half = ring // 2
    hbm = pl.BlockSpec(memory_space=pl.ANY)
    dma = pltpu.SemaphoreType.DMA
    outs = [(group,) + a.shape for a in (tok, tok[:EDGE], par, doc)] + [(2, ring) + halves.shape[1:]]
    types = [a.dtype for a in (tok, tok, par, doc, halves)]
    return pl.pallas_call(
        functools.partial(start_kernel, ring, group),
        out_shape=[jax.ShapeDtypeStruct(s, t) for s, t in zip(outs, types)],
        in_specs=[hbm] * 4,
        out_specs=[hbm] * 5,
        scratch_shapes=[
            dma((3, group - 1)), dma((3, group - 1)), dma((3,)),
            dma, dma,
            dma((group - 1,)), dma((group - 1,)),
            dma((2,)), dma((2,)),
            dma((2, half - 1)), dma((2, half - 1)),
            dma((2, half)), dma((2, half)),
        ],
        compiler_params=pltpu.CompilerParams(
            collective_id=cid, has_side_effects=True, vmem_limit_bytes=VMEM_LIMIT
        ),
        cost_estimate=lasting(35),
        name="start",
    )(tok, par, doc, halves)


def pick(rows, states, at):
    shape = (rows, states * LANE)
    lower = (lax.broadcasted_iota(jnp.int32, shape, 0) - at) * LANE
    place = lax.broadcasted_iota(jnp.int32, shape, 1)
    return jnp.where((place >= lower) & (place < lower + LANE), 1.0, 0.0)


def spread(rows, states, at):
    return jnp.dot(rows, pick(rows.shape[1], states, at).astype(BF16), preferred_element_type=F32)


def collected(wide_rows, states, columns, at):
    shape = (states * LANE, columns)
    lower = (lax.broadcasted_iota(jnp.int32, shape, 1) - at) * LANE
    place = lax.broadcasted_iota(jnp.int32, shape, 0)
    ones = jnp.where((place >= lower) & (place < lower + LANE), 1.0, 0.0).astype(BF16)
    coarse = wide_rows.astype(BF16)
    rest = (wide_rows - coarse.astype(F32)).astype(BF16)
    return dot_nn(coarse, ones) + dot_nn(rest, ones)


def position_of(shape, axis, steps):
    row = lax.broadcasted_iota(jnp.int32, shape, axis)
    return (row & (SEG - 1)) * steps + (row >> 3)


def permutation(length):
    shape = (length, length)
    at = position_of(shape, 0, length // SEG)
    return jnp.where(at == lax.broadcasted_iota(jnp.int32, shape, 1), 1.0, 0.0).astype(BF16)


def rolled(value, by):
    return pltpu.roll(value, by % SEG, 0)


def lanes_of(g):
    return pl.ds(pl.multiple_of(g * LANE, LANE), LANE)


def rows_of(j):
    return pl.ds(pl.multiple_of(j * SEG, SEG), SEG)


def wide(ref, n, lanes):
    return jnp.broadcast_to(ref[pl.ds(n, 1), lanes], (SEG, LANE))


def state_cols(n):
    return slice(n * LANE, (n + 1) * LANE)


def dot_nt(a, b):
    return lax.dot_general(a, b, (((1,), (1,)), ((), ())), preferred_element_type=F32)


def dot_tn(a, b):
    return lax.dot_general(a, b, (((0,), (0,)), ((), ())), preferred_element_type=F32)


def dot_nn(a, b):
    return jnp.dot(a, b, preferred_element_type=F32)


def rms_scale(values):
    return lax.rsqrt(jnp.mean(values * values, axis=-1, keepdims=True) + EPS)


def norm_grads(values, scale, gain, d_out):
    unit = values * scale
    d_unit = d_out * gain
    d_values = scale * (d_unit - unit * jnp.mean(d_unit * unit, axis=-1, keepdims=True))
    return d_values, d_out * unit


def silu_slope(v):
    s = jax.nn.sigmoid(v)
    return s * (1.0 + v * (1.0 - s))


def seg_of():
    return lax.broadcasted_iota(jnp.int32, (SEG, LANE), 0)


def lag_masks(place, doc_ref, documents, stream, length, taps):
    at = place * length + position_of((length, LANE), 0, length // SEG)
    masks = [None]
    for lag in range(1, taps):
        cut = None
        for d in range(documents):
            begin = doc_ref[stream, 0, d]
            here = (begin > at - lag) & (begin <= at)
            cut = here if cut is None else cut | here
        masks.append(jnp.where(cut, 0.0, 1.0))
    hit = None
    for d in range(documents):
        here = doc_ref[stream, 0, d] == at
        hit = here if hit is None else hit | here
    return masks, jnp.where(hit, CUT, 0.0)


def enter_kernel(
    taps, documents, place_ref, doc_ref, tok, edge, gain, wx, wz, conv, wproj,
    n1_o, ext_o, pre_o, uf_o, u_o, z_o, part_o, cut_o,
):
    length = tok.shape[1]
    steps = length // SEG
    place = place_ref[0]
    gains = gain[0:1]

    def normal(rows):
        return (rows * rms_scale(rows) * gains).astype(BF16)

    n1_o[0, :length] = normal(dot_nn(permutation(length), tok[0]))
    n1_o[0, length:] = normal(jnp.where(place > 0, edge[0].astype(F32), 0.0))
    inner = dot_nn(n1_o[0], wx[0]).astype(BF16).astype(F32)
    z_o[0] = dot_nn(n1_o[0, :length], wz[0]).astype(BF16)
    masks, cut = lag_masks(place, doc_ref, documents, pl.program_id(0), length, taps)
    cut_o[0] = cut
    seg = seg_of()
    behind = taps - 1
    for g in range(inner.shape[1] // LANE):
        cols = slice(g * LANE, (g + 1) * LANE)
        rows, before = inner[:length, cols], inner[length:, cols]
        parts = []
        for i in range(behind):
            j = steps - behind + i
            last = jnp.broadcast_to(before[EDGE - behind + i : EDGE - behind + i + 1], (SEG, LANE))
            parts.append(jnp.where(seg == 0, last, rolled(rows[j * SEG : (j + 1) * SEG], 1)))
        ext = jnp.concatenate(parts + [rows], axis=0)
        ext_o[0, :, cols] = ext
        pre = conv[taps : taps + 1, cols] + conv[0:1, cols] * rows
        for lag in range(1, taps):
            window = ext[(behind - lag) * SEG : (behind - lag) * SEG + length]
            pre = pre + conv[lag : lag + 1, cols] * window * masks[lag]
        pre_o[0, :, cols] = pre
        u = (pre * jax.nn.sigmoid(pre)).astype(BF16)
        u_o[0, :, cols] = u
        uf_o[0, :, cols] = u.astype(F32)
    part_o[0] = dot_nt(u_o[0], wproj[...]).astype(BF16)


def summary_kernel(
    states, b_at, proj_i, wdt, bias, uf, cut, a_ref,
    step_o, sig_o, hx_ref, sx_ref, hd_o, sd_ref, bb, st_s, dr_s, hd_s,
):
    length, width = step_o.shape[1:]
    groups, steps = width // LANE, length // SEG
    proj = proj_i[0]
    bb[...] = spread(proj, states, b_at)
    pre = dot_nn(proj, wdt[...]) + bias[0:1]
    step_size = jnp.maximum(pre, 0.0) + jnp.log1p(jnp.exp(-jnp.abs(pre)))
    step_o[0] = step_size
    sig_o[0] = jax.nn.sigmoid(pre)
    dr_s[...] = step_size * uf[0]
    for g in range(groups):
        cols = slice(g * LANE, (g + 1) * LANE)
        st_s[:, cols] = step_size[:, cols] + cut[0]
    zero = jnp.zeros((SEG, LANE), F32)
    seg = seg_of()

    def group(g, _):
        lanes = lanes_of(g)
        a = [wide(a_ref, n, lanes) for n in range(states)]
        a_two = [LOG2E * value for value in a]

        def step(j, carry):
            rows = rows_of(j)
            st = st_s[rows, lanes]
            dr = dr_s[rows, lanes]
            new = [carry[0] + st]
            for n in range(states):
                new.append(jnp.exp2(st * a_two[n]) * carry[n + 1] + bb[rows, state_cols(n)] * dr)
            return tuple(new)

        out = lax.fori_loop(0, steps, step, (zero,) * (states + 1), unroll=8)
        total, h = out[0], list(out[1:])
        for k in (1, 2, 4):
            ok = seg >= k
            for n in range(states):
                h[n] = h[n] + jnp.where(ok, jnp.exp(total * a[n]) * rolled(h[n], k), 0.0)
            total = total + jnp.where(ok, rolled(total, k), 0.0)
        ok = seg >= 1
        sx_ref[0, :, lanes] = jnp.where(ok, rolled(total, 1), 0.0)
        sd_ref[0, :, lanes] = total[SEG - 1 : SEG]
        for n in range(states):
            hx_ref[0, n, :, lanes] = jnp.where(ok, rolled(h[n], 1), 0.0)
            hd_s[pl.ds(n, 1), lanes] = h[n][SEG - 1 : SEG]
        return 0

    lax.fori_loop(0, groups, group, 0)
    hd_o[0] = hd_s[...].astype(BF16)


def entering(e_ref, finals, sums, a_ref, place, ahead):
    ring = finals.shape[0]
    e_ref[...] = jnp.zeros_like(e_ref)

    def one(lap, _):
        c = lap if ahead else ring - 1 - lap
        use = (c < place) if ahead else (c > place)

        @pl.when(use)
        def _():
            e_ref[...] = jnp.exp(sums[c, 0] * a_ref[...]) * e_ref[...] + finals[c, 0].astype(F32)

        return 0

    lax.fori_loop(0, ring, one, 0)


def output_kernel(
    group, states, b_at, proj, step_i, uf, cut, a_ref, hx_ref, sx_ref, finals, sums, z, skip, wout,
    y_o, gated_o, terms_o, e_o, bb, cb, st_s, dr_s, mix_s, send, recv, own_s,
):
    at = pl.program_id(0)
    mine = lax.axis_index("wa")
    barrier = pltpu.get_barrier_semaphore()
    goals = [lax.rem(mine + 1 + i, group) for i in range(group - 1)]
    sends = [
        remote(mix_s.at[i], terms_o.at[mine], send.at[i], recv.at[i], {"wa": who})
        for i, who in enumerate(goals)
    ]

    @pl.when(at == 0)
    def _():
        for who in goals:
            hello(barrier, "wa", who)

    length, width = step_i.shape[1:]
    groups, steps = width // LANE, length // SEG
    bb[...] = spread(proj[0], states, b_at)
    cb[...] = spread(proj[0], states, b_at + states)
    e_ref = e_o.at[0]
    entering(e_ref, finals, sums, a_ref, lax.axis_index("ctx"), True)
    dr_s[...] = step_i[0] * uf[0]
    for g in range(groups):
        cols = slice(g * LANE, (g + 1) * LANE)
        st_s[:, cols] = step_i[0, :, cols] + cut[0]

    def lane_group(g, _):
        lanes = lanes_of(g)
        a = [wide(a_ref, n, lanes) for n in range(states)]
        a_two = [LOG2E * value for value in a]
        sx = sx_ref[0, :, lanes]
        first = tuple(
            jnp.exp(sx * a[n]) * wide(e_ref, n, lanes) + hx_ref[0, n, :, lanes]
            for n in range(states)
        )
        gain = wide(skip, 1, lanes)

        def step(j, h):
            rows = rows_of(j)
            st = st_s[rows, lanes]
            dr = dr_s[rows, lanes]
            new = []
            y = gain * uf[0, rows, lanes]
            for n in range(states):
                state = jnp.exp2(st * a_two[n]) * h[n] + bb[rows, state_cols(n)] * dr
                new.append(state)
                y = y + cb[rows, state_cols(n)] * state
            y_o[0, rows, lanes] = y
            return tuple(new)

        lax.fori_loop(0, steps, step, first, unroll=8)
        return 0

    lax.fori_loop(0, groups, lane_group, 0)
    zf = z[0].astype(F32)
    gated = (y_o[0] * (zf * jax.nn.sigmoid(zf))).astype(BF16)
    gated_o[0] = gated
    mix_s[at] = dot_nn(gated, wout[...]).astype(BF16)
    for i, copy in enumerate(sends):

        @pl.when(at == i)
        def _():
            if i == 0:
                pl.semaphore_wait(barrier, group - 1)
            copy.start()

    @pl.when(at == group - 1)
    def _():
        kept = pltpu.make_async_copy(mix_s.at[group - 1], terms_o.at[mine], own_s)
        kept.start()
        for copy in sends + [kept]:
            copy.wait()


def route_kernel(
    experts, terms, tok, gain, router, route, keep, grad,
    h1_o, n2_o, up_o, cols_o, match_o, out_o, sums_o,
):
    length, width = tok.shape
    shift = permutation(length)
    mix = terms[0].astype(F32)
    for w in range(1, terms.shape[0]):
        mix = mix + terms[w].astype(F32)
    h1 = dot_nn(shift, tok[...]) + mix
    h1_o[...] = h1
    n2 = (h1 * rms_scale(h1) * gain[1:2]).astype(BF16)
    n2_o[...] = n2
    logits = dot_nt(n2, router[...])
    lane = lax.broadcasted_iota(jnp.int32, (length, LANE), 1)
    kind = lax.broadcasted_iota(jnp.int32, (LANE, length), 0)
    named = route[...]
    onehot = jnp.where(kind == named, 1.0, 0.0)
    one = lax.broadcasted_iota(jnp.int32, (length, length), 0)
    two = lax.broadcasted_iota(jnp.int32, (length, length), 1)
    earlier = jnp.where(one < two, 1.0, 0.0).astype(BF16)
    before = dot_nn(onehot.astype(BF16), earlier)
    within = jnp.sum(before * onehot, axis=0, keepdims=True)
    slot = named.astype(F32) * (length // 2) + within
    facts = jnp.where(kind == experts, slot, jnp.where(kind == experts + 1, keep[...].astype(F32), onehot))
    facts = dot_nt(shift, facts.astype(BF16))
    onehot = jnp.where(lane < experts, facts, 0.0)
    slot = jnp.sum(jnp.where(lane == experts, facts, 0.0), axis=1, keepdims=True)
    kept = jnp.sum(jnp.where(lane == experts + 1, facts, 0.0), axis=1, keepdims=True)
    sig = jax.nn.sigmoid(jnp.sum(logits * onehot, axis=1, keepdims=True))
    gates = kept * sig
    cols_o[...] = jnp.where(
        lane == experts, gates, jnp.where(lane == experts + 1, gates * (1.0 - sig), onehot)
    )
    up = dot_nn(shift, grad[...])
    up_o[...] = up
    slots = match_o.shape[1]
    spot = lax.broadcasted_iota(jnp.int32, (length, slots), 1).astype(F32)
    match = jnp.where(slot == spot, 1.0, 0.0).astype(BF16)
    match_o[...] = match
    out_o[0] = dot_tn(match, n2).astype(BF16).reshape(out_o.shape[1:])
    out_o[1] = dot_tn(match, (gates * up).astype(BF16)).astype(BF16).reshape(out_o.shape[1:])
    sums_o[...] = jnp.broadcast_to(jnp.sum(mix * mix, keepdims=True), (SEG, LANE))


def pack_kernel(up, down, out):
    width, units = up.shape
    line = lax.broadcasted_iota(jnp.int32, (units, units), 0)
    same = jnp.where(line == lax.broadcasted_iota(jnp.int32, (units, units), 1), 1.0, 0.0)
    out[:, :width] = dot_nt(same.astype(BF16), up[...]).astype(BF16)
    out[:, width:] = down[...]


def prepare_kernel(
    experts, small, own, wx_t, wdt, wout, conv_w, a_log,
    gain_o, router_o, wx_o, wdt_o, wout_o, conv_o, rows_o, a_o, wide_s,
):
    width = wout.shape[1]
    group = small.shape[0]
    share = width // group
    for w in range(group):
        wide_s[:, w * share : (w + 1) * share] = small[w, :, :share].astype(F32)
    gain_o[0:1] = wide_s[SEG - 2 : SEG - 1]
    gain_o[1:2] = wide_s[SEG - 1 : SEG]
    gain_o[2:] = jnp.zeros((SEG - 2, width), F32)
    rows = wide_s[SEG:]
    row = lax.broadcasted_iota(jnp.int32, rows.shape, 0)
    router_o[...] = jnp.zeros_like(router_o)
    router_o[: 2 * SEG] = jnp.concatenate(
        [jnp.where(row < experts, rows, 0.0), jnp.zeros_like(rows)], axis=0
    ).astype(BF16)
    local = wout.shape[0]
    for out, src in ((wx_o, wx_t), (wdt_o, wdt), (a_o, None)):
        out[...] = jnp.zeros_like(out)
        if src is not None:
            out[: src.shape[0], :local] = src[...]
    a_o[...] = jnp.full(a_o.shape, -1.0, F32)
    a_o[:, :local] = -jnp.exp(a_log[...].astype(F32))
    wout_o[...] = jnp.zeros_like(wout_o)
    wout_o[:local] = wout[...]
    conv_o[...] = jnp.zeros_like(conv_o)
    taps = conv_w.shape[0]
    conv_o[:taps, :local] = conv_w[...].astype(F32)
    mine = own[...].astype(F32)
    rows_o[...] = jnp.zeros_like(rows_o)
    for h in range(2):
        cols = slice(h * share, (h + 1) * share)
        conv_o[taps : taps + 1, cols] = mine[h : h + 1, :share]
        rows_o[0:1, cols] = mine[2 + h : 3 + h, :share]
        rows_o[1:2, cols] = mine[4 + h : 5 + h, :share]


def block_rows(value, c, rows):
    low = c * rows
    have = max(0, min(rows, value.shape[0] - low))
    if have == rows:
        return value[low : low + rows]
    blank = jnp.zeros((rows - have, value.shape[1]), value.dtype)
    return blank if have == 0 else jnp.concatenate([value[low : low + have], blank], axis=0)


def pack_zo_kernel(ring, in_rows, local, n1, d_z, d_mix, gated, out):
    width = n1.shape[1]
    lanes = d_z.shape[1]
    grad_z = dot_tn(n1[...], d_z[...])
    grad_o = dot_tn(gated[...], d_mix[...])
    side = jnp.zeros((grad_o.shape[0], lanes - width // 2), F32)
    first = jnp.concatenate([grad_o[:, : width // 2], side], axis=1)
    second = jnp.concatenate([grad_o[:, width // 2 :], side], axis=1)
    rows = in_rows // 2
    for c in range(ring):
        out[c // 2, c % 2, :, :lanes] = block_rows(grad_z, c, in_rows).astype(BF16)
        both = [block_rows(first[:local], c, rows), block_rows(second[:local], c, rows)]
        out[c // 2, c % 2, :, lanes:] = jnp.concatenate(both, axis=0).astype(BF16)


def pack_rest_kernel(
    ring, in_rows, small_rows, group, experts, ranked, mine_ref, n1, d_x, gx, gdt, ga, a_ref, gconv, bias, skip,
    gain_mix, gains, gain_moe, router, out_sums, mix_sum, out, small_s, wide_s,
):
    lanes = d_x.shape[1]
    width = n1.shape[1]
    share = width // group
    grad_x = dot_tn(n1[...], d_x[...])
    small_s[...] = jnp.zeros_like(small_s)
    at = 0
    grad_a = jnp.sum(ga[...], axis=1) * a_ref[...]
    for part in (gx[...], gdt[:ranked], grad_a, gconv[...]):
        small_s[at : at + part.shape[0]] = part
        at += part.shape[0]
    small_s[at : at + 1] = bias[...]
    small_s[at + SEG : at + SEG + 1] = skip[...]
    wide_s[...] = jnp.zeros_like(wide_s)
    wide_s[0:1] = gain_mix[...] / gains[0:1]
    wide_s[1:2] = gain_moe[...]
    wide_s[2 : 2 + experts] = router[:experts]
    lane = lax.broadcasted_iota(jnp.int32, (group, LANE), 1)
    row = lax.broadcasted_iota(jnp.int32, (group, LANE), 0)
    stats = jnp.where(
        lane == 0, out_sums[0:1], jnp.where(lane == 1, mix_sum[0:1], jnp.where(lane == 2, out_sums[1:2], 0.0))
    )
    stats = jnp.where(row == mine_ref[0], stats, 0.0)
    stats = jnp.concatenate([stats, jnp.zeros((group, lanes - LANE), F32)], axis=1)
    bottom = jnp.zeros((16 - 2 * group, lanes), F32)
    small_each = small_s.shape[0] // ring
    for c in range(ring):
        if c < 2 + experts:
            full = [wide_s[c : c + 1, w * share : (w + 1) * share] for w in range(group)]
            full = jnp.concatenate(full, axis=0)
            full = jnp.concatenate([full, jnp.zeros((group, lanes - share), F32)], axis=1)
        else:
            full = jnp.zeros((group, lanes), F32)
        small = small_s[c * small_each : (c + 1) * small_each]
        blank = jnp.zeros((small_rows - small_each, lanes), F32)
        parts = [block_rows(grad_x, c, in_rows), small]
        if small_rows > small_each:
            parts.append(blank)
        rows = jnp.concatenate(parts + [full, stats, bottom], axis=0)
        out[c // 2, c % 2] = rows.astype(BF16)


def store_in_order(out, rows, order_s):
    steps = rows.shape[0] // SEG
    for g in range(rows.shape[1] // LANE):
        cols = slice(g * LANE, (g + 1) * LANE)
        for j in range(steps):
            order_s[g, pl.ds(j, SEG, stride=steps), :] = rows[j * SEG : (j + 1) * SEG, cols]
        out[:, cols] = order_s[g]


def input_gradient(taps, last_ref, terms, edges, tok, gain, dh, out_o, dn_s, order_s):
    length = tok.shape[0]
    steps = length // SEG
    behind = taps - 1
    total = terms[0, :length].astype(F32)
    edge = edges[0].astype(F32)
    for w in range(1, terms.shape[0]):
        total = total + terms[w, :length].astype(F32)
        edge = edge + edges[w].astype(F32)
    edge = jnp.where(last_ref[0] > 0, 0.0, edge)
    dn_s[...] = total
    seg = lax.broadcasted_iota(jnp.int32, (SEG, tok.shape[1]), 0)
    for i in range(behind):
        j = pl.ds((steps - behind + i) * SEG, SEG)
        row = EDGE - behind + i
        came = jnp.broadcast_to(edge[row : row + 1], seg.shape)
        dn_s[j, :] += jnp.where(seg == SEG - 1, came, 0.0)
    x = dot_nn(permutation(length), tok[...])
    d_x, _ = norm_grads(x, rms_scale(x), gain[0:1], dn_s[...])
    result = dh[...] + d_x
    store_in_order(out_o, result, order_s)


def unpack_kernel(
    ring, group, in_rows, small_rows, experts, states, ranked, taps, denom, mine_ref, done, up_down,
    last_ref, terms, edges, tok, gain, dh, res,
    in_o, out_o, up_o, down_o, taps_o, wx_o, wdt_o, a_o, vec_o, stat_o, grad_o, layer_o,
    small_s, full_s, dn_s, order_s,
):
    c = pl.program_id(0)
    width = in_o.shape[1]

    @pl.when(c == 1)
    def _():
        store_in_order(layer_o, res[...], order_s)
        input_gradient(taps, last_ref, terms, edges, tok, gain, dh, grad_o, dn_s, order_s)

    local = width // 2
    small_each = small_s.shape[0] // ring
    base = 2 * in_rows

    @pl.when(c == 0)
    def _():
        line = lax.broadcasted_iota(jnp.int32, (width, width), 0)
        same = jnp.where(line == lax.broadcasted_iota(jnp.int32, (width, width), 1), 1.0, 0.0)
        up_o[...] = dot_nt(same.astype(BF16), up_down[:, :width])
        down_o[...] = up_down[:, width:].astype(F32)
        full_s[...] = jnp.zeros_like(full_s)

    @pl.when(c * in_rows < width)
    def _():
        rows = done[0, :base, :].astype(F32)
        in_o[...] = jnp.concatenate([rows[:in_rows, :local], rows[in_rows:, :local]], axis=1)
        low = base + 16 + small_rows
        rows = done[0, low : low + in_rows, :].astype(F32)
        half = in_rows // 2
        out_o[...] = jnp.concatenate([rows[:half, :local], rows[half:, :local]], axis=1)

    small = done[0, base + 16 : base + 16 + small_rows, :].astype(F32)
    small_s[pl.ds(pl.multiple_of(c * small_each, SEG), small_each), :] = small[:small_each]
    tile = done[0, base : base + 16, :].astype(F32)
    row = lax.broadcasted_iota(jnp.int32, tile.shape, 0)
    own = jnp.sum(jnp.where(row == mine_ref[0], tile, 0.0), axis=0, keepdims=True)
    spot = lax.broadcasted_iota(jnp.int32, full_s.shape, 0)
    full_s[...] += jnp.where(spot == c, own, 0.0)

    @pl.when(c == 0)
    def _():
        sums = jnp.sum(jnp.where(row == group + mine_ref[0], tile, 0.0), axis=0, keepdims=True)
        stat_o[...] = jnp.sqrt(sums[:, :LANE] / denom)

    @pl.when(c == ring - 1)
    def _():
        at = 0
        wx_o[...] = small_s[: wx_o.shape[0], :local]
        at += up_to(wx_o.shape[0], LANE)
        wdt_o[...] = small_s[at : at + ranked, :local]
        at += ranked
        a_o[...] = small_s[at : at + states, :local]
        at += states
        taps_o[...] = small_s[at : at + taps, :local]
        vec_o[:SEG] = full_s[...]
        vec_o[SEG : SEG + 1] = small_s[at + taps : at + taps + 1]
        at += SEG
        vec_o[SEG + 1 : SEG + 2] = small_s[at : at + 1]
        vec_o[SEG + 2 : SEG + 3] = small_s[at + SEG : at + SEG + 1]


def middle_kernel(
    experts, group, chunks,
    mix_ref, tok, gain, router, route, keep, grad, w_ref,
    g_ref, layer_o, dh_o, dmix_o, router_o, gain_o, sums_o, mix_o,
    layer_s, dh_s, dmix_s, leave_sem,
    h1_s, n2_s, up_s, cols_s, match_s, x_ref, r_ref,
    got, w_s, g_s, act_s, slope_s, pre_s, acc, out_s,
    w_sem, g_sem, s1, r1, own1, s2, r2, own2,
):
    mine, mates = mates_of(group)
    count, width = x_ref.shape[2:]
    slots = group * count
    block = w_ref.shape[0] // chunks

    def load(t):
        at = pl.ds(pl.multiple_of(lax.rem(t, chunks) * block, block), block)
        slot = lax.rem(t, 2)
        return pltpu.make_async_copy(w_ref.at[at], w_s.at[slot], w_sem.at[slot])

    load(0).start()
    greet("wa", group)
    route_kernel(
        experts, mix_ref, tok, gain, router, route, keep, grad,
        h1_s, n2_s, up_s, cols_s, match_s, x_ref, mix_o,
    )
    sent = []
    for h in range(2):
        for k, who in enumerate(mates):
            copy = remote(x_ref.at[h, who], got.at[h, mine], s1.at[h, k], r1.at[h, k], {"wa": who})
            copy.start()
            sent.append(copy)
        pltpu.make_async_copy(x_ref.at[h, mine], got.at[h, mine], own1.at[h]).start()

    def arrived(h):
        pltpu.make_async_copy(x_ref.at[h, mine], got.at[h, mine], own1.at[h]).wait()
        for copy in sent[h * len(mates) : (h + 1) * len(mates)]:
            copy.wait_recv()
        return got[h].reshape(slots, width)

    def chunk(i):
        return pl.ds(pl.multiple_of(i * block, block), block)

    def returned(h):
        out_s[h] = acc[...].astype(BF16).reshape(group, count, width)
        for k, who in enumerate(mates):
            copy = remote(out_s.at[h, who], r_ref.at[h, mine], s2.at[h, k], r2.at[h, k], {"wa": who})
            copy.start()
            sent.append(copy)
        pltpu.make_async_copy(out_s.at[h, mine], r_ref.at[h, mine], own2.at[h]).start()

    rows = arrived(0)
    acc[...] = jnp.zeros_like(acc)

    def forward(i, _):
        load(i).wait()
        load(i + 1).start()
        w = w_s.at[lax.rem(i, 2)]
        hidden = dot_nt(w[:, :width], rows)
        c = 0.7978845608
        t = jnp.tanh(c * (hidden + 0.044715 * hidden * hidden * hidden))
        act = (0.5 * hidden * (1.0 + t)).astype(BF16)
        act_s[chunk(i), :] = act
        slope_s[chunk(i), :] = 0.5 * (1.0 + t) + 0.5 * hidden * (1.0 - t * t) * c * (
            1.0 + 3.0 * 0.044715 * hidden * hidden
        )
        acc[...] += dot_tn(act, w[:, width:])
        return 0

    lax.fori_loop(0, chunks, forward, 0)
    returned(0)
    d_out = arrived(1)
    acc[...] = jnp.zeros_like(acc)

    def backward(i, _):
        load(chunks + i).wait()

        @pl.when(i < chunks - 1)
        def _():
            load(chunks + i + 1).start()

        w = w_s.at[lax.rem(chunks + i, 2)]
        d_pre = (dot_nt(w[:, width:], d_out) * slope_s[chunk(i), :]).astype(BF16)
        pre_s[chunk(i), :] = d_pre
        acc[...] += dot_tn(d_pre, w[:, :width])
        return 0

    lax.fori_loop(0, chunks, backward, 0)
    returned(1)

    def store(i):
        slot = lax.rem(i, 2)
        return pltpu.make_async_copy(g_s.at[slot], g_ref.at[chunk(i)], g_sem.at[slot])

    def gradients(i, _):
        @pl.when(i >= 2)
        def _():
            store(i - 2).wait()

        g = g_s.at[lax.rem(i, 2)]
        g[:, :width] = dot_nn(pre_s[chunk(i), :], got[0].reshape(slots, width)).astype(BF16)
        g[:, width:] = dot_nn(act_s[chunk(i), :], got[1].reshape(slots, width)).astype(BF16)
        store(i).start()
        return 0

    lax.fori_loop(0, chunks, gradients, 0)
    store(chunks - 2).wait()
    store(chunks - 1).wait()
    for h in range(2):
        pltpu.make_async_copy(out_s.at[h, mine], r_ref.at[h, mine], own2.at[h]).wait()
    for copy in sent[: 2 * len(mates)]:
        copy.wait_send()
    for copy in sent[2 * len(mates) :]:
        copy.wait()
    combine_kernel(
        experts, r_ref, match_s, h1_s, n2_s, up_s, cols_s, gain, router,
        layer_s, dh_s, dmix_s, router_o, gain_o, sums_o,
    )
    leaving = [
        pltpu.make_async_copy(src, dst, leave_sem.at[i])
        for i, (src, dst) in enumerate(((dmix_s, dmix_o), (dh_s, dh_o), (layer_s, layer_o)))
    ]
    for copy in leaving:
        copy.start()
    for copy in leaving:
        copy.wait()


def middle(experts, terms, tok, gains, router, route, keep, grad, w, chunks, cid, us):
    group = lax.axis_size("wa")
    units = w.shape[0]
    length, width = tok.shape
    slots = experts * (length // 2)
    block = units // chunks
    dma = pltpu.SemaphoreType.DMA
    hbm = pl.BlockSpec(memory_space=pltpu.HBM)
    vmem = pl.BlockSpec(memory_space=pltpu.VMEM)
    anywhere = pl.BlockSpec(memory_space=pl.ANY)
    two = dma((2, group - 1))
    rows = pltpu.VMEM((2, group, slots // group, width), BF16)
    shapes = [
        (w.shape, BF16), ((length, width), F32), ((length, width), F32), ((length, width), BF16),
        ((LANE, width), F32), ((1, width), F32), ((SEG, LANE), F32), ((SEG, LANE), F32),
    ]
    return pl.pallas_call(
        functools.partial(middle_kernel, experts, group, chunks),
        out_shape=[jax.ShapeDtypeStruct(shape, dtype) for shape, dtype in shapes],
        in_specs=[vmem] * 7 + [hbm],
        out_specs=[hbm] + [anywhere] * 3 + [vmem] * 4,
        scratch_shapes=[
            pltpu.VMEM((length, width), F32), pltpu.VMEM((length, width), F32),
            pltpu.VMEM((length, width), BF16), dma((3,)),
            pltpu.VMEM((length, width), F32),
            pltpu.VMEM((length, width), BF16),
            pltpu.VMEM((length, width), F32),
            pltpu.VMEM((length, LANE), F32),
            pltpu.VMEM((length, slots), BF16),
            rows, rows, rows,
            pltpu.VMEM((2, block, 2 * width), BF16),
            pltpu.VMEM((2, block, 2 * width), BF16),
            pltpu.VMEM((units, slots), BF16),
            pltpu.VMEM((units, slots), F32),
            pltpu.VMEM((units, slots), BF16),
            pltpu.VMEM((slots, width), F32),
            rows,
            dma((2,)), dma((2,)),
            two, two, dma((2,)), two, two, dma((2,)),
        ],
        compiler_params=pltpu.CompilerParams(
            collective_id=cid, has_side_effects=True, vmem_limit_bytes=VMEM_LIMIT + 20 * 2**20
        ),
        cost_estimate=lasting(us),
        name="middle",
    )(terms, tok, gains, router, route, keep, grad, w)


def combine_kernel(
    experts, back, match, h1_i, n2, up_i, cols, gain, router,
    out_o, dh_o, dmix_o, router_o, gain_o, sums_o,
):
    length, width = h1_i.shape
    h1, up = h1_i[...], up_i[...]
    lane = lax.broadcasted_iota(jnp.int32, (length, LANE), 1)
    facts = cols[...]

    def column(at):
        return jnp.sum(jnp.where(lane == at, facts, 0.0), axis=1, keepdims=True)

    gates, slope = column(experts), column(experts + 1)
    onehot = jnp.where(lane < experts, facts, 0.0)
    slots = match.shape[1]
    rows = dot_nn(match[...], back[0].reshape(slots, width))
    moe = gates * rows
    result = h1 + moe
    out_o[...] = result
    d_gate = jnp.sum(rows * up, axis=1, keepdims=True)
    d_logits = (onehot * (d_gate * slope)).astype(BF16)
    router_o[...] = dot_tn(d_logits, n2[...])
    d_n2 = dot_nn(match[...], back[1].reshape(slots, width)) + dot_nn(d_logits, router[...])
    d_norm, terms = norm_grads(h1, rms_scale(h1), gain[1:2], d_n2)
    gain_o[...] = jnp.sum(terms, axis=0, keepdims=True)
    d_h1 = up + d_norm
    dh_o[...] = d_h1
    dmix_o[...] = d_h1.astype(BF16)
    sums_o[0:1] = jnp.broadcast_to(jnp.sum(result * result, keepdims=True), (1, LANE))
    sums_o[1:2] = jnp.broadcast_to(jnp.sum(moe * moe, keepdims=True), (1, LANE))


def gate_back_kernel(
    count, states, c_at, own, wout, y, z, uf, proj, step_i, cut, a_ref,
    dy_o, dz_o, skip_o, fx_ref, tx_ref, fd_o, mix_o, cb, st_s, fd_s, got, send, recv, own_s,
):
    length, width = step_i.shape[1:]
    groups, steps = width // LANE, length // SEG
    at = pl.program_id(0)
    mine = lax.axis_index("wa")
    goals = [lax.rem(mine + k, count) for k in range(1, count)]
    sends = [
        remote(own, got.at[mine], send.at[k], recv.at[k], {"wa": who}) for k, who in enumerate(goals)
    ]
    kept = pltpu.make_async_copy(own, got.at[mine], own_s)

    @pl.when(at == 0)
    def _():
        kept.start()
        greet("wa", count)
        for copy in sends:
            copy.start()
        kept.wait()

    for k, copy in enumerate(sends):

        @pl.when(at == k + 1)
        def _():
            copy.wait_recv()

    d_mix = got[lax.rem(mine + count - at, count)]
    mix_o[0] = d_mix
    d_gated = dot_nt(d_mix, wout[...])
    zf = z[0].astype(F32)
    dy = d_gated * (zf * jax.nn.sigmoid(zf))
    dy_o[0] = dy
    dz_o[0, :length] = (d_gated * y[0] * silu_slope(zf)).astype(BF16)
    dz_o[0, length:] = jnp.zeros((EDGE, width), BF16)

    @pl.when(pl.program_id(0) == 0)
    def _():
        skip_o[...] = jnp.zeros_like(skip_o)

    skip_o[...] += jnp.sum(dy * uf[0], axis=0, keepdims=True)
    cb[...] = spread(proj[0], states, c_at)
    for g in range(groups):
        cols = slice(g * LANE, (g + 1) * LANE)
        st_s[:, cols] = step_i[0, :, cols] + cut[0]
    zero = jnp.zeros((SEG, LANE), F32)
    seg = seg_of()

    def group(g, _):
        lanes = lanes_of(g)
        a = [wide(a_ref, n, lanes) for n in range(states)]
        a_two = [LOG2E * value for value in a]

        def step(lap, carry):
            rows = rows_of(steps - 1 - lap)
            st = st_s[rows, lanes]
            d = dy_o[0, rows, lanes]
            new = [carry[0] + st]
            for n in range(states):
                new.append(jnp.exp2(st * a_two[n]) * (carry[n + 1] + cb[rows, state_cols(n)] * d))
            return tuple(new)

        out = lax.fori_loop(0, steps, step, (zero,) * (states + 1), unroll=8)
        total, f = out[0], list(out[1:])
        for k in (1, 2, 4):
            ok = seg < SEG - k
            for n in range(states):
                f[n] = f[n] + jnp.where(ok, jnp.exp(total * a[n]) * rolled(f[n], -k), 0.0)
            total = total + jnp.where(ok, rolled(total, -k), 0.0)
        ok = seg < SEG - 1
        tx_ref[0, :, lanes] = jnp.where(ok, rolled(total, -1), 0.0)
        for n in range(states):
            fx_ref[0, n, :, lanes] = jnp.where(ok, rolled(f[n], -1), 0.0)
            fd_s[pl.ds(n, 1), lanes] = f[n][0:1]
        return 0

    lax.fori_loop(0, groups, group, 0)
    fd_o[0] = fd_s[...].astype(BF16)

    @pl.when(at == count - 1)
    def _():
        for copy in sends:
            copy.wait_send()


def scan_back_kernel(
    states, b_at, proj, step_i, sig, uf, cut, dy_i, a_ref, skip, wdt, hx_ref, sx_ref, e_i,
    fx_ref, tx_ref, finals, sums, g_ref, p_ref,
    part_o, du_o, dt_o, bias_o, ga_ref, g_o,
    bb, cb, dec, pri, accb, accc, st_s, dr_s, ds_s, out_s,
    from_pair, kept, came, load, ctx_s, ctx_r,
):
    ring = finals.shape[0]
    half = ring // 2
    _, chip, lane, _, peers = neighbours(ring)
    own_half = pltpu.make_async_copy(g_ref.at[:, lane], kept, load.at[0])
    pair_half = pltpu.make_async_copy(p_ref, from_pair, load.at[1])
    targets = [lax.rem(chip + k, half) for k in range(1, half)]
    scattered = [
        remote(kept.at[to], came.at[k], ctx_s.at[k], ctx_r.at[k], {"ctx": who})
        for k, (to, who) in enumerate(zip(targets, peers))
    ]
    at = pl.program_id(0)

    @pl.when(at == 0)
    def _():
        own_half.start()
        pair_half.start()
        barrier = pltpu.get_barrier_semaphore()
        for who in peers:
            hello(barrier, "ctx", who)
        pl.semaphore_wait(barrier, half - 1)
        own_half.wait()
        pair_half.wait()
        for to, copy in zip(targets, scattered):
            add_rows(kept.at[to], [kept.at[to], from_pair.at[to]], kept.shape[1])
            copy.start()
        add_rows(kept.at[chip], [kept.at[chip], from_pair.at[chip]], kept.shape[1])

    @pl.when(at == pl.num_programs(0) - 1)
    def _():
        for copy in scattered:
            copy.wait()
        add_rows(g_o, [kept.at[chip]] + [came.at[k] for k in range(half - 1)], kept.shape[1])

    length, width = step_i.shape[1:]
    groups, steps = width // LANE, length // SEG
    bb[...] = spread(proj[0], states, b_at)
    cb[...] = spread(proj[0], states, b_at + states)
    accb[...] = jnp.zeros_like(accb)
    accc[...] = jnp.zeros_like(accc)
    entering(out_s, finals, sums, a_ref, lax.axis_index("ctx"), False)
    e_ref = e_i.at[0]
    dr_s[...] = step_i[0] * uf[0]
    for g in range(groups):
        cols = slice(g * LANE, (g + 1) * LANE)
        st_s[:, cols] = step_i[0, :, cols] + cut[0]

    @pl.when(pl.program_id(0) == 0)
    def _():
        ga_ref[...] = jnp.zeros_like(ga_ref)
        dt_o[...] = jnp.zeros_like(dt_o)
        bias_o[...] = jnp.zeros_like(bias_o)

    def group(g, _):
        lanes = lanes_of(g)
        a = [wide(a_ref, n, lanes) for n in range(states)]
        a_two = [LOG2E * value for value in a]
        sx = sx_ref[0, :, lanes]
        first = tuple(
            jnp.exp(sx * a[n]) * wide(e_ref, n, lanes) + hx_ref[0, n, :, lanes]
            for n in range(states)
        )

        def ahead(j, h):
            rows = rows_of(j)
            st = st_s[rows, lanes]
            dr = dr_s[rows, lanes]
            new = []
            for n in range(states):
                decay = jnp.exp2(st * a_two[n])
                dec[rows, state_cols(n)] = decay
                pri[rows, state_cols(n)] = h[n]
                new.append(decay * h[n] + bb[rows, state_cols(n)] * dr)
            return tuple(new)

        last = lax.fori_loop(0, steps, ahead, first, unroll=8)
        end = rows_of(steps)
        for n in range(states):
            pri[end, state_cols(n)] = last[n]
        tx = tx_ref[0, :, lanes]
        flow = tuple(
            jnp.exp(tx * a[n]) * wide(out_s, n, lanes) + fx_ref[0, n, :, lanes]
            for n in range(states)
        )
        gain = wide(skip, 1, lanes)

        def back(lap, f):
            j = steps - 1 - lap
            rows = rows_of(j)
            after = rows_of(j + 1)
            st = step_i[0, rows, lanes]
            dr = dr_s[rows, lanes]
            dy = dy_i[0, rows, lanes]
            new = []
            d_step = None
            d_drive = None
            for n in range(states):
                cols = state_cols(n)
                d = f[n] + cb[rows, cols] * dy
                accc[rows, cols] += pri[after, cols] * dy
                accb[rows, cols] += d * dr
                flowing = dec[rows, cols] * d
                new.append(flowing)
                d_log = flowing * pri[rows, cols]
                ga_ref[n, :, lanes] += d_log * st
                part = d_log * a[n]
                d_step = part if d_step is None else d_step + part
                part = d * bb[rows, cols]
                d_drive = part if d_drive is None else d_drive + part
            ds_s[rows, lanes] = (d_step + d_drive * uf[0, rows, lanes]) * sig[0, rows, lanes]
            du_o[0, rows, lanes] = d_drive * st + dy * gain
            return tuple(new)

        lax.fori_loop(0, steps, back, flow, unroll=8)
        return 0

    lax.fori_loop(0, groups, group, 0)
    d_pre = ds_s[...]
    bias_o[...] += jnp.sum(d_pre, axis=0, keepdims=True)
    d_pre = d_pre.astype(BF16)
    dt_o[...] += dot_tn(proj[0], d_pre)
    columns = part_o.shape[2]
    part = dot_nt(d_pre, wdt[...])
    part = part + collected(accb[...], states, columns, b_at)
    part = part + collected(accc[...], states, columns, b_at + states)
    part_o[0] = part.astype(BF16)


def conv_back_kernel(
    taps, documents, place_ref, doc_ref, proj_i, wproj, du, pre, ext, u, conv, dz, wx, wz, n1,
    dx_o, dn_o, gconv_o, gx_o, gain_o, dext,
):
    length, width = du.shape[1:]
    steps = length // SEG
    behind = taps - 1

    @pl.when(pl.program_id(0) == 0)
    def _():
        gconv_o[...] = jnp.zeros_like(gconv_o)
        gx_o[...] = jnp.zeros_like(gx_o)
        gain_o[...] = jnp.zeros_like(gain_o)

    proj = proj_i[0]
    gx_o[...] += dot_tn(proj, u[0])
    d_u = dot_nn(proj, wproj[...]) + du[0]
    masks, _ = lag_masks(place_ref[0], doc_ref, documents, pl.program_id(0), length, taps)
    seg = seg_of()
    row = lax.broadcasted_iota(jnp.int32, (EDGE, LANE), 0)
    for g in range(width // LANE):
        cols = slice(g * LANE, (g + 1) * LANE)
        d = d_u[:, cols] * silu_slope(pre[0, :, cols])
        gconv_o[taps : taps + 1, cols] += jnp.sum(d, axis=0, keepdims=True)
        dext[...] = jnp.zeros_like(dext)
        for lag in range(taps):
            weighted = d if lag == 0 else d * masks[lag]
            at = pl.ds((behind - lag) * SEG, length)
            gconv_o[lag : lag + 1, cols] += jnp.sum(weighted * ext[0, at, cols], axis=0, keepdims=True)
            dext[at, :] += weighted * conv[lag : lag + 1, cols]
        before = jnp.zeros((EDGE, LANE), F32)
        for i in range(behind):
            head = dext[i * SEG : (i + 1) * SEG]
            j = pl.ds((steps + i) * SEG, SEG)
            dext[j, :] += jnp.where(seg < SEG - 1, rolled(head, -1), 0.0)
            first = jnp.broadcast_to(head[0:1], (EDGE, LANE))
            before = before + jnp.where(row == EDGE - behind + i, first, 0.0)
        dx_o[0, :length, cols] = dext[behind * SEG :].astype(BF16)
        dx_o[0, length:, cols] = before.astype(BF16)
    d_n1 = dot_nt(dx_o[0], wx[0]) + dot_nt(dz[0], wz[0])
    gain_o[...] += jnp.sum(d_n1 * n1[0].astype(F32), axis=0, keepdims=True)
    dn_o[0] = d_n1.astype(BF16)


SMEM = "smem"
ANY = "any"


def by_stream(shape, at, order):
    block = tuple(1 if i == at else n for i, n in enumerate(shape))
    rank = len(shape)

    def index(s):
        return tuple(order(s) if i == at else 0 for i in range(rank))

    return pl.BlockSpec(block, index)


def whole(shape):
    return pl.BlockSpec(shape, lambda s: (0,) * len(shape))


def call(kernel, name, grid, args, outs, scratch, us, cid=None, limit=VMEM_LIMIT, order=lambda s: s):
    arrays, specs = [], []
    for array, at in args:
        arrays.append(array)
        if at == SMEM:
            specs.append(pl.BlockSpec(memory_space=pltpu.SMEM))
        elif at == ANY:
            specs.append(pl.BlockSpec(memory_space=pl.ANY))
        elif callable(at):
            specs.append(at(array.shape))
        else:
            specs.append(whole(array.shape) if at is None else by_stream(array.shape, at, order))
    out_specs = []
    for shape, _, at in outs:
        if callable(at):
            out_specs.append(at(shape))
        elif at == ANY:
            out_specs.append(pl.BlockSpec(memory_space=pl.ANY))
        else:
            out_specs.append(whole(shape) if at is None else by_stream(shape, at, order))
    return pl.pallas_call(
        kernel,
        grid=(grid,),
        out_shape=[jax.ShapeDtypeStruct(shape, dtype) for shape, dtype, _ in outs],
        in_specs=specs,
        out_specs=out_specs,
        scratch_shapes=scratch,
        compiler_params=pltpu.CompilerParams(
            vmem_limit_bytes=limit, collective_id=cid, has_side_effects=cid is not None
        ),
        cost_estimate=lasting(us),
        name=name,
    )(*arrays)


def padded_to(array, width, axis):
    pads = [(0, 0)] * array.ndim
    pads[axis] = (0, width - array.shape[axis])
    return jnp.pad(array, pads)


def up_to(n, multiple):
    return -(-n // multiple) * multiple


def body(
    tokens, out_grad, doc_starts, routes, keep_mask, norm_mix, w_in, conv_w, conv_b, w_x, w_dt,
    dt_bias, a_log, d_skip, w_out, norm_moe, w_router, w_up, w_down,
):
    group = lax.axis_size("wa")
    ring = lax.axis_size("ctx")
    mine = lax.axis_index("wa")
    place = lax.axis_index("ctx")
    length, width = tokens.shape[1:]
    taps, local = conv_w.shape
    states = a_log.shape[0]
    ranked = w_dt.shape[0]
    experts = w_router.shape[1]
    padded = up_to(local, LANE)
    columns = up_to(w_x.shape[1], LANE)
    steps = length // SEG
    rows = length + EDGE
    slots = experts * (length // 2)
    share = norm_mix.shape[0]
    order_vmem = pltpu.VMEM((width // LANE, length, LANE), F32)
    place_s = place.astype(jnp.int32).reshape(1)
    mine_s = mine.astype(jnp.int32).reshape(1)
    last_s = (place == ring - 1).astype(jnp.int32).reshape(1)
    f32_vmem = lambda *shape: pltpu.VMEM(shape, F32)

    (own_experts,) = call(
        pack_kernel, "pack", 1, [(w_up[0], None), (w_down[0], None)],
        [((w_down.shape[1], 2 * width), BF16, None)], [], 3, None, LARGE_LIMIT,
    )
    expert_w = lax.all_gather(own_experts, "ctx", axis=0, tiled=True)

    in_rows = up_to(-(-width // ring), 16)
    blank = ring * in_rows - width
    part_in = jnp.pad(w_in, ((0, blank), (0, 0))) if blank else w_in
    part_in = lax.dynamic_slice_in_dim(part_in, place * in_rows, in_rows, 0)
    halves = jnp.stack([part_in[:, :local], part_in[:, local:]], axis=0)
    halves = jnp.pad(halves, ((0, 0), (0, 0), (0, padded - local)))
    small = jnp.concatenate([conv_b, dt_bias, d_skip, norm_mix, norm_moe], axis=0).reshape(SEG, share)
    small = jnp.concatenate([small, jnp.pad(w_router.T, ((0, SEG - experts), (0, 0)))], axis=0)
    small = padded_to(small, up_to(share, LANE), 1)
    documents = doc_starts.shape[1]
    doc_tile = jnp.pad(doc_starts, ((0, SEG - 1), (0, LANE - documents)))
    all_rows, all_edges, smalls, docs, w_blocks = start(tokens[0], small, doc_tile, halves, 1)
    proj_in = w_blocks.reshape(2, ring * in_rows, padded)[:, :width]
    of_x = lambda shape: pl.BlockSpec((1,) + shape[1:], lambda i: (0, 0, 0))
    of_z = lambda shape: pl.BlockSpec((1,) + shape[1:], lambda i: (1, 0, 0))
    par = (SEG, padded)
    gains, router, wproj, wdt, wout, conv, vectors, a_mat = call(
        functools.partial(prepare_kernel, experts), "prepare", 1,
        [(smalls, None), (small, None), (w_x.T, None), (w_dt, None), (w_out, None), (conv_w, None),
         (a_log, None)],
        [((SEG, width), F32, None), ((LANE, width), BF16, None), ((columns, padded), BF16, None),
         ((columns, padded), BF16, None), ((padded, width), BF16, None), (par, F32, None),
         (par, F32, None), ((states, padded), F32, None)],
        [f32_vmem(2 * SEG, width)], 3,
    )

    vec = (group, length, padded)
    n1, ext, pre_conv, u_f, u, z, part, cut = call(
        functools.partial(enter_kernel, taps, documents), "enter", group,
        [(place_s, SMEM), (docs, SMEM), (all_rows, 0), (all_edges, 0), (gains, None),
         (proj_in, of_x), (proj_in, of_z), (conv, None), (wproj, None)],
        [((group, rows, width), BF16, 0), ((group, (taps - 1) * SEG + length, padded), F32, 0),
         (vec, F32, 0), (vec, F32, 0), (vec, BF16, 0), (vec, BF16, 0),
         ((group, length, columns), BF16, 0), ((group, length, LANE), F32, 0)],
        [], 8,
    )
    projected = sum_all(part, 2, 11)
    seg_states = (group, states, SEG, padded)
    seg_sums = (group, SEG, padded)
    dev_states = (group, states, padded)
    dev_sums = (group, 1, padded)
    spread_vmem = f32_vmem(length, states * LANE)
    lane_vmem = f32_vmem(length, padded)
    state_vmem = f32_vmem(states, padded)
    step_size, sig, h_in, s_in, h_dev, s_dev = call(
        functools.partial(summary_kernel, states, ranked), "scan_summary", group,
        [(projected, 0), (wdt, None), (vectors, None), (u_f, 0), (cut, 0), (a_mat, None)],
        [(vec, F32, 0), (vec, F32, 0), (seg_states, F32, 0),
         (seg_sums, F32, 0), (dev_states, BF16, 0), (dev_sums, F32, 0)],
        [spread_vmem, lane_vmem, lane_vmem, state_vmem], 10,
    )
    all_h, all_s = carry([h_dev, s_dev], 3, 10)
    dma = pltpu.SemaphoreType.DMA
    y_full, gated, mix_terms, e_in = call(
        functools.partial(output_kernel, group, states, ranked), "scan_output", group,
        [(projected, 0), (step_size, 0), (u_f, 0), (cut, 0), (a_mat, None), (h_in, 0),
         (s_in, 0), (all_h, 1), (all_s, 1), (z, 0), (vectors, None), (wout, None)],
        [(vec, F32, 0), (vec, BF16, 0), ((group, length, width), BF16, ANY), (dev_states, F32, 0)],
        [spread_vmem, spread_vmem, lane_vmem, lane_vmem, pltpu.VMEM((group, length, width), BF16),
         dma((group - 1,)), dma((group - 1,)), dma], 27, 4, VMEM_LIMIT,
        lambda s: lax.rem(lax.axis_index("wa") + 1 + s, group),
    )

    row_f = (length, width)
    grad_experts, result, d_h1, d_mix_own, grad_router, grad_gain_moe, out_sums, mix_sum = middle(
        experts, mix_terms, tokens[0], gains, router, routes[0].T, keep_mask, out_grad[0], expert_w, 8, 5, 85
    )
    share_experts = lax.psum_scatter(grad_experts, "ctx", scatter_dimension=0, tiled=True)

    d_y, d_z, grad_skip, f_in, t_in, f_dev, d_mix = call(
        functools.partial(gate_back_kernel, group, states, ranked + states), "gate_back", group,
        [(d_mix_own, ANY), (wout, None), (y_full, 0), (z, 0), (u_f, 0), (projected, 0), (step_size, 0),
         (cut, 0), (a_mat, None)],
        [(vec, F32, 0), ((group, rows, padded), BF16, 0), ((1, padded), F32, None),
         (seg_states, F32, 0), (seg_sums, F32, 0), (dev_states, BF16, 0), ((group, length, width), BF16, 0)],
        [spread_vmem, lane_vmem, state_vmem, pltpu.VMEM((group, length, width), BF16),
         dma((group - 1,)), dma((group - 1,)), dma], 28, 7, VMEM_LIMIT,
        lambda s: lax.rem(lax.axis_index("wa") + group - s, group),
    )
    flat_n1 = n1.reshape(group * rows, width)
    zo_shape = (ring // 2, 2, in_rows, 2 * padded)
    (grad_zo,) = call(
        functools.partial(pack_zo_kernel, ring, in_rows, local), "pack_zo", 1,
        [(flat_n1, None), (d_z.reshape(group * rows, padded), None),
         (d_mix.reshape(group * length, width), None), (gated.reshape(group * length, padded), None)],
        [(zo_shape, BF16, None)], [], 5,
    )
    all_f, pair_zo = carry([f_dev], 8, 10, grad_zo)
    zo_half = pltpu.VMEM((ring // 2, in_rows, 2 * padded), BF16)
    dma = pltpu.SemaphoreType.DMA
    d_part, d_u, grad_dt, grad_step_bias, grad_a, chunk_zo = call(
        functools.partial(scan_back_kernel, states, ranked), "scan_back", group,
        [(projected, 0), (step_size, 0), (sig, 0), (u_f, 0), (cut, 0), (d_y, 0),
         (a_mat, None), (vectors, None), (wdt, None), (h_in, 0), (s_in, 0), (e_in, 0), (f_in, 0),
         (t_in, 0), (all_f, 1), (all_s, 1), (grad_zo, ANY), (pair_zo, ANY)],
        [((group, length, columns), BF16, 0), (vec, F32, 0), ((columns, padded), F32, None),
         ((1, padded), F32, None), ((states, SEG, padded), F32, None), ((in_rows, 2 * padded), BF16, None)],
        [spread_vmem, spread_vmem, spread_vmem, f32_vmem(length + SEG, states * LANE), spread_vmem,
         spread_vmem, lane_vmem, lane_vmem, lane_vmem, state_vmem,
         zo_half, zo_half, pltpu.VMEM((ring // 2 - 1, in_rows, 2 * padded), BF16),
         dma((2,)), dma((ring // 2 - 1,)), dma((ring // 2 - 1,))], 34, 12,
    )
    d_projected = sum_all(d_part, 9, 11)
    d_x, d_n1_part, grad_conv, grad_x, gain_terms = call(
        functools.partial(conv_back_kernel, taps, documents), "conv_back", group,
        [(place_s, SMEM), (docs, SMEM), (d_projected, 0), (wproj, None), (d_u, 0), (pre_conv, 0),
         (ext, 0), (u, 0), (conv, None), (d_z, 0), (proj_in, of_x), (proj_in, of_z), (n1, 0)],
        [((group, rows, padded), BF16, 0), ((group, rows, width), BF16, 0),
         ((SEG, padded), F32, None), ((columns, padded), F32, None), ((1, width), F32, None)],
        [f32_vmem((taps - 1) * SEG + length, LANE)], 10,
    )
    small_all = columns + up_to(ranked, SEG) + states + 3 * SEG
    small_each = up_to(-(-small_all // ring), SEG)
    small_rows = up_to(small_each, 16)
    (packed,) = call(
        functools.partial(pack_rest_kernel, ring, in_rows, small_rows, group, experts, ranked),
        "pack_rest", 1,
        [(mine_s, SMEM), (flat_n1, None), (d_x.reshape(group * rows, padded), None), (grad_x, None),
         (grad_dt, None), (grad_a, None), (a_mat, None), (grad_conv, None), (grad_step_bias, None),
         (grad_skip, None), (gain_terms, None), (gains, None), (grad_gain_moe, None),
         (grad_router, None), (out_sums, None), (mix_sum, None)],
        [((ring // 2, 2, in_rows + small_rows + 16, padded), BF16, None)],
        [f32_vmem(ring * small_each, padded), f32_vmem(SEG, width)], 5,
    )
    done, d_n1_terms, d_edges = finish(packed, chunk_zo, d_n1_part, in_rows, small_rows, 11)
    blocks = width // in_rows
    of_rows = lambda shape: pl.BlockSpec(
        (shape[0] // blocks, shape[1]), lambda i: (jnp.minimum(i, blocks - 1), 0)
    )
    unpacked = call(
        functools.partial(
            unpack_kernel, ring, group, in_rows, small_rows, experts, states, ranked, taps,
            float(length * ring * width),
        ),
        "unpack", ring,
        [(mine_s, SMEM), (done, 0), (share_experts, None), (last_s, SMEM), (d_n1_terms, None),
         (d_edges, None), (tokens[0], None), (gains, None), (d_h1, None), (result, None)],
        [((width, 2 * local), F32, of_rows), ((local, width), F32, of_rows),
         ((width, w_down.shape[1]), F32, None), ((w_down.shape[1], width), F32, None),
         ((taps, local), F32, None), ((w_x.shape[1], local), F32, None), ((ranked, local), F32, None),
         ((states, local), F32, None), ((2 * SEG, padded), F32, None), ((1, LANE), F32, None),
         (row_f, F32, None), (row_f, F32, None)],
        [f32_vmem(ring * small_each, padded), f32_vmem(SEG, padded), f32_vmem(length, width), order_vmem],
        9,
    )
    share_in, share_out, share_up, share_down, g_taps, g_wx, g_wdt, g_a, vecs, stats, input_grad, layer_out = unpacked
    fulls, vecs = vecs[:SEG, :share], vecs[SEG:, :local]
    return (
        layer_out[None],
        input_grad[None],
        fulls[0],
        share_in,
        g_taps,
        vecs[0],
        g_wx.T,
        g_wdt,
        vecs[1],
        g_a,
        vecs[2],
        share_out,
        fulls[1],
        fulls[2 : 2 + experts].T,
        share_up[None],
        share_down[None],
        stats[:, :3],
    )


def solution(mesh):
    placed = (
        P("wa", "ctx", None),
        P("wa", "ctx", None),
        P("wa", None),
        P("wa", "ctx", None),
        P("wa", "ctx"),
        P("wa"),
        P(None, "wa"),
        P(None, "wa"),
        P("wa"),
        P("wa", None),
        P(None, "wa"),
        P("wa"),
        P(None, "wa"),
        P("wa"),
        P("wa", None),
        P("wa"),
        P("wa", None),
        P("wa", None, "ctx"),
        P("wa", "ctx", None),
    )
    return jax.shard_map(
        body,
        mesh=mesh,
        in_specs=placed,
        out_specs=(
            P("wa", "ctx", None),
            P("wa", "ctx", None),
            P("wa"),
            P(None, "wa"),
            P(None, "wa"),
            P("wa"),
            P("wa", None),
            P(None, "wa"),
            P("wa"),
            P(None, "wa"),
            P("wa"),
            P("wa", None),
            P("wa"),
            P("wa", None),
            P("wa", None, "ctx"),
            P("wa", "ctx", None),
            P("wa", None),
        ),
        check_vma=False,
    )
```
